32 devices in a mesh: dp: 4 (over y, x), ctx: 8 (over z, core).
Axes of the slice: x: 2, y: 2, z: 4, core: 2. Of those that a mesh axis runs over, the one named last changes fastest.
Arguments:
- tokens: bfloat16 [8, 1024, 1024], P('dp', 'ctx'), may hold values from -6 to 6
- segments: int32 [8, 1024], P('dp', 'ctx'), may hold values from 0 to 18, as said below
- cotangent: bfloat16 [8, 1024, 1024], P('dp', 'ctx'), may hold values from -6 to 6
- triple_weight: bfloat16 [2, 1024, 3072], P(None, ('dp', 'ctx')), may hold values from -0.1875 to 0.1875
- triple_bias: bfloat16 [2, 3072], P(None, ('dp', 'ctx')), may hold values from -1.75 to 1.75
- proj_weight: bfloat16 [2, 1024, 1024], P(None, ('dp', 'ctx')), may hold values from -1 to 1
- proj_bias: bfloat16 [2, 1024], P(None, ('dp', 'ctx')), may hold values from -1.75 to 1.75
- inner_weight: bfloat16 [2, 1024, 4096], P(None, ('dp', 'ctx')), may hold values from -0.1875 to 0.1875
- inner_bias: bfloat16 [2, 4096], P(None, ('dp', 'ctx')), may hold values from -1.75 to 1.75
- outer_weight: bfloat16 [2, 4096, 1024], P(None, ('dp', 'ctx')), may hold values from -0.09375 to 0.09375
- outer_bias: bfloat16 [2, 1024], P(None, ('dp', 'ctx')), may hold values from -1.75 to 1.75
- first_gain: bfloat16 [2, 1024], P(None, ('dp', 'ctx')), may hold values from 0.25 to 1.75
- first_shift: bfloat16 [2, 1024], P(None, ('dp', 'ctx')), may hold values from -1.75 to 1.75
- second_gain: bfloat16 [2, 1024], P(None, ('dp', 'ctx')), may hold values from 0.25 to 1.75
- second_shift: bfloat16 [2, 1024], P(None, ('dp', 'ctx')), may hold values from -1.75 to 1.75
Outputs:
- output: bfloat16 [8, 1024, 1024], P('dp', 'ctx')
- tokens_grad: bfloat16 [8, 1024, 1024], P('dp', 'ctx')
- triple_weight_grad: float32 [2, 1024, 3072], P(None, ('dp', 'ctx'))
- triple_bias_grad: float32 [2, 2048], P(None, ('dp', 'ctx'))
- value_bias_grad: float32 [2, 1024], P(None, ('dp', 'ctx'))
- proj_weight_grad: float32 [2, 1024, 1024], P(None, ('dp', 'ctx'))
- proj_bias_grad: float32 [2, 1024], P(None, ('dp', 'ctx'))
- inner_weight_grad: float32 [2, 1024, 4096], P(None, ('dp', 'ctx'))
- inner_bias_grad: float32 [2, 4096], P(None, ('dp', 'ctx'))
- outer_weight_grad: float32 [2, 4096, 1024], P(None, ('dp', 'ctx'))
- outer_bias_grad: float32 [2, 1024], P(None, ('dp', 'ctx'))
- first_gain_grad: float32 [2, 1024], P(None, ('dp', 'ctx'))
- first_shift_grad: float32 [2, 1024], P(None, ('dp', 'ctx'))
- second_gain_grad: float32 [2, 1024], P(None, ('dp', 'ctx'))
- second_shift_grad: float32 [2, 1024], P(None, ('dp', 'ctx'))
The draws below stay inside these ranges and needn't reach their ends.
Inputs may be any that keep to these rules, and one draw needn't show every extreme that they name: `segments`: along each sequence the numbers never fall, except for a trailing run of zeros that marks padding; each document is a run of one number; documents before the padding hold 60 to 800 tokens, the last one before the padding possibly fewer, and that last one is numbered 1024 // 60 + 1; of the 2 sequences of each index of dp, one is a single document without padding and the others are packed documents with padding.
All inputs are finite; a program needn't handle non-finite values.
Results may differ from the reference program's by a relative error of at most 0.019.
Values may be sent and summed in bfloat16 or wider, within the bound.
A program may use at most 320 MiB of HBM per device.

```python
import math
import jax
import jax.numpy as jnp
from jax import lax

D = 1024
HD = 64
FF = 4096
ROT = 16
LAYERS = 2
DOC_MIN = 60
DOC_MAX = 800
SEQ_LOC = 2
SEQS = 8
LEN = 1024


def draw_segments(key, part):
    key = jax.random.fold_in(key, 11)
    count = LEN // DOC_MIN + 2
    top_number = LEN // DOC_MIN + 1
    key_len, key_big, key_pad, key_long = jax.random.split(key, 4)
    lengths = jax.random.randint(key_len, (SEQS, count), DOC_MIN, DOC_MAX + 1)
    which_big = jax.random.randint(key_big, (SEQS, 1), 0, 2)
    column = jnp.arange(count, dtype=jnp.int32)[None, :]
    lengths = jnp.where(column == which_big, DOC_MAX, lengths).astype(jnp.int32)
    ends = jnp.cumsum(lengths, axis=1)
    place = jnp.arange(LEN, dtype=jnp.int32)
    ident = 1 + jnp.sum((ends[:, None, :] <= place[None, :, None]).astype(jnp.int32), axis=2)
    padding = jax.random.randint(key_pad, (SEQS, 1), 1, 2 * DOC_MIN)
    inside = place[None, :] < LEN - padding
    last_number = jnp.max(jnp.where(inside, ident, 0), axis=1, keepdims=True)
    ident = ident + (top_number - last_number)
    ident = jnp.where(inside, ident, 0)
    groups = SEQS // SEQ_LOC
    chosen = jax.random.randint(key_long, (groups, 1), 0, SEQ_LOC)
    chosen = (chosen + SEQ_LOC * jnp.arange(groups, dtype=jnp.int32)[:, None]).reshape(-1)
    whole = jnp.any(jnp.arange(SEQS, dtype=jnp.int32)[:, None] == chosen[None, :], axis=1)
    return jnp.where(whole[:, None], top_number, ident).astype(jnp.int32)


def level_of(own_key, shape, pieces, least, largest):
    loudness, own = 1.0, jax.random.fold_in(own_key, 6)
    for position, parts in pieces:
        heights = jnp.exp(jax.random.uniform(jax.random.fold_in(own, position), (parts,), jnp.float32, least / len(pieces), largest / len(pieces)))
        loudness = loudness * jnp.repeat(heights, shape[position] // parts).reshape([-1 if axis == position else 1 for axis in range(len(shape))])
    return loudness


def gaussian(key, shape, spread, reach, shards=(), held_as=jnp.bfloat16):
    values = jax.random.normal(key, shape, jnp.float32) * spread
    if len(shards) > 0:
        values = level_of(key, shape, shards, -0.22, 0.18) * values
    return jnp.clip(values, min=-reach, max=reach).astype(held_as)


def setup_inputs(seed: int = 0) -> dict:
    seeds = jax.random.split(jax.random.key(seed), 16)
    return {
        "tokens": gaussian(seeds[0], (SEQS, LEN, D), 1.0, 6.0, ((0, 4), (1, 8))),
        "segments": draw_segments(jax.random.fold_in(seeds[15], 71), 0),
        "cotangent": gaussian(seeds[2], (SEQS, LEN, D), 1.0, 6.0, ((0, 4), (1, 8))),
        "triple_weight": gaussian(seeds[3], (LAYERS, D, 3 * D), D ** -0.5, 0.1875, ((1, 32),)),
        "triple_bias": gaussian(seeds[4], (LAYERS, 3 * D), 0.3, 1.75, ((1, 32),)),
        "proj_weight": gaussian(seeds[5], (LAYERS, D, D), (D // 32) ** -0.5, 1.0, ((1, 32),)),
        "proj_bias": gaussian(seeds[6], (LAYERS, D), 0.3, 1.75, ((1, 32),)),
        "inner_weight": gaussian(seeds[7], (LAYERS, D, FF), D ** -0.5, 0.1875, ((1, 32),)),
        "inner_bias": gaussian(seeds[8], (LAYERS, FF), 0.3, 1.75, ((1, 32),)),
        "outer_weight": gaussian(seeds[9], (LAYERS, FF, D), FF ** -0.5, 0.09375, ((1, 32),)),
        "outer_bias": gaussian(seeds[10], (LAYERS, D), 0.3, 1.75, ((1, 32),)),
        "first_gain": jnp.clip(1.0 + 0.15 * jax.random.normal(seeds[11], (LAYERS, D), jnp.float32), 0.25, 1.75).astype(jnp.bfloat16),
        "first_shift": gaussian(seeds[12], (LAYERS, D), 0.3, 1.75, ((1, 32),)),
        "second_gain": jnp.clip(1.0 + 0.15 * jax.random.normal(seeds[13], (LAYERS, D), jnp.float32), 0.25, 1.75).astype(jnp.bfloat16),
        "second_shift": gaussian(seeds[14], (LAYERS, D), 0.3, 1.75, ((1, 32),)),
    }


@jax.custom_vjp
def low(v):
    return lax.optimization_barrier(v.astype(jnp.bfloat16)).astype(jnp.float32)

@jax.custom_vjp
def low_back(v):
    return v

def low_keep(v):
    return (low(v), None)

def low_pass(kept, grad):
    return (grad,)

def back_keep(v):
    return (v, None)

def back_low(kept, grad):
    return (low(grad),)
low.defvjp(low_keep, low_pass)
low_back.defvjp(back_keep, back_low)
EPSILON = 1e-05
NEG_LARGE = -1e+30
HIGHEST = lax.Precision.HIGHEST

def layer_norm(hidden, gain_vector, shift_vector):
    centred = hidden - lax.optimization_barrier(jnp.mean(hidden, axis=-1, keepdims=True))
    inverse = lax.rsqrt(lax.optimization_barrier(jnp.mean(centred * centred, axis=-1, keepdims=True)) + EPSILON)
    return centred * inverse * gain_vector + shift_vector

def rotary_tables(positions, half_rot):
    frequency = 10000.0 ** (-(2.0 * jnp.arange(half_rot, dtype=jnp.float32)) / (2 * half_rot))
    angles = positions.astype(jnp.float32)[:, None] * frequency[None, :]
    return (jnp.cos(angles)[:, None, :], jnp.sin(angles)[:, None, :])

def rotate(head_values, cosine, sine_table, direction):
    half_rot = cosine.shape[-1]
    front = head_values[..., :half_rot]
    behind = head_values[..., half_rot:2 * half_rot]
    return jnp.concatenate([front * cosine - direction * behind * sine_table, behind * cosine + direction * front * sine_table, head_values[..., 2 * half_rot:]], axis=-1)

def product(left, right):
    return jnp.dot(left, right, precision=HIGHEST, preferred_element_type=jnp.float32)

def block(hidden, segs, weights):
    triple_matrix, triple_offset, proj_matrix, proj_offset, inner_matrix, inner_offset, outer_matrix, outer_offset, gain_one, shift_one, gain_two, shift_two = weights
    group_size, length, model_width = hidden.shape
    row_count = group_size * length
    head_count = model_width // HD
    positions = jnp.arange(length, dtype=jnp.int32)
    cosine, sine_table = rotary_tables(positions, ROT // 2)
    normed_one = low(layer_norm(hidden, gain_one, shift_one)).reshape(row_count, model_width)
    triple = low_back(product(normed_one, triple_matrix) + triple_offset)
    triple = triple.reshape(group_size, length, 3, head_count, HD)
    queries = low(rotate(triple[:, :, 0], cosine, sine_table, 1.0))
    key_rows = low(rotate(triple[:, :, 1], cosine, sine_table, 1.0))
    value_rows = low(triple[:, :, 2])
    scores = low_back(jnp.einsum('gqhd,gkhd->ghqk', queries, key_rows, precision=HIGHEST) * (1.0 / math.sqrt(HD)))
    causal = positions[None, :] <= positions[:, None]
    same_doc = segs[:, :, None] == segs[:, None, :]
    live = (segs[:, :, None] != 0) | (positions[None, :] == positions[:, None])[None]
    allowed_pairs = (causal[None] & same_doc & live)[:, None]
    attention = low(jax.nn.softmax(jnp.where(allowed_pairs, scores, NEG_LARGE), axis=-1))
    attended = jnp.einsum('ghqk,gkhd->gqhd', attention, value_rows, precision=HIGHEST).reshape(row_count, model_width)
    attended = low(low_back(attended))
    branch_attend = low_back(product(attended, proj_matrix) + proj_offset)
    normed_two = low(layer_norm(hidden, gain_two, shift_two)).reshape(row_count, model_width)
    inner_pre = low_back(product(normed_two, inner_matrix) + inner_offset)
    activated = low(jax.nn.gelu(inner_pre, approximate=False))
    branch_mixer = low_back(product(activated, outer_matrix) + outer_offset)
    return hidden + (branch_attend + branch_mixer).reshape(group_size, length, model_width)

def reference(tokens, segments, cotangent, triple_weight, triple_bias, proj_weight, proj_bias, inner_weight, inner_bias, outer_weight, outer_bias, first_gain, first_shift, second_gain, second_shift):
    params = tuple((item.astype(jnp.float32) for item in (triple_weight, triple_bias, proj_weight, proj_bias, inner_weight, inner_bias, outer_weight, outer_bias, first_gain, first_shift, second_gain, second_shift)))
    seq_count, length, model_width = tokens.shape
    group_size = math.gcd(seq_count, max(1, 4096 // length))
    step_count = seq_count // group_size

    def regroup(array):
        return array.reshape((step_count, group_size) + array.shape[1:])

    def forward(hidden, weights, segs):
        for which_layer in range(LAYERS):
            hidden = block(hidden, segs, tuple((item[which_layer] for item in weights)))
        return hidden

    def step(totals, item):
        hidden, segs, grad_out = item
        result, pull = jax.vjp(lambda start_value, weights: forward(start_value, weights, segs), hidden.astype(jnp.float32), params)
        grad_in, grad_params = pull(grad_out.astype(jnp.float32))
        totals = jax.tree.map(lambda left, right: left + right, totals, grad_params)
        return (totals, (result.astype(jnp.bfloat16), grad_in.astype(jnp.bfloat16)))
    zeros = jax.tree.map(jnp.zeros_like, params)
    totals, (outputs, grads_in) = lax.scan(step, zeros, (regroup(tokens), regroup(segments), regroup(cotangent)))
    split_at = 2 * model_width
    return (outputs.reshape(tokens.shape), grads_in.reshape(tokens.shape), totals[0], totals[1][:, :split_at], totals[1][:, split_at:], totals[2], totals[3], totals[4], totals[5], totals[6], totals[7], totals[8], totals[9], totals[10], totals[11])
```

```python
import functools
import math

import jax
import jax.numpy as jnp
from jax import lax
from jax.experimental import pallas as pl
from jax.experimental.pallas import tpu as pltpu
from jax.sharding import Mesh
from jax.sharding import PartitionSpec as P

HD = 64
ROT = 16
EPSILON = 1e-05
NEG_LARGE = -1e30
MESH = pl.DeviceIdType.MESH
BF16 = jnp.bfloat16
F32 = jnp.float32
VMEM_LIMIT = 60 * 1024 * 1024


def dot(a, b, dims):
    return lax.dot_general(a, b, (dims, ((), ())), preferred_element_type=F32)


NN = ((1,), (0,))
NT = ((1,), (1,))
TN = ((0,), (0,))


def rows_of(b, size):
    return pl.ds(pl.multiple_of(b * size, size), size)


def group_barrier(tn):
    t = lax.axis_index("t")
    zc, co = t // 2, lax.rem(t, 2)
    chips = tn // 2
    sem = pltpu.get_barrier_semaphore()
    peers = [zc * 2 + 1 - co] + [lax.rem(zc + k, chips) * 2 + co for k in range(1, chips)]
    for p in peers:
        pl.semaphore_signal(sem, inc=1, device_id={"t": p}, device_id_type=MESH)
    pl.semaphore_wait(sem, len(peers))


class Spread:
    def __init__(self, tn, buf, size, ssem, fsem, rsem):
        self.tn, self.buf, self.size = tn, buf, size
        self.ssem, self.fsem, self.rsem = ssem, fsem, rsem
        self.t = lax.axis_index("t")
        self.zc, self.co = self.t // 2, lax.rem(self.t, 2)
        self.chips = tn // 2

    def copy(self, block, send, to):
        ref = self.buf.at[rows_of(block, self.size)]
        return pltpu.make_async_remote_copy(
            ref, ref, send, self.rsem.at[block], device_id={"t": to}, device_id_type=MESH
        )

    def start(self):
        for k in range(1, self.chips):
            chip = lax.rem(self.zc + k, self.chips)
            self.copy(self.t, self.ssem.at[k], chip * 2 + self.co).start()
        self.copy(self.t, self.ssem.at[0], self.zc * 2 + 1 - self.co).start()

    def peer_core(self):
        b = self.zc * 2 + 1 - self.co
        self.copy(b, self.ssem.at[0], b).wait_recv()
        return b

    def same_core(self, k):
        b = lax.rem(self.zc + self.chips - k, self.chips) * 2 + self.co
        self.copy(b, self.fsem.at[k], b).wait_recv()
        self.copy(b, self.fsem.at[k], self.zc * 2 + 1 - self.co).start()
        return b

    def other_core(self, k):
        b = lax.rem(self.zc + self.chips - k, self.chips) * 2 + 1 - self.co
        self.copy(b, self.fsem.at[k], b).wait_recv()
        return b

    def finish(self):
        for k in range(self.chips):
            self.copy(self.t, self.ssem.at[k], self.t).wait_send()
        for k in range(1, self.chips):
            self.copy(self.t, self.fsem.at[k], self.t).wait_send()


class Gather:
    def __init__(self, tn, tocore, fromcore, toici, fromici, sems):
        self.tn = tn
        self.tocore, self.fromcore, self.toici, self.fromici = tocore, fromcore, toici, fromici
        self.cs, self.cr, self.ls, self.lr = sems
        self.t = lax.axis_index("t")
        self.zc, self.co = self.t // 2, lax.rem(self.t, 2)
        self.chips = tn // 2

    def core_copy(self, chip):
        return pltpu.make_async_remote_copy(
            self.tocore.at[chip],
            self.fromcore.at[chip],
            self.cs.at[chip],
            self.cr.at[chip],
            device_id={"t": self.zc * 2 + 1 - self.co},
            device_id_type=MESH,
        )

    def link_copy(self, chip, slot):
        return pltpu.make_async_remote_copy(
            self.toici.at[chip],
            self.fromici.at[slot],
            self.ls.at[chip],
            self.lr.at[slot],
            device_id={"t": chip * 2 + self.co},
            device_id_type=MESH,
        )

    def send_core(self, chip):
        self.core_copy(chip).start()

    def send_link(self, chip):
        self.core_copy(chip).wait_recv()
        self.toici[chip] = (self.toici[chip].astype(F32) + self.fromcore[chip].astype(F32)).astype(BF16)
        self.link_copy(chip, self.zc).start()

    def total(self):
        self.core_copy(self.zc).wait_recv()
        value = self.fromcore[self.zc].astype(F32)
        for k in range(1, self.chips):
            chip = lax.rem(self.zc + k, self.chips)
            self.link_copy(chip, chip).wait_recv()
            value = value + self.fromici[chip].astype(F32)
        return value

    def finish(self):
        for chip in range(self.chips):
            self.core_copy(chip).wait_send()
        for k in range(1, self.chips):
            chip = lax.rem(self.zc + k, self.chips)
            self.link_copy(chip, self.zc).wait_send()


def norm_stats(x):
    mean = jnp.mean(x, axis=-1, keepdims=True)
    centred = x - mean
    inverse = lax.rsqrt(jnp.mean(centred * centred, axis=-1, keepdims=True) + EPSILON)
    return centred * inverse, inverse


def widen(tab, width):
    return jnp.concatenate([tab] * (width // tab.shape[1]), axis=1)


def turn(x, cos, sa, sb, sign):
    width = x.shape[1]
    cos, sa, sb = widen(cos, width), widen(sa, width), widen(sb, width)
    side = pltpu.roll(x, width - ROT // 2, 1) * sa + pltpu.roll(x, ROT // 2, 1) * sb
    return x * cos + sign * side


def head_masks(width, dtype):
    lane = lax.broadcasted_iota(jnp.int32, (1, width), 1) // HD
    return [(lane == h).astype(F32).astype(dtype) for h in range(width // HD)]


def pair_bias(qb, kb, size, segcol, segrow):
    qpos = lax.broadcasted_iota(jnp.int32, (size, size), 0) + qb * size
    kpos = lax.broadcasted_iota(jnp.int32, (size, size), 1) + kb * size
    same = segcol[rows_of(qb, size), :] == segrow[:, rows_of(kb, size)]
    return jnp.where(same & (kpos <= qpos), 0.0, NEG_LARGE)


TILE = 256


def forward_kernel(
    tn, size,
    x_ref, wt, wi, wo, wp, vec, bt, bi, segcol, segrow, ctab, satab, sbtab,
    xo_ref, n_ref, q_ref, k_ref, v_ref, o_ref, lse_ref, g_ref, gp_ref,
    keep, tocore, fromcore, toici, fromici, ssem, fsem, rsem, cs, cr, ls, lr,
):
    chips = tn // 2
    width = q_ref.shape[1]
    heads = width // HD
    units = g_ref.shape[1]
    group_barrier(tn)
    spread = Spread(tn, n_ref, size, ssem, fsem, rsem)
    gather = Gather(tn, tocore, fromcore, toici, fromici, (cs, cr, ls, lr))
    t, zc, co = spread.t, spread.zc, spread.co
    own_n, _ = norm_stats(x_ref[...])
    n_ref[rows_of(t, size), :] = own_n.astype(BF16)
    spread.start()

    def project(b):
        rows = rows_of(b, size)
        n = n_ref[rows, :].astype(F32)
        h1 = (n * vec[0:1, :] + vec[1:2, :]).astype(BF16)
        h2 = (n * vec[2:3, :] + vec[3:4, :]).astype(BF16)
        cos, sa, sb = ctab[rows, :], satab[rows, :], sbtab[rows, :]
        q = dot(h1, wt[:, 0:width], NN) + bt[:, 0:width]
        q_ref[rows, :] = (turn(q, cos, sa, sb, 1.0).astype(BF16).astype(F32) * (1.0 / math.sqrt(HD))).astype(BF16)
        k = dot(h1, wt[:, width : 2 * width], NN) + bt[:, width : 2 * width]
        k_ref[rows, :] = turn(k, cos, sa, sb, 1.0).astype(BF16)
        v = dot(h1, wt[:, 2 * width : 3 * width], NN) + bt[:, 2 * width : 3 * width]
        v_ref[rows, :] = v.astype(BF16)

        def mix(j, carry):
            cols = rows_of(j, TILE)
            u = dot(h2, wi[:, cols], NN) + bi[:, cols]
            half = 0.5 + 0.5 * lax.erf(u * (1.0 / math.sqrt(2.0)))
            g_ref[rows, cols] = (u * half).astype(BF16)
            bell = jnp.exp(-0.5 * u * u) * (1.0 / math.sqrt(2.0 * math.pi))
            gp_ref[rows, cols] = (half + u * bell).astype(BF16)
            return carry

        lax.fori_loop(0, units // TILE, mix, 0)

    project(t)
    project(spread.peer_core())
    for i in range(1, chips):
        project(spread.same_core(i))
        project(spread.other_core(i))

    masks = head_masks(width, F32)
    lane = lax.broadcasted_iota(jnp.int32, (1, 128), 1)

    def attend(b):
        rows = rows_of(b, size)
        qb = q_ref[rows, :]
        qs = [qb * masks[h].astype(BF16) for h in range(heads)]

        def step(i, carry):
            peaks, sums, acc = carry
            kb = b - i
            keys = k_ref[rows_of(kb, size), :]
            vals = v_ref[rows_of(kb, size), :]
            bias = pair_bias(b, kb, size, segcol, segrow)
            new_peaks, new_sums = [], []
            scale = jnp.zeros((size, width), F32)
            add = jnp.zeros((size, width), F32)
            for h in range(heads):
                s = dot(qs[h], keys, NT) + bias
                peak = jnp.maximum(peaks[h], jnp.max(s, axis=1, keepdims=True))
                p = jnp.exp(s - peak)
                fade = jnp.exp(peaks[h] - peak)
                new_peaks.append(peak)
                new_sums.append(sums[h] * fade + jnp.sum(p, axis=1, keepdims=True))
                scale = scale + fade * masks[h]
                add = add + dot(p.astype(BF16), vals * masks[h].astype(BF16), NN)
            return tuple(new_peaks), tuple(new_sums), acc * scale + add

        start = (
            tuple(jnp.full((size, 1), NEG_LARGE, F32) for _ in range(heads)),
            tuple(jnp.zeros((size, 1), F32) for _ in range(heads)),
            jnp.zeros((size, width), F32),
        )
        peaks, sums, acc = lax.fori_loop(0, b + 1, step, start)
        scale = jnp.zeros((size, width), F32)
        lse = jnp.zeros((size, 128), F32)
        for h in range(heads):
            scale = scale + (1.0 / sums[h]) * masks[h]
            lse = jnp.where(lane == h, peaks[h] + jnp.log(sums[h]), lse)
        lse_ref[rows, :] = lse
        o_ref[rows, :] = acc * scale

    def partial(b, store):
        attend(b)
        rows = rows_of(b, size)

        def part(j, carry):
            cols = rows_of(j, TILE)
            store(cols, dot(g_ref[rows, :], wo[:, cols], NN) + dot(o_ref[rows, :].astype(BF16), wp[:, cols], NN))
            return carry

        lax.fori_loop(0, x_ref.shape[1] // TILE, part, 0)

    def into(ref, chip):
        def store(cols, value):
            ref[chip, :, cols] = value.astype(BF16)

        return store

    def into_keep(cols, value):
        keep[:, cols] = value

    for i in range(1, chips):
        chip = lax.rem(zc + i, chips)
        partial(chip * 2 + 1 - co, into(tocore, chip))
        gather.send_core(chip)
        partial(chip * 2 + co, into(toici, chip))
        gather.send_link(chip)
    partial(zc * 2 + 1 - co, into(tocore, zc))
    gather.send_core(zc)
    partial(t, into_keep)
    xo_ref[...] = x_ref[...] + vec[4:5, :] + keep[...] + gather.total()
    spread.finish()
    gather.finish()


def backward_kernel(
    tn, size,
    dy_ref, x_ref, wt, wi, wo, wp, vec, segcol, segrow, ctab, satab, sbtab,
    n_ref, q_ref, k_ref, v_ref, o_ref, lse_ref, g_ref, gp_ref,
    dx_ref, dwt, dwi, dwo, dwp, dvec, dbt, dbi,
    gb, do, du, dt, dq, dk, dv, dh2, keep,
    tocore, fromcore, toici, fromici, ssem, fsem, rsem, cs, cr, ls, lr,
):
    chips = tn // 2
    width = q_ref.shape[1]
    heads = width // HD
    units = g_ref.shape[1]
    model = x_ref.shape[1]
    group_barrier(tn)
    spread = Spread(tn, gb, size, ssem, fsem, rsem)
    gather = Gather(tn, tocore, fromcore, toici, fromici, (cs, cr, ls, lr))
    t, zc, co = spread.t, spread.zc, spread.co
    own = dy_ref[...].astype(F32).astype(BF16)
    gb[rows_of(t, size), :] = own
    spread.start()
    dvec[...] = jnp.zeros_like(dvec)
    dbt[...] = jnp.zeros_like(dbt)
    dbi[...] = jnp.zeros_like(dbi)
    dvec[4:5, :] = jnp.sum(own.astype(F32), axis=0, keepdims=True)
    dq[...] = jnp.zeros_like(dq)
    dk[...] = jnp.zeros_like(dk)
    dv[...] = jnp.zeros_like(dv)

    def mixer(b):
        rows = rows_of(b, size)
        grad = gb[rows, :]
        do[rows, :] = dot(grad, wp[...], NT).astype(BF16)

        def unit(j, carry):
            cols = rows_of(j, TILE)
            d = (dot(grad, wo[cols, :], NT) * gp_ref[rows, cols].astype(F32)).astype(BF16)
            du[rows, cols] = d
            dbi[0:1, cols] += jnp.sum(d.astype(F32), axis=0, keepdims=True)
            return carry

        lax.fori_loop(0, units // TILE, unit, 0)

        def back(j, carry):
            cols = rows_of(j, TILE)
            d = dot(du[rows, :], wi[cols, :], NT)
            dvec[2:3, cols] += jnp.sum(d * n_ref[rows, cols].astype(F32), axis=0, keepdims=True)
            dvec[3:4, cols] += jnp.sum(d, axis=0, keepdims=True)
            dh2[rows, cols] = d * vec[2:3, cols]
            return carry

        lax.fori_loop(0, model // TILE, back, 0)

    mixer(t)
    mixer(spread.peer_core())
    for i in range(1, chips):
        mixer(spread.same_core(i))
        mixer(spread.other_core(i))

    masks = head_masks(width, BF16)
    lane = lax.broadcasted_iota(jnp.int32, (1, 128), 1)
    up = zc >= (chips + 1) // 2
    tsize = tn

    def pair(qb, kb):
        qrows, krows = rows_of(qb, size), rows_of(kb, size)
        q, keys, vals = q_ref[qrows, :], k_ref[krows, :], v_ref[krows, :]
        grad = do[qrows, :]
        prod = grad.astype(F32) * o_ref[qrows, :]
        lse = lse_ref[qrows, :]
        bias = pair_bias(qb, kb, size, segcol, segrow)
        dq_new = jnp.zeros((size, width), F32)
        dk_new = jnp.zeros((size, width), F32)
        dv_new = jnp.zeros((size, width), F32)
        for h in range(heads):
            qh, gh = q * masks[h], grad * masks[h]
            total = jnp.sum(jnp.where(lane == h, lse, 0.0), axis=1, keepdims=True)
            delta = jnp.sum(prod * masks[h].astype(F32), axis=1, keepdims=True)
            p = jnp.exp(dot(qh, keys, NT) + bias - total)
            ds = (p * (dot(gh, vals, NT) - delta)).astype(BF16)
            dv_new = dv_new + dot(p.astype(BF16), gh, TN)
            dk_new = dk_new + dot(ds, qh, TN)
            dq_new = dq_new + dot(ds, keys * masks[h], NN)
        dq[qrows, :] += dq_new
        dk[krows, :] += dk_new
        dv[krows, :] += dv_new

    def attend_back(stage):
        pivot = jnp.where(up, stage, tsize - 1 - stage)

        def step(j, carry):
            pair(jnp.where(up, pivot + j, pivot), jnp.where(up, pivot, pivot - j))
            return carry

        lax.fori_loop(0, tsize - stage, step, 0)
        rows = rows_of(pivot, size)
        cos, sa, sb = ctab[rows, :], satab[rows, :], sbtab[rows, :]
        dt[rows, 0:width] = turn(dq[rows, :] * (1.0 / math.sqrt(HD)), cos, sa, sb, -1.0).astype(BF16)
        dt[rows, width : 2 * width] = turn(dk[rows, :], cos, sa, sb, -1.0).astype(BF16)
        dt[rows, 2 * width : 3 * width] = dv[rows, :].astype(BF16)
        block = dt[rows, :]
        dbt[...] += jnp.sum(block.astype(F32), axis=0, keepdims=True)

        def back(j, carry):
            cols = rows_of(j, TILE)
            d = dot(block, wt[cols, :], NT)
            dvec[0:1, cols] += jnp.sum(d * n_ref[rows, cols].astype(F32), axis=0, keepdims=True)
            dvec[1:2, cols] += jnp.sum(d, axis=0, keepdims=True)
            dh2[rows, cols] = dh2[rows, cols] + d * vec[0:1, cols]
            return carry

        lax.fori_loop(0, model // TILE, back, 0)
        value = dh2[rows, :]
        chip, core = pivot // 2, lax.rem(pivot, 2)

        @pl.when(core != co)
        def _():
            tocore[chip] = value.astype(BF16)
            gather.send_core(chip)

        @pl.when((core == co) & (chip != zc))
        def _():
            toici[chip] = value.astype(BF16)

        @pl.when(pivot == t)
        def _():
            keep[...] = value

        if stage % 2 == 1:

            @pl.when(chip != zc)
            def _():
                gather.send_link(chip)

    for stage in range(tn):
        attend_back(stage)

    def grad_one(j, carry):
        cols = rows_of(j, TILE)
        h1 = (n_ref[:, cols].astype(F32) * vec[0:1, cols] + vec[1:2, cols]).astype(BF16)
        dwt[cols, :] = dot(h1, dt[...], TN).astype(dwt.dtype)
        return carry

    lax.fori_loop(0, model // TILE, grad_one, 0)

    def grad_two(j, carry):
        cols = rows_of(j, TILE)
        h2 = (n_ref[:, cols].astype(F32) * vec[2:3, cols] + vec[3:4, cols]).astype(BF16)
        dwi[cols, :] = dot(h2, du[...], TN).astype(dwi.dtype)
        return carry

    lax.fori_loop(0, model // TILE, grad_two, 0)

    def grad_three(j, carry):
        cols = rows_of(j, TILE)
        dwo[cols, :] = dot(g_ref[:, cols], gb[...], TN).astype(dwo.dtype)
        return carry

    lax.fori_loop(0, units // TILE, grad_three, 0)
    small = min(TILE, width)

    def grad_four(j, carry):
        cols = rows_of(j, small)
        dwp[cols, :] = dot(o_ref[:, cols].astype(BF16), gb[...], TN).astype(dwp.dtype)
        return carry

    lax.fori_loop(0, width // small, grad_four, 0)

    own_n, inverse = norm_stats(x_ref[...])
    e = keep[...] + gather.total()
    inner = e - jnp.mean(e, axis=-1, keepdims=True) - own_n * jnp.mean(e * own_n, axis=-1, keepdims=True)
    dx_ref[...] = dy_ref[...].astype(F32) + inner * inverse
    spread.finish()
    gather.finish()


VM = pl.BlockSpec(memory_space=pltpu.VMEM)


def shape(dims, dtype):
    return jax.ShapeDtypeStruct(tuple(dims), dtype)


def group_sems(chips, tn):
    dma = pltpu.SemaphoreType.DMA
    return [dma((chips,)), dma((chips,)), dma((tn,)), dma((chips,)), dma((chips,)), dma((chips,)), dma((chips,))]


def group_buffers(chips, size, model):
    return [pltpu.VMEM((chips, size, model), BF16) for _ in range(4)]


def params_of(cid):
    return pltpu.CompilerParams(collective_id=cid, has_side_effects=True, vmem_limit_bytes=VMEM_LIMIT)


def forward_layer(tn, x, weights, vec, bt, bi, tables):
    wt, wi, wo, wp = weights
    size, model = x.shape
    length = size * tn
    width, units, chips = wp.shape[0], wo.shape[0], tn // 2
    outs = (
        shape((size, model), F32),
        shape((length, model), BF16),
        shape((length, width), BF16),
        shape((length, width), BF16),
        shape((length, width), BF16),
        shape((length, width), F32),
        shape((length, 128), F32),
        shape((length, units), BF16),
        shape((length, units), BF16),
    )
    return pl.pallas_call(
        functools.partial(forward_kernel, tn, size),
        out_shape=outs,
        in_specs=[VM] * 13,
        out_specs=[VM] * len(outs),
        scratch_shapes=[pltpu.VMEM((size, model), F32)] + group_buffers(chips, size, model) + group_sems(chips, tn),
        compiler_params=params_of(0),
        name="forward",
    )(x, wt, wi, wo, wp, vec, bt, bi, *tables)


def backward_layer(tn, dy, x, weights, vec, tables, kept):
    wt, wi, wo, wp = weights
    size, model = x.shape
    length = size * tn
    width, units, chips = wp.shape[0], wo.shape[0], tn // 2
    outs = (
        shape((size, model), F32),
        shape(wt.shape, BF16),
        shape(wi.shape, BF16),
        shape(wo.shape, BF16),
        shape(wp.shape, BF16),
        shape((8, model), F32),
        shape((1, 3 * width), F32),
        shape((1, units), F32),
    )
    return pl.pallas_call(
        functools.partial(backward_kernel, tn, size),
        out_shape=outs,
        in_specs=[VM] * 20,
        out_specs=[VM] * len(outs),
        scratch_shapes=[
            pltpu.VMEM((length, model), BF16),
            pltpu.VMEM((length, width), BF16),
            pltpu.VMEM((length, units), BF16),
            pltpu.VMEM((length, 3 * width), BF16),
            pltpu.VMEM((length, width), F32),
            pltpu.VMEM((length, width), F32),
            pltpu.VMEM((length, width), F32),
            pltpu.VMEM((length, model), F32),
            pltpu.VMEM((size, model), F32),
        ]
        + group_buffers(chips, size, model)
        + group_sems(chips, tn),
        compiler_params=params_of(1),
        name="backward",
    )(dy, x, wt, wi, wo, wp, vec, *tables, *kept)


GROUPS = ("dp", "h")
EVERY = ("dp", "h", "t")


def to_group(tn, blocks):
    h, t = lax.axis_index("h"), lax.axis_index("t")
    count = 2 * tn
    parity = lax.rem(t, 2)
    got = []
    for j in range(2):
        moves = [(c, ((c + j) % 2) * tn + c // 2) for c in range(count)]
        piece = jnp.where(lax.rem(parity + j, 2) == 0, blocks[0], blocks[1])
        got.append(lax.ppermute(piece, ("h", "t"), moves))
    low = jnp.where(h == 0, got[0], got[1])
    high = jnp.where(h == 0, got[1], got[0])
    return jnp.concatenate([low, high], axis=0)


def from_group(tn, rows):
    h, t = lax.axis_index("h"), lax.axis_index("t")
    count = 2 * tn
    parity = lax.rem(t, 2)
    size = rows.shape[0] // 2
    got = []
    for j in range(2):
        moves = [(((c + j) % 2) * tn + c // 2, c) for c in range(count)]
        piece = jnp.where(lax.rem(h + j, 2) == 0, rows[:size], rows[size:])
        got.append(lax.ppermute(piece, ("h", "t"), moves))
    first = jnp.where(parity == 0, got[0], got[1])
    second = jnp.where(parity == 0, got[1], got[0])
    return jnp.stack([first, second], axis=0)


def proj_moves(gn, tn):
    return [(r, (r % gn) * tn + r // gn) for r in range(gn * tn)]


def slice_columns(weight, gn, tn):
    rows, cols = weight.shape
    return weight.reshape(rows, gn, tn, cols // (gn * tn)).transpose(2, 0, 1, 3).reshape(tn, rows, cols // tn)


def slice_triple(weight, tn):
    rows, cols = weight.shape
    return weight.reshape(rows, 3, tn, cols // (3 * tn)).transpose(2, 0, 1, 3).reshape(tn, rows, cols // tn)


def gather_weights(gn, tn, triple, proj, inner, outer):
    def spread(parts):
        moved = lax.all_to_all(parts, "t", 0, 0, tiled=True)
        whole = lax.all_gather(moved.reshape(-1, moved.shape[-1]), GROUPS, axis=0, tiled=True)
        return whole

    wt = spread(slice_triple(triple, tn))
    wi = spread(slice_columns(inner, gn, tn))
    wo = lax.all_gather(outer, GROUPS, axis=0, tiled=True)
    wp = lax.all_gather(lax.ppermute(proj, EVERY, proj_moves(gn, tn)), GROUPS, axis=0, tiled=True)
    return wt, wi, wo, wp


def reduce_weights(gn, tn, dwt, dwi, dwo, dwp):
    def back(parts):
        mine = lax.psum_scatter(parts, GROUPS, scatter_dimension=0, tiled=True)
        rows = mine.shape[0] // tn
        return lax.all_to_all(mine.reshape(tn, rows, -1), "t", 0, 0, tiled=True).astype(F32)

    triple = back(dwt)
    rows = triple.shape[1]
    triple = triple.reshape(tn, rows, 3, -1).transpose(1, 2, 0, 3).reshape(rows, -1)
    inner = back(dwi)
    inner = inner.reshape(tn, rows, gn, -1).transpose(1, 2, 0, 3).reshape(rows, -1)
    outer = lax.psum_scatter(dwo, GROUPS, scatter_dimension=0, tiled=True).astype(F32)
    proj = lax.psum_scatter(dwp, GROUPS, scatter_dimension=0, tiled=True)
    proj = lax.ppermute(proj, EVERY, [(b, a) for a, b in proj_moves(gn, tn)]).astype(F32)
    return triple, proj, inner, outer


def per_device(
    gn, tn,
    tokens, segments, cotangent, triple_weight, triple_bias, proj_weight, proj_bias, inner_weight, inner_bias,
    outer_weight, outer_bias, first_gain, first_shift, second_gain, second_shift,
):
    layers = triple_weight.shape[0]
    model = tokens.shape[2]
    span = tokens.shape[1] * 2 * tn
    h, t = lax.axis_index("h"), lax.axis_index("t")
    device = (lax.axis_index("dp") * 2 + h) * tn + t
    shards = gn * tn
    heads_wide = model // tn
    units = outer_weight.shape[1] * gn

    x = to_group(tn, tokens).astype(F32)
    cot = to_group(tn, cotangent).astype(F32)
    segs_all = lax.all_gather(segments, ("h", "t"), axis=1, tiled=True)
    segs = jnp.where(h == 0, segs_all[0], segs_all[1])
    place = jnp.arange(span, dtype=jnp.int32)
    segs = jnp.where(segs == 0, -1 - place, segs)
    freq = 10000.0 ** (-(2.0 * jnp.arange(ROT // 2, dtype=F32)) / ROT)
    angle = place.astype(F32)[:, None] * freq[None, :]
    cosine, sine = jnp.cos(angle), jnp.sin(angle)
    none = jnp.zeros((span, HD - ROT), F32)
    empty = jnp.zeros_like(sine)
    ctab = jnp.concatenate([cosine, cosine, none + 1.0] * (128 // HD), axis=1)
    satab = jnp.concatenate([-sine, empty, none] * (128 // HD), axis=1)
    sbtab = jnp.concatenate([empty, sine, none] * (128 // HD), axis=1)
    tables = (segs[:, None], segs[None, :], ctab, satab, sbtab)

    small = (triple_bias, inner_bias, proj_bias, outer_bias, first_gain, first_shift, second_gain, second_shift)
    packed = jnp.concatenate(small, axis=1)
    packed = lax.all_gather(packed[None], EVERY, axis=0, tiled=True).astype(F32)
    starts = [0]
    for item in small:
        starts.append(starts[-1] + item.shape[1])

    def vector(layer, i):
        return packed[:, layer, starts[i] : starts[i + 1]].reshape(-1)

    weights, vecs, bts, bis = [], [], [], []
    for layer in range(layers):
        weights.append(
            gather_weights(
                gn, tn, triple_weight[layer], proj_weight[layer], inner_weight[layer], outer_weight[layer]
            )
        )
        bt = lax.dynamic_index_in_dim(vector(layer, 0).reshape(3, tn, heads_wide), t, 1, keepdims=False)
        bts.append(bt.reshape(1, -1))
        bi = lax.dynamic_index_in_dim(vector(layer, 1).reshape(gn, tn, -1), t, 1, keepdims=False)
        bis.append(bi.reshape(1, -1))
        zero = jnp.zeros((model,), F32)
        vecs.append(
            jnp.stack(
                [vector(layer, 4), vector(layer, 5), vector(layer, 6), vector(layer, 7)]
                + [vector(layer, 2) + vector(layer, 3), zero, zero, zero]
            )
        )

    inputs, kept = [], []
    for layer in range(layers):
        inputs.append(x)
        x, *saved = forward_layer(tn, x, weights[layer], vecs[layer], bts[layer], bis[layer], tables)
        kept.append(saved)
    output = from_group(tn, x.astype(BF16))
    grad = cot
    mats, flats = [None] * layers, [None] * layers
    for layer in reversed(range(layers)):
        grad, dwt, dwi, dwo, dwp, dvec, dbt, dbi = backward_layer(
            tn, grad, inputs[layer], weights[layer], vecs[layer], tables, kept[layer]
        )
        mats[layer] = reduce_weights(gn, tn, dwt, dwi, dwo, dwp)
        triple = lax.dynamic_update_slice(
            jnp.zeros((3, tn, heads_wide), F32), dbt.reshape(3, 1, heads_wide), (0, t, 0)
        )
        inner = lax.dynamic_update_slice(
            jnp.zeros((gn, tn, units // gn), F32), dbi.reshape(gn, 1, units // gn), (0, t, 0)
        )
        flats[layer] = jnp.concatenate([dvec[:5].reshape(-1), triple.reshape(-1), inner.reshape(-1)])
    tokens_grad = from_group(tn, grad.astype(BF16))
    summed = lax.psum(jnp.stack(flats), EVERY)

    def own(start, length):
        piece = length // shards
        return lax.dynamic_slice_in_dim(summed, start + device * piece, piece, 1)

    base = 5 * model
    bias_sum = own(4 * model, model)
    return (
        output,
        tokens_grad,
        jnp.stack([m[0] for m in mats]),
        own(base, 2 * model),
        own(base + 2 * model, model),
        jnp.stack([m[1] for m in mats]),
        bias_sum,
        jnp.stack([m[2] for m in mats]),
        own(base + 3 * model, units * tn),
        jnp.stack([m[3] for m in mats]),
        bias_sum,
        own(0, model),
        own(model, model),
        own(2 * model, model),
        own(3 * model, model),
    )


def solution(mesh):
    dp, ctx = mesh.shape["dp"], mesh.shape["ctx"]
    tn = ctx // 2
    gn = 2 * dp
    fine = Mesh(mesh.devices.reshape(dp, 2, tn), EVERY)
    seq = P("dp", ("h", "t"), None)
    mat = P(None, EVERY, None)
    row = P(None, EVERY)
    in_specs = (seq, P("dp", ("h", "t")), seq, mat, row, mat, row, mat, row, mat, row, row, row, row, row)
    out_specs = (seq, seq, mat, row, row, mat, row, mat, row, mat, row, row, row, row, row)
    return jax.shard_map(
        functools.partial(per_device, gn, tn), mesh=fine, in_specs=in_specs, out_specs=out_specs, check_vma=False
    )
```

```python
import functools
import math

import jax
import jax.numpy as jnp
from jax import lax
from jax.experimental import pallas as pl
from jax.experimental.pallas import tpu as pltpu
from jax.sharding import Mesh
from jax.sharding import PartitionSpec as P

HD = 64
ROT = 16
EPSILON = 1e-05
NEG_LARGE = -1e30
MESH = pl.DeviceIdType.MESH
BF16 = jnp.bfloat16
F32 = jnp.float32
VMEM_LIMIT = 60 * 1024 * 1024


def dot(a, b, dims):
    return lax.dot_general(a, b, (dims, ((), ())), preferred_element_type=F32)


NN = ((1,), (0,))
NT = ((1,), (1,))
TN = ((0,), (0,))


def rows_of(b, size):
    return pl.ds(pl.multiple_of(b * size, size), size)


def group_barrier(tn):
    t = lax.axis_index("t")
    zc, co = t // 2, lax.rem(t, 2)
    chips = tn // 2
    sem = pltpu.get_barrier_semaphore()
    peers = [zc * 2 + 1 - co] + [lax.rem(zc + k, chips) * 2 + co for k in range(1, chips)]
    for p in peers:
        pl.semaphore_signal(sem, inc=1, device_id={"t": p}, device_id_type=MESH)
    pl.semaphore_wait(sem, len(peers))


class Spread:
    def __init__(self, tn, buf, size, ssem, fsem, rsem):
        self.tn, self.buf, self.size = tn, buf, size
        self.ssem, self.fsem, self.rsem = ssem, fsem, rsem
        self.t = lax.axis_index("t")
        self.zc, self.co = self.t // 2, lax.rem(self.t, 2)
        self.chips = tn // 2

    def copy(self, block, send, to):
        ref = self.buf.at[rows_of(block, self.size)]
        return pltpu.make_async_remote_copy(
            ref, ref, send, self.rsem.at[block], device_id={"t": to}, device_id_type=MESH
        )

    def start(self):
        for k in range(1, self.chips):
            chip = lax.rem(self.zc + k, self.chips)
            self.copy(self.t, self.ssem.at[k], chip * 2 + self.co).start()
        self.copy(self.t, self.ssem.at[0], self.zc * 2 + 1 - self.co).start()

    def peer_core(self):
        b = self.zc * 2 + 1 - self.co
        self.copy(b, self.ssem.at[0], b).wait_recv()
        return b

    def same_core(self, k):
        b = lax.rem(self.zc + self.chips - k, self.chips) * 2 + self.co
        self.copy(b, self.fsem.at[k], b).wait_recv()
        self.copy(b, self.fsem.at[k], self.zc * 2 + 1 - self.co).start()
        return b

    def other_core(self, k):
        b = lax.rem(self.zc + self.chips - k, self.chips) * 2 + 1 - self.co
        self.copy(b, self.fsem.at[k], b).wait_recv()
        return b

    def finish(self):
        for k in range(self.chips):
            self.copy(self.t, self.ssem.at[k], self.t).wait_send()
        for k in range(1, self.chips):
            self.copy(self.t, self.fsem.at[k], self.t).wait_send()


class Gather:
    def __init__(self, tn, tocore, fromcore, toici, fromici, sems):
        self.tn = tn
        self.tocore, self.fromcore, self.toici, self.fromici = tocore, fromcore, toici, fromici
        self.cs, self.cr, self.ls, self.lr = sems
        self.t = lax.axis_index("t")
        self.zc, self.co = self.t // 2, lax.rem(self.t, 2)
        self.chips = tn // 2

    def core_copy(self, chip):
        return pltpu.make_async_remote_copy(
            self.tocore.at[chip],
            self.fromcore.at[chip],
            self.cs.at[chip],
            self.cr.at[chip],
            device_id={"t": self.zc * 2 + 1 - self.co},
            device_id_type=MESH,
        )

    def link_copy(self, chip, slot):
        return pltpu.make_async_remote_copy(
            self.toici.at[chip],
            self.fromici.at[slot],
            self.ls.at[chip],
            self.lr.at[slot],
            device_id={"t": chip * 2 + self.co},
            device_id_type=MESH,
        )

    def send_core(self, chip):
        self.core_copy(chip).start()

    def send_link(self, chip):
        self.core_copy(chip).wait_recv()
        self.toici[chip] = (self.toici[chip].astype(F32) + self.fromcore[chip].astype(F32)).astype(BF16)
        self.link_copy(chip, self.zc).start()

    def total(self):
        self.core_copy(self.zc).wait_recv()
        value = self.fromcore[self.zc].astype(F32)
        for k in range(1, self.chips):
            chip = lax.rem(self.zc + k, self.chips)
            self.link_copy(chip, chip).wait_recv()
            value = value + self.fromici[chip].astype(F32)
        return value

    def finish(self):
        for chip in range(self.chips):
            self.core_copy(chip).wait_send()
        for k in range(1, self.chips):
            chip = lax.rem(self.zc + k, self.chips)
            self.link_copy(chip, self.zc).wait_send()


def norm_stats(x):
    mean = jnp.mean(x, axis=-1, keepdims=True)
    centred = x - mean
    inverse = lax.rsqrt(jnp.mean(centred * centred, axis=-1, keepdims=True) + EPSILON)
    return centred * inverse, inverse


def widen(tab, width):
    return jnp.concatenate([tab] * (width // tab.shape[1]), axis=1)


def turn(x, cos, sa, sb, sign):
    width = x.shape[1]
    cos, sa, sb = widen(cos, width), widen(sa, width), widen(sb, width)
    side = pltpu.roll(x, width - ROT // 2, 1) * sa + pltpu.roll(x, ROT // 2, 1) * sb
    return x * cos + sign * side


def head_masks(width, dtype):
    lane = lax.broadcasted_iota(jnp.int32, (1, width), 1) // HD
    return [(lane == h).astype(F32).astype(dtype) for h in range(width // HD)]


def pair_bias(qb, kb, size, segcol, segrow):
    qpos = lax.broadcasted_iota(jnp.int32, (size, size), 0) + qb * size
    kpos = lax.broadcasted_iota(jnp.int32, (size, size), 1) + kb * size
    same = segcol[rows_of(qb, size), :] == segrow[:, rows_of(kb, size)]
    return jnp.where(same & (kpos <= qpos), 0.0, NEG_LARGE)


TILE = 256


def forward_kernel(
    tn, size,
    x_ref, wt, wi, wo, wp, vec, bt, bi, segcol, segrow, ctab, satab, sbtab,
    xo_ref, n_ref, q_ref, k_ref, v_ref, o_ref, lse_ref, g_ref, gp_ref,
    keep, tocore, fromcore, toici, fromici, ssem, fsem, rsem, cs, cr, ls, lr,
):
    chips = tn // 2
    width = q_ref.shape[1]
    heads = width // HD
    units = g_ref.shape[1]
    group_barrier(tn)
    spread = Spread(tn, n_ref, size, ssem, fsem, rsem)
    gather = Gather(tn, tocore, fromcore, toici, fromici, (cs, cr, ls, lr))
    t, zc, co = spread.t, spread.zc, spread.co
    own_n, _ = norm_stats(x_ref[...])
    n_ref[rows_of(t, size), :] = own_n.astype(BF16)
    spread.start()

    def project(b):
        rows = rows_of(b, size)
        n = n_ref[rows, :].astype(F32)
        h1 = (n * vec[0:1, :] + vec[1:2, :]).astype(BF16)
        h2 = (n * vec[2:3, :] + vec[3:4, :]).astype(BF16)
        cos, sa, sb = ctab[rows, :], satab[rows, :], sbtab[rows, :]
        q = dot(h1, wt[:, 0:width], NN) + bt[:, 0:width]
        q_ref[rows, :] = (turn(q, cos, sa, sb, 1.0).astype(BF16).astype(F32) * (1.0 / math.sqrt(HD))).astype(BF16)
        k = dot(h1, wt[:, width : 2 * width], NN) + bt[:, width : 2 * width]
        k_ref[rows, :] = turn(k, cos, sa, sb, 1.0).astype(BF16)
        v = dot(h1, wt[:, 2 * width : 3 * width], NN) + bt[:, 2 * width : 3 * width]
        v_ref[rows, :] = v.astype(BF16)

        def mix(j, carry):
            cols = rows_of(j, TILE)
            u = dot(h2, wi[:, cols], NN) + bi[:, cols]
            half = 0.5 + 0.5 * lax.erf(u * (1.0 / math.sqrt(2.0)))
            g_ref[rows, cols] = (u * half).astype(BF16)
            bell = jnp.exp(-0.5 * u * u) * (1.0 / math.sqrt(2.0 * math.pi))
            gp_ref[rows, cols] = (half + u * bell).astype(BF16)
            return carry

        lax.fori_loop(0, units // TILE, mix, 0)

    project(t)
    project(spread.peer_core())
    for i in range(1, chips):
        project(spread.same_core(i))
        project(spread.other_core(i))

    masks = head_masks(width, F32)
    lane = lax.broadcasted_iota(jnp.int32, (1, 128), 1)

    def attend(b):
        rows = rows_of(b, size)
        qb = q_ref[rows, :]
        qs = [qb * masks[h].astype(BF16) for h in range(heads)]

        def step(i, carry):
            peaks, sums, acc = carry
            kb = b - i
            keys = k_ref[rows_of(kb, size), :]
            vals = v_ref[rows_of(kb, size), :]
            bias = pair_bias(b, kb, size, segcol, segrow)
            new_peaks, new_sums = [], []
            scale = jnp.zeros((size, width), F32)
            add = jnp.zeros((size, width), F32)
            for h in range(heads):
                s = dot(qs[h], keys, NT) + bias
                peak = jnp.maximum(peaks[h], jnp.max(s, axis=1, keepdims=True))
                p = jnp.exp(s - peak)
                fade = jnp.exp(peaks[h] - peak)
                new_peaks.append(peak)
                new_sums.append(sums[h] * fade + jnp.sum(p, axis=1, keepdims=True))
                scale = scale + fade * masks[h]
                add = add + dot(p.astype(BF16), vals * masks[h].astype(BF16), NN)
            return tuple(new_peaks), tuple(new_sums), acc * scale + add

        start = (
            tuple(jnp.full((size, 1), NEG_LARGE, F32) for _ in range(heads)),
            tuple(jnp.zeros((size, 1), F32) for _ in range(heads)),
            jnp.zeros((size, width), F32),
        )
        peaks, sums, acc = lax.fori_loop(0, b + 1, step, start)
        scale = jnp.zeros((size, width), F32)
        lse = jnp.zeros((size, 128), F32)
        for h in range(heads):
            scale = scale + (1.0 / sums[h]) * masks[h]
            lse = jnp.where(lane == h, peaks[h] + jnp.log(sums[h]), lse)
        lse_ref[rows, :] = lse
        o_ref[rows, :] = acc * scale

    def partial(b, store):
        attend(b)
        rows = rows_of(b, size)

        def part(j, carry):
            cols = rows_of(j, TILE)
            store(cols, dot(g_ref[rows, :], wo[:, cols], NN) + dot(o_ref[rows, :].astype(BF16), wp[:, cols], NN))
            return carry

        lax.fori_loop(0, x_ref.shape[1] // TILE, part, 0)

    def into(ref, chip):
        def store(cols, value):
            ref[chip, :, cols] = value.astype(BF16)

        return store

    def into_keep(cols, value):
        keep[:, cols] = value

    for i in range(1, chips):
        chip = lax.rem(zc + i, chips)
        partial(chip * 2 + 1 - co, into(tocore, chip))
        gather.send_core(chip)
        partial(chip * 2 + co, into(toici, chip))
        gather.send_link(chip)
    partial(zc * 2 + 1 - co, into(tocore, zc))
    gather.send_core(zc)
    partial(t, into_keep)
    xo_ref[...] = x_ref[...] + vec[4:5, :] + keep[...] + gather.total()
    spread.finish()
    gather.finish()


def backward_kernel(
    tn, size,
    dy_ref, x_ref, wt, wi, wo, wp, vec, segcol, segrow, ctab, satab, sbtab,
    n_ref, q_ref, k_ref, v_ref, o_ref, lse_ref, g_ref, gp_ref,
    dx_ref, dwt, dwi, dwo, dwp, dvec, dbt, dbi,
    gb, do, du, dt, dq, dk, dv, dh2, keep,
    tocore, fromcore, toici, fromici, ssem, fsem, rsem, cs, cr, ls, lr,
):
    chips = tn // 2
    width = q_ref.shape[1]
    heads = width // HD
    units = g_ref.shape[1]
    model = x_ref.shape[1]
    group_barrier(tn)
    spread = Spread(tn, gb, size, ssem, fsem, rsem)
    gather = Gather(tn, tocore, fromcore, toici, fromici, (cs, cr, ls, lr))
    t, zc, co = spread.t, spread.zc, spread.co
    own = dy_ref[...].astype(F32).astype(BF16)
    gb[rows_of(t, size), :] = own
    spread.start()
    dvec[...] = jnp.zeros_like(dvec)
    dbt[...] = jnp.zeros_like(dbt)
    dbi[...] = jnp.zeros_like(dbi)
    dvec[4:5, :] = jnp.sum(own.astype(F32), axis=0, keepdims=True)
    dq[...] = jnp.zeros_like(dq)
    dk[...] = jnp.zeros_like(dk)
    dv[...] = jnp.zeros_like(dv)

    def mixer(b):
        rows = rows_of(b, size)
        grad = gb[rows, :]
        do[rows, :] = dot(grad, wp[...], NT).astype(BF16)

        def unit(j, carry):
            cols = rows_of(j, TILE)
            d = (dot(grad, wo[cols, :], NT) * gp_ref[rows, cols].astype(F32)).astype(BF16)
            du[rows, cols] = d
            dbi[0:1, cols] += jnp.sum(d.astype(F32), axis=0, keepdims=True)
            return carry

        lax.fori_loop(0, units // TILE, unit, 0)

        def back(j, carry):
            cols = rows_of(j, TILE)
            d = dot(du[rows, :], wi[cols, :], NT)
            dvec[2:3, cols] += jnp.sum(d * n_ref[rows, cols].astype(F32), axis=0, keepdims=True)
            dvec[3:4, cols] += jnp.sum(d, axis=0, keepdims=True)
            dh2[rows, cols] = d * vec[2:3, cols]
            return carry

        lax.fori_loop(0, model // TILE, back, 0)

    mixer(t)
    mixer(spread.peer_core())
    for i in range(1, chips):
        mixer(spread.same_core(i))
        mixer(spread.other_core(i))

    masks = head_masks(width, BF16)
    lane = lax.broadcasted_iota(jnp.int32, (1, 128), 1)
    up = zc >= (chips + 1) // 2
    tsize = tn

    def pair(qb, kb):
        qrows, krows = rows_of(qb, size), rows_of(kb, size)
        q, keys, vals = q_ref[qrows, :], k_ref[krows, :], v_ref[krows, :]
        grad = do[qrows, :]
        prod = grad.astype(F32) * o_ref[qrows, :]
        lse = lse_ref[qrows, :]
        bias = pair_bias(qb, kb, size, segcol, segrow)
        dq_new = jnp.zeros((size, width), F32)
        dk_new = jnp.zeros((size, width), F32)
        dv_new = jnp.zeros((size, width), F32)
        for h in range(heads):
            qh, gh = q * masks[h], grad * masks[h]
            total = jnp.sum(jnp.where(lane == h, lse, 0.0), axis=1, keepdims=True)
            delta = jnp.sum(prod * masks[h].astype(F32), axis=1, keepdims=True)
            p = jnp.exp(dot(qh, keys, NT) + bias - total)
            ds = (p * (dot(gh, vals, NT) - delta)).astype(BF16)
            dv_new = dv_new + dot(p.astype(BF16), gh, TN)
            dk_new = dk_new + dot(ds, qh, TN)
            dq_new = dq_new + dot(ds, keys * masks[h], NN)
        dq[qrows, :] += dq_new
        dk[krows, :] += dk_new
        dv[krows, :] += dv_new

    def attend_back(stage):
        pivot = jnp.where(up, stage, tsize - 1 - stage)

        def step(j, carry):
            pair(jnp.where(up, pivot + j, pivot), jnp.where(up, pivot, pivot - j))
            return carry

        lax.fori_loop(0, tsize - stage, step, 0)
        rows = rows_of(pivot, size)
        cos, sa, sb = ctab[rows, :], satab[rows, :], sbtab[rows, :]
        dt[rows, 0:width] = turn(dq[rows, :] * (1.0 / math.sqrt(HD)), cos, sa, sb, -1.0).astype(BF16)
        dt[rows, width : 2 * width] = turn(dk[rows, :], cos, sa, sb, -1.0).astype(BF16)
        dt[rows, 2 * width : 3 * width] = dv[rows, :].astype(BF16)
        block = dt[rows, :]
        dbt[...] += jnp.sum(block.astype(F32), axis=0, keepdims=True)

        def back(j, carry):
            cols = rows_of(j, TILE)
            d = dot(block, wt[cols, :], NT)
            dvec[0:1, cols] += jnp.sum(d * n_ref[rows, cols].astype(F32), axis=0, keepdims=True)
            dvec[1:2, cols] += jnp.sum(d, axis=0, keepdims=True)
            dh2[rows, cols] = dh2[rows, cols] + d * vec[0:1, cols]
            return carry

        lax.fori_loop(0, model // TILE, back, 0)
        value = dh2[rows, :]
        chip, core = pivot // 2, lax.rem(pivot, 2)

        @pl.when(core != co)
        def _():
            tocore[chip] = value.astype(BF16)
            gather.send_core(chip)

        @pl.when((core == co) & (chip != zc))
        def _():
            toici[chip] = value.astype(BF16)

        @pl.when(pivot == t)
        def _():
            keep[...] = value

        if stage % 2 == 1:

            @pl.when(chip != zc)
            def _():
                gather.send_link(chip)

    for stage in range(tn):
        attend_back(stage)

    def grad_one(j, carry):
        cols = rows_of(j, TILE)
        h1 = (n_ref[:, cols].astype(F32) * vec[0:1, cols] + vec[1:2, cols]).astype(BF16)
        dwt[cols, :] = dot(h1, dt[...], TN).astype(dwt.dtype)
        return carry

    lax.fori_loop(0, model // TILE, grad_one, 0)

    def grad_two(j, carry):
        cols = rows_of(j, TILE)
        h2 = (n_ref[:, cols].astype(F32) * vec[2:3, cols] + vec[3:4, cols]).astype(BF16)
        dwi[cols, :] = dot(h2, du[...], TN).astype(dwi.dtype)
        return carry

    lax.fori_loop(0, model // TILE, grad_two, 0)

    def grad_three(j, carry):
        cols = rows_of(j, TILE)
        dwo[cols, :] = dot(g_ref[:, cols], gb[...], TN).astype(dwo.dtype)
        return carry

    lax.fori_loop(0, units // TILE, grad_three, 0)
    small = min(TILE, width)

    def grad_four(j, carry):
        cols = rows_of(j, small)
        dwp[cols, :] = dot(o_ref[:, cols].astype(BF16), gb[...], TN).astype(dwp.dtype)
        return carry

    lax.fori_loop(0, width // small, grad_four, 0)

    own_n, inverse = norm_stats(x_ref[...])
    e = keep[...] + gather.total()
    inner = e - jnp.mean(e, axis=-1, keepdims=True) - own_n * jnp.mean(e * own_n, axis=-1, keepdims=True)
    dx_ref[...] = dy_ref[...].astype(F32) + inner * inverse
    spread.finish()
    gather.finish()


VM = pl.BlockSpec(memory_space=pltpu.VMEM)


def shape(dims, dtype):
    return jax.ShapeDtypeStruct(tuple(dims), dtype)


def group_sems(chips, tn):
    dma = pltpu.SemaphoreType.DMA
    return [dma((chips,)), dma((chips,)), dma((tn,)), dma((chips,)), dma((chips,)), dma((chips,)), dma((chips,))]


def group_buffers(chips, size, model):
    return [pltpu.VMEM((chips, size, model), BF16) for _ in range(4)]


def params_of(cid):
    return pltpu.CompilerParams(collective_id=cid, has_side_effects=True, vmem_limit_bytes=VMEM_LIMIT)


def forward_layer(tn, x, weights, vec, bt, bi, tables):
    wt, wi, wo, wp = weights
    size, model = x.shape
    length = size * tn
    width, units, chips = wp.shape[0], wo.shape[0], tn // 2
    outs = (
        shape((size, model), F32),
        shape((length, model), BF16),
        shape((length, width), BF16),
        shape((length, width), BF16),
        shape((length, width), BF16),
        shape((length, width), F32),
        shape((length, 128), F32),
        shape((length, units), BF16),
        shape((length, units), BF16),
    )
    return pl.pallas_call(
        functools.partial(forward_kernel, tn, size),
        out_shape=outs,
        in_specs=[VM] * 13,
        out_specs=[VM] * len(outs),
        scratch_shapes=[pltpu.VMEM((size, model), F32)] + group_buffers(chips, size, model) + group_sems(chips, tn),
        compiler_params=params_of(0),
        name="forward",
    )(x, wt, wi, wo, wp, vec, bt, bi, *tables)


def backward_layer(tn, dy, x, weights, vec, tables, kept):
    wt, wi, wo, wp = weights
    size, model = x.shape
    length = size * tn
    width, units, chips = wp.shape[0], wo.shape[0], tn // 2
    outs = (
        shape((size, model), F32),
        shape(wt.shape, BF16),
        shape(wi.shape, BF16),
        shape(wo.shape, BF16),
        shape(wp.shape, BF16),
        shape((8, model), F32),
        shape((1, 3 * width), F32),
        shape((1, units), F32),
    )
    return pl.pallas_call(
        functools.partial(backward_kernel, tn, size),
        out_shape=outs,
        in_specs=[VM] * 20,
        out_specs=[VM] * len(outs),
        scratch_shapes=[
            pltpu.VMEM((length, model), BF16),
            pltpu.VMEM((length, width), BF16),
            pltpu.VMEM((length, units), BF16),
            pltpu.VMEM((length, 3 * width), BF16),
            pltpu.VMEM((length, width), F32),
            pltpu.VMEM((length, width), F32),
            pltpu.VMEM((length, width), F32),
            pltpu.VMEM((length, model), F32),
            pltpu.VMEM((size, model), F32),
        ]
        + group_buffers(chips, size, model)
        + group_sems(chips, tn),
        compiler_params=params_of(1),
        name="backward",
    )(dy, x, wt, wi, wo, wp, vec, *tables, *kept)


class Place:
    def __init__(self, gn, tn):
        self.gn, self.tn = gn, tn
        self.h, self.t = lax.axis_index("h"), lax.axis_index("t")
        self.g = lax.axis_index("dp") * 2 + self.h
        self.c = self.h * tn + self.t
        self.bits = [1 << i for i in range(gn.bit_length() - 1)]

    def group(self, g):
        return {"dp": g // 2, "h": lax.rem(g, 2)}

    def line(self, c):
        return {"h": c // self.tn, "t": lax.rem(c, self.tn)}

    def other(self, k):
        return lax.rem(self.t + k, self.tn)


def flip(value, bit):
    return value + bit * (1 - 2 * lax.rem(value // bit, 2))


def remote(src, dst, send, recv, device):
    return pltpu.make_async_remote_copy(src, dst, send, recv, device_id=device, device_id_type=MESH)


def runs_by_step(place, bits):
    runs, steps = [(place.g, 1)], []
    for bit in bits:
        steps.append((bit, runs))
        if len(runs) == 1 and runs[0][1] == bit:
            runs = [(runs[0][0] // (2 * bit) * (2 * bit), 2 * bit)]
        else:
            runs = runs + [(flip(start, bit), count) for start, count in runs]
    return steps


def bit_orders(place):
    bits = place.bits
    return [bits, bits[:1] + bits[:0:-1]]


class Doubling:
    def __init__(self, place, ref, block, cols, order, sems, slot):
        self.place, self.ref, self.block, self.cols = place, ref, block, cols
        self.steps = runs_by_step(place, order)
        self.send, self.recv, self.slot = sems[0], sems[1], slot
        self.plan = []
        index = 0
        for bit, runs in self.steps:
            entry = []
            for start, count in runs:
                entry.append((bit, start, count, index))
                index += 1
            self.plan.append(entry)

    def copy(self, bit, start, count, index):
        rows = pl.ds(pl.multiple_of(start * self.block, self.block), count * self.block)
        ref = self.ref.at[rows, self.cols]
        return remote(
            ref,
            ref,
            self.send.at[self.slot, index],
            self.recv.at[self.slot, index],
            self.place.group(flip(self.place.g, bit)),
        )

    def begin(self, step):
        for bit, start, count, index in self.plan[step]:
            self.copy(bit, start, count, index).start()

    def arrive(self, step):
        for bit, start, count, index in self.plan[step]:
            self.copy(bit, flip(start, bit), count, index).wait_recv()

    def advance(self, step):
        if step > 0:
            self.arrive(step - 1)
        if step < len(self.plan):
            self.begin(step)

    def finish(self):
        for entry in self.plan:
            for item in entry:
                self.copy(*item).wait_send()


def doubling_slots(place):
    return sum(1 << i for i in range(len(place.bits)))


def halves(cols):
    return [pl.ds(0, cols // 2), pl.ds(cols // 2, cols // 2)]


def line_barrier(place, extra):
    sem = pltpu.get_barrier_semaphore()
    span = 2 * place.tn
    for k in range(1, span):
        pl.semaphore_signal(sem, inc=1, device_id=place.line(lax.rem(place.c + k, span)), device_id_type=MESH)
    for bit in place.bits[1:]:
        pl.semaphore_signal(sem, inc=1, device_id=place.group(flip(place.g, bit)), device_id_type=MESH)
    peers = span - 1 + len(place.bits) - 1
    source, moved = extra

    @pl.when(moved)
    def _():
        pl.semaphore_signal(sem, inc=1, device_id=source, device_id_type=MESH)
        pl.semaphore_wait(sem, peers + 1)

    @pl.when(jnp.logical_not(moved))
    def _():
        pl.semaphore_wait(sem, peers)


def proj_places(place):
    gn, tn = place.gn, place.tn
    r = place.g * tn + place.t
    target = place.group(lax.rem(r, gn)) | {"t": r // gn}
    q = place.t * gn + place.g
    source = place.group(q // tn) | {"t": lax.rem(q, tn)}
    return target, source, r, q


def open_kernel(
    gn, tn, layers,
    tok, cot, seg, vec, ti, outer, proj,
    tok_o, cot_o, seg_o, vec_o, *rest,
):
    wts, wis, wos, wps = (rest[i * layers : (i + 1) * layers] for i in range(4))
    (ssem, rsem, lsem, asend, arecv, psend, precv, msend, mrecv, gsend, grecv) = rest[4 * layers :]
    place = Place(gn, tn)
    g, t, c = place.g, place.t, place.c
    span = 2 * tn
    target, source, r, q = proj_places(place)
    moved = q != r
    line_barrier(place, (source, moved))
    local, sends = [], []

    def near(src, dst):
        cp = pltpu.make_async_copy(src, dst, lsem.at[len(local)])
        cp.start()
        local.append(cp)

    half = tok.shape[1]

    def move(src, dst, slot):
        for i in range(2):
            to = i * tn + c // 2
            rows = pl.ds(pl.multiple_of(lax.rem(c, 2) * half, half), half)

            @pl.when(to == c)
            def _():
                pltpu.make_async_copy(src.at[i], dst.at[rows], msend.at[slot, i]).start()

            @pl.when(to != c)
            def _():
                remote(
                    src.at[i], dst.at[rows], msend.at[slot, i], mrecv.at[slot, lax.rem(c, 2)], place.line(to)
                ).start()

    def moved_in(src, dst, slot):
        for i in range(2):
            to = i * tn + c // 2
            rows = pl.ds(pl.multiple_of(lax.rem(c, 2) * half, half), half)

            @pl.when(to == c)
            def _():
                pltpu.make_async_copy(src.at[i], dst.at[rows], msend.at[slot, i]).wait()

            @pl.when(to != c)
            def _():
                remote(
                    src.at[i], dst.at[rows], msend.at[slot, i], mrecv.at[slot, lax.rem(c, 2)], place.line(to)
                ).wait_send()

        for s in range(2):

            @pl.when(2 * t + s != c)
            def _():
                rows = pl.ds(s * half, half)
                remote(
                    src.at[0], dst.at[rows], msend.at[slot, 0], mrecv.at[slot, s], place.line(c)
                ).wait_recv()

    move(tok, tok_o, 0)

    def slot_rows(index, size):
        return pl.ds(pl.multiple_of(index * size, size), size)

    def share(src_of, dst, slot):
        size = src_of(0).shape[0]
        rows = slot_rows(g * tn + t, size)
        near(src_of(t), dst.at[rows])
        for k in range(1, tn):
            to = place.other(k)
            cp = remote(
                src_of(to), dst.at[rows], asend.at[slot, k], arecv.at[slot, t], {"t": to}
            )
            cp.start()
            sends.append(cp)

    def shared(dst, slot, size):
        for k in range(1, tn):
            frm = place.other(k)
            ref = dst.at[slot_rows(g * tn + frm, size)]
            remote(ref, ref, asend.at[slot, k], arecv.at[slot, frm], {"t": frm}).wait_recv()

    depth = ti[0].shape[2]
    triple_cols, inner_cols = wts[0].shape[1], wis[0].shape[1]
    vec_rows = vec.shape[0]
    shares = [(lambda to: vec, vec_o, vec_rows)]
    for layer in range(layers):
        lay = layer
        shares.append((lambda to, lay=lay: ti[0].at[lay, to], wts[layer], depth))
        shares.append((lambda to, lay=lay: ti[1].at[lay, to], wis[layer], depth))
    for slot, (src_of, dst, size) in enumerate(shares):
        share(src_of, dst, slot)
    prows = proj.shape[1]
    orows = outer.shape[1]
    for layer in range(layers):
        near(outer.at[layer], wos[layer].at[slot_rows(g, orows)])
        src = proj.at[layer]

        @pl.when(moved)
        def _():
            dst = wps[layer].at[slot_rows(lax.rem(r, gn), prows)]
            remote(src, dst, psend.at[layer], precv.at[layer], target).start()

        @pl.when(jnp.logical_not(moved))
        def _():
            pltpu.make_async_copy(src, wps[layer].at[slot_rows(g, prows)], psend.at[layer]).start()

    near(seg, seg_o.at[slot_rows(c, 8)])
    for k in range(1, span):
        to = lax.rem(c + k, span)
        cp = remote(seg, seg_o.at[slot_rows(c, 8)], gsend.at[k], grecv.at[c], place.line(to))
        cp.start()
        sends.append(cp)
    move(cot, cot_o, 1)

    sems = (ssem, rsem)
    orders = bit_orders(place)
    chunks, slot = [], 0
    waits = []

    def add(ref, block, ready):
        nonlocal slot
        parts = []
        cols = ref.shape[1]
        pieces = halves(cols) if cols >= 256 else [pl.ds(0, cols)]
        for i, piece in enumerate(pieces):
            parts.append(Doubling(place, ref, block, piece, orders[i], sems, slot))
            slot += 1
        chunks.append(parts)
        waits.append(ready)

    for cp in local:
        cp.wait()
    add(vec_o, tn * vec_rows, lambda: shared(vec_o, 0, vec_rows))
    for layer in range(layers):
        base = 1 + 2 * layer

        def proj_ready(layer=layer):
            ref = wps[layer].at[slot_rows(g, prows)]

            @pl.when(moved)
            def _():
                cp = remote(ref, ref, psend.at[layer], precv.at[layer], target)
                cp.wait_recv()
                cp.wait_send()

            @pl.when(jnp.logical_not(moved))
            def _():
                pltpu.make_async_copy(proj.at[layer], ref, psend.at[layer]).wait()

        add(wts[layer], tn * depth, lambda base=base, layer=layer: shared(wts[layer], base, depth))
        add(wis[layer], tn * depth, lambda base=base, layer=layer: shared(wis[layer], base + 1, depth))
        add(wos[layer], orows, lambda: None)
        add(wps[layer], prows, proj_ready)
    steps = len(place.bits) + 1
    for turn in range(len(chunks) + steps - 1):
        for step in range(steps):
            i = turn - step
            if 0 <= i < len(chunks):
                if step == 0:
                    waits[i]()
                for part in chunks[i]:
                    part.advance(step)
    for parts in chunks:
        for part in parts:
            part.finish()
    for cp in sends:
        cp.wait_send()
    for k in range(1, span):
        frm = lax.rem(c + k, span)
        ref = seg_o.at[slot_rows(frm, 8)]
        remote(ref, ref, gsend.at[k], grecv.at[frm], place.line(frm)).wait_recv()
    moved_in(tok, tok_o, 0)
    moved_in(cot, cot_o, 1)


ANY = pl.BlockSpec(memory_space=pl.ANY)


def open_call(gn, tn, tokens, cotangent, segments, vec, tri, inn, outer, proj):
    layers = outer.shape[0]
    _, half, model = tokens.shape
    rows = tn * tri.shape[2]
    dma = pltpu.SemaphoreType.DMA

    def body(tok, cot, seg, vec, tri, inn, *rest):
        open_kernel(gn, tn, layers, tok, cot, seg, vec, (tri, inn), *rest)

    outs = (
        [shape((2 * half, model), BF16)] * 2
        + [shape((2 * tn * 8, 128), jnp.int32), shape((gn * tn * vec.shape[0], 128), BF16)]
        + [shape((gn * rows, tri.shape[3]), BF16)] * layers
        + [shape((gn * rows, inn.shape[3]), BF16)] * layers
        + [shape((gn * outer.shape[1], model), BF16)] * layers
        + [shape((gn * proj.shape[1], model), BF16)] * layers
    )
    slots = 1 + 8 * layers
    return pl.pallas_call(
        body,
        out_shape=tuple(outs),
        in_specs=[ANY] * 8,
        out_specs=tuple([ANY] * len(outs)),
        scratch_shapes=[
            dma((slots, gn)), dma((slots, gn)), dma((2 + 3 * layers,)),
            dma((1 + 2 * layers, tn)), dma((1 + 2 * layers, tn)),
            dma((layers,)), dma((layers,)), dma((2, 2)), dma((2, 2)),
            dma((2 * tn,)), dma((2 * tn,)),
        ],
        compiler_params=params_of(2),
        name="opening",
    )(tokens, cotangent, segments, vec, tri, inn, outer, proj)


class Halving:
    def __init__(self, place, acc, inbox, block, cols, order, sems, slot):
        self.place, self.acc, self.inbox, self.block, self.cols = place, acc, inbox, block, cols
        self.send, self.recv, self.slot = sems[0], sems[1], slot
        self.plan, index, base = [], 0, 0
        for bit, runs in reversed(runs_by_step(place, order)):
            entry = []
            for start, count in runs:
                entry.append((bit, start, count, index, base))
                index += 1
                base += count
            self.plan.append(entry)

    def copy(self, bit, start, count, index, base):
        rows = pl.ds(pl.multiple_of(flip(start, bit) * self.block, self.block), count * self.block)
        return remote(
            self.acc.at[rows, self.cols],
            self.inbox.at[pl.ds(base * self.block, count * self.block), self.cols],
            self.send.at[self.slot, index],
            self.recv.at[self.slot, index],
            self.place.group(flip(self.place.g, bit)),
        )

    def advance(self, step):
        if step > 0:
            for item in self.plan[step - 1]:
                self.copy(*item).wait_recv()
                _, start, count, _, base = item

                def add(i, carry):
                    rows = pl.ds(pl.multiple_of((start + i) * self.block, self.block), self.block)
                    came = pl.ds(pl.multiple_of((base + i) * self.block, self.block), self.block)
                    value = self.acc[rows, self.cols].astype(F32) + self.inbox[came, self.cols].astype(F32)
                    self.acc[rows, self.cols] = value.astype(BF16)
                    return carry

                lax.fori_loop(0, count, add, 0)
        if step < len(self.plan):
            for item in self.plan[step]:
                self.copy(*item).start()

    def finish(self):
        for entry in self.plan:
            for item in entry:
                self.copy(*item).wait_send()


def close_kernel(
    gn, tn, layers,
    out_in, grad_in, flat, dwts, dwis, dwos, dwps,
    out_o, grad_o, flat_o, triple_o, proj_o, inner_o, outer_o,
    accs, boxes, cross, projbox, flatbox,
    lsem, hs, hr, cs, cr, ps, pr, ms, mr, fs, fr,
):
    place = Place(gn, tn)
    g, t, c = place.g, place.t, place.c
    target, source, r, q = proj_places(place)
    moved = q != r
    loads = []
    for i, src in enumerate(dwts + dwis + dwos + dwps):
        cp = pltpu.make_async_copy(src, accs[i], lsem.at[i])
        cp.start()
        loads.append(cp)
    line_barrier(place, (target, moved))
    half = out_o.shape[1]

    def move(src, dst, slot):
        for s in range(2):
            to = 2 * t + s

            @pl.when(to == c)
            def _():
                pltpu.make_async_copy(src.at[pl.ds(s * half, half)], dst.at[place.h], ms.at[slot, s]).start()

            @pl.when(to != c)
            def _():
                remote(
                    src.at[pl.ds(s * half, half)], dst.at[place.h], ms.at[slot, s], mr.at[slot, place.h], place.line(to)
                ).start()

    def moved_in(src, dst, slot):
        for s in range(2):
            to = 2 * t + s

            @pl.when(to == c)
            def _():
                pltpu.make_async_copy(src.at[pl.ds(s * half, half)], dst.at[place.h], ms.at[slot, s]).wait()

            @pl.when(to != c)
            def _():
                remote(
                    src.at[pl.ds(s * half, half)], dst.at[place.h], ms.at[slot, s], mr.at[slot, place.h], place.line(to)
                ).wait_send()

        for i in range(2):

            @pl.when(i * tn + c // 2 != c)
            def _():
                remote(
                    src.at[pl.ds(0, half)], dst.at[i], ms.at[slot, 0], mr.at[slot, i], place.line(c)
                ).wait_recv()

    move(grad_in, grad_o, 0)
    move(out_in, out_o, 1)
    orders = bit_orders(place)
    chunks, slot = [], 0
    plans = []
    for layer in reversed(range(layers)):
        for kind in range(4):
            plans.append((kind, layer))
    for kind, layer in plans:
        i = kind * layers + layer
        acc = accs[i]
        block = acc.shape[0] // gn
        parts = []
        for k, cols in enumerate(halves(acc.shape[1])):
            parts.append(Halving(place, acc, boxes[kind].at[layer], block, cols, orders[k], (hs, hr), slot))
            slot += 1
        chunks.append(parts)

    tbits = [1 << i for i in range(tn.bit_length() - 1)]
    exchanges = [("g", bit) for bit in place.bits] + [("t", bit) for bit in tbits]
    flat_o[...] = flat[...]

    def exchange(k):
        kind, bit = exchanges[k]
        to = place.group(flip(g, bit)) if kind == "g" else {"t": flip(t, bit)}
        return remote(flatbox.at[0, k], flatbox.at[1, k], fs.at[k], fr.at[k], to)

    def flat_turn(k):
        if k > 0 and k <= len(exchanges):
            exchange(k - 1).wait_recv()
            flat_o[...] += flatbox[1, k - 1]
        if k < len(exchanges):
            flatbox[0, k] = flat_o[...]
            exchange(k).start()

    steps = len(place.bits) + 1

    def cross_copy(kind, layer, to, slot_of):
        acc = accs[kind * layers + layer]
        rows = acc.shape[0] // (gn * tn)
        src = acc.at[pl.ds(pl.multiple_of((g * tn + to) * rows, rows), rows)]
        return remote(
            src, cross[kind].at[layer, t], cs.at[kind, layer, slot_of], cr.at[kind, layer, t], {"t": to}
        )

    def proj_copy(layer):
        acc = accs[3 * layers + layer]
        rows = acc.shape[0] // gn
        src = acc.at[pl.ds(pl.multiple_of(g * rows, rows), rows)]
        return src, remote(src, projbox.at[layer], ps.at[layer], pr.at[layer], source)

    def owned(kind, layer):
        acc = accs[kind * layers + layer]
        if kind < 2:
            rows = acc.shape[0] // (gn * tn)
            for k in range(1, tn):
                cross_copy(kind, layer, place.other(k), k).start()
            cross[kind][layer, t] = acc[pl.ds(pl.multiple_of((g * tn + t) * rows, rows), rows), :]
        elif kind == 2:
            rows = acc.shape[0] // gn
            outer_o[layer] = acc[pl.ds(pl.multiple_of(g * rows, rows), rows), :].astype(F32)
        else:

            @pl.when(moved)
            def _():
                proj_copy(layer)[1].start()

            @pl.when(jnp.logical_not(moved))
            def _():
                rows = acc.shape[0] // gn
                projbox[layer] = acc[pl.ds(pl.multiple_of(g * rows, rows), rows), :]

    def settle(kind, layer):
        if kind < 2:
            for k in range(1, tn):
                frm = place.other(k)
                remote(
                    cross[kind].at[layer, frm], cross[kind].at[layer, frm], cs.at[kind, layer, k],
                    cr.at[kind, layer, frm], {"t": frm},
                ).wait_recv()
            groups = 3 if kind == 0 else gn
            out = triple_o if kind == 0 else inner_o
            wide = cross[kind].shape[3] // groups
            for s in range(tn):
                for i in range(groups):
                    at = (i * tn + s) * wide
                    out[layer, :, at : at + wide] = cross[kind][layer, s, :, i * wide : (i + 1) * wide].astype(F32)
        elif kind == 3:

            @pl.when(moved)
            def _():
                proj_copy(layer)[1].wait_recv()

            proj_o[layer] = projbox[layer].astype(F32)

    total = len(chunks) + steps + 1
    for turn in range(max(total, len(exchanges) + 1)):
        if turn <= len(exchanges):
            flat_turn(turn)
        for step in range(steps + 2):
            i = turn - step
            if 0 <= i < len(chunks):
                kind, layer = plans[i]
                if step == 0:
                    loads[kind * layers + layer].wait()
                if step < steps:
                    for part in chunks[i]:
                        part.advance(step)
                if step == steps - 1:
                    owned(kind, layer)
                if step == steps + 1:
                    settle(kind, layer)
    for k in range(len(exchanges)):
        exchange(k).wait_send()
    for (kind, layer), parts in zip(plans, chunks):
        for part in parts:
            part.finish()
        if kind < 2:
            for k in range(1, tn):
                cross_copy(kind, layer, place.other(k), k).wait_send()
        elif kind == 3:

            @pl.when(moved)
            def _():
                proj_copy(layer)[1].wait_send()

    moved_in(grad_in, grad_o, 0)
    moved_in(out_in, out_o, 1)


def close_call(gn, tn, output, grad, flat, mats):
    layers = len(mats)
    size, model = output.shape
    dwts, dwis, dwos, dwps = ([m[k] for m in mats] for k in range(4))
    dma = pltpu.SemaphoreType.DMA
    width3, units = dwts[0].shape[1], dwis[0].shape[1]
    shard = dwts[0].shape[0] // (gn * tn)
    prows, orows = dwps[0].shape[0] // gn, dwos[0].shape[0] // gn
    every = dwts + dwis + dwos + dwps
    boxes = [
        pltpu.VMEM((layers, (gn - 1) * m.shape[0] // gn, m.shape[1]), BF16)
        for m in (dwts[0], dwis[0], dwos[0], dwps[0])
    ]
    exchanges = (gn * tn).bit_length() - 1

    def body(out_in, grad_in, flat_in, *rest):
        refs = list(rest)
        groups = [refs[i * layers : (i + 1) * layers] for i in range(4)]
        outs = refs[4 * layers : 4 * layers + 7]
        rest = refs[4 * layers + 7 :]
        accs, rest = rest[: 4 * layers], rest[4 * layers :]
        box, rest = rest[:4], rest[4:]
        cross, rest = rest[:2], rest[2:]
        close_kernel(gn, tn, layers, out_in, grad_in, flat_in, *groups, *outs, accs, box, cross, *rest)

    outs = (
        shape((2, size // 2, model), BF16),
        shape((2, size // 2, model), BF16),
        shape(flat.shape, F32),
        shape((layers, shard, width3 * tn), F32),
        shape((layers, prows, model), F32),
        shape((layers, shard, units * tn), F32),
        shape((layers, orows, model), F32),
    )
    slots = 8 * layers
    return pl.pallas_call(
        body,
        out_shape=outs,
        in_specs=[ANY, ANY, VM] + [ANY] * (4 * layers),
        out_specs=(ANY, ANY, VM, VM, VM, VM, VM),
        scratch_shapes=[pltpu.VMEM(m.shape, BF16) for m in every]
        + boxes
        + [
            pltpu.VMEM((layers, tn, shard, width3), BF16),
            pltpu.VMEM((layers, tn, shard, units), BF16),
            pltpu.VMEM((layers, prows, model), BF16),
            pltpu.VMEM((2, exchanges) + flat.shape, F32),
            dma((4 * layers,)),
            dma((slots, gn)), dma((slots, gn)),
            dma((2, layers, tn)), dma((2, layers, tn)),
            dma((layers,)), dma((layers,)),
            dma((2, 2)), dma((2, 2)),
            dma((exchanges,)), dma((exchanges,)),
        ],
        compiler_params=params_of(3),
        name="closing",
    )(output, grad, flat, *dwts, *dwis, *dwos, *dwps)


GROUPS = ("dp", "h")
EVERY = ("dp", "h", "t")


def to_group(tn, blocks):
    h, t = lax.axis_index("h"), lax.axis_index("t")
    count = 2 * tn
    parity = lax.rem(t, 2)
    got = []
    for j in range(2):
        moves = [(c, ((c + j) % 2) * tn + c // 2) for c in range(count)]
        piece = jnp.where(lax.rem(parity + j, 2) == 0, blocks[0], blocks[1])
        got.append(lax.ppermute(piece, ("h", "t"), moves))
    low = jnp.where(h == 0, got[0], got[1])
    high = jnp.where(h == 0, got[1], got[0])
    return jnp.concatenate([low, high], axis=0)


def from_group(tn, rows):
    h, t = lax.axis_index("h"), lax.axis_index("t")
    count = 2 * tn
    parity = lax.rem(t, 2)
    size = rows.shape[0] // 2
    got = []
    for j in range(2):
        moves = [(((c + j) % 2) * tn + c // 2, c) for c in range(count)]
        piece = jnp.where(lax.rem(h + j, 2) == 0, rows[:size], rows[size:])
        got.append(lax.ppermute(piece, ("h", "t"), moves))
    first = jnp.where(parity == 0, got[0], got[1])
    second = jnp.where(parity == 0, got[1], got[0])
    return jnp.stack([first, second], axis=0)


def proj_moves(gn, tn):
    return [(r, (r % gn) * tn + r // gn) for r in range(gn * tn)]


def slice_columns(weight, gn, tn):
    rows, cols = weight.shape
    return weight.reshape(rows, gn, tn, cols // (gn * tn)).transpose(2, 0, 1, 3).reshape(tn, rows, cols // tn)


def slice_triple(weight, tn):
    rows, cols = weight.shape
    return weight.reshape(rows, 3, tn, cols // (3 * tn)).transpose(2, 0, 1, 3).reshape(tn, rows, cols // tn)


def gather_weights(gn, tn, triple, proj, inner, outer):
    def spread(parts):
        moved = lax.all_to_all(parts, "t", 0, 0, tiled=True)
        whole = lax.all_gather(moved.reshape(-1, moved.shape[-1]), GROUPS, axis=0, tiled=True)
        return whole

    wt = spread(slice_triple(triple, tn))
    wi = spread(slice_columns(inner, gn, tn))
    wo = lax.all_gather(outer, GROUPS, axis=0, tiled=True)
    wp = lax.all_gather(lax.ppermute(proj, EVERY, proj_moves(gn, tn)), GROUPS, axis=0, tiled=True)
    return wt, wi, wo, wp


def reduce_weights(gn, tn, dwt, dwi, dwo, dwp):
    def back(parts):
        mine = lax.psum_scatter(parts, GROUPS, scatter_dimension=0, tiled=True)
        rows = mine.shape[0] // tn
        return lax.all_to_all(mine.reshape(tn, rows, -1), "t", 0, 0, tiled=True).astype(F32)

    triple = back(dwt)
    rows = triple.shape[1]
    triple = triple.reshape(tn, rows, 3, -1).transpose(1, 2, 0, 3).reshape(rows, -1)
    inner = back(dwi)
    inner = inner.reshape(tn, rows, gn, -1).transpose(1, 2, 0, 3).reshape(rows, -1)
    outer = lax.psum_scatter(dwo, GROUPS, scatter_dimension=0, tiled=True).astype(F32)
    proj = lax.psum_scatter(dwp, GROUPS, scatter_dimension=0, tiled=True)
    proj = lax.ppermute(proj, EVERY, [(b, a) for a, b in proj_moves(gn, tn)]).astype(F32)
    return triple, proj, inner, outer


def per_device(
    gn, tn,
    tokens, segments, cotangent, triple_weight, triple_bias, proj_weight, proj_bias, inner_weight, inner_bias,
    outer_weight, outer_bias, first_gain, first_shift, second_gain, second_shift,
):
    layers = triple_weight.shape[0]
    model = tokens.shape[2]
    span = tokens.shape[1] * 2 * tn
    h, t = lax.axis_index("h"), lax.axis_index("t")
    device = (lax.axis_index("dp") * 2 + h) * tn + t
    shards = gn * tn
    heads_wide = model // tn
    units = outer_weight.shape[1] * gn

    small = (triple_bias, inner_bias, proj_bias, outer_bias, first_gain, first_shift, second_gain, second_shift)
    starts = [0]
    for item in small:
        starts.append(starts[-1] + item.shape[1])
    packed = jnp.concatenate(small, axis=1)
    rows = triple_weight.shape[1]
    direct = rows % 16 == 0
    if direct:
        count = -(-packed.size // 2048) * 2048
        vec = jnp.pad(packed.reshape(-1), (0, count - packed.size)).reshape(-1, 128)
        opened = open_call(
            gn, tn, tokens, cotangent, jnp.pad(segments, ((0, 6), (0, 0))), vec,
            triple_weight.reshape(layers, rows, 3, tn, -1).transpose(0, 3, 1, 2, 4).reshape(layers, tn, rows, -1),
            inner_weight.reshape(layers, rows, gn, tn, -1).transpose(0, 3, 1, 2, 4).reshape(layers, tn, rows, -1),
            outer_weight, proj_weight,
        )
        x, cot, segs_all, vec_all = opened[0].astype(F32), opened[1].astype(F32), opened[2], opened[3]
        weights = [tuple(opened[4 + k * layers + layer] for k in (0, 1, 2, 3)) for layer in range(layers)]
        segs_all = segs_all.reshape(2 * tn, 8, -1)[:, :2].transpose(1, 0, 2).reshape(2, span)
        everything = vec_all.reshape(shards, -1)[:, : packed.size].reshape((shards,) + packed.shape).astype(F32)
    else:
        x = to_group(tn, tokens).astype(F32)
        cot = to_group(tn, cotangent).astype(F32)
        segs_all = lax.all_gather(segments, ("h", "t"), axis=1, tiled=True)
        everything = lax.all_gather(packed[None], EVERY, axis=0, tiled=True).astype(F32)
        weights = [
            gather_weights(
                gn, tn, triple_weight[layer], proj_weight[layer], inner_weight[layer], outer_weight[layer]
            )
            for layer in range(layers)
        ]
    segs = jnp.where(h == 0, segs_all[0], segs_all[1])
    place = jnp.arange(span, dtype=jnp.int32)
    segs = jnp.where(segs == 0, -1 - place, segs)
    freq = 10000.0 ** (-(2.0 * jnp.arange(ROT // 2, dtype=F32)) / ROT)
    angle = place.astype(F32)[:, None] * freq[None, :]
    cosine, sine = jnp.cos(angle), jnp.sin(angle)
    none = jnp.zeros((span, HD - ROT), F32)
    empty = jnp.zeros_like(sine)
    ctab = jnp.concatenate([cosine, cosine, none + 1.0] * (128 // HD), axis=1)
    satab = jnp.concatenate([-sine, empty, none] * (128 // HD), axis=1)
    sbtab = jnp.concatenate([empty, sine, none] * (128 // HD), axis=1)
    tables = (segs[:, None], segs[None, :], ctab, satab, sbtab)

    def vector(layer, i):
        return everything[:, layer, starts[i] : starts[i + 1]].reshape(-1)

    vecs, bts, bis = [], [], []
    for layer in range(layers):
        bt = lax.dynamic_index_in_dim(vector(layer, 0).reshape(3, tn, heads_wide), t, 1, keepdims=False)
        bts.append(bt.reshape(1, -1))
        bi = lax.dynamic_index_in_dim(vector(layer, 1).reshape(gn, tn, -1), t, 1, keepdims=False)
        bis.append(bi.reshape(1, -1))
        zero = jnp.zeros((model,), F32)
        vecs.append(
            jnp.stack(
                [vector(layer, 4), vector(layer, 5), vector(layer, 6), vector(layer, 7)]
                + [vector(layer, 2) + vector(layer, 3), zero, zero, zero]
            )
        )

    inputs, kept = [], []
    for layer in range(layers):
        inputs.append(x)
        x, *saved = forward_layer(tn, x, weights[layer], vecs[layer], bts[layer], bis[layer], tables)
        kept.append(saved)
    output = x.astype(BF16)
    grad = cot
    mats, flats = [None] * layers, [None] * layers
    for layer in reversed(range(layers)):
        grad, dwt, dwi, dwo, dwp, dvec, dbt, dbi = backward_layer(
            tn, grad, inputs[layer], weights[layer], vecs[layer], tables, kept[layer]
        )
        mats[layer] = (dwt, dwi, dwo, dwp)
        triple = lax.dynamic_update_slice(
            jnp.zeros((3, tn, heads_wide), F32), dbt.reshape(3, 1, heads_wide), (0, t, 0)
        )
        inner = lax.dynamic_update_slice(
            jnp.zeros((gn, tn, units // gn), F32), dbi.reshape(gn, 1, units // gn), (0, t, 0)
        )
        flats[layer] = jnp.concatenate([dvec[:5].reshape(-1), triple.reshape(-1), inner.reshape(-1)])
    tokens_grad = grad.astype(BF16)
    flat = jnp.stack(flats)
    if direct:
        output, tokens_grad, summed, triple, proj, inner, outer = close_call(
            gn, tn, output, tokens_grad, flat.reshape(-1, 1024), mats
        )
        summed = summed.reshape(flat.shape)
    else:
        output, tokens_grad = from_group(tn, output), from_group(tn, tokens_grad)
        done = [reduce_weights(gn, tn, *m) for m in mats]
        triple, proj, inner, outer = (jnp.stack([m[k] for m in done]) for k in range(4))
        summed = lax.psum(flat, EVERY)

    def own(start, length):
        piece = length // shards
        return lax.dynamic_slice_in_dim(summed, start + device * piece, piece, 1)

    base = 5 * model
    bias_sum = own(4 * model, model)
    return (
        output,
        tokens_grad,
        triple,
        own(base, 2 * model),
        own(base + 2 * model, model),
        proj,
        bias_sum,
        inner,
        own(base + 3 * model, units * tn),
        outer,
        bias_sum,
        own(0, model),
        own(model, model),
        own(2 * model, model),
        own(3 * model, model),
    )


def solution(mesh):
    dp, ctx = mesh.shape["dp"], mesh.shape["ctx"]
    tn = ctx // 2
    gn = 2 * dp
    fine = Mesh(mesh.devices.reshape(dp, 2, tn), EVERY)
    seq = P("dp", ("h", "t"), None)
    mat = P(None, EVERY, None)
    row = P(None, EVERY)
    in_specs = (seq, P("dp", ("h", "t")), seq, mat, row, mat, row, mat, row, mat, row, row, row, row, row)
    out_specs = (seq, seq, mat, row, row, mat, row, mat, row, mat, row, row, row, row, row)
    return jax.shard_map(
        functools.partial(per_device, gn, tn), mesh=fine, in_specs=in_specs, out_specs=out_specs, check_vma=False
    )
```

```python
import functools
import math

import jax
import jax.numpy as jnp
import numpy as np
from jax import lax
from jax.experimental import pallas as pl
from jax.experimental.pallas import tpu as pltpu
from jax.sharding import Mesh
from jax.sharding import PartitionSpec as P

HD = 64
ROT = 16
EPSILON = 1e-05
NEG_LARGE = -1e30
MESH = pl.DeviceIdType.MESH
BF16 = jnp.bfloat16
F32 = jnp.float32
VMEM_LIMIT = 60 * 1024 * 1024


def dot(a, b, dims):
    return lax.dot_general(a, b, (dims, ((), ())), preferred_element_type=F32)


NN = ((1,), (0,))
NT = ((1,), (1,))
TN = ((0,), (0,))


def rows_of(b, size):
    return pl.ds(pl.multiple_of(b * size, size), size)


def group_barrier(tn):
    t = lax.axis_index("t")
    zc, co = t // 2, lax.rem(t, 2)
    chips = tn // 2
    sem = pltpu.get_barrier_semaphore()
    peers = [zc * 2 + 1 - co] + [lax.rem(zc + k, chips) * 2 + co for k in range(1, chips)]
    for p in peers:
        pl.semaphore_signal(sem, inc=1, device_id={"t": p}, device_id_type=MESH)
    pl.semaphore_wait(sem, len(peers))


class Spread:
    def __init__(self, tn, buf, size, ssem, fsem, rsem):
        self.tn, self.buf, self.size = tn, buf, size
        self.ssem, self.fsem, self.rsem = ssem, fsem, rsem
        self.t = lax.axis_index("t")
        self.zc, self.co = self.t // 2, lax.rem(self.t, 2)
        self.chips = tn // 2

    def copy(self, block, send, to):
        ref = self.buf.at[rows_of(block, self.size)]
        return pltpu.make_async_remote_copy(
            ref, ref, send, self.rsem.at[block], device_id={"t": to}, device_id_type=MESH
        )

    def start(self):
        for k in range(1, self.chips):
            chip = lax.rem(self.zc + k, self.chips)
            self.copy(self.t, self.ssem.at[k], chip * 2 + self.co).start()
        self.copy(self.t, self.ssem.at[0], self.zc * 2 + 1 - self.co).start()

    def peer_core(self):
        b = self.zc * 2 + 1 - self.co
        self.copy(b, self.ssem.at[0], b).wait_recv()
        return b

    def same_core(self, k):
        b = lax.rem(self.zc + self.chips - k, self.chips) * 2 + self.co
        self.copy(b, self.fsem.at[k], b).wait_recv()
        self.copy(b, self.fsem.at[k], self.zc * 2 + 1 - self.co).start()
        return b

    def other_core(self, k):
        b = lax.rem(self.zc + self.chips - k, self.chips) * 2 + 1 - self.co
        self.copy(b, self.fsem.at[k], b).wait_recv()
        return b

    def finish(self):
        for k in range(self.chips):
            self.copy(self.t, self.ssem.at[k], self.t).wait_send()
        for k in range(1, self.chips):
            self.copy(self.t, self.fsem.at[k], self.t).wait_send()


class Gather:
    def __init__(self, tn, tocore, fromcore, toici, fromici, sems):
        self.tn = tn
        self.tocore, self.fromcore, self.toici, self.fromici = tocore, fromcore, toici, fromici
        self.cs, self.cr, self.ls, self.lr = sems
        self.t = lax.axis_index("t")
        self.zc, self.co = self.t // 2, lax.rem(self.t, 2)
        self.chips = tn // 2

    def core_copy(self, chip):
        return pltpu.make_async_remote_copy(
            self.tocore.at[chip],
            self.fromcore.at[chip],
            self.cs.at[chip],
            self.cr.at[chip],
            device_id={"t": self.zc * 2 + 1 - self.co},
            device_id_type=MESH,
        )

    def link_copy(self, chip, slot):
        return pltpu.make_async_remote_copy(
            self.toici.at[chip],
            self.fromici.at[slot],
            self.ls.at[chip],
            self.lr.at[slot],
            device_id={"t": chip * 2 + self.co},
            device_id_type=MESH,
        )

    def send_core(self, chip):
        self.core_copy(chip).start()

    def send_link(self, chip):
        self.core_copy(chip).wait_recv()
        self.toici[chip] = (self.toici[chip].astype(F32) + self.fromcore[chip].astype(F32)).astype(BF16)
        self.link_copy(chip, self.zc).start()

    def total(self):
        self.core_copy(self.zc).wait_recv()
        value = self.fromcore[self.zc].astype(F32)
        for k in range(1, self.chips):
            chip = lax.rem(self.zc + k, self.chips)
            self.link_copy(chip, chip).wait_recv()
            value = value + self.fromici[chip].astype(F32)
        return value

    def finish(self):
        for chip in range(self.chips):
            self.core_copy(chip).wait_send()
        for k in range(1, self.chips):
            chip = lax.rem(self.zc + k, self.chips)
            self.link_copy(chip, self.zc).wait_send()


def norm_stats(x):
    mean = jnp.mean(x, axis=-1, keepdims=True)
    centred = x - mean
    inverse = lax.rsqrt(jnp.mean(centred * centred, axis=-1, keepdims=True) + EPSILON)
    return centred * inverse, inverse


def widen(tab, width):
    return jnp.concatenate([tab] * (width // tab.shape[1]), axis=1)


def turn(x, cos, sa, sb, sign):
    width = x.shape[1]
    cos, sa, sb = widen(cos, width), widen(sa, width), widen(sb, width)
    side = pltpu.roll(x, width - ROT // 2, 1) * sa + pltpu.roll(x, ROT // 2, 1) * sb
    return x * cos + sign * side


def head_masks(width, dtype):
    lane = lax.broadcasted_iota(jnp.int32, (1, width), 1) // HD
    return [(lane == h).astype(F32).astype(dtype) for h in range(width // HD)]


def pair_bias(qb, kb, size, segcol, segrow):
    qpos = lax.broadcasted_iota(jnp.int32, (size, size), 0) + qb * size
    kpos = lax.broadcasted_iota(jnp.int32, (size, size), 1) + kb * size
    same = segcol[rows_of(qb, size), :] == segrow[:, rows_of(kb, size)]
    return jnp.where(same & (kpos <= qpos), 0.0, NEG_LARGE)


TILE = 256
SKEW = 1


class Forward:
    def __init__(self, tn, size, x, w, vecs, segs, tables, kept, keep):
        self.tn, self.size, self.chips = tn, size, tn // 2
        self.x, self.keep = x, keep
        self.wt, self.wi, self.wo, self.wp = w
        self.vec, self.bt, self.bi = vecs
        self.segcol, self.segrow = segs
        self.tables = tables
        self.n, self.q, self.k, self.v, self.o, self.lse, self.g, self.gp = kept
        self.width, self.units = self.q.shape[1], self.g.shape[1]
        self.heads = self.width // HD

    def norm(self, t):
        own, _ = norm_stats(self.x[...])
        self.n[rows_of(t, self.size), :] = own.astype(BF16)

    def heads_in(self, b):
        width, vec, bt = self.width, self.vec, self.bt
        rows = rows_of(b, self.size)
        h1 = (self.n[rows, :].astype(F32) * vec[0:1, :] + vec[1:2, :]).astype(BF16)
        cos, sa, sb = (tab[rows, :] for tab in self.tables)
        q = dot(h1, self.wt[:, 0:width], NN) + bt[:, 0:width]
        low = turn(q, cos, sa, sb, 1.0).astype(BF16).astype(F32)
        self.q[rows, :] = (low * (1.0 / math.sqrt(HD))).astype(BF16)
        k = dot(h1, self.wt[:, width : 2 * width], NN) + bt[:, width : 2 * width]
        self.k[rows, :] = turn(k, cos, sa, sb, 1.0).astype(BF16)
        v = dot(h1, self.wt[:, 2 * width : 3 * width], NN) + bt[:, 2 * width : 3 * width]
        self.v[rows, :] = v.astype(BF16)

    def mixer_in(self, b):
        rows = rows_of(b, self.size)
        h2 = (self.n[rows, :].astype(F32) * self.vec[2:3, :] + self.vec[3:4, :]).astype(BF16)

        def mix(j, carry):
            cols = rows_of(j, TILE)
            u = dot(h2, self.wi[:, cols], NN) + self.bi[:, cols]
            half = 0.5 + 0.5 * lax.erf(u * (1.0 / math.sqrt(2.0)))
            self.g[rows, cols] = (u * half).astype(BF16)
            bell = jnp.exp(-0.5 * u * u) * (1.0 / math.sqrt(2.0 * math.pi))
            self.gp[rows, cols] = (half + u * bell).astype(BF16)
            return carry

        lax.fori_loop(0, self.units // TILE, mix, 0)

    def attend(self, b):
        size, width, heads = self.size, self.width, self.heads
        masks = head_masks(width, F32)
        lane = lax.broadcasted_iota(jnp.int32, (1, 128), 1)
        rows = rows_of(b, size)
        qb = self.q[rows, :]
        qs = [qb * masks[h].astype(BF16) for h in range(heads)]

        def step(i, carry):
            peaks, sums, acc = carry
            kb = b - i
            keys = self.k[rows_of(kb, size), :]
            vals = self.v[rows_of(kb, size), :]
            bias = pair_bias(b, kb, size, self.segcol, self.segrow)
            new_peaks, new_sums = [], []
            scale = jnp.zeros((size, width), F32)
            add = jnp.zeros((size, width), F32)
            for h in range(heads):
                s = dot(qs[h], keys, NT) + bias
                peak = jnp.maximum(peaks[h], jnp.max(s, axis=1, keepdims=True))
                p = jnp.exp(s - peak)
                fade = jnp.exp(peaks[h] - peak)
                new_peaks.append(peak)
                new_sums.append(sums[h] * fade + jnp.sum(p, axis=1, keepdims=True))
                scale = scale + fade * masks[h]
                add = add + dot(p.astype(BF16), vals * masks[h].astype(BF16), NN)
            return tuple(new_peaks), tuple(new_sums), acc * scale + add

        start = (
            tuple(jnp.full((size, 1), NEG_LARGE, F32) for _ in range(heads)),
            tuple(jnp.zeros((size, 1), F32) for _ in range(heads)),
            jnp.zeros((size, width), F32),
        )
        peaks, sums, acc = lax.fori_loop(0, b + 1, step, start)
        scale = jnp.zeros((size, width), F32)
        lse = jnp.zeros((size, 128), F32)
        for h in range(heads):
            scale = scale + (1.0 / sums[h]) * masks[h]
            lse = jnp.where(lane == h, peaks[h] + jnp.log(sums[h]), lse)
        self.lse[rows, :] = lse
        self.o[rows, :] = acc * scale

    def branches(self, b, store):
        rows = rows_of(b, self.size)

        def part(j, carry):
            cols = rows_of(j, TILE)
            value = dot(self.g[rows, :], self.wo[:, cols], NN)
            store(cols, value + dot(self.o[rows, :].astype(BF16), self.wp[:, cols], NN))
            return carry

        lax.fori_loop(0, self.x.shape[1] // TILE, part, 0)

    def into(self, ref, chip):
        def store(cols, value):
            ref[chip, :, cols] = value.astype(BF16)

        return store

    def into_keep(self, cols, value):
        self.keep[:, cols] = value


def arrivals(spread):
    yield spread.t
    yield spread.peer_core()
    for i in range(1, spread.chips):
        yield spread.same_core(i)
        yield spread.other_core(i)


def far_first(spread):
    out = []
    for i in range(1, spread.chips):
        chip = lax.rem(spread.zc + i, spread.chips)
        out += [chip * 2 + 1 - spread.co, chip * 2 + spread.co]
    return out + [spread.zc * 2 + 1 - spread.co, spread.t]


def branch_sums(layer, spread, gather, tick=lambda: None):
    for i in range(1, spread.chips):
        chip = lax.rem(spread.zc + i, spread.chips)
        layer.branches(chip * 2 + 1 - spread.co, layer.into(gather.tocore, chip))
        gather.send_core(chip)
        layer.branches(chip * 2 + spread.co, layer.into(gather.toici, chip))
        gather.send_link(chip)
        tick()
    layer.branches(spread.zc * 2 + 1 - spread.co, layer.into(gather.tocore, spread.zc))
    gather.send_core(spread.zc)
    layer.branches(spread.t, layer.into_keep)
    tick()


def forward_kernel(
    tn, size,
    x_ref, wt, wi, wo, wp, vec, bt, bi, segcol, segrow, ctab, satab, sbtab,
    xo_ref, n_ref, q_ref, k_ref, v_ref, o_ref, lse_ref, g_ref, gp_ref,
    keep, tocore, fromcore, toici, fromici, ssem, fsem, rsem, cs, cr, ls, lr,
):
    group_barrier(tn)
    spread = Spread(tn, n_ref, size, ssem, fsem, rsem)
    gather = Gather(tn, tocore, fromcore, toici, fromici, (cs, cr, ls, lr))
    layer = Forward(
        tn, size, x_ref, (wt, wi, wo, wp), (vec, bt, bi), (segcol, segrow), (ctab, satab, sbtab),
        (n_ref, q_ref, k_ref, v_ref, o_ref, lse_ref, g_ref, gp_ref), keep,
    )
    layer.norm(spread.t)
    spread.start()
    for b in arrivals(spread):
        layer.heads_in(b)
        layer.mixer_in(b)
    for b in far_first(spread):
        layer.attend(b)
    branch_sums(layer, spread, gather)
    xo_ref[...] = x_ref[...] + vec[4:5, :] + keep[...] + gather.total()
    spread.finish()
    gather.finish()


def backward_kernel(
    tn, size,
    dy_ref, x_ref, wt, wi, wo, wp, vec, segcol, segrow, ctab, satab, sbtab,
    n_ref, q_ref, k_ref, v_ref, o_ref, lse_ref, g_ref, gp_ref,
    dx_ref, dwt, dwi, dwo, dwp, dvec, dbt, dbi,
    gb, do, du, dt, dq, dk, dv, dh2, keep,
    tocore, fromcore, toici, fromici, ssem, fsem, rsem, cs, cr, ls, lr,
):
    chips = tn // 2
    width = q_ref.shape[1]
    heads = width // HD
    units = g_ref.shape[1]
    model = x_ref.shape[1]
    group_barrier(tn)
    spread = Spread(tn, gb, size, ssem, fsem, rsem)
    gather = Gather(tn, tocore, fromcore, toici, fromici, (cs, cr, ls, lr))
    t, zc, co = spread.t, spread.zc, spread.co
    own = dy_ref[...].astype(F32).astype(BF16)
    gb[rows_of(t, size), :] = own
    spread.start()
    dvec[...] = jnp.zeros_like(dvec)
    dbt[...] = jnp.zeros_like(dbt)
    dbi[...] = jnp.zeros_like(dbi)
    dvec[4:5, :] = jnp.sum(own.astype(F32), axis=0, keepdims=True)
    dq[...] = jnp.zeros_like(dq)
    dk[...] = jnp.zeros_like(dk)
    dv[...] = jnp.zeros_like(dv)

    def mixer(b):
        rows = rows_of(b, size)
        grad = gb[rows, :]
        do[rows, :] = dot(grad, wp[...], NT).astype(BF16)

        def unit(j, carry):
            cols = rows_of(j, TILE)
            d = (dot(grad, wo[cols, :], NT) * gp_ref[rows, cols].astype(F32)).astype(BF16)
            du[rows, cols] = d
            dbi[0:1, cols] += jnp.sum(d.astype(F32), axis=0, keepdims=True)
            return carry

        lax.fori_loop(0, units // TILE, unit, 0)

        def back(j, carry):
            cols = rows_of(j, TILE)
            d = dot(du[rows, :], wi[cols, :], NT)
            dvec[2:3, cols] += jnp.sum(d * n_ref[rows, cols].astype(F32), axis=0, keepdims=True)
            dvec[3:4, cols] += jnp.sum(d, axis=0, keepdims=True)
            dh2[rows, cols] = d * vec[2:3, cols]
            return carry

        lax.fori_loop(0, model // TILE, back, 0)

    mixer(t)
    mixer(spread.peer_core())
    for i in range(1, chips):
        mixer(spread.same_core(i))
        mixer(spread.other_core(i))

    masks = head_masks(width, BF16)
    lane = lax.broadcasted_iota(jnp.int32, (1, 128), 1)
    up = zc >= (chips + 1) // 2
    tsize = tn

    def pair(qb, kb):
        qrows, krows = rows_of(qb, size), rows_of(kb, size)
        q, keys, vals = q_ref[qrows, :], k_ref[krows, :], v_ref[krows, :]
        grad = do[qrows, :]
        prod = grad.astype(F32) * o_ref[qrows, :]
        lse = lse_ref[qrows, :]
        bias = pair_bias(qb, kb, size, segcol, segrow)
        dq_new = jnp.zeros((size, width), F32)
        dk_new = jnp.zeros((size, width), F32)
        dv_new = jnp.zeros((size, width), F32)
        for h in range(heads):
            qh, gh = q * masks[h], grad * masks[h]
            total = jnp.sum(jnp.where(lane == h, lse, 0.0), axis=1, keepdims=True)
            delta = jnp.sum(prod * masks[h].astype(F32), axis=1, keepdims=True)
            p = jnp.exp(dot(qh, keys, NT) + bias - total)
            ds = (p * (dot(gh, vals, NT) - delta)).astype(BF16)
            dv_new = dv_new + dot(p.astype(BF16), gh, TN)
            dk_new = dk_new + dot(ds, qh, TN)
            dq_new = dq_new + dot(ds, keys * masks[h], NN)
        dq[qrows, :] += dq_new
        dk[krows, :] += dk_new
        dv[krows, :] += dv_new

    def attend_back(stage):
        pivot = jnp.where(up, stage, tsize - 1 - stage)

        def step(j, carry):
            pair(jnp.where(up, pivot + j, pivot), jnp.where(up, pivot, pivot - j))
            return carry

        lax.fori_loop(0, tsize - stage, step, 0)
        rows = rows_of(pivot, size)
        cos, sa, sb = ctab[rows, :], satab[rows, :], sbtab[rows, :]
        dt[rows, 0:width] = turn(dq[rows, :] * (1.0 / math.sqrt(HD)), cos, sa, sb, -1.0).astype(BF16)
        dt[rows, width : 2 * width] = turn(dk[rows, :], cos, sa, sb, -1.0).astype(BF16)
        dt[rows, 2 * width : 3 * width] = dv[rows, :].astype(BF16)
        block = dt[rows, :]
        dbt[...] += jnp.sum(block.astype(F32), axis=0, keepdims=True)

        def back(j, carry):
            cols = rows_of(j, TILE)
            d = dot(block, wt[cols, :], NT)
            dvec[0:1, cols] += jnp.sum(d * n_ref[rows, cols].astype(F32), axis=0, keepdims=True)
            dvec[1:2, cols] += jnp.sum(d, axis=0, keepdims=True)
            dh2[rows, cols] = dh2[rows, cols] + d * vec[0:1, cols]
            return carry

        lax.fori_loop(0, model // TILE, back, 0)
        value = dh2[rows, :]
        chip, core = pivot // 2, lax.rem(pivot, 2)

        @pl.when(core != co)
        def _():
            tocore[chip] = value.astype(BF16)
            gather.send_core(chip)

        @pl.when((core == co) & (chip != zc))
        def _():
            toici[chip] = value.astype(BF16)

        @pl.when(pivot == t)
        def _():
            keep[...] = value

        if stage % 2 == 1:

            @pl.when(chip != zc)
            def _():
                gather.send_link(chip)

    for stage in range(tn):
        attend_back(stage)

    def grad_one(j, carry):
        cols = rows_of(j, TILE)
        h1 = (n_ref[:, cols].astype(F32) * vec[0:1, cols] + vec[1:2, cols]).astype(BF16)
        dwt[cols, :] = dot(h1, dt[...], TN).astype(dwt.dtype)
        return carry

    lax.fori_loop(0, model // TILE, grad_one, 0)

    def grad_two(j, carry):
        cols = rows_of(j, TILE)
        h2 = (n_ref[:, cols].astype(F32) * vec[2:3, cols] + vec[3:4, cols]).astype(BF16)
        dwi[cols, :] = dot(h2, du[...], TN).astype(dwi.dtype)
        return carry

    lax.fori_loop(0, model // TILE, grad_two, 0)

    def grad_three(j, carry):
        cols = rows_of(j, TILE)
        dwo[cols, :] = dot(g_ref[:, cols], gb[...], TN).astype(dwo.dtype)
        return carry

    lax.fori_loop(0, units // TILE, grad_three, 0)
    small = min(TILE, width)

    def grad_four(j, carry):
        cols = rows_of(j, small)
        dwp[cols, :] = dot(o_ref[:, cols].astype(BF16), gb[...], TN).astype(dwp.dtype)
        return carry

    lax.fori_loop(0, width // small, grad_four, 0)

    own_n, inverse = norm_stats(x_ref[...])
    e = keep[...] + gather.total()
    inner = e - jnp.mean(e, axis=-1, keepdims=True) - own_n * jnp.mean(e * own_n, axis=-1, keepdims=True)
    dx_ref[...] = dy_ref[...].astype(F32) + inner * inverse
    spread.finish()
    gather.finish()


VM = pl.BlockSpec(memory_space=pltpu.VMEM)


def shape(dims, dtype):
    return jax.ShapeDtypeStruct(tuple(dims), dtype)


def group_sems(chips, tn):
    dma = pltpu.SemaphoreType.DMA
    return [dma((chips,)), dma((chips,)), dma((tn,)), dma((chips,)), dma((chips,)), dma((chips,)), dma((chips,))]


def group_buffers(chips, size, model):
    return [pltpu.VMEM((chips, size, model), BF16) for _ in range(4)]


def params_of(cid):
    return pltpu.CompilerParams(collective_id=cid, has_side_effects=True, vmem_limit_bytes=VMEM_LIMIT)


def forward_layer(tn, x, weights, vec, bt, bi, tables):
    wt, wi, wo, wp = weights
    size, model = x.shape
    length = size * tn
    width, units, chips = wp.shape[0], wo.shape[0], tn // 2
    outs = (
        shape((size, model), F32),
        shape((length, model), BF16),
        shape((length, width), BF16),
        shape((length, width), BF16),
        shape((length, width), BF16),
        shape((length, width), F32),
        shape((length, 128), F32),
        shape((length, units), BF16),
        shape((length, units), BF16),
    )
    return pl.pallas_call(
        functools.partial(forward_kernel, tn, size),
        out_shape=outs,
        in_specs=[VM] * 13,
        out_specs=[VM] * len(outs),
        scratch_shapes=[pltpu.VMEM((size, model), F32)] + group_buffers(chips, size, model) + group_sems(chips, tn),
        compiler_params=params_of(0),
        name="forward",
    )(x, wt, wi, wo, wp, vec, bt, bi, *tables)


def backward_layer(tn, dy, x, weights, vec, tables, kept):
    wt, wi, wo, wp = weights
    size, model = x.shape
    length = size * tn
    width, units, chips = wp.shape[0], wo.shape[0], tn // 2
    outs = (
        shape((size, model), F32),
        shape(wt.shape, BF16),
        shape(wi.shape, BF16),
        shape(wo.shape, BF16),
        shape(wp.shape, BF16),
        shape((8, model), F32),
        shape((1, 3 * width), F32),
        shape((1, units), F32),
    )
    return pl.pallas_call(
        functools.partial(backward_kernel, tn, size),
        out_shape=outs,
        in_specs=[VM] * 20,
        out_specs=[VM] * len(outs),
        scratch_shapes=[
            pltpu.VMEM((length, model), BF16),
            pltpu.VMEM((length, width), BF16),
            pltpu.VMEM((length, units), BF16),
            pltpu.VMEM((length, 3 * width), BF16),
            pltpu.VMEM((length, width), F32),
            pltpu.VMEM((length, width), F32),
            pltpu.VMEM((length, width), F32),
            pltpu.VMEM((length, model), F32),
            pltpu.VMEM((size, model), F32),
        ]
        + group_buffers(chips, size, model)
        + group_sems(chips, tn),
        compiler_params=params_of(1),
        name="backward",
    )(dy, x, wt, wi, wo, wp, vec, *tables, *kept)


class Place:
    def __init__(self, gn, tn):
        self.gn, self.tn = gn, tn
        self.h, self.t = lax.axis_index("h"), lax.axis_index("t")
        self.g = lax.axis_index("dp") * 2 + self.h
        self.c = self.h * tn + self.t
        self.bits = [1 << i for i in range(gn.bit_length() - 1)]

    def group(self, g):
        return {"dp": g // 2, "h": lax.rem(g, 2)}

    def line(self, c):
        return {"h": c // self.tn, "t": lax.rem(c, self.tn)}

    def other(self, k):
        return lax.rem(self.t + k, self.tn)


def flip(value, bit):
    return value + bit * (1 - 2 * lax.rem(value // bit, 2))


def remote(src, dst, send, recv, device):
    return pltpu.make_async_remote_copy(src, dst, send, recv, device_id=device, device_id_type=MESH)


def runs_by_step(place, bits):
    runs, steps = [(place.g, 1)], []
    for bit in bits:
        steps.append((bit, runs))
        if len(runs) == 1 and runs[0][1] == bit:
            runs = [(runs[0][0] // (2 * bit) * (2 * bit), 2 * bit)]
        else:
            runs = runs + [(flip(start, bit), count) for start, count in runs]
    return steps


def bit_orders(place):
    bits = place.bits
    return [bits, bits[:1] + bits[:0:-1]]


class Doubling:
    def __init__(self, place, ref, block, cols, order, sems, slot):
        self.place, self.ref, self.block, self.cols, self.order = place, ref, block, cols, order
        self.send, self.recv, self.slot = sems[0], sems[1], slot
        self.levels = [[] for _ in order]
        for i, bit in enumerate(order):
            for bits in range(1 << i):
                held = [order[j] for j in range(i) if bits >> j & 1]
                self.levels[len(held)].append((bit, held))

    def at(self, held):
        g = self.place.g
        for bit in held:
            g = flip(g, bit)
        return g

    def copy(self, bit, held):
        start = self.at(held)
        rows = pl.ds(pl.multiple_of(start * self.block, self.block), self.block)
        ref = self.ref.at[rows, self.cols]
        index = sum(held) + bit
        return remote(
            ref,
            ref,
            self.send.at[self.slot, index],
            self.recv.at[self.slot, index],
            self.place.group(flip(self.place.g, bit)),
        )

    def arrive(self, held):
        start = self.at(held)
        rows = pl.ds(pl.multiple_of(start * self.block, self.block), self.block)
        ref = self.ref.at[rows, self.cols]
        index = sum(held)
        peer = self.place.group(flip(self.place.g, held[-1]))
        remote(ref, ref, self.send.at[self.slot, index], self.recv.at[self.slot, index], peer).wait_recv()

    def advance(self, level):
        seen = set()
        for bit, held in self.levels[level]:
            if held and tuple(held) not in seen:
                seen.add(tuple(held))
                self.arrive(held)
            self.copy(bit, held).start()

    def whole(self):
        last = self.order[-1]
        for level in self.levels:
            for bit, held in level:
                if bit == last:
                    self.arrive(held + [bit])

    def finish(self):
        for level in self.levels:
            for item in level:
                self.copy(*item).wait_send()


def halves(cols):
    return [pl.ds(0, cols // 2), pl.ds(cols // 2, cols // 2)]


def line_barrier(place, extra):
    sem = pltpu.get_barrier_semaphore()
    span = 2 * place.tn
    for k in range(1, span):
        pl.semaphore_signal(sem, inc=1, device_id=place.line(lax.rem(place.c + k, span)), device_id_type=MESH)
    for bit in place.bits[1:]:
        pl.semaphore_signal(sem, inc=1, device_id=place.group(flip(place.g, bit)), device_id_type=MESH)
    peers = span - 1 + len(place.bits) - 1
    source, moved = extra

    @pl.when(moved)
    def _():
        pl.semaphore_signal(sem, inc=1, device_id=source, device_id_type=MESH)
        pl.semaphore_wait(sem, peers + 1)

    @pl.when(jnp.logical_not(moved))
    def _():
        pl.semaphore_wait(sem, peers)


def proj_places(place):
    gn, tn = place.gn, place.tn
    r = place.g * tn + place.t
    target = place.group(lax.rem(r, gn)) | {"t": r // gn}
    q = place.t * gn + place.g
    source = place.group(q // tn) | {"t": lax.rem(q, tn)}
    return target, source, r, q


def slot_rows(index, size):
    return pl.ds(pl.multiple_of(index * size, size), size)


class Opening:
    def __init__(self, place, layers, tok, cot, seg, vec, tri, inn, outer, proj, tok_o, cot_o, seg_o, vec_o, w, sems):
        self.place, self.layers = place, layers
        self.tok, self.cot, self.seg, self.vec = tok, cot, seg, vec
        self.tri, self.inn, self.outer, self.proj = tri, inn, outer, proj
        self.tok_o, self.cot_o, self.seg_o, self.vec_o = tok_o, cot_o, seg_o, vec_o
        self.wts, self.wis, self.wos, self.wps = w
        (
            self.ssem, self.rsem, self.lsem, self.asend, self.arecv, self.psend, self.precv,
            self.msend, self.mrecv, self.gsend, self.grecv,
        ) = sems
        self.half = tok.shape[1]
        self.target, self.source, self.r, self.q = proj_places(place)
        self.moved = self.q != self.r
        self.local, self.sends, self.shared_with = [], [], {}
        self.locals_of = {}

    def barrier(self):
        line_barrier(self.place, (self.source, self.moved))

    def near(self, src, dst, key):
        cp = pltpu.make_async_copy(src, dst, self.lsem.at[len(self.local)])
        cp.start()
        self.local.append(cp)
        self.locals_of[key] = cp

    def hop(self, src, dst, slot, i):
        c, tn = self.place.c, self.place.tn
        to = i * tn + c // 2
        rows = slot_rows(lax.rem(c, 2), self.half)
        near = pltpu.make_async_copy(src.at[i], dst.at[rows], self.msend.at[slot, i])
        far = remote(
            src.at[i], dst.at[rows], self.msend.at[slot, i], self.mrecv.at[slot, lax.rem(c, 2)],
            self.place.line(to),
        )
        return to == c, near, far

    def move(self, src, dst, slot):
        for i in range(2):
            stays, near, far = self.hop(src, dst, slot, i)
            pl.when(stays)(near.start)
            pl.when(jnp.logical_not(stays))(far.start)

    def moved_in(self, src, dst, slot):
        for i in range(2):
            stays, near, far = self.hop(src, dst, slot, i)
            pl.when(stays)(near.wait)
            pl.when(jnp.logical_not(stays))(far.wait_send)
        for s in range(2):
            cp = remote(
                src.at[0], dst.at[pl.ds(s * self.half, self.half)], self.msend.at[slot, 0],
                self.mrecv.at[slot, s], self.place.line(self.place.c),
            )
            pl.when(2 * self.place.t + s != self.place.c)(cp.wait_recv)

    def share(self, key, src_of, dst, size, slot):
        g, t, tn = self.place.g, self.place.t, self.place.tn
        rows = slot_rows(g * tn + t, size)
        self.near(src_of(t), dst.at[rows], key)
        for k in range(1, tn):
            to = self.place.other(k)
            cp = remote(src_of(to), dst.at[rows], self.asend.at[slot, k], self.arecv.at[slot, t], {"t": to})
            cp.start()
            self.sends.append(cp)
        self.shared_with[key] = (dst, size, slot)

    def shared(self, key):
        dst, size, slot = self.shared_with[key]
        self.locals_of[key].wait()
        for k in range(1, self.place.tn):
            frm = self.place.other(k)
            ref = dst.at[slot_rows(self.place.g * self.place.tn + frm, size)]
            remote(ref, ref, self.asend.at[slot, k], self.arecv.at[slot, frm], {"t": frm}).wait_recv()

    def share_layer(self, layer):
        depth = self.tri.shape[2]
        base = 1 + 2 * layer
        self.share(("t", layer), lambda to: self.tri.at[layer, to], self.wts[layer], depth, base)
        self.share(("i", layer), lambda to: self.inn.at[layer, to], self.wis[layer], depth, base + 1)
        g = self.place.g
        self.near(self.outer.at[layer], self.wos[layer].at[slot_rows(g, self.outer.shape[1])], ("o", layer))
        here, far = self.proj_copies(layer)
        pl.when(self.moved)(far.start)
        pl.when(jnp.logical_not(self.moved))(here.start)

    def proj_copies(self, layer):
        prows = self.proj.shape[1]
        src = self.proj.at[layer]
        here = pltpu.make_async_copy(src, self.wps[layer].at[slot_rows(self.place.g, prows)], self.psend.at[layer])
        dst = self.wps[layer].at[slot_rows(lax.rem(self.r, self.place.gn), prows)]
        return here, remote(src, dst, self.psend.at[layer], self.precv.at[layer], self.target)

    def proj_ready(self, layer):
        here, far = self.proj_copies(layer)

        @pl.when(self.moved)
        def _():
            far.wait_recv()
            far.wait_send()

        pl.when(jnp.logical_not(self.moved))(here.wait)

    def start(self):
        place, span = self.place, 2 * self.place.tn
        self.move(self.tok, self.tok_o, 0)
        vec_rows = self.vec.shape[0]
        self.share("v", lambda to: self.vec, self.vec_o, vec_rows, 0)
        self.near(self.seg, self.seg_o.at[slot_rows(place.c, 8)], "s")
        for k in range(1, span):
            to = lax.rem(place.c + k, span)
            dst = self.seg_o.at[slot_rows(place.c, 8)]
            cp = remote(self.seg, dst, self.gsend.at[k], self.grecv.at[place.c], place.line(to))
            cp.start()
            self.sends.append(cp)
        for layer in range(self.layers):
            self.share_layer(layer)
        orders = bit_orders(place)
        self.chunks, slot = [], 0
        tn, depth = place.tn, self.tri.shape[2]
        todo = []
        for layer in range(self.layers):
            todo += [
                [(("t", layer), self.wts[layer], tn * depth)],
                [(("i", layer), self.wis[layer], tn * depth)],
                [
                    (("o", layer), self.wos[layer], self.outer.shape[1]),
                    (("p", layer), self.wps[layer], self.proj.shape[1]),
                ],
            ]
        todo[0].insert(0, ("v", self.vec_o, tn * vec_rows))
        self.keys = [[key for key, _, _ in chunk] for chunk in todo]
        for chunk in todo:
            parts = []
            for _, ref, block in chunk:
                pieces = halves(ref.shape[1]) if ref.shape[1] >= 256 else [pl.ds(0, ref.shape[1])]
                for i, piece in enumerate(pieces):
                    parts.append(Doubling(place, ref, block, piece, orders[i], (self.ssem, self.rsem), slot))
                    slot += 1
            self.chunks.append(parts)
        self.steps = len(place.bits)
        self.turn, self.turns = 0, len(self.chunks) + SKEW * (self.steps - 1)
        self.complete = set()

    def ready(self, i):
        for key in self.keys[i]:
            if key == "v" or key[0] in ("t", "i"):
                self.shared(key)
            elif key[0] == "o":
                self.locals_of[key].wait()
            else:
                self.proj_ready(key[1])

    def tick(self, until=None):
        while self.turn < self.turns and (until is None or self.turn <= until):
            for step in reversed(range(self.steps)):
                i = self.turn - SKEW * step
                if 0 <= i < len(self.chunks):
                    if step == 0:
                        self.ready(i)
                    for part in self.chunks[i]:
                        part.advance(step)
            self.turn += 1
            if until is None:
                break

    def have(self, key):
        i = [key in keys for keys in self.keys].index(True)
        if i not in self.complete:
            self.complete.add(i)
            self.tick(i + SKEW * (self.steps - 1))
            for part in self.chunks[i]:
                part.whole()

    def segments_in(self):
        place, span = self.place, 2 * self.place.tn
        self.locals_of["s"].wait()
        for k in range(1, span):
            frm = lax.rem(place.c + k, span)
            ref = self.seg_o.at[slot_rows(frm, 8)]
            remote(ref, ref, self.gsend.at[k], self.grecv.at[frm], place.line(frm)).wait_recv()

    def finish(self):
        self.tick(self.turns)
        for parts in self.chunks:
            for part in parts:
                part.finish()
        for cp in self.sends:
            cp.wait_send()


def ascend_kernel(
    gn, tn, layers, size,
    tok, cot, seg, vec, tri, inn, outer, proj, ctab, satab, sbtab, e32, m32, e96, m96,
    cot_o, out_o, segcol, segrow, vecs_o, bts_o, bis_o, xs_o, w_o, kept_o,
    w, kept, xs, x_low, out_low, keep, seg_in, vec_in, vec_wide, bt_wide,
    bufs, group, opening_sems, save_sem, tok_sem,
):
    place = Place(gn, tn)
    opening = Opening(
        place, layers, tok, cot, seg, vec, tri, inn, outer, proj, x_low, cot_o, seg_in, vec_in, w, opening_sems
    )
    opening.barrier()
    opening.start()
    saves = []

    def save(src, dst):
        cp = pltpu.make_async_copy(src, dst, save_sem.at[len(saves)])
        cp.start()
        saves.append(cp)

    opening.tick(1)
    opening.moved_in(tok, x_low, 0)
    xs[0][...] = x_low[...].astype(F32)
    spreads, gathers, stages = [], [], []
    for layer in range(layers):
        ssem, fsem, rsem, cs, cr, ls, lr = group[layer]
        spreads.append(Spread(tn, kept[layer][0], size, ssem, fsem, rsem))
        gathers.append(Gather(tn, *bufs, (cs, cr, ls, lr)))
        stages.append(
            Forward(
                tn, size, xs[layer], tuple(w[k][layer] for k in range(4)),
                (vecs_o.at[layer], bts_o.at[layer], bis_o.at[layer]), (segcol, segrow), (ctab, satab, sbtab),
                kept[layer], keep,
            )
        )
    stages[0].norm(place.t)
    spreads[0].start()
    opening.segments_in()
    block = segcol.shape[0] // (2 * tn)
    eye = lax.broadcasted_iota(jnp.int32, (block, block), 0) == lax.broadcasted_iota(jnp.int32, (block, block), 1)
    for i in range(2 * tn):
        row = jnp.where(place.h == 0, seg_in[8 * i : 8 * i + 1, :], seg_in[8 * i + 1 : 8 * i + 2, :])
        spot = lax.broadcasted_iota(jnp.int32, (1, block), 1) + i * block
        row = jnp.where(row == 0, -1 - spot, row).astype(F32)
        segrow[:, i * block : (i + 1) * block] = row
        segcol[i * block : (i + 1) * block, :] = jnp.sum(jnp.where(eye, row, 0.0), axis=1, keepdims=True)
    opening.have("v")
    shards = gn * tn
    vec_rows = vec.shape[0]
    vec_wide[...] = vec_in[...].astype(F32)
    lane = lax.broadcasted_iota(jnp.int32, (1, 128), 1)
    for layer in range(layers):

        def line(k):
            return vec_wide[pl.ds(4 * layer + k, shards, stride=vec_rows), :]

        def spread_out(value, place_of, mask):
            return jnp.sum(dot(value.astype(BF16), place_of, NN) * mask, axis=0, keepdims=True)

        thick = line(2)
        parts = [jnp.where(lane // 32 == i, thick, 0.0) for i in range(4)]
        thin = line(3)
        gains = [jnp.where(lane // 32 == i, thin, 0.0) for i in range(2)]
        rows = [spread_out(p, e32[...], m32[...]) for p in parts + gains]
        vecs_o[layer] = jnp.concatenate(
            [rows[2], rows[3], rows[4], rows[5], rows[0] + rows[1]] + [jnp.zeros_like(rows[0])] * 3, axis=0
        )
        bt_wide[...] = spread_out(line(1), e96[...], m96[...])
        wide = bts_o.shape[2] // 3
        for i in range(3):
            start = pl.multiple_of(i * wide * tn + place.t * wide, 128)
            bts_o[layer, :, i * wide : (i + 1) * wide] = bt_wide[:, pl.ds(start, wide)]
        for i in range(gn):
            bis_o[layer, :, i * 128 : (i + 1) * 128] = vec_wide[
                pl.ds((i * tn + place.t) * vec_rows + 4 * layer, 1), :
            ]

    for layer in range(layers):
        stage, spread, gather = stages[layer], spreads[layer], gathers[layer]
        if layer > 0:
            stage.norm(place.t)
            spread.start()
        opening.have(("t", layer))
        for i, b in enumerate(arrivals(spread)):
            stage.heads_in(b)
            if i == 1:
                opening.tick()
        if layer == 0:
            opening.move(cot, cot_o, 1)
        for i, b in enumerate(far_first(spread)):
            stage.attend(b)
            if i == 1:
                opening.tick()
        opening.have(("i", layer))
        save(kept[layer][0], kept_o[layer][0])
        for i in range(1, 6):
            save(kept[layer][i], kept_o[layer][i])
        for i, b in enumerate(far_first(spread)):
            stage.mixer_in(b)
            if i == 1:
                opening.tick()
        save(kept[layer][6], kept_o[layer][6])
        save(kept[layer][7], kept_o[layer][7])
        opening.have(("o", layer))
        for k in range(4):
            save(w[k][layer], w_o[k][layer])
        branch_sums(stage, spread, gather, opening.tick)
        total = xs[layer][...] + vecs_o[layer, 4:5, :] + keep[...] + gather.total()
        if layer + 1 < layers:
            xs[layer + 1][...] = total
        else:
            out_low[...] = total.astype(BF16)
            save(out_low, out_o)
        save(xs[layer], xs_o[layer])
        spread.finish()
        gather.finish()
    opening.finish()
    opening.moved_in(cot, cot_o, 1)
    for cp in saves:
        cp.wait()


ANY = pl.BlockSpec(memory_space=pl.ANY)


def constant_tables(span, shards, model):
    angle = np.arange(span, dtype=np.float32)[:, None] * (
        np.float32(10000.0) ** (-(2.0 * np.arange(ROT // 2, dtype=np.float32)) / np.float32(ROT))
    )
    cosine, sine = np.cos(angle).astype(np.float32), np.sin(angle).astype(np.float32)
    none, empty = np.zeros((span, HD - ROT), np.float32), np.zeros_like(sine)
    reps = 128 // HD
    ctab = np.concatenate([cosine, cosine, none + 1.0] * reps, axis=1)
    satab = np.concatenate([-sine, empty, none] * reps, axis=1)
    sbtab = np.concatenate([empty, sine, none] * reps, axis=1)
    return tuple(jnp.asarray(tab, F32) for tab in (ctab, satab, sbtab))


def placement(piece, shards):
    j, col = np.arange(128)[:, None], np.arange(piece * shards)[None, :]
    put = (j % piece == col % piece) if 128 % piece == 0 else (j == col % piece)
    mask = np.arange(shards)[:, None] == col // piece
    return jnp.asarray(put, BF16), jnp.asarray(mask, F32)


def kept_shapes(length, model, width, units):
    return [
        ((length, model), BF16),
        ((length, width), BF16),
        ((length, width), BF16),
        ((length, width), BF16),
        ((length, width), F32),
        ((length, 128), F32),
        ((length, units), BF16),
        ((length, units), BF16),
    ]


def ascend_call(gn, tn, tokens, cotangent, segments, vec, tri, inn, outer, proj, tables, placing):
    layers = outer.shape[0]
    _, half, model = tokens.shape
    size = 2 * half
    length = size * tn
    depth = tri.shape[2]
    wshapes = [
        (gn * tn * depth, tri.shape[3]), (gn * tn * depth, inn.shape[3]),
        (gn * outer.shape[1], model), (gn * proj.shape[1], model),
    ]
    width, units, chips = wshapes[3][0], wshapes[2][0], tn // 2
    kept = kept_shapes(length, model, width, units)
    dma = pltpu.SemaphoreType.DMA
    outs = [
        (shape((size, model), BF16), ANY),
        (shape((size, model), BF16), ANY),
        (shape((length, 1), F32), VM),
        (shape((1, length), F32), VM),
        (shape((layers, 8, model), F32), VM),
        (shape((layers, 1, 3 * width), F32), VM),
        (shape((layers, 1, units), F32), VM),
    ]
    outs += [(shape((size, model), F32), ANY)] * layers
    for dims in wshapes:
        outs += [(shape(dims, BF16), ANY)] * layers
    for _ in range(layers):
        outs += [(shape(*item), ANY) for item in kept]
    scratch = []
    for dims in wshapes:
        scratch += [pltpu.VMEM(dims, BF16)] * layers
    for _ in range(layers):
        scratch += [pltpu.VMEM(*item) for item in kept]
    scratch += [pltpu.VMEM((size, model), F32)] * layers
    scratch += [
        pltpu.VMEM((size, model), BF16),
        pltpu.VMEM((size, model), BF16),
        pltpu.VMEM((size, model), F32),
        pltpu.VMEM((2 * tn * 8, 128), jnp.int32),
        pltpu.VMEM((gn * tn * vec.shape[0], 128), BF16),
        pltpu.VMEM((gn * tn * vec.shape[0], 128), F32),
        pltpu.VMEM((1, 3 * model), F32),
    ]
    scratch += group_buffers(chips, size, model)
    for _ in range(layers):
        scratch += group_sems(chips, tn)
    slots = 1 + 8 * layers
    scratch += [
        dma((slots, gn)), dma((slots, gn)), dma((2 + 3 * layers,)),
        dma((1 + 2 * layers, tn)), dma((1 + 2 * layers, tn)),
        dma((layers,)), dma((layers,)), dma((2, 2)), dma((2, 2)),
        dma((2 * tn,)), dma((2 * tn,)),
    ]
    scratch += [dma((14 * layers,)), dma((1,))]

    def body(*refs):
        refs = list(refs)

        def take(count):
            out, refs[:] = refs[:count], refs[count:]
            return out

        ins = take(15)
        cot_o, out_o, segcol, segrow, vecs_o, bts_o, bis_o = take(7)
        xs_o = take(layers)
        w_o = [take(layers) for _ in range(4)]
        kept_o = [take(8) for _ in range(layers)]
        w = [take(layers) for _ in range(4)]
        kept_s = [take(8) for _ in range(layers)]
        xs = take(layers)
        x_low, out_low, keep, seg_in, vec_in, vec_wide, bt_wide = take(7)
        bufs = take(4)
        group = [take(7) for _ in range(layers)]
        sems = take(11)
        save_sem, tok_sem = take(2)
        ascend_kernel(
            gn, tn, layers, size, *ins, cot_o, out_o, segcol, segrow, vecs_o, bts_o, bis_o, xs_o, w_o, kept_o,
            w, kept_s, xs, x_low, out_low, keep, seg_in, vec_in, vec_wide, bt_wide, bufs, group, sems,
            save_sem, tok_sem,
        )

    return pl.pallas_call(
        body,
        out_shape=tuple(o for o, _ in outs),
        in_specs=[ANY] * 8 + [VM] * 7,
        out_specs=tuple(spec for _, spec in outs),
        scratch_shapes=scratch,
        compiler_params=params_of(2),
        name="ascend",
    )(tokens, cotangent, segments, vec, tri, inn, outer, proj, *tables, *placing)


class Halving:
    def __init__(self, place, acc, inbox, block, cols, order, sems, slot):
        self.place, self.acc, self.inbox, self.block, self.cols = place, acc, inbox, block, cols
        self.send, self.recv, self.slot = sems[0], sems[1], slot
        self.plan, index, base = [], 0, 0
        for bit, runs in reversed(runs_by_step(place, order)):
            entry = []
            for start, count in runs:
                entry.append((bit, start, count, index, base))
                index += 1
                base += count
            self.plan.append(entry)

    def copy(self, bit, start, count, index, base):
        rows = pl.ds(pl.multiple_of(flip(start, bit) * self.block, self.block), count * self.block)
        return remote(
            self.acc.at[rows, self.cols],
            self.inbox.at[pl.ds(base * self.block, count * self.block), self.cols],
            self.send.at[self.slot, index],
            self.recv.at[self.slot, index],
            self.place.group(flip(self.place.g, bit)),
        )

    def advance(self, step):
        if step > 0:
            for item in self.plan[step - 1]:
                self.copy(*item).wait_recv()
                _, start, count, _, base = item

                def add(i, carry):
                    rows = pl.ds(pl.multiple_of((start + i) * self.block, self.block), self.block)
                    came = pl.ds(pl.multiple_of((base + i) * self.block, self.block), self.block)
                    value = self.acc[rows, self.cols].astype(F32) + self.inbox[came, self.cols].astype(F32)
                    self.acc[rows, self.cols] = value.astype(BF16)
                    return carry

                lax.fori_loop(0, count, add, 0)
        if step < len(self.plan):
            for item in self.plan[step]:
                self.copy(*item).start()

    def finish(self):
        for entry in self.plan:
            for item in entry:
                self.copy(*item).wait_send()


def close_kernel(
    gn, tn, layers,
    out_in, grad_in, flat, dwts, dwis, dwos, dwps,
    out_o, grad_o, flat_o, triple_o, proj_o, inner_o, outer_o,
    accs, boxes, cross, projbox, flatbox,
    lsem, hs, hr, cs, cr, ps, pr, ms, mr, fs, fr,
):
    place = Place(gn, tn)
    g, t, c = place.g, place.t, place.c
    target, source, r, q = proj_places(place)
    moved = q != r
    loads = []
    for i, src in enumerate(dwts + dwis + dwos + dwps):
        cp = pltpu.make_async_copy(src, accs[i], lsem.at[i])
        cp.start()
        loads.append(cp)
    line_barrier(place, (target, moved))
    half = out_o.shape[1]

    def move(src, dst, slot):
        for s in range(2):
            to = 2 * t + s

            @pl.when(to == c)
            def _():
                pltpu.make_async_copy(src.at[pl.ds(s * half, half)], dst.at[place.h], ms.at[slot, s]).start()

            @pl.when(to != c)
            def _():
                remote(
                    src.at[pl.ds(s * half, half)], dst.at[place.h], ms.at[slot, s], mr.at[slot, place.h], place.line(to)
                ).start()

    def moved_in(src, dst, slot):
        for s in range(2):
            to = 2 * t + s

            @pl.when(to == c)
            def _():
                pltpu.make_async_copy(src.at[pl.ds(s * half, half)], dst.at[place.h], ms.at[slot, s]).wait()

            @pl.when(to != c)
            def _():
                remote(
                    src.at[pl.ds(s * half, half)], dst.at[place.h], ms.at[slot, s], mr.at[slot, place.h], place.line(to)
                ).wait_send()

        for i in range(2):

            @pl.when(i * tn + c // 2 != c)
            def _():
                remote(
                    src.at[pl.ds(0, half)], dst.at[i], ms.at[slot, 0], mr.at[slot, i], place.line(c)
                ).wait_recv()

    move(grad_in, grad_o, 0)
    move(out_in, out_o, 1)
    orders = bit_orders(place)
    chunks, slot = [], 0
    plans = []
    for layer in reversed(range(layers)):
        for kind in range(4):
            plans.append((kind, layer))
    for kind, layer in plans:
        i = kind * layers + layer
        acc = accs[i]
        block = acc.shape[0] // gn
        parts = []
        for k, cols in enumerate(halves(acc.shape[1])):
            parts.append(Halving(place, acc, boxes[kind].at[layer], block, cols, orders[k], (hs, hr), slot))
            slot += 1
        chunks.append(parts)

    tbits = [1 << i for i in range(tn.bit_length() - 1)]
    exchanges = [("g", bit) for bit in place.bits] + [("t", bit) for bit in tbits]
    flat_o[...] = flat[...]

    def exchange(k):
        kind, bit = exchanges[k]
        to = place.group(flip(g, bit)) if kind == "g" else {"t": flip(t, bit)}
        return remote(flatbox.at[0, k], flatbox.at[1, k], fs.at[k], fr.at[k], to)

    def flat_turn(k):
        if k > 0 and k <= len(exchanges):
            exchange(k - 1).wait_recv()
            flat_o[...] += flatbox[1, k - 1]
        if k < len(exchanges):
            flatbox[0, k] = flat_o[...]
            exchange(k).start()

    steps = len(place.bits) + 1

    def cross_copy(kind, layer, to, slot_of):
        acc = accs[kind * layers + layer]
        rows = acc.shape[0] // (gn * tn)
        src = acc.at[pl.ds(pl.multiple_of((g * tn + to) * rows, rows), rows)]
        return remote(
            src, cross[kind].at[layer, t], cs.at[kind, layer, slot_of], cr.at[kind, layer, t], {"t": to}
        )

    def proj_copy(layer):
        acc = accs[3 * layers + layer]
        rows = acc.shape[0] // gn
        src = acc.at[pl.ds(pl.multiple_of(g * rows, rows), rows)]
        return src, remote(src, projbox.at[layer], ps.at[layer], pr.at[layer], source)

    def owned(kind, layer):
        acc = accs[kind * layers + layer]
        if kind < 2:
            rows = acc.shape[0] // (gn * tn)
            for k in range(1, tn):
                cross_copy(kind, layer, place.other(k), k).start()
            cross[kind][layer, t] = acc[pl.ds(pl.multiple_of((g * tn + t) * rows, rows), rows), :]
        elif kind == 2:
            rows = acc.shape[0] // gn
            outer_o[layer] = acc[pl.ds(pl.multiple_of(g * rows, rows), rows), :].astype(F32)
        else:

            @pl.when(moved)
            def _():
                proj_copy(layer)[1].start()

            @pl.when(jnp.logical_not(moved))
            def _():
                rows = acc.shape[0] // gn
                projbox[layer] = acc[pl.ds(pl.multiple_of(g * rows, rows), rows), :]

    def settle(kind, layer):
        if kind < 2:
            for k in range(1, tn):
                frm = place.other(k)
                remote(
                    cross[kind].at[layer, frm], cross[kind].at[layer, frm], cs.at[kind, layer, k],
                    cr.at[kind, layer, frm], {"t": frm},
                ).wait_recv()
            groups = 3 if kind == 0 else gn
            out = triple_o if kind == 0 else inner_o
            wide = cross[kind].shape[3] // groups
            for s in range(tn):
                for i in range(groups):
                    at = (i * tn + s) * wide
                    out[layer, :, at : at + wide] = cross[kind][layer, s, :, i * wide : (i + 1) * wide].astype(F32)
        elif kind == 3:

            @pl.when(moved)
            def _():
                proj_copy(layer)[1].wait_recv()

            proj_o[layer] = projbox[layer].astype(F32)

    turns = len(chunks) + SKEW * (steps + 1)
    for turn in range(max(turns, len(exchanges) + 1)):
        if turn <= len(exchanges):
            flat_turn(turn)
        for step in reversed(range(steps + 2)):
            i = turn - SKEW * step
            if 0 <= i < len(chunks):
                kind, layer = plans[i]
                if step == 0:
                    loads[kind * layers + layer].wait()
                if step < steps:
                    for part in chunks[i]:
                        part.advance(step)
                if step == steps - 1:
                    owned(kind, layer)
                if step == steps + 1:
                    settle(kind, layer)
    for k in range(len(exchanges)):
        exchange(k).wait_send()
    for (kind, layer), parts in zip(plans, chunks):
        for part in parts:
            part.finish()
        if kind < 2:
            for k in range(1, tn):
                cross_copy(kind, layer, place.other(k), k).wait_send()
        elif kind == 3:

            @pl.when(moved)
            def _():
                proj_copy(layer)[1].wait_send()

    moved_in(grad_in, grad_o, 0)
    moved_in(out_in, out_o, 1)


def close_call(gn, tn, output, grad, flat, mats):
    layers = len(mats)
    size, model = output.shape
    dwts, dwis, dwos, dwps = ([m[k] for m in mats] for k in range(4))
    dma = pltpu.SemaphoreType.DMA
    width3, units = dwts[0].shape[1], dwis[0].shape[1]
    shard = dwts[0].shape[0] // (gn * tn)
    prows, orows = dwps[0].shape[0] // gn, dwos[0].shape[0] // gn
    every = dwts + dwis + dwos + dwps
    boxes = [
        pltpu.VMEM((layers, (gn - 1) * m.shape[0] // gn, m.shape[1]), BF16)
        for m in (dwts[0], dwis[0], dwos[0], dwps[0])
    ]
    exchanges = (gn * tn).bit_length() - 1

    def body(out_in, grad_in, flat_in, *rest):
        refs = list(rest)
        groups = [refs[i * layers : (i + 1) * layers] for i in range(4)]
        outs = refs[4 * layers : 4 * layers + 7]
        rest = refs[4 * layers + 7 :]
        accs, rest = rest[: 4 * layers], rest[4 * layers :]
        box, rest = rest[:4], rest[4:]
        cross, rest = rest[:2], rest[2:]
        close_kernel(gn, tn, layers, out_in, grad_in, flat_in, *groups, *outs, accs, box, cross, *rest)

    outs = (
        shape((2, size // 2, model), BF16),
        shape((2, size // 2, model), BF16),
        shape(flat.shape, F32),
        shape((layers, shard, width3 * tn), F32),
        shape((layers, prows, model), F32),
        shape((layers, shard, units * tn), F32),
        shape((layers, orows, model), F32),
    )
    slots = 8 * layers
    return pl.pallas_call(
        body,
        out_shape=outs,
        in_specs=[ANY, ANY, VM] + [ANY] * (4 * layers),
        out_specs=(ANY, ANY, VM, VM, VM, VM, VM),
        scratch_shapes=[pltpu.VMEM(m.shape, BF16) for m in every]
        + boxes
        + [
            pltpu.VMEM((layers, tn, shard, width3), BF16),
            pltpu.VMEM((layers, tn, shard, units), BF16),
            pltpu.VMEM((layers, prows, model), BF16),
            pltpu.VMEM((2, exchanges) + flat.shape, F32),
            dma((4 * layers,)),
            dma((slots, gn)), dma((slots, gn)),
            dma((2, layers, tn)), dma((2, layers, tn)),
            dma((layers,)), dma((layers,)),
            dma((2, 2)), dma((2, 2)),
            dma((exchanges,)), dma((exchanges,)),
        ],
        compiler_params=params_of(3),
        name="closing",
    )(output, grad, flat, *dwts, *dwis, *dwos, *dwps)


GROUPS = ("dp", "h")
EVERY = ("dp", "h", "t")


def to_group(tn, blocks):
    h, t = lax.axis_index("h"), lax.axis_index("t")
    count = 2 * tn
    parity = lax.rem(t, 2)
    got = []
    for j in range(2):
        moves = [(c, ((c + j) % 2) * tn + c // 2) for c in range(count)]
        piece = jnp.where(lax.rem(parity + j, 2) == 0, blocks[0], blocks[1])
        got.append(lax.ppermute(piece, ("h", "t"), moves))
    low = jnp.where(h == 0, got[0], got[1])
    high = jnp.where(h == 0, got[1], got[0])
    return jnp.concatenate([low, high], axis=0)


def from_group(tn, rows):
    h, t = lax.axis_index("h"), lax.axis_index("t")
    count = 2 * tn
    parity = lax.rem(t, 2)
    size = rows.shape[0] // 2
    got = []
    for j in range(2):
        moves = [(((c + j) % 2) * tn + c // 2, c) for c in range(count)]
        piece = jnp.where(lax.rem(h + j, 2) == 0, rows[:size], rows[size:])
        got.append(lax.ppermute(piece, ("h", "t"), moves))
    first = jnp.where(parity == 0, got[0], got[1])
    second = jnp.where(parity == 0, got[1], got[0])
    return jnp.stack([first, second], axis=0)


def proj_moves(gn, tn):
    return [(r, (r % gn) * tn + r // gn) for r in range(gn * tn)]


def slice_columns(weight, gn, tn):
    rows, cols = weight.shape
    return weight.reshape(rows, gn, tn, cols // (gn * tn)).transpose(2, 0, 1, 3).reshape(tn, rows, cols // tn)


def slice_triple(weight, tn):
    rows, cols = weight.shape
    return weight.reshape(rows, 3, tn, cols // (3 * tn)).transpose(2, 0, 1, 3).reshape(tn, rows, cols // tn)


def gather_weights(gn, tn, triple, proj, inner, outer):
    def spread(parts):
        moved = lax.all_to_all(parts, "t", 0, 0, tiled=True)
        whole = lax.all_gather(moved.reshape(-1, moved.shape[-1]), GROUPS, axis=0, tiled=True)
        return whole

    wt = spread(slice_triple(triple, tn))
    wi = spread(slice_columns(inner, gn, tn))
    wo = lax.all_gather(outer, GROUPS, axis=0, tiled=True)
    wp = lax.all_gather(lax.ppermute(proj, EVERY, proj_moves(gn, tn)), GROUPS, axis=0, tiled=True)
    return wt, wi, wo, wp


def reduce_weights(gn, tn, dwt, dwi, dwo, dwp):
    def back(parts):
        mine = lax.psum_scatter(parts, GROUPS, scatter_dimension=0, tiled=True)
        rows = mine.shape[0] // tn
        return lax.all_to_all(mine.reshape(tn, rows, -1), "t", 0, 0, tiled=True).astype(F32)

    triple = back(dwt)
    rows = triple.shape[1]
    triple = triple.reshape(tn, rows, 3, -1).transpose(1, 2, 0, 3).reshape(rows, -1)
    inner = back(dwi)
    inner = inner.reshape(tn, rows, gn, -1).transpose(1, 2, 0, 3).reshape(rows, -1)
    outer = lax.psum_scatter(dwo, GROUPS, scatter_dimension=0, tiled=True).astype(F32)
    proj = lax.psum_scatter(dwp, GROUPS, scatter_dimension=0, tiled=True)
    proj = lax.ppermute(proj, EVERY, [(b, a) for a, b in proj_moves(gn, tn)]).astype(F32)
    return triple, proj, inner, outer


def per_device(
    gn, tn,
    tokens, segments, cotangent, triple_weight, triple_bias, proj_weight, proj_bias, inner_weight, inner_bias,
    outer_weight, outer_bias, first_gain, first_shift, second_gain, second_shift,
):
    layers = triple_weight.shape[0]
    model = tokens.shape[2]
    span = tokens.shape[1] * 2 * tn
    h, t = lax.axis_index("h"), lax.axis_index("t")
    device = (lax.axis_index("dp") * 2 + h) * tn + t
    shards = gn * tn
    heads_wide = model // tn
    units = outer_weight.shape[1] * gn

    rows = triple_weight.shape[1]
    block = tokens.shape[1]
    tables = constant_tables(span, shards, model)
    direct = rows % 16 == 0 and block == 128 and layers * 4 <= 16
    if direct:
        head = jnp.stack(
            [
                inner_bias,
                jnp.pad(triple_bias, ((0, 0), (0, 128 - triple_bias.shape[1]))),
                jnp.concatenate([proj_bias, outer_bias, first_gain, first_shift], axis=1),
                jnp.pad(jnp.concatenate([second_gain, second_shift], axis=1), ((0, 0), (0, 64))),
            ],
            axis=1,
        ).reshape(4 * layers, 128)
        opened = ascend_call(
            gn, tn, tokens, cotangent, jnp.pad(segments, ((0, 6), (0, 0))),
            jnp.pad(head, ((0, 16 - 4 * layers), (0, 0))),
            triple_weight.reshape(layers, rows, 3, tn, -1).transpose(0, 3, 1, 2, 4).reshape(layers, tn, rows, -1),
            inner_weight.reshape(layers, rows, gn, tn, -1).transpose(0, 3, 1, 2, 4).reshape(layers, tn, rows, -1),
            outer_weight, proj_weight, tables,
            placement(model // shards, shards) + placement(3 * model // shards, shards),
        )
        opened = list(opened)
        cot, output, segcol, segrow, vecs, _, _ = opened[:7]
        inputs = opened[7 : 7 + layers]
        weights = [tuple(opened[7 + layers + k * layers + layer] for k in range(4)) for layer in range(layers)]
        kept = [opened[7 + 5 * layers + 8 * i : 7 + 5 * layers + 8 * (i + 1)] for i in range(layers)]
        cot = cot.astype(F32)
        tables = (segcol, segrow) + tables
    else:
        small = (triple_bias, inner_bias, proj_bias, outer_bias, first_gain, first_shift, second_gain, second_shift)
        starts = [0]
        for item in small:
            starts.append(starts[-1] + item.shape[1])
        packed = jnp.concatenate(small, axis=1)
        x = to_group(tn, tokens).astype(F32)
        cot = to_group(tn, cotangent).astype(F32)
        segs_all = lax.all_gather(segments, ("h", "t"), axis=1, tiled=True)
        everything = lax.all_gather(packed[None], EVERY, axis=0, tiled=True).astype(F32)
        weights = [
            gather_weights(
                gn, tn, triple_weight[layer], proj_weight[layer], inner_weight[layer], outer_weight[layer]
            )
            for layer in range(layers)
        ]
        segs = jnp.where(h == 0, segs_all[0], segs_all[1])
        segs = jnp.where(segs == 0, -1 - jnp.arange(span, dtype=jnp.int32), segs).astype(F32)
        tables = (segs[:, None], segs[None, :]) + tables

        def vector(layer, i):
            return everything[:, layer, starts[i] : starts[i + 1]].reshape(-1)

        vecs, inputs, kept = [], [], []
        for layer in range(layers):
            bt = lax.dynamic_index_in_dim(vector(layer, 0).reshape(3, tn, heads_wide), t, 1, keepdims=False)
            bi = lax.dynamic_index_in_dim(vector(layer, 1).reshape(gn, tn, -1), t, 1, keepdims=False)
            zero = jnp.zeros((model,), F32)
            vecs.append(
                jnp.stack(
                    [vector(layer, 4), vector(layer, 5), vector(layer, 6), vector(layer, 7)]
                    + [vector(layer, 2) + vector(layer, 3), zero, zero, zero]
                )
            )
            inputs.append(x)
            x, *saved = forward_layer(
                tn, x, weights[layer], vecs[layer], bt.reshape(1, -1), bi.reshape(1, -1), tables
            )
            kept.append(saved)
        output = x.astype(BF16)
    grad = cot
    mats, flats = [None] * layers, [None] * layers
    for layer in reversed(range(layers)):
        grad, dwt, dwi, dwo, dwp, dvec, dbt, dbi = backward_layer(
            tn, grad, inputs[layer], weights[layer], vecs[layer], tables, kept[layer]
        )
        mats[layer] = (dwt, dwi, dwo, dwp)
        triple = lax.dynamic_update_slice(
            jnp.zeros((3, tn, heads_wide), F32), dbt.reshape(3, 1, heads_wide), (0, t, 0)
        )
        inner = lax.dynamic_update_slice(
            jnp.zeros((gn, tn, units // gn), F32), dbi.reshape(gn, 1, units // gn), (0, t, 0)
        )
        flats[layer] = jnp.concatenate([dvec[:5].reshape(-1), triple.reshape(-1), inner.reshape(-1)])
    tokens_grad = grad.astype(BF16)
    flat = jnp.stack(flats)
    if direct:
        output, tokens_grad, summed, triple, proj, inner, outer = close_call(
            gn, tn, output, tokens_grad, flat.reshape(-1, 1024), mats
        )
        summed = summed.reshape(flat.shape)
    else:
        output, tokens_grad = from_group(tn, output), from_group(tn, tokens_grad)
        done = [reduce_weights(gn, tn, *m) for m in mats]
        triple, proj, inner, outer = (jnp.stack([m[k] for m in done]) for k in range(4))
        summed = lax.psum(flat, EVERY)

    def own(start, length):
        piece = length // shards
        return lax.dynamic_slice_in_dim(summed, start + device * piece, piece, 1)

    base = 5 * model
    bias_sum = own(4 * model, model)
    return (
        output,
        tokens_grad,
        triple,
        own(base, 2 * model),
        own(base + 2 * model, model),
        proj,
        bias_sum,
        inner,
        own(base + 3 * model, units * tn),
        outer,
        bias_sum,
        own(0, model),
        own(model, model),
        own(2 * model, model),
        own(3 * model, model),
    )


def solution(mesh):
    dp, ctx = mesh.shape["dp"], mesh.shape["ctx"]
    tn = ctx // 2
    gn = 2 * dp
    fine = Mesh(mesh.devices.reshape(dp, 2, tn), EVERY)
    seq = P("dp", ("h", "t"), None)
    mat = P(None, EVERY, None)
    row = P(None, EVERY)
    in_specs = (seq, P("dp", ("h", "t")), seq, mat, row, mat, row, mat, row, mat, row, row, row, row, row)
    out_specs = (seq, seq, mat, row, row, mat, row, mat, row, mat, row, row, row, row, row)
    return jax.shard_map(
        functools.partial(per_device, gn, tn), mesh=fine, in_specs=in_specs, out_specs=out_specs, check_vma=False
    )
```

```python
import functools
import math

import jax
import jax.numpy as jnp
import numpy as np
from jax import lax
from jax.experimental import pallas as pl
from jax.experimental.pallas import tpu as pltpu
from jax.sharding import Mesh
from jax.sharding import PartitionSpec as P

HD = 64
ROT = 16
EPSILON = 1e-05
NEG_LARGE = -1e30
MESH = pl.DeviceIdType.MESH
BF16 = jnp.bfloat16
F32 = jnp.float32
VMEM_LIMIT = 60 * 1024 * 1024


def dot(a, b, dims):
    return lax.dot_general(a, b, (dims, ((), ())), preferred_element_type=F32)


NN = ((1,), (0,))
NT = ((1,), (1,))
TN = ((0,), (0,))


def rows_of(b, size):
    return pl.ds(pl.multiple_of(b * size, size), size)


def group_barrier(tn):
    t = lax.axis_index("t")
    zc, co = t // 2, lax.rem(t, 2)
    chips = tn // 2
    sem = pltpu.get_barrier_semaphore()
    peers = [zc * 2 + 1 - co] + [lax.rem(zc + k, chips) * 2 + co for k in range(1, chips)]
    for p in peers:
        pl.semaphore_signal(sem, inc=1, device_id={"t": p}, device_id_type=MESH)
    pl.semaphore_wait(sem, len(peers))


class Spread:
    def __init__(self, tn, buf, size, ssem, fsem, rsem):
        self.tn, self.buf, self.size = tn, buf, size
        self.ssem, self.fsem, self.rsem = ssem, fsem, rsem
        self.t = lax.axis_index("t")
        self.zc, self.co = self.t // 2, lax.rem(self.t, 2)
        self.chips = tn // 2

    def copy(self, block, send, to):
        ref = self.buf.at[rows_of(block, self.size)]
        return pltpu.make_async_remote_copy(
            ref, ref, send, self.rsem.at[block], device_id={"t": to}, device_id_type=MESH
        )

    def start(self):
        for k in range(1, self.chips):
            chip = lax.rem(self.zc + k, self.chips)
            self.copy(self.t, self.ssem.at[k], chip * 2 + self.co).start()
        self.copy(self.t, self.ssem.at[0], self.zc * 2 + 1 - self.co).start()

    def peer_core(self):
        b = self.zc * 2 + 1 - self.co
        self.copy(b, self.ssem.at[0], b).wait_recv()
        return b

    def same_core(self, k):
        b = lax.rem(self.zc + self.chips - k, self.chips) * 2 + self.co
        self.copy(b, self.fsem.at[k], b).wait_recv()
        self.copy(b, self.fsem.at[k], self.zc * 2 + 1 - self.co).start()
        return b

    def other_core(self, k):
        b = lax.rem(self.zc + self.chips - k, self.chips) * 2 + 1 - self.co
        self.copy(b, self.fsem.at[k], b).wait_recv()
        return b

    def finish(self):
        for k in range(self.chips):
            self.copy(self.t, self.ssem.at[k], self.t).wait_send()
        for k in range(1, self.chips):
            self.copy(self.t, self.fsem.at[k], self.t).wait_send()


class Gather:
    def __init__(self, tn, tocore, fromcore, toici, fromici, sems):
        self.tn = tn
        self.tocore, self.fromcore, self.toici, self.fromici = tocore, fromcore, toici, fromici
        self.cs, self.cr, self.ls, self.lr = sems
        self.t = lax.axis_index("t")
        self.zc, self.co = self.t // 2, lax.rem(self.t, 2)
        self.chips = tn // 2

    def core_copy(self, chip):
        return pltpu.make_async_remote_copy(
            self.tocore.at[chip],
            self.fromcore.at[chip],
            self.cs.at[chip],
            self.cr.at[chip],
            device_id={"t": self.zc * 2 + 1 - self.co},
            device_id_type=MESH,
        )

    def link_copy(self, chip, slot):
        return pltpu.make_async_remote_copy(
            self.toici.at[chip],
            self.fromici.at[slot],
            self.ls.at[chip],
            self.lr.at[slot],
            device_id={"t": chip * 2 + self.co},
            device_id_type=MESH,
        )

    def send_core(self, chip):
        self.core_copy(chip).start()

    def send_link(self, chip):
        self.core_copy(chip).wait_recv()
        self.toici[chip] = (self.toici[chip].astype(F32) + self.fromcore[chip].astype(F32)).astype(BF16)
        self.link_copy(chip, self.zc).start()

    def total(self):
        self.core_copy(self.zc).wait_recv()
        value = self.fromcore[self.zc].astype(F32)
        for k in range(1, self.chips):
            chip = lax.rem(self.zc + k, self.chips)
            self.link_copy(chip, chip).wait_recv()
            value = value + self.fromici[chip].astype(F32)
        return value

    def finish(self):
        for chip in range(self.chips):
            self.core_copy(chip).wait_send()
        for k in range(1, self.chips):
            chip = lax.rem(self.zc + k, self.chips)
            self.link_copy(chip, self.zc).wait_send()


def norm_stats(x):
    mean = jnp.mean(x, axis=-1, keepdims=True)
    centred = x - mean
    inverse = lax.rsqrt(jnp.mean(centred * centred, axis=-1, keepdims=True) + EPSILON)
    return centred * inverse, inverse


def widen(tab, width):
    return jnp.concatenate([tab] * (width // tab.shape[1]), axis=1)


def turn(x, cos, sine, sign):
    width = x.shape[1]
    cos, sine = widen(cos, width), widen(sine, width)
    front = lax.rem(lax.broadcasted_iota(jnp.int32, (1, width), 1), HD) < ROT // 2
    partner = jnp.where(front, pltpu.roll(x, width - ROT // 2, 1), pltpu.roll(x, ROT // 2, 1))
    return x * cos + sign * (partner * sine)


def head_masks(width, dtype):
    lane = lax.broadcasted_iota(jnp.int32, (1, width), 1) // HD
    return [(lane == h).astype(F32).astype(dtype) for h in range(width // HD)]


def pair_bias(qb, kb, size, segcol, segrow):
    qpos = lax.broadcasted_iota(jnp.int32, (size, size), 0) + qb * size
    kpos = lax.broadcasted_iota(jnp.int32, (size, size), 1) + kb * size
    same = segcol[rows_of(qb, size), :] == segrow[:, rows_of(kb, size)]
    return jnp.where(same & (kpos <= qpos), 0.0, NEG_LARGE)


TILE = 256
SKEW = 1


class Forward:
    def __init__(self, tn, size, x, w, vecs, segs, tables, kept, keep):
        self.tn, self.size, self.chips = tn, size, tn // 2
        self.x, self.keep = x, keep
        self.wt, self.wi, self.wo, self.wp = w
        self.vec, self.bt, self.bi = vecs
        self.segcol, self.segrow = segs
        self.tables = tables
        self.n, self.q, self.k, self.v, self.o, self.lse, self.g, self.gp = kept
        self.width, self.units = self.q.shape[1], self.g.shape[1]
        self.heads = self.width // HD

    def norm(self, t):
        own, _ = norm_stats(self.x[...])
        self.n[rows_of(t, self.size), :] = own.astype(BF16)

    def heads_in(self, b):
        width, vec, bt = self.width, self.vec, self.bt
        rows = rows_of(b, self.size)
        h1 = (self.n[rows, :].astype(F32) * vec[0:1, :] + vec[1:2, :]).astype(BF16)
        cos, sine = (tab[rows, :] for tab in self.tables)
        q = dot(h1, self.wt[:, 0:width], NN) + bt[:, 0:width]
        low = turn(q, cos, sine, 1.0).astype(BF16).astype(F32)
        self.q[rows, :] = (low * (1.0 / math.sqrt(HD))).astype(BF16)
        k = dot(h1, self.wt[:, width : 2 * width], NN) + bt[:, width : 2 * width]
        self.k[rows, :] = turn(k, cos, sine, 1.0).astype(BF16)
        v = dot(h1, self.wt[:, 2 * width : 3 * width], NN) + bt[:, 2 * width : 3 * width]
        self.v[rows, :] = v.astype(BF16)

    def mixer_in(self, b):
        rows = rows_of(b, self.size)
        h2 = (self.n[rows, :].astype(F32) * self.vec[2:3, :] + self.vec[3:4, :]).astype(BF16)

        def mix(j, carry):
            cols = rows_of(j, TILE)
            u = dot(h2, self.wi[:, cols], NN) + self.bi[:, cols]
            half = 0.5 + 0.5 * lax.erf(u * (1.0 / math.sqrt(2.0)))
            self.g[rows, cols] = (u * half).astype(BF16)
            bell = jnp.exp(-0.5 * u * u) * (1.0 / math.sqrt(2.0 * math.pi))
            self.gp[rows, cols] = (half + u * bell).astype(BF16)
            return carry

        lax.fori_loop(0, self.units // TILE, mix, 0)

    def attend(self, b):
        size, width, heads = self.size, self.width, self.heads
        masks = head_masks(width, F32)
        lane = lax.broadcasted_iota(jnp.int32, (1, 128), 1)
        rows = rows_of(b, size)
        qb = self.q[rows, :]
        qs = [qb * masks[h].astype(BF16) for h in range(heads)]

        def step(i, carry):
            peaks, sums, acc = carry
            kb = b - i
            keys = self.k[rows_of(kb, size), :]
            vals = self.v[rows_of(kb, size), :]
            bias = pair_bias(b, kb, size, self.segcol, self.segrow)
            new_peaks, new_sums = [], []
            scale = jnp.zeros((size, width), F32)
            add = jnp.zeros((size, width), F32)
            for h in range(heads):
                s = dot(qs[h], keys, NT) + bias
                peak = jnp.maximum(peaks[h], jnp.max(s, axis=1, keepdims=True))
                p = jnp.exp(s - peak)
                fade = jnp.exp(peaks[h] - peak)
                new_peaks.append(peak)
                new_sums.append(sums[h] * fade + jnp.sum(p, axis=1, keepdims=True))
                scale = scale + fade * masks[h]
                add = add + dot(p.astype(BF16), vals * masks[h].astype(BF16), NN)
            return tuple(new_peaks), tuple(new_sums), acc * scale + add

        start = (
            tuple(jnp.full((size, 1), NEG_LARGE, F32) for _ in range(heads)),
            tuple(jnp.zeros((size, 1), F32) for _ in range(heads)),
            jnp.zeros((size, width), F32),
        )
        peaks, sums, acc = lax.fori_loop(0, b + 1, step, start)
        scale = jnp.zeros((size, width), F32)
        lse = jnp.zeros((size, 128), F32)
        for h in range(heads):
            scale = scale + (1.0 / sums[h]) * masks[h]
            lse = jnp.where(lane == h, peaks[h] + jnp.log(sums[h]), lse)
        self.lse[rows, :] = lse
        self.o[rows, :] = acc * scale

    def branches(self, b, store):
        rows = rows_of(b, self.size)

        def part(j, carry):
            cols = rows_of(j, TILE)
            value = dot(self.g[rows, :], self.wo[:, cols], NN)
            store(cols, value + dot(self.o[rows, :].astype(BF16), self.wp[:, cols], NN))
            return carry

        lax.fori_loop(0, self.x.shape[1] // TILE, part, 0)

    def into(self, ref, chip):
        def store(cols, value):
            ref[chip, :, cols] = value.astype(BF16)

        return store

    def into_keep(self, cols, value):
        self.keep[:, cols] = value


def arrivals(spread):
    yield spread.t
    yield spread.peer_core()
    for i in range(1, spread.chips):
        yield spread.same_core(i)
        yield spread.other_core(i)


def far_first(spread):
    out = []
    for i in range(1, spread.chips):
        chip = lax.rem(spread.zc + i, spread.chips)
        out += [chip * 2 + 1 - spread.co, chip * 2 + spread.co]
    return out + [spread.zc * 2 + 1 - spread.co, spread.t]


def branch_sums(layer, spread, gather, tick=lambda: None):
    for i in range(1, spread.chips):
        chip = lax.rem(spread.zc + i, spread.chips)
        layer.branches(chip * 2 + 1 - spread.co, layer.into(gather.tocore, chip))
        gather.send_core(chip)
        layer.branches(chip * 2 + spread.co, layer.into(gather.toici, chip))
        gather.send_link(chip)
        tick()
    layer.branches(spread.zc * 2 + 1 - spread.co, layer.into(gather.tocore, spread.zc))
    gather.send_core(spread.zc)
    layer.branches(spread.t, layer.into_keep)
    tick()


def forward_kernel(
    tn, size,
    x_ref, wt, wi, wo, wp, vec, bt, bi, segcol, segrow, ctab, stab,
    xo_ref, n_ref, q_ref, k_ref, v_ref, o_ref, lse_ref, g_ref, gp_ref,
    keep, tocore, fromcore, toici, fromici, ssem, fsem, rsem, cs, cr, ls, lr,
):
    group_barrier(tn)
    spread = Spread(tn, n_ref, size, ssem, fsem, rsem)
    gather = Gather(tn, tocore, fromcore, toici, fromici, (cs, cr, ls, lr))
    layer = Forward(
        tn, size, x_ref, (wt, wi, wo, wp), (vec, bt, bi), (segcol, segrow), (ctab, stab),
        (n_ref, q_ref, k_ref, v_ref, o_ref, lse_ref, g_ref, gp_ref), keep,
    )
    layer.norm(spread.t)
    spread.start()
    for b in arrivals(spread):
        layer.heads_in(b)
        layer.mixer_in(b)
    for b in far_first(spread):
        layer.attend(b)
    branch_sums(layer, spread, gather)
    xo_ref[...] = x_ref[...] + vec[4:5, :] + keep[...] + gather.total()
    spread.finish()
    gather.finish()


def backward_kernel(
    tn, size,
    dy_ref, x_ref, wt, wi, wo, wp, vec, segcol, segrow, ctab, stab,
    n_ref, q_ref, k_ref, v_ref, o_ref, lse_ref, g_ref, gp_ref,
    dx_ref, dwt, dwi, dwo, dwp, dvec, dbt, dbi,
    gb, do, du, dt, dq, dk, dv, dh2, keep,
    tocore, fromcore, toici, fromici, ssem, fsem, rsem, cs, cr, ls, lr,
):
    chips = tn // 2
    width = q_ref.shape[1]
    heads = width // HD
    units = g_ref.shape[1]
    model = x_ref.shape[1]
    group_barrier(tn)
    spread = Spread(tn, gb, size, ssem, fsem, rsem)
    gather = Gather(tn, tocore, fromcore, toici, fromici, (cs, cr, ls, lr))
    t, zc, co = spread.t, spread.zc, spread.co
    own = dy_ref[...].astype(F32).astype(BF16)
    gb[rows_of(t, size), :] = own
    spread.start()
    dvec[...] = jnp.zeros_like(dvec)
    dbt[...] = jnp.zeros_like(dbt)
    dbi[...] = jnp.zeros_like(dbi)
    dvec[4:5, :] = jnp.sum(own.astype(F32), axis=0, keepdims=True)
    dq[...] = jnp.zeros_like(dq)
    dk[...] = jnp.zeros_like(dk)
    dv[...] = jnp.zeros_like(dv)

    def mixer(b):
        rows = rows_of(b, size)
        grad = gb[rows, :]
        do[rows, :] = dot(grad, wp[...], NT).astype(BF16)

        def unit(j, carry):
            cols = rows_of(j, TILE)
            d = (dot(grad, wo[cols, :], NT) * gp_ref[rows, cols].astype(F32)).astype(BF16)
            du[rows, cols] = d
            dbi[0:1, cols] += jnp.sum(d.astype(F32), axis=0, keepdims=True)
            return carry

        lax.fori_loop(0, units // TILE, unit, 0)

        def back(j, carry):
            cols = rows_of(j, TILE)
            d = dot(du[rows, :], wi[cols, :], NT)
            dvec[2:3, cols] += jnp.sum(d * n_ref[rows, cols].astype(F32), axis=0, keepdims=True)
            dvec[3:4, cols] += jnp.sum(d, axis=0, keepdims=True)
            dh2[rows, cols] = d * vec[2:3, cols]
            return carry

        lax.fori_loop(0, model // TILE, back, 0)

    mixer(t)
    mixer(spread.peer_core())
    for i in range(1, chips):
        mixer(spread.same_core(i))
        mixer(spread.other_core(i))

    masks = head_masks(width, BF16)
    lane = lax.broadcasted_iota(jnp.int32, (1, 128), 1)
    up = zc >= (chips + 1) // 2
    tsize = tn

    def pair(qb, kb):
        qrows, krows = rows_of(qb, size), rows_of(kb, size)
        q, keys, vals = q_ref[qrows, :], k_ref[krows, :], v_ref[krows, :]
        grad = do[qrows, :]
        prod = grad.astype(F32) * o_ref[qrows, :]
        lse = lse_ref[qrows, :]
        bias = pair_bias(qb, kb, size, segcol, segrow)
        dq_new = jnp.zeros((size, width), F32)
        dk_new = jnp.zeros((size, width), F32)
        dv_new = jnp.zeros((size, width), F32)
        for h in range(heads):
            qh, gh = q * masks[h], grad * masks[h]
            total = jnp.sum(jnp.where(lane == h, lse, 0.0), axis=1, keepdims=True)
            delta = jnp.sum(prod * masks[h].astype(F32), axis=1, keepdims=True)
            p = jnp.exp(dot(qh, keys, NT) + bias - total)
            ds = (p * (dot(gh, vals, NT) - delta)).astype(BF16)
            dv_new = dv_new + dot(p.astype(BF16), gh, TN)
            dk_new = dk_new + dot(ds, qh, TN)
            dq_new = dq_new + dot(ds, keys * masks[h], NN)
        dq[qrows, :] += dq_new
        dk[krows, :] += dk_new
        dv[krows, :] += dv_new

    def attend_back(stage):
        pivot = jnp.where(up, stage, tsize - 1 - stage)

        def step(j, carry):
            pair(jnp.where(up, pivot + j, pivot), jnp.where(up, pivot, pivot - j))
            return carry

        lax.fori_loop(0, tsize - stage, step, 0)
        rows = rows_of(pivot, size)
        cos, sine = ctab[rows, :], stab[rows, :]
        dt[rows, 0:width] = turn(dq[rows, :] * (1.0 / math.sqrt(HD)), cos, sine, -1.0).astype(BF16)
        dt[rows, width : 2 * width] = turn(dk[rows, :], cos, sine, -1.0).astype(BF16)
        dt[rows, 2 * width : 3 * width] = dv[rows, :].astype(BF16)
        block = dt[rows, :]
        dbt[...] += jnp.sum(block.astype(F32), axis=0, keepdims=True)

        def back(j, carry):
            cols = rows_of(j, TILE)
            d = dot(block, wt[cols, :], NT)
            dvec[0:1, cols] += jnp.sum(d * n_ref[rows, cols].astype(F32), axis=0, keepdims=True)
            dvec[1:2, cols] += jnp.sum(d, axis=0, keepdims=True)
            dh2[rows, cols] = dh2[rows, cols] + d * vec[0:1, cols]
            return carry

        lax.fori_loop(0, model // TILE, back, 0)
        value = dh2[rows, :]
        chip, core = pivot // 2, lax.rem(pivot, 2)

        @pl.when(core != co)
        def _():
            tocore[chip] = value.astype(BF16)
            gather.send_core(chip)

        @pl.when((core == co) & (chip != zc))
        def _():
            toici[chip] = value.astype(BF16)

        @pl.when(pivot == t)
        def _():
            keep[...] = value

        if stage % 2 == 1:

            @pl.when(chip != zc)
            def _():
                gather.send_link(chip)

    for stage in range(tn):
        attend_back(stage)

    def grad_one(j, carry):
        cols = rows_of(j, TILE)
        h1 = (n_ref[:, cols].astype(F32) * vec[0:1, cols] + vec[1:2, cols]).astype(BF16)
        dwt[cols, :] = dot(h1, dt[...], TN).astype(dwt.dtype)
        return carry

    lax.fori_loop(0, model // TILE, grad_one, 0)

    def grad_two(j, carry):
        cols = rows_of(j, TILE)
        h2 = (n_ref[:, cols].astype(F32) * vec[2:3, cols] + vec[3:4, cols]).astype(BF16)
        dwi[cols, :] = dot(h2, du[...], TN).astype(dwi.dtype)
        return carry

    lax.fori_loop(0, model // TILE, grad_two, 0)

    def grad_three(j, carry):
        cols = rows_of(j, TILE)
        dwo[cols, :] = dot(g_ref[:, cols], gb[...], TN).astype(dwo.dtype)
        return carry

    lax.fori_loop(0, units // TILE, grad_three, 0)
    small = min(TILE, width)

    def grad_four(j, carry):
        cols = rows_of(j, small)
        dwp[cols, :] = dot(o_ref[:, cols].astype(BF16), gb[...], TN).astype(dwp.dtype)
        return carry

    lax.fori_loop(0, width // small, grad_four, 0)

    own_n, inverse = norm_stats(x_ref[...])
    e = keep[...] + gather.total()
    inner = e - jnp.mean(e, axis=-1, keepdims=True) - own_n * jnp.mean(e * own_n, axis=-1, keepdims=True)
    dx_ref[...] = dy_ref[...].astype(F32) + inner * inverse
    spread.finish()
    gather.finish()


VM = pl.BlockSpec(memory_space=pltpu.VMEM)


def shape(dims, dtype):
    return jax.ShapeDtypeStruct(tuple(dims), dtype)


def group_sems(chips, tn):
    dma = pltpu.SemaphoreType.DMA
    return [dma((chips,)), dma((chips,)), dma((tn,)), dma((chips,)), dma((chips,)), dma((chips,)), dma((chips,))]


def group_buffers(chips, size, model):
    return [pltpu.VMEM((chips, size, model), BF16) for _ in range(4)]


def params_of(cid):
    return pltpu.CompilerParams(collective_id=cid, has_side_effects=True, vmem_limit_bytes=VMEM_LIMIT)


def forward_layer(tn, x, weights, vec, bt, bi, tables):
    wt, wi, wo, wp = weights
    size, model = x.shape
    length = size * tn
    width, units, chips = wp.shape[0], wo.shape[0], tn // 2
    outs = (
        shape((size, model), F32),
        shape((length, model), BF16),
        shape((length, width), BF16),
        shape((length, width), BF16),
        shape((length, width), BF16),
        shape((length, width), F32),
        shape((length, 128), F32),
        shape((length, units), BF16),
        shape((length, units), BF16),
    )
    return pl.pallas_call(
        functools.partial(forward_kernel, tn, size),
        out_shape=outs,
        in_specs=[VM] * 12,
        out_specs=[VM] * len(outs),
        scratch_shapes=[pltpu.VMEM((size, model), F32)] + group_buffers(chips, size, model) + group_sems(chips, tn),
        compiler_params=params_of(0),
        name="forward",
    )(x, wt, wi, wo, wp, vec, bt, bi, *tables)


def backward_layer(tn, dy, x, weights, vec, tables, kept):
    wt, wi, wo, wp = weights
    size, model = x.shape
    length = size * tn
    width, units, chips = wp.shape[0], wo.shape[0], tn // 2
    outs = (
        shape((size, model), F32),
        shape(wt.shape, BF16),
        shape(wi.shape, BF16),
        shape(wo.shape, BF16),
        shape(wp.shape, BF16),
        shape((8, model), F32),
        shape((1, 3 * width), F32),
        shape((1, units), F32),
    )
    return pl.pallas_call(
        functools.partial(backward_kernel, tn, size),
        out_shape=outs,
        in_specs=[VM] * 19,
        out_specs=[VM] * len(outs),
        scratch_shapes=[
            pltpu.VMEM((length, model), BF16),
            pltpu.VMEM((length, width), BF16),
            pltpu.VMEM((length, units), BF16),
            pltpu.VMEM((length, 3 * width), BF16),
            pltpu.VMEM((length, width), F32),
            pltpu.VMEM((length, width), F32),
            pltpu.VMEM((length, width), F32),
            pltpu.VMEM((length, model), F32),
            pltpu.VMEM((size, model), F32),
        ]
        + group_buffers(chips, size, model)
        + group_sems(chips, tn),
        compiler_params=params_of(1),
        name="backward",
    )(dy, x, wt, wi, wo, wp, vec, *tables, *kept)


class Place:
    def __init__(self, gn, tn):
        self.gn, self.tn = gn, tn
        self.h, self.t = lax.axis_index("h"), lax.axis_index("t")
        self.g = lax.axis_index("dp") * 2 + self.h
        self.c = self.h * tn + self.t
        self.bits = [1 << i for i in range(gn.bit_length() - 1)]

    def group(self, g):
        return {"dp": g // 2, "h": lax.rem(g, 2)}

    def line(self, c):
        return {"h": c // self.tn, "t": lax.rem(c, self.tn)}

    def other(self, k):
        return lax.rem(self.t + k, self.tn)


def flip(value, bit):
    return value + bit * (1 - 2 * lax.rem(value // bit, 2))


def remote(src, dst, send, recv, device):
    return pltpu.make_async_remote_copy(src, dst, send, recv, device_id=device, device_id_type=MESH)


def runs_by_step(place, bits):
    runs, steps = [(place.g, 1)], []
    for bit in bits:
        steps.append((bit, runs))
        if len(runs) == 1 and runs[0][1] == bit:
            runs = [(runs[0][0] // (2 * bit) * (2 * bit), 2 * bit)]
        else:
            runs = runs + [(flip(start, bit), count) for start, count in runs]
    return steps


def bit_orders(place):
    bits = place.bits
    return [bits, bits[:1] + bits[:0:-1]]


class Doubling:
    def __init__(self, place, ref, block, cols, order, sems, slot):
        self.place, self.ref, self.block, self.cols, self.order = place, ref, block, cols, order
        self.send, self.recv, self.slot = sems[0], sems[1], slot
        self.levels = [[] for _ in order]
        for i, bit in enumerate(order):
            for bits in range(1 << i):
                held = [order[j] for j in range(i) if bits >> j & 1]
                self.levels[len(held)].append((bit, held))

    def at(self, held):
        g = self.place.g
        for bit in held:
            g = flip(g, bit)
        return g

    def copy(self, bit, held):
        start = self.at(held)
        rows = pl.ds(pl.multiple_of(start * self.block, self.block), self.block)
        ref = self.ref.at[rows, self.cols]
        index = sum(held) + bit
        return remote(
            ref,
            ref,
            self.send.at[self.slot, index],
            self.recv.at[self.slot, index],
            self.place.group(flip(self.place.g, bit)),
        )

    def arrive(self, held):
        start = self.at(held)
        rows = pl.ds(pl.multiple_of(start * self.block, self.block), self.block)
        ref = self.ref.at[rows, self.cols]
        index = sum(held)
        peer = self.place.group(flip(self.place.g, held[-1]))
        remote(ref, ref, self.send.at[self.slot, index], self.recv.at[self.slot, index], peer).wait_recv()

    def advance(self, level):
        seen = set()
        for bit, held in self.levels[level]:
            if held and tuple(held) not in seen:
                seen.add(tuple(held))
                self.arrive(held)
            self.copy(bit, held).start()

    def whole(self):
        last = self.order[-1]
        for level in self.levels:
            for bit, held in level:
                if bit == last:
                    self.arrive(held + [bit])

    def finish(self):
        for level in self.levels:
            for item in level:
                self.copy(*item).wait_send()


def halves(cols):
    return [pl.ds(0, cols // 2), pl.ds(cols // 2, cols // 2)]


def line_barrier(place, extra):
    sem = pltpu.get_barrier_semaphore()
    span = 2 * place.tn
    for k in range(1, span):
        pl.semaphore_signal(sem, inc=1, device_id=place.line(lax.rem(place.c + k, span)), device_id_type=MESH)
    for bit in place.bits[1:]:
        pl.semaphore_signal(sem, inc=1, device_id=place.group(flip(place.g, bit)), device_id_type=MESH)
    peers = span - 1 + len(place.bits) - 1
    source, moved = extra

    @pl.when(moved)
    def _():
        pl.semaphore_signal(sem, inc=1, device_id=source, device_id_type=MESH)
        pl.semaphore_wait(sem, peers + 1)

    @pl.when(jnp.logical_not(moved))
    def _():
        pl.semaphore_wait(sem, peers)


def proj_places(place):
    gn, tn = place.gn, place.tn
    r = place.g * tn + place.t
    target = place.group(lax.rem(r, gn)) | {"t": r // gn}
    q = place.t * gn + place.g
    source = place.group(q // tn) | {"t": lax.rem(q, tn)}
    return target, source, r, q


def slot_rows(index, size):
    return pl.ds(pl.multiple_of(index * size, size), size)


class Opening:
    def __init__(self, place, layers, tok, cot, seg, vec, tri, inn, outer, proj, tok_o, cot_o, seg_o, vec_o, w, sems):
        self.place, self.layers = place, layers
        self.tok, self.cot, self.seg, self.vec = tok, cot, seg, vec
        self.tri, self.inn, self.outer, self.proj = tri, inn, outer, proj
        self.tok_o, self.cot_o, self.seg_o, self.vec_o = tok_o, cot_o, seg_o, vec_o
        self.wts, self.wis, self.wos, self.wps = w
        (
            self.ssem, self.rsem, self.lsem, self.asend, self.arecv, self.psend, self.precv,
            self.msend, self.mrecv, self.gsend, self.grecv,
        ) = sems
        self.half = tok.shape[1]
        self.target, self.source, self.r, self.q = proj_places(place)
        self.moved = self.q != self.r
        self.local, self.sends, self.shared_with = [], [], {}
        self.locals_of = {}

    def barrier(self):
        line_barrier(self.place, (self.source, self.moved))

    def near(self, src, dst, key):
        cp = pltpu.make_async_copy(src, dst, self.lsem.at[len(self.local)])
        cp.start()
        self.local.append(cp)
        self.locals_of[key] = cp

    def hop(self, src, dst, slot, i):
        c, tn = self.place.c, self.place.tn
        to = i * tn + c // 2
        rows = slot_rows(lax.rem(c, 2), self.half)
        near = pltpu.make_async_copy(src.at[i], dst.at[rows], self.msend.at[slot, i])
        far = remote(
            src.at[i], dst.at[rows], self.msend.at[slot, i], self.mrecv.at[slot, lax.rem(c, 2)],
            self.place.line(to),
        )
        return to == c, near, far

    def move(self, src, dst, slot):
        for i in range(2):
            stays, near, far = self.hop(src, dst, slot, i)
            pl.when(stays)(near.start)
            pl.when(jnp.logical_not(stays))(far.start)

    def moved_in(self, src, dst, slot):
        for i in range(2):
            stays, near, far = self.hop(src, dst, slot, i)
            pl.when(stays)(near.wait)
            pl.when(jnp.logical_not(stays))(far.wait_send)
        for s in range(2):
            cp = remote(
                src.at[0], dst.at[pl.ds(s * self.half, self.half)], self.msend.at[slot, 0],
                self.mrecv.at[slot, s], self.place.line(self.place.c),
            )
            pl.when(2 * self.place.t + s != self.place.c)(cp.wait_recv)

    def share(self, key, src_of, dst, size, slot):
        g, t, tn = self.place.g, self.place.t, self.place.tn
        rows = slot_rows(g * tn + t, size)
        self.near(src_of(t), dst.at[rows], key)
        for k in range(1, tn):
            to = self.place.other(k)
            cp = remote(src_of(to), dst.at[rows], self.asend.at[slot, k], self.arecv.at[slot, t], {"t": to})
            cp.start()
            self.sends.append(cp)
        self.shared_with[key] = (dst, size, slot)

    def shared(self, key):
        dst, size, slot = self.shared_with[key]
        self.locals_of[key].wait()
        for k in range(1, self.place.tn):
            frm = self.place.other(k)
            ref = dst.at[slot_rows(self.place.g * self.place.tn + frm, size)]
            remote(ref, ref, self.asend.at[slot, k], self.arecv.at[slot, frm], {"t": frm}).wait_recv()

    def share_layer(self, layer):
        depth = self.tri.shape[2]
        base = 1 + 2 * layer
        self.share(("t", layer), lambda to: self.tri.at[layer, to], self.wts[layer], depth, base)
        self.share(("i", layer), lambda to: self.inn.at[layer, to], self.wis[layer], depth, base + 1)
        g = self.place.g
        self.near(self.outer.at[layer], self.wos[layer].at[slot_rows(g, self.outer.shape[1])], ("o", layer))
        here, far = self.proj_copies(layer)
        pl.when(self.moved)(far.start)
        pl.when(jnp.logical_not(self.moved))(here.start)

    def proj_copies(self, layer):
        prows = self.proj.shape[1]
        src = self.proj.at[layer]
        here = pltpu.make_async_copy(src, self.wps[layer].at[slot_rows(self.place.g, prows)], self.psend.at[layer])
        dst = self.wps[layer].at[slot_rows(lax.rem(self.r, self.place.gn), prows)]
        return here, remote(src, dst, self.psend.at[layer], self.precv.at[layer], self.target)

    def proj_ready(self, layer):
        here, far = self.proj_copies(layer)

        @pl.when(self.moved)
        def _():
            far.wait_recv()
            far.wait_send()

        pl.when(jnp.logical_not(self.moved))(here.wait)

    def start(self):
        place, span = self.place, 2 * self.place.tn
        self.move(self.tok, self.tok_o, 0)
        vec_rows = self.vec.shape[0]
        self.share("v", lambda to: self.vec, self.vec_o, vec_rows, 0)
        self.near(self.seg, self.seg_o.at[slot_rows(place.c, 8)], "s")
        for k in range(1, span):
            to = lax.rem(place.c + k, span)
            dst = self.seg_o.at[slot_rows(place.c, 8)]
            cp = remote(self.seg, dst, self.gsend.at[k], self.grecv.at[place.c], place.line(to))
            cp.start()
            self.sends.append(cp)
        for layer in range(self.layers):
            self.share_layer(layer)
        orders = bit_orders(place)
        self.chunks, slot = [], 0
        tn, depth = place.tn, self.tri.shape[2]
        todo = []
        for layer in range(self.layers):
            todo += [
                [(("t", layer), self.wts[layer], tn * depth)],
                [(("i", layer), self.wis[layer], tn * depth)],
                [
                    (("o", layer), self.wos[layer], self.outer.shape[1]),
                    (("p", layer), self.wps[layer], self.proj.shape[1]),
                ],
            ]
        todo[0].insert(0, ("v", self.vec_o, tn * vec_rows))
        self.keys = [[key for key, _, _ in chunk] for chunk in todo]
        for chunk in todo:
            parts = []
            for _, ref, block in chunk:
                pieces = halves(ref.shape[1]) if ref.shape[1] >= 256 else [pl.ds(0, ref.shape[1])]
                for i, piece in enumerate(pieces):
                    parts.append(Doubling(place, ref, block, piece, orders[i], (self.ssem, self.rsem), slot))
                    slot += 1
            self.chunks.append(parts)
        self.steps = len(place.bits)
        self.turn, self.turns = 0, len(self.chunks) + SKEW * (self.steps - 1)
        self.complete = set()

    def ready(self, i):
        for key in self.keys[i]:
            if key == "v" or key[0] in ("t", "i"):
                self.shared(key)
            elif key[0] == "o":
                self.locals_of[key].wait()
            else:
                self.proj_ready(key[1])

    def tick(self, until=None):
        while self.turn < self.turns and (until is None or self.turn <= until):
            for step in reversed(range(self.steps)):
                i = self.turn - SKEW * step
                if 0 <= i < len(self.chunks):
                    if step == 0:
                        self.ready(i)
                    for part in self.chunks[i]:
                        part.advance(step)
            self.turn += 1
            if until is None:
                break

    def have(self, key):
        i = [key in keys for keys in self.keys].index(True)
        if i not in self.complete:
            self.complete.add(i)
            self.tick(i + SKEW * (self.steps - 1))
            for part in self.chunks[i]:
                part.whole()

    def segments_in(self):
        place, span = self.place, 2 * self.place.tn
        self.locals_of["s"].wait()
        for k in range(1, span):
            frm = lax.rem(place.c + k, span)
            ref = self.seg_o.at[slot_rows(frm, 8)]
            remote(ref, ref, self.gsend.at[k], self.grecv.at[frm], place.line(frm)).wait_recv()

    def finish(self):
        self.tick(self.turns)
        for parts in self.chunks:
            for part in parts:
                part.finish()
        for cp in self.sends:
            cp.wait_send()


def ascend_kernel(
    gn, tn, layers, size,
    tok, cot, seg, vec, tri, inn, outer, proj, ctab, stab, e32, m32, e96, m96,
    cot_o, out_o, segcol, segrow, vecs_o, bts_o, bis_o, xs_o, w_o, kept_o,
    w, kept, xs, x_low, out_low, keep, seg_in, vec_in, vec_wide, bt_wide,
    bufs, group, opening_sems, save_sem, tok_sem,
):
    place = Place(gn, tn)
    opening = Opening(
        place, layers, tok, cot, seg, vec, tri, inn, outer, proj, x_low, cot_o, seg_in, vec_in, w, opening_sems
    )
    opening.barrier()
    opening.start()
    saves = []

    def save(src, dst):
        cp = pltpu.make_async_copy(src, dst, save_sem.at[len(saves)])
        cp.start()
        saves.append(cp)

    opening.tick(1)
    opening.moved_in(tok, x_low, 0)
    xs[0][...] = x_low[...].astype(F32)
    spreads, gathers, stages = [], [], []
    for layer in range(layers):
        ssem, fsem, rsem, cs, cr, ls, lr = group[layer]
        spreads.append(Spread(tn, kept[layer][0], size, ssem, fsem, rsem))
        gathers.append(Gather(tn, *bufs, (cs, cr, ls, lr)))
        stages.append(
            Forward(
                tn, size, xs[layer], tuple(w[k][layer] for k in range(4)),
                (vecs_o.at[layer], bts_o.at[layer], bis_o.at[layer]), (segcol, segrow), (ctab, stab),
                kept[layer], keep,
            )
        )
    stages[0].norm(place.t)
    spreads[0].start()
    opening.segments_in()
    block = segcol.shape[0] // (2 * tn)
    eye = lax.broadcasted_iota(jnp.int32, (block, block), 0) == lax.broadcasted_iota(jnp.int32, (block, block), 1)
    for i in range(2 * tn):
        row = jnp.where(place.h == 0, seg_in[8 * i : 8 * i + 1, :], seg_in[8 * i + 1 : 8 * i + 2, :])
        spot = lax.broadcasted_iota(jnp.int32, (1, block), 1) + i * block
        row = jnp.where(row == 0, -1 - spot, row).astype(F32)
        segrow[:, i * block : (i + 1) * block] = row
        segcol[i * block : (i + 1) * block, :] = jnp.sum(jnp.where(eye, row, 0.0), axis=1, keepdims=True)
    opening.have("v")
    shards = gn * tn
    vec_rows = vec.shape[0]
    vec_wide[...] = vec_in[...].astype(F32)
    lane = lax.broadcasted_iota(jnp.int32, (1, 128), 1)
    for layer in range(layers):

        def line(k):
            return vec_wide[pl.ds(4 * layer + k, shards, stride=vec_rows), :]

        def spread_out(value, place_of, mask):
            return jnp.sum(dot(value.astype(BF16), place_of, NN) * mask, axis=0, keepdims=True)

        thick = line(2)
        parts = [jnp.where(lane // 32 == i, thick, 0.0) for i in range(4)]
        thin = line(3)
        gains = [jnp.where(lane // 32 == i, thin, 0.0) for i in range(2)]
        rows = [spread_out(p, e32[...], m32[...]) for p in parts + gains]
        vecs_o[layer] = jnp.concatenate(
            [rows[2], rows[3], rows[4], rows[5], rows[0] + rows[1]] + [jnp.zeros_like(rows[0])] * 3, axis=0
        )
        bt_wide[...] = spread_out(line(1), e96[...], m96[...])
        wide = bts_o.shape[2] // 3
        for i in range(3):
            start = pl.multiple_of(i * wide * tn + place.t * wide, 128)
            bts_o[layer, :, i * wide : (i + 1) * wide] = bt_wide[:, pl.ds(start, wide)]
        for i in range(gn):
            bis_o[layer, :, i * 128 : (i + 1) * 128] = vec_wide[
                pl.ds((i * tn + place.t) * vec_rows + 4 * layer, 1), :
            ]

    for layer in range(layers):
        stage, spread, gather = stages[layer], spreads[layer], gathers[layer]
        if layer > 0:
            stage.norm(place.t)
            spread.start()
        opening.have(("t", layer))
        for i, b in enumerate(arrivals(spread)):
            stage.heads_in(b)
            if i == 1:
                opening.tick()
        if layer == 0:
            opening.move(cot, cot_o, 1)
        for i, b in enumerate(far_first(spread)):
            stage.attend(b)
            if i == 1:
                opening.tick()
        opening.have(("i", layer))
        save(kept[layer][0], kept_o[layer][0])
        for i in range(1, 6):
            save(kept[layer][i], kept_o[layer][i])
        for i, b in enumerate(far_first(spread)):
            stage.mixer_in(b)
            if i == 1:
                opening.tick()
        save(kept[layer][6], kept_o[layer][6])
        save(kept[layer][7], kept_o[layer][7])
        opening.have(("o", layer))
        for k in range(4):
            save(w[k][layer], w_o[k][layer])
        branch_sums(stage, spread, gather, opening.tick)
        total = xs[layer][...] + vecs_o[layer, 4:5, :] + keep[...] + gather.total()
        if layer + 1 < layers:
            xs[layer + 1][...] = total
        else:
            out_low[...] = total.astype(BF16)
            save(out_low, out_o)
        save(xs[layer], xs_o[layer])
        spread.finish()
        gather.finish()
    opening.finish()
    opening.moved_in(cot, cot_o, 1)
    for cp in saves:
        cp.wait()


ANY = pl.BlockSpec(memory_space=pl.ANY)


def constant_tables(span, shards, model):
    angle = np.arange(span, dtype=np.float32)[:, None] * (
        np.float32(10000.0) ** (-(2.0 * np.arange(ROT // 2, dtype=np.float32)) / np.float32(ROT))
    )
    cosine, sine = np.cos(angle).astype(np.float32), np.sin(angle).astype(np.float32)
    none = np.zeros((span, HD - ROT), np.float32)
    reps = 128 // HD
    ctab = np.concatenate([cosine, cosine, none + 1.0] * reps, axis=1)
    stab = np.concatenate([-sine, sine, none] * reps, axis=1)
    return tuple(jnp.asarray(tab, F32) for tab in (ctab, stab))


def placement(piece, shards):
    j, col = np.arange(128)[:, None], np.arange(piece * shards)[None, :]
    put = (j % piece == col % piece) if 128 % piece == 0 else (j == col % piece)
    mask = np.arange(shards)[:, None] == col // piece
    return jnp.asarray(put, BF16), jnp.asarray(mask, F32)


def kept_shapes(length, model, width, units):
    return [
        ((length, model), BF16),
        ((length, width), BF16),
        ((length, width), BF16),
        ((length, width), BF16),
        ((length, width), F32),
        ((length, 128), F32),
        ((length, units), BF16),
        ((length, units), BF16),
    ]


def ascend_call(gn, tn, tokens, cotangent, segments, vec, tri, inn, outer, proj, tables, placing):
    layers = outer.shape[0]
    _, half, model = tokens.shape
    size = 2 * half
    length = size * tn
    depth = tri.shape[2]
    wshapes = [
        (gn * tn * depth, tri.shape[3]), (gn * tn * depth, inn.shape[3]),
        (gn * outer.shape[1], model), (gn * proj.shape[1], model),
    ]
    width, units, chips = wshapes[3][0], wshapes[2][0], tn // 2
    kept = kept_shapes(length, model, width, units)
    dma = pltpu.SemaphoreType.DMA
    outs = [
        (shape((size, model), BF16), ANY),
        (shape((size, model), BF16), ANY),
        (shape((length, 1), F32), VM),
        (shape((1, length), F32), VM),
        (shape((layers, 8, model), F32), VM),
        (shape((layers, 1, 3 * width), F32), VM),
        (shape((layers, 1, units), F32), VM),
    ]
    outs += [(shape((size, model), F32), ANY)] * layers
    for dims in wshapes:
        outs += [(shape(dims, BF16), ANY)] * layers
    for _ in range(layers):
        outs += [(shape(*item), ANY) for item in kept]
    scratch = []
    for dims in wshapes:
        scratch += [pltpu.VMEM(dims, BF16)] * layers
    for _ in range(layers):
        scratch += [pltpu.VMEM(*item) for item in kept]
    scratch += [pltpu.VMEM((size, model), F32)] * layers
    scratch += [
        pltpu.VMEM((size, model), BF16),
        pltpu.VMEM((size, model), BF16),
        pltpu.VMEM((size, model), F32),
        pltpu.VMEM((2 * tn * 8, 128), jnp.int32),
        pltpu.VMEM((gn * tn * vec.shape[0], 128), BF16),
        pltpu.VMEM((gn * tn * vec.shape[0], 128), F32),
        pltpu.VMEM((1, 3 * model), F32),
    ]
    scratch += group_buffers(chips, size, model)
    for _ in range(layers):
        scratch += group_sems(chips, tn)
    slots = 1 + 8 * layers
    scratch += [
        dma((slots, gn)), dma((slots, gn)), dma((2 + 3 * layers,)),
        dma((1 + 2 * layers, tn)), dma((1 + 2 * layers, tn)),
        dma((layers,)), dma((layers,)), dma((2, 2)), dma((2, 2)),
        dma((2 * tn,)), dma((2 * tn,)),
    ]
    scratch += [dma((14 * layers,)), dma((1,))]

    def body(*refs):
        refs = list(refs)

        def take(count):
            out, refs[:] = refs[:count], refs[count:]
            return out

        ins = take(14)
        cot_o, out_o, segcol, segrow, vecs_o, bts_o, bis_o = take(7)
        xs_o = take(layers)
        w_o = [take(layers) for _ in range(4)]
        kept_o = [take(8) for _ in range(layers)]
        w = [take(layers) for _ in range(4)]
        kept_s = [take(8) for _ in range(layers)]
        xs = take(layers)
        x_low, out_low, keep, seg_in, vec_in, vec_wide, bt_wide = take(7)
        bufs = take(4)
        group = [take(7) for _ in range(layers)]
        sems = take(11)
        save_sem, tok_sem = take(2)
        ascend_kernel(
            gn, tn, layers, size, *ins, cot_o, out_o, segcol, segrow, vecs_o, bts_o, bis_o, xs_o, w_o, kept_o,
            w, kept_s, xs, x_low, out_low, keep, seg_in, vec_in, vec_wide, bt_wide, bufs, group, sems,
            save_sem, tok_sem,
        )

    return pl.pallas_call(
        body,
        out_shape=tuple(o for o, _ in outs),
        in_specs=[ANY] * 8 + [VM] * 6,
        out_specs=tuple(spec for _, spec in outs),
        scratch_shapes=scratch,
        compiler_params=params_of(2),
        name="ascend",
    )(tokens, cotangent, segments, vec, tri, inn, outer, proj, *tables, *placing)


class Halving:
    def __init__(self, place, acc, inbox, block, cols, order, sems, slot):
        self.place, self.acc, self.inbox, self.block, self.cols = place, acc, inbox, block, cols
        self.send, self.recv, self.slot = sems[0], sems[1], slot
        self.plan, index, base = [], 0, 0
        for bit, runs in reversed(runs_by_step(place, order)):
            entry = []
            for start, count in runs:
                entry.append((bit, start, count, index, base))
                index += 1
                base += count
            self.plan.append(entry)

    def copy(self, bit, start, count, index, base):
        rows = pl.ds(pl.multiple_of(flip(start, bit) * self.block, self.block), count * self.block)
        return remote(
            self.acc.at[rows, self.cols],
            self.inbox.at[pl.ds(base * self.block, count * self.block), self.cols],
            self.send.at[self.slot, index],
            self.recv.at[self.slot, index],
            self.place.group(flip(self.place.g, bit)),
        )

    def advance(self, step):
        if step > 0:
            for item in self.plan[step - 1]:
                self.copy(*item).wait_recv()
                _, start, count, _, base = item

                def add(i, carry):
                    rows = pl.ds(pl.multiple_of((start + i) * self.block, self.block), self.block)
                    came = pl.ds(pl.multiple_of((base + i) * self.block, self.block), self.block)
                    value = self.acc[rows, self.cols].astype(F32) + self.inbox[came, self.cols].astype(F32)
                    self.acc[rows, self.cols] = value.astype(BF16)
                    return carry

                lax.fori_loop(0, count, add, 0)
        if step < len(self.plan):
            for item in self.plan[step]:
                self.copy(*item).start()

    def finish(self):
        for entry in self.plan:
            for item in entry:
                self.copy(*item).wait_send()

class Reducing:
    def __init__(self, place, layers, accs, boxes, outs, sems):
        self.place, self.layers = place, layers
        self.accs, self.boxes = accs, boxes
        self.cross, self.proj_o, self.outer_o = outs[:2], outs[2], outs[3]
        self.hs, self.hr, self.cs, self.cr, self.ps, self.pr, self.os = sems
        self.target, self.source, self.r, self.q = proj_places(place)
        self.moved = self.q != self.r
        orders = bit_orders(place)
        self.parts, slot = {}, 0
        for layer in range(layers):
            for kind in range(4):
                acc = accs[kind][layer]
                parts = []
                for k, cols in enumerate(halves(acc.shape[1])):
                    box = boxes[kind].at[layer]
                    block = acc.shape[0] // place.gn
                    parts.append(Halving(place, acc, box, block, cols, orders[k], (self.hs, self.hr), slot))
                    slot += 1
                self.parts[kind, layer] = parts
        self.steps = len(place.bits) + 1
        self.taken = {key: 0 for key in self.parts}

    def advance(self, kind, layer):
        step = self.taken[kind, layer]
        self.taken[kind, layer] = step + 1
        for part in self.parts[kind, layer]:
            part.advance(step)
        if step == self.steps - 1:
            self.owned(kind, layer)

    def own_rows(self, kind, layer, index, pieces):
        acc = self.accs[kind][layer]
        rows = acc.shape[0] // pieces
        return acc.at[slot_rows(index, rows)]

    def cross_copy(self, kind, layer, k):
        place = self.place
        to = place.other(k)
        src = self.own_rows(kind, layer, place.g * place.tn + to, place.gn * place.tn)
        dst = self.cross[kind].at[layer, place.t]
        return remote(src, dst, self.cs.at[kind, layer, k], self.cr.at[kind, layer, place.t], {"t": to})

    def proj_copies(self, layer):
        src = self.own_rows(3, layer, self.place.g, self.place.gn)
        here = pltpu.make_async_copy(src, self.proj_o.at[layer], self.ps.at[layer])
        return here, remote(src, self.proj_o.at[layer], self.ps.at[layer], self.pr.at[layer], self.source)

    def own_copy(self, kind, layer):
        place = self.place
        if kind == 2:
            src, dst = self.own_rows(2, layer, place.g, place.gn), self.outer_o.at[layer]
        else:
            src = self.own_rows(kind, layer, place.g * place.tn + place.t, place.gn * place.tn)
            dst = self.cross[kind].at[layer, place.t]
        return pltpu.make_async_copy(src, dst, self.os.at[kind, layer])

    def owned(self, kind, layer):
        if kind < 3:
            self.own_copy(kind, layer).start()
        if kind < 2:
            for k in range(1, self.place.tn):
                self.cross_copy(kind, layer, k).start()
        if kind == 3:
            here, far = self.proj_copies(layer)
            pl.when(self.moved)(far.start)
            pl.when(jnp.logical_not(self.moved))(here.start)

    def finish(self):
        for (kind, layer), parts in self.parts.items():
            for part in parts:
                part.finish()
            if kind < 3:
                self.own_copy(kind, layer).wait()
            if kind < 2:
                for k in range(1, self.place.tn):
                    frm = self.place.other(k)
                    ref = self.cross[kind].at[layer, frm]
                    remote(
                        ref, ref, self.cs.at[kind, layer, k], self.cr.at[kind, layer, frm], {"t": frm}
                    ).wait_recv()
                    self.cross_copy(kind, layer, k).wait_send()
            if kind == 3:
                here, far = self.proj_copies(layer)
                pl.when(self.moved)(far.wait)
                pl.when(jnp.logical_not(self.moved))(here.wait)


def descend_kernel(
    gn, tn, layers, size,
    cot, out_in, segcol, segrow, vecs, ctab, stab, xs, ws, kepts,
    out_o, grad_o, flat_o, triple_o, inner_o, proj_o, outer_o,
    w, kept, dy, x, gb, do, dt, dk, dv, keep, dbt, dbi, bufs, accs, boxes, flatbox,
    group, reduce_sems, load_sem, ms, mr, fs, fr,
):
    place = Place(gn, tn)
    g, t, c = place.g, place.t, place.c
    wt, wi, wo, wp = w
    n, q, k, v, o, lse, gact, gp = kept
    chips = tn // 2
    width, units, model = q.shape[1], gact.shape[1], dy.shape[1]
    heads = width // HD
    dq, dh, du = o, gact, gp
    loads = {}

    def load(layer, names):
        for name in names:
            if name == "x":
                src, dst = xs[layer], x
            elif name == "cot":
                src, dst = cot, gb.at[rows_of(t, size)]
            elif name[0] == "w":
                i = int(name[1])
                src, dst = ws[i][layer], w[i]
            else:
                i = int(name[1])
                src, dst = kepts[layer][i], kept[i]
            cp = pltpu.make_async_copy(src, dst, load_sem.at[len(loads)])
            cp.start()
            loads[layer, name] = cp

    waited = set()

    def need(layer, names):
        for name in names:
            if (layer, name) not in waited:
                waited.add((layer, name))
                loads[layer, name].wait()

    last = layers - 1
    load(last, ["cot", "w3", "k4", "w2", "k7", "k6", "k0", "w1", "k1", "k2", "k3", "k5", "w0", "x"])
    reducing = Reducing(place, layers, accs, boxes, (triple_o, inner_o, proj_o, outer_o), reduce_sems)
    line_barrier(place, (reducing.target, reducing.moved))
    half = out_o.shape[1]

    def hop(src, dst, slot, s):
        to = 2 * t + s
        part = src.at[pl.ds(s * half, half)]
        near = pltpu.make_async_copy(part, dst.at[place.h], ms.at[slot, s])
        far = remote(part, dst.at[place.h], ms.at[slot, s], mr.at[slot, place.h], place.line(to))
        return to == c, near, far

    def move(src, dst, slot):
        for s in range(2):
            stays, near, far = hop(src, dst, slot, s)
            pl.when(stays)(near.start)
            pl.when(jnp.logical_not(stays))(far.start)

    def moved_in(src, dst, slot):
        for s in range(2):
            stays, near, far = hop(src, dst, slot, s)
            pl.when(stays)(near.wait)
            pl.when(jnp.logical_not(stays))(far.wait_send)
        for i in range(2):
            cp = remote(
                src.at[pl.ds(0, half)], dst.at[i], ms.at[slot, 0], mr.at[slot, i], place.line(c)
            )
            pl.when(i * tn + c // 2 != c)(cp.wait_recv)

    exchanges = [("g", bit) for bit in place.bits] + [("t", 1 << i) for i in range(tn.bit_length() - 1)]

    def exchange(layer, i):
        kind, bit = exchanges[i]
        to = place.group(flip(g, bit)) if kind == "g" else {"t": flip(t, bit)}
        return remote(flat_o.at[layer], flatbox.at[layer, i], fs.at[layer, i], fr.at[layer, i], to)

    def flat_turn(layer, i):
        if i > 0:
            exchange(layer, i - 1).wait()
            flat_o[layer] += flatbox[layer, i - 1]
        if i < len(exchanges):
            exchange(layer, i).start()

    masks = head_masks(width, BF16)
    lane = lax.broadcasted_iota(jnp.int32, (1, 128), 1)
    up = place.t // 2 >= (chips + 1) // 2

    def pair(qb, kb):
        qrows, krows = rows_of(qb, size), rows_of(kb, size)
        queries, keys, vals = q[qrows, :], k[krows, :], v[krows, :]
        grad = do[qrows, :]
        side = lse[qrows, :]
        bias = pair_bias(qb, kb, size, segcol, segrow)
        dq_new = jnp.zeros((size, width), F32)
        dk_new = jnp.zeros((size, width), F32)
        dv_new = jnp.zeros((size, width), F32)
        for h in range(heads):
            qh, gh = queries * masks[h], grad * masks[h]
            total = jnp.sum(jnp.where(lane == h, side, 0.0), axis=1, keepdims=True)
            delta = jnp.sum(jnp.where(lane == 64 + h, side, 0.0), axis=1, keepdims=True)
            p = jnp.exp(dot(qh, keys, NT) + bias - total)
            ds = (p * (dot(gh, vals, NT) - delta)).astype(BF16)
            dv_new = dv_new + dot(p.astype(BF16), gh, TN)
            dk_new = dk_new + dot(ds, qh, TN)
            dq_new = dq_new + dot(ds, keys * masks[h], NN)
        dq[qrows, :] += dq_new
        dk[krows, :] += dk_new
        dv[krows, :] += dv_new

    def columns(count, tile, body):
        def step(j, carry):
            body(rows_of(j, tile))
            return carry

        lax.fori_loop(0, count // tile, step, 0)

    need(last, ["cot"])
    dy[...] = gb[rows_of(t, size), :].astype(F32)
    flat_o[...] = jnp.zeros_like(flat_o)

    for layer in reversed(range(layers)):
        flat = flat_o.at[layer]
        vec = vecs.at[layer]
        dwt, dwi, dwo, dwp = (accs[i][layer] for i in range(4))
        ssem, fsem, rsem, cs, cr, ls, lr = group[layer]
        spread = Spread(tn, gb, size, ssem, fsem, rsem)
        gather = Gather(tn, *bufs, (cs, cr, ls, lr))
        zc, co = spread.zc, spread.co

        def tick(kind, late, layer=layer):
            if layer + late < layers and reducing.taken[kind, layer + late] < reducing.steps:
                reducing.advance(kind, layer + late)

        own = dy[...].astype(BF16)
        gb[rows_of(t, size), :] = own
        spread.start()
        if layer == last:
            move(out_in, out_o, 0)
        flat[4:5, :] = jnp.sum(own.astype(F32), axis=0, keepdims=True)
        dbt[...] = jnp.zeros_like(dbt)
        dbi[...] = jnp.zeros_like(dbi)
        dk[...] = jnp.zeros_like(dk)
        dv[...] = jnp.zeros_like(dv)
        tick(2, 1)
        tick(3, 1)
        if layer < last:
            flat_turn(layer + 1, 0)
        for count, b in enumerate(arrivals(spread)):
            need(layer, ["w3", "k4", "w2", "k7", "k5"])
            rows = rows_of(b, size)
            grad = gb[rows, :]
            heads_grad = dot(grad, wp[...], NT).astype(BF16)
            do[rows, :] = heads_grad
            prod = heads_grad.astype(F32) * o[rows, :]
            side = lse[rows, :]
            for h in range(heads):
                delta = jnp.sum(prod * masks[h].astype(F32), axis=1, keepdims=True)
                side = jnp.where(lane == 64 + h, delta, side)
            lse[rows, :] = side

            def unit(cols):
                d = (dot(grad, wo[cols, :], NT) * gp[rows, cols].astype(F32)).astype(BF16)
                du[rows, cols] = d
                dbi[0:1, cols] += jnp.sum(d.astype(F32), axis=0, keepdims=True)

            columns(units, TILE, unit)
            if layer < last:
                flat_turn(layer + 1, count + 1)
            if count == 1:
                tick(1, 1)
        need(layer, ["k6"])
        spread.finish()

        def grad_outer(cols):
            dwo[cols, :] = dot(gact[:, cols], gb[...], TN).astype(BF16)

        columns(units, TILE, grad_outer)

        def grad_proj(cols):
            dwp[cols, :] = dot(o[:, cols].astype(BF16), gb[...], TN).astype(BF16)

        columns(width, TILE, grad_proj)
        tick(2, 1)
        tick(3, 1)
        tick(2, 0)
        tick(3, 0)
        if layer < last:
            flat_turn(layer + 1, len(exchanges))
        need(layer, ["w1", "k0"])
        if layer > 0:
            load(layer - 1, ["w2", "w3"])
        dq[...] = jnp.zeros_like(dq)
        for b in range(tn):
            rows = pl.ds(b * size, size)

            def back(cols):
                d = dot(du[rows, :], wi[cols, :], NT)
                flat[2:3, cols] += jnp.sum(d * n[rows, cols].astype(F32), axis=0, keepdims=True)
                flat[3:4, cols] += jnp.sum(d, axis=0, keepdims=True)
                dh[rows, cols] = (d * vec[2:3, cols]).astype(BF16)

            columns(model, TILE, back)

        def grad_inner(cols):
            h2 = (n[:, cols].astype(F32) * vec[2:3, cols] + vec[3:4, cols]).astype(BF16)
            dwi[cols, :] = dot(h2, du[...], TN).astype(BF16)

        columns(model, TILE, grad_inner)
        tick(1, 1)
        tick(0, 1)
        tick(1, 0)
        if layer > 0:
            load(layer - 1, ["w1", "k7"])
        need(layer, ["k1", "k2", "k3", "w0"])

        for stage in range(tn):
            pivot = jnp.where(up, stage, tn - 1 - stage)

            def step(j, carry):
                pair(jnp.where(up, pivot + j, pivot), jnp.where(up, pivot, pivot - j))
                return carry

            lax.fori_loop(0, tn - stage, step, 0)
            rows = rows_of(pivot, size)
            cos, sine = ctab[rows, :], stab[rows, :]
            dt[rows, 0:width] = turn(dq[rows, :] * (1.0 / math.sqrt(HD)), cos, sine, -1.0).astype(BF16)
            dt[rows, width : 2 * width] = turn(dk[rows, :], cos, sine, -1.0).astype(BF16)
            dt[rows, 2 * width : 3 * width] = dv[rows, :].astype(BF16)
            block = dt[rows, :]
            dbt[...] += jnp.sum(block.astype(F32), axis=0, keepdims=True)
            chip, core = pivot // 2, lax.rem(pivot, 2)

            def back(cols):
                d = dot(block, wt[cols, :], NT)
                flat[0:1, cols] += jnp.sum(d * n[rows, cols].astype(F32), axis=0, keepdims=True)
                flat[1:2, cols] += jnp.sum(d, axis=0, keepdims=True)
                value = dh[rows, cols].astype(F32) + d * vec[0:1, cols]

                @pl.when(core != co)
                def _():
                    gather.tocore[chip, :, cols] = value.astype(BF16)

                @pl.when((core == co) & (chip != zc))
                def _():
                    gather.toici[chip, :, cols] = value.astype(BF16)

                @pl.when(pivot == t)
                def _():
                    keep[:, cols] = value

            columns(model, TILE, back)

            @pl.when(core != co)
            def _():
                gather.send_core(chip)

            if stage % 2 == 1:

                @pl.when(chip != zc)
                def _():
                    gather.send_link(chip)

            if stage == 0:
                tick(1, 1)
                tick(0, 1)
            if stage == 1:
                tick(2, 0)
                tick(3, 0)
            if stage == 2:
                tick(0, 1)
        tick(1, 0)

        wide = width
        for i in range(3):
            start = pl.multiple_of(t * wide, 128)
            flat[5 + i : 6 + i, pl.ds(start, wide)] = dbt[:, i * wide : (i + 1) * wide]
        for i in range(gn):
            row, start = divmod(i * tn * 128, model)
            flat[8 + row : 9 + row, pl.ds(pl.multiple_of(start + t * 128, 128), 128)] = dbi[:, i * 128 : (i + 1) * 128]
        if layer > 0:
            load(layer - 1, ["w0", "k1", "k2", "k3", "k4", "k5", "k6"])

        def grad_triple(cols):
            h1 = (n[:, cols].astype(F32) * vec[0:1, cols] + vec[1:2, cols]).astype(BF16)
            dwt[cols, :] = dot(h1, dt[...], TN).astype(BF16)

        columns(model, TILE, grad_triple)
        if layer > 0:
            load(layer - 1, ["k0"])
        tick(0, 0)
        tick(2, 0)
        tick(3, 0)
        if layer == 0:
            flat_turn(0, 0)
        need(layer, ["x"])
        own_n, inverse = norm_stats(x[...])
        e = keep[...] + gather.total()
        inner = e - jnp.mean(e, axis=-1, keepdims=True) - own_n * jnp.mean(e * own_n, axis=-1, keepdims=True)
        dy[...] = dy[...] + inner * inverse
        if layer > 0:
            load(layer - 1, ["x"])
        gather.finish()

    low = gb.at[pl.ds(0, size)]
    low[...] = dy[...].astype(BF16)
    move(low, grad_o, 1)
    rest = [(1, 0), (0, 0), (2, 0), (3, 0), (1, 0), (0, 0), (0, 0)]
    for i, (kind, layer) in enumerate(rest):
        if i + 1 <= len(exchanges):
            flat_turn(0, i + 1)
        reducing.advance(kind, layer)
    for layer in reversed(range(layers)):
        for kind in range(4):
            while reducing.taken[kind, layer] < reducing.steps:
                reducing.advance(kind, layer)
    reducing.finish()
    moved_in(out_in, out_o, 0)
    moved_in(low, grad_o, 1)


def descend_call(gn, tn, cot, output, segcol, segrow, vecs, tables, xs, ws, kepts):
    layers = len(xs)
    size, model = output.shape
    length = size * tn
    shapes = [ws[i][0].shape for i in range(4)]
    width, units, chips = shapes[3][0], shapes[2][0], tn // 2
    kept = kept_shapes(length, model, width, units)
    dma = pltpu.SemaphoreType.DMA
    shard = shapes[0][0] // (gn * tn)
    prows, orows = shapes[3][0] // gn, shapes[2][0] // gn
    exchanges = (gn * tn).bit_length() - 1
    outs = (
        shape((2, size // 2, model), BF16),
        shape((2, size // 2, model), BF16),
        shape((layers, 16, model), F32),
        shape((layers, tn, shard, 3 * width), BF16),
        shape((layers, tn, shard, units), BF16),
        shape((layers, prows, model), BF16),
        shape((layers, orows, model), BF16),
    )
    scratch = [pltpu.VMEM(dims, BF16) for dims in shapes]
    scratch += [pltpu.VMEM(*item) for item in kept]
    scratch += [
        pltpu.VMEM((size, model), F32),
        pltpu.VMEM((size, model), F32),
        pltpu.VMEM((length, model), BF16),
        pltpu.VMEM((length, width), BF16),
        pltpu.VMEM((length, 3 * width), BF16),
        pltpu.VMEM((length, width), F32),
        pltpu.VMEM((length, width), F32),
        pltpu.VMEM((size, model), F32),
        pltpu.VMEM((1, 3 * width), F32),
        pltpu.VMEM((1, units), F32),
    ]
    scratch += group_buffers(chips, size, model)
    for dims in shapes:
        scratch += [pltpu.VMEM(dims, BF16)] * layers
    scratch += [pltpu.VMEM((layers, (gn - 1) * dims[0] // gn, dims[1]), BF16) for dims in shapes]
    scratch += [pltpu.VMEM((layers, exchanges, 16, model), F32)]
    for _ in range(layers):
        scratch += group_sems(chips, tn)
    slots = 8 * layers
    scratch += [
        dma((slots, gn)), dma((slots, gn)), dma((2, layers, tn)), dma((2, layers, tn)), dma((layers,)), dma((layers,)),
        dma((3, layers)),
        dma((14 * layers,)), dma((2, 2)), dma((2, 2)), dma((layers, exchanges)), dma((layers, exchanges)),
    ]

    def body(*refs):
        refs = list(refs)

        def take(count):
            out, refs[:] = refs[:count], refs[count:]
            return out

        ins = take(7)
        x_in = take(layers)
        w_in = [take(layers) for _ in range(4)]
        kept_in = [take(8) for _ in range(layers)]
        results = take(7)
        w, kept_s = take(4), take(8)
        work = take(10)
        bufs = take(4)
        accs = [take(layers) for _ in range(4)]
        boxes = take(4)
        flatbox = take(1)[0]
        group = [take(7) for _ in range(layers)]
        reduce_sems = take(7)
        descend_kernel(
            gn, tn, layers, size, *ins, x_in, w_in, kept_in, *results, w, kept_s, *work, bufs, accs, boxes,
            flatbox, group, reduce_sems, *take(5),
        )

    flat_ws = [ws[i][layer] for i in range(4) for layer in range(layers)]
    flat_kept = [ref for layer in range(layers) for ref in kepts[layer]]
    return pl.pallas_call(
        body,
        out_shape=outs,
        in_specs=[ANY, ANY] + [VM] * 5 + [ANY] * (layers + len(flat_ws) + len(flat_kept)),
        out_specs=(ANY, ANY, VM, ANY, ANY, ANY, ANY),
        scratch_shapes=scratch,
        compiler_params=params_of(3),
        name="descend",
    )(cot, output, segcol, segrow, vecs, *tables, *xs, *flat_ws, *flat_kept)


GROUPS = ("dp", "h")
EVERY = ("dp", "h", "t")


def to_group(tn, blocks):
    h, t = lax.axis_index("h"), lax.axis_index("t")
    count = 2 * tn
    parity = lax.rem(t, 2)
    got = []
    for j in range(2):
        moves = [(c, ((c + j) % 2) * tn + c // 2) for c in range(count)]
        piece = jnp.where(lax.rem(parity + j, 2) == 0, blocks[0], blocks[1])
        got.append(lax.ppermute(piece, ("h", "t"), moves))
    low = jnp.where(h == 0, got[0], got[1])
    high = jnp.where(h == 0, got[1], got[0])
    return jnp.concatenate([low, high], axis=0)


def from_group(tn, rows):
    h, t = lax.axis_index("h"), lax.axis_index("t")
    count = 2 * tn
    parity = lax.rem(t, 2)
    size = rows.shape[0] // 2
    got = []
    for j in range(2):
        moves = [(((c + j) % 2) * tn + c // 2, c) for c in range(count)]
        piece = jnp.where(lax.rem(h + j, 2) == 0, rows[:size], rows[size:])
        got.append(lax.ppermute(piece, ("h", "t"), moves))
    first = jnp.where(parity == 0, got[0], got[1])
    second = jnp.where(parity == 0, got[1], got[0])
    return jnp.stack([first, second], axis=0)


def proj_moves(gn, tn):
    return [(r, (r % gn) * tn + r // gn) for r in range(gn * tn)]


def slice_columns(weight, gn, tn):
    rows, cols = weight.shape
    return weight.reshape(rows, gn, tn, cols // (gn * tn)).transpose(2, 0, 1, 3).reshape(tn, rows, cols // tn)


def slice_triple(weight, tn):
    rows, cols = weight.shape
    return weight.reshape(rows, 3, tn, cols // (3 * tn)).transpose(2, 0, 1, 3).reshape(tn, rows, cols // tn)


def gather_weights(gn, tn, triple, proj, inner, outer):
    def spread(parts):
        moved = lax.all_to_all(parts, "t", 0, 0, tiled=True)
        whole = lax.all_gather(moved.reshape(-1, moved.shape[-1]), GROUPS, axis=0, tiled=True)
        return whole

    wt = spread(slice_triple(triple, tn))
    wi = spread(slice_columns(inner, gn, tn))
    wo = lax.all_gather(outer, GROUPS, axis=0, tiled=True)
    wp = lax.all_gather(lax.ppermute(proj, EVERY, proj_moves(gn, tn)), GROUPS, axis=0, tiled=True)
    return wt, wi, wo, wp


def reduce_weights(gn, tn, dwt, dwi, dwo, dwp):
    def back(parts):
        mine = lax.psum_scatter(parts, GROUPS, scatter_dimension=0, tiled=True)
        rows = mine.shape[0] // tn
        return lax.all_to_all(mine.reshape(tn, rows, -1), "t", 0, 0, tiled=True).astype(F32)

    triple = back(dwt)
    rows = triple.shape[1]
    triple = triple.reshape(tn, rows, 3, -1).transpose(1, 2, 0, 3).reshape(rows, -1)
    inner = back(dwi)
    inner = inner.reshape(tn, rows, gn, -1).transpose(1, 2, 0, 3).reshape(rows, -1)
    outer = lax.psum_scatter(dwo, GROUPS, scatter_dimension=0, tiled=True).astype(F32)
    proj = lax.psum_scatter(dwp, GROUPS, scatter_dimension=0, tiled=True)
    proj = lax.ppermute(proj, EVERY, [(b, a) for a, b in proj_moves(gn, tn)]).astype(F32)
    return triple, proj, inner, outer


def per_device(
    gn, tn,
    tokens, segments, cotangent, triple_weight, triple_bias, proj_weight, proj_bias, inner_weight, inner_bias,
    outer_weight, outer_bias, first_gain, first_shift, second_gain, second_shift,
):
    layers = triple_weight.shape[0]
    model = tokens.shape[2]
    span = tokens.shape[1] * 2 * tn
    h, t = lax.axis_index("h"), lax.axis_index("t")
    device = (lax.axis_index("dp") * 2 + h) * tn + t
    shards = gn * tn
    heads_wide = model // tn
    units = outer_weight.shape[1] * gn

    rows = triple_weight.shape[1]
    block = tokens.shape[1]
    tables = constant_tables(span, shards, model)
    direct = rows % 16 == 0 and block == 128 and layers * 4 <= 16 and units == model
    if direct:
        head = jnp.stack(
            [
                inner_bias,
                jnp.pad(triple_bias, ((0, 0), (0, 128 - triple_bias.shape[1]))),
                jnp.concatenate([proj_bias, outer_bias, first_gain, first_shift], axis=1),
                jnp.pad(jnp.concatenate([second_gain, second_shift], axis=1), ((0, 0), (0, 64))),
            ],
            axis=1,
        ).reshape(4 * layers, 128)
        opened = ascend_call(
            gn, tn, tokens, cotangent, jnp.pad(segments, ((0, 6), (0, 0))),
            jnp.pad(head, ((0, 16 - 4 * layers), (0, 0))),
            triple_weight.reshape(layers, rows, 3, tn, -1).transpose(0, 3, 1, 2, 4).reshape(layers, tn, rows, -1),
            inner_weight.reshape(layers, rows, gn, tn, -1).transpose(0, 3, 1, 2, 4).reshape(layers, tn, rows, -1),
            outer_weight, proj_weight, tables,
            placement(model // shards, shards) + placement(3 * model // shards, shards),
        )
        opened = list(opened)
        cot, output, segcol, segrow, vecs, _, _ = opened[:7]
        inputs = opened[7 : 7 + layers]
        weights = [tuple(opened[7 + layers + k * layers + layer] for k in range(4)) for layer in range(layers)]
        kept = [opened[7 + 5 * layers + 8 * i : 7 + 5 * layers + 8 * (i + 1)] for i in range(layers)]
        output, tokens_grad, summed, triple, inner, proj, outer = descend_call(
            gn, tn, cot, output, segcol, segrow, vecs, tables, inputs,
            [[weights[layer][k] for layer in range(layers)] for k in range(4)], kept,
        )
        summed = summed.reshape(layers, -1)
        triple = triple.reshape(layers, tn, rows, 3, -1).transpose(0, 2, 3, 1, 4).reshape(layers, rows, -1).astype(F32)
        inner = inner.reshape(layers, tn, rows, gn, -1).transpose(0, 2, 3, 1, 4).reshape(layers, rows, -1).astype(F32)
        proj, outer = proj.astype(F32), outer.astype(F32)
    else:
        small = (triple_bias, inner_bias, proj_bias, outer_bias, first_gain, first_shift, second_gain, second_shift)
        starts = [0]
        for item in small:
            starts.append(starts[-1] + item.shape[1])
        packed = jnp.concatenate(small, axis=1)
        x = to_group(tn, tokens).astype(F32)
        cot = to_group(tn, cotangent).astype(F32)
        segs_all = lax.all_gather(segments, ("h", "t"), axis=1, tiled=True)
        everything = lax.all_gather(packed[None], EVERY, axis=0, tiled=True).astype(F32)
        weights = [
            gather_weights(
                gn, tn, triple_weight[layer], proj_weight[layer], inner_weight[layer], outer_weight[layer]
            )
            for layer in range(layers)
        ]
        segs = jnp.where(h == 0, segs_all[0], segs_all[1])
        segs = jnp.where(segs == 0, -1 - jnp.arange(span, dtype=jnp.int32), segs).astype(F32)
        tables = (segs[:, None], segs[None, :]) + tables

        def vector(layer, i):
            return everything[:, layer, starts[i] : starts[i + 1]].reshape(-1)

        vecs, inputs, kept = [], [], []
        for layer in range(layers):
            bt = lax.dynamic_index_in_dim(vector(layer, 0).reshape(3, tn, heads_wide), t, 1, keepdims=False)
            bi = lax.dynamic_index_in_dim(vector(layer, 1).reshape(gn, tn, -1), t, 1, keepdims=False)
            zero = jnp.zeros((model,), F32)
            vecs.append(
                jnp.stack(
                    [vector(layer, 4), vector(layer, 5), vector(layer, 6), vector(layer, 7)]
                    + [vector(layer, 2) + vector(layer, 3), zero, zero, zero]
                )
            )
            inputs.append(x)
            x, *saved = forward_layer(
                tn, x, weights[layer], vecs[layer], bt.reshape(1, -1), bi.reshape(1, -1), tables
            )
            kept.append(saved)
        output = x.astype(BF16)
        grad = cot
        mats, flats = [None] * layers, [None] * layers
        for layer in reversed(range(layers)):
            grad, dwt, dwi, dwo, dwp, dvec, dbt, dbi = backward_layer(
                tn, grad, inputs[layer], weights[layer], vecs[layer], tables, kept[layer]
            )
            mats[layer] = reduce_weights(gn, tn, dwt, dwi, dwo, dwp)
            part = lax.dynamic_update_slice(
                jnp.zeros((3, tn, heads_wide), F32), dbt.reshape(3, 1, heads_wide), (0, t, 0)
            )
            side = lax.dynamic_update_slice(
                jnp.zeros((gn, tn, units // gn), F32), dbi.reshape(gn, 1, units // gn), (0, t, 0)
            )
            flats[layer] = jnp.concatenate([dvec[:5].reshape(-1), part.reshape(-1), side.reshape(-1)])
        output, tokens_grad = from_group(tn, output), from_group(tn, grad.astype(BF16))
        triple, proj, inner, outer = (jnp.stack([m[k] for m in mats]) for k in range(4))
        summed = lax.psum(jnp.stack(flats), EVERY)

    def own(start, length):
        piece = length // shards
        return lax.dynamic_slice_in_dim(summed, start + device * piece, piece, 1)

    base = 5 * model
    bias_sum = own(4 * model, model)
    return (
        output,
        tokens_grad,
        triple,
        own(base, 2 * model),
        own(base + 2 * model, model),
        proj,
        bias_sum,
        inner,
        own(base + 3 * model, units * tn),
        outer,
        bias_sum,
        own(0, model),
        own(model, model),
        own(2 * model, model),
        own(3 * model, model),
    )


def solution(mesh):
    dp, ctx = mesh.shape["dp"], mesh.shape["ctx"]
    tn = ctx // 2
    gn = 2 * dp
    fine = Mesh(mesh.devices.reshape(dp, 2, tn), EVERY)
    seq = P("dp", ("h", "t"), None)
    mat = P(None, EVERY, None)
    row = P(None, EVERY)
    in_specs = (seq, P("dp", ("h", "t")), seq, mat, row, mat, row, mat, row, mat, row, row, row, row, row)
    out_specs = (seq, seq, mat, row, row, mat, row, mat, row, mat, row, row, row, row, row)
    return jax.shard_map(
        functools.partial(per_device, gn, tn), mesh=fine, in_specs=in_specs, out_specs=out_specs, check_vma=False
    )
```

```python
import functools
import math

import jax
import jax.numpy as jnp
import numpy as np
from jax import lax
from jax.experimental import pallas as pl
from jax.experimental.pallas import tpu as pltpu
from jax.sharding import Mesh
from jax.sharding import PartitionSpec as P

HD = 64
ROT = 16
EPSILON = 1e-05
NEG_LARGE = -1e30
MESH = pl.DeviceIdType.MESH
BF16 = jnp.bfloat16
F32 = jnp.float32
VMEM_LIMIT = 60 * 1024 * 1024


def dot(a, b, dims):
    return lax.dot_general(a, b, (dims, ((), ())), preferred_element_type=F32)


NN = ((1,), (0,))
NT = ((1,), (1,))
TN = ((0,), (0,))


def rows_of(b, size):
    return pl.ds(pl.multiple_of(b * size, size), size)


def group_barrier(tn):
    t = lax.axis_index("t")
    zc, co = t // 2, lax.rem(t, 2)
    chips = tn // 2
    sem = pltpu.get_barrier_semaphore()
    peers = [zc * 2 + 1 - co] + [lax.rem(zc + k, chips) * 2 + co for k in range(1, chips)]
    for p in peers:
        pl.semaphore_signal(sem, inc=1, device_id={"t": p}, device_id_type=MESH)
    pl.semaphore_wait(sem, len(peers))


class Spread:
    def __init__(self, tn, buf, size, ssem, fsem, rsem):
        self.tn, self.buf, self.size = tn, buf, size
        self.ssem, self.fsem, self.rsem = ssem, fsem, rsem
        self.t = lax.axis_index("t")
        self.zc, self.co = self.t // 2, lax.rem(self.t, 2)
        self.chips = tn // 2

    def copy(self, block, send, to):
        ref = self.buf.at[rows_of(block, self.size)]
        return pltpu.make_async_remote_copy(
            ref, ref, send, self.rsem.at[block], device_id={"t": to}, device_id_type=MESH
        )

    def start(self):
        for k in range(1, self.chips):
            chip = lax.rem(self.zc + k, self.chips)
            self.copy(self.t, self.ssem.at[k], chip * 2 + self.co).start()
        self.copy(self.t, self.ssem.at[0], self.zc * 2 + 1 - self.co).start()

    def peer_core(self):
        b = self.zc * 2 + 1 - self.co
        self.copy(b, self.ssem.at[0], b).wait_recv()
        return b

    def same_core(self, k):
        b = lax.rem(self.zc + self.chips - k, self.chips) * 2 + self.co
        self.copy(b, self.fsem.at[k], b).wait_recv()
        self.copy(b, self.fsem.at[k], self.zc * 2 + 1 - self.co).start()
        return b

    def other_core(self, k):
        b = lax.rem(self.zc + self.chips - k, self.chips) * 2 + 1 - self.co
        self.copy(b, self.fsem.at[k], b).wait_recv()
        return b

    def finish(self):
        for k in range(self.chips):
            self.copy(self.t, self.ssem.at[k], self.t).wait_send()
        for k in range(1, self.chips):
            self.copy(self.t, self.fsem.at[k], self.t).wait_send()


class Gather:
    def __init__(self, tn, tocore, fromcore, toici, fromici, sems):
        self.tn = tn
        self.tocore, self.fromcore, self.toici, self.fromici = tocore, fromcore, toici, fromici
        self.cs, self.cr, self.ls, self.lr = sems
        self.t = lax.axis_index("t")
        self.zc, self.co = self.t // 2, lax.rem(self.t, 2)
        self.chips = tn // 2

    def core_copy(self, chip):
        return pltpu.make_async_remote_copy(
            self.tocore.at[chip],
            self.fromcore.at[chip],
            self.cs.at[chip],
            self.cr.at[chip],
            device_id={"t": self.zc * 2 + 1 - self.co},
            device_id_type=MESH,
        )

    def link_copy(self, chip, slot):
        return pltpu.make_async_remote_copy(
            self.toici.at[chip],
            self.fromici.at[slot],
            self.ls.at[chip],
            self.lr.at[slot],
            device_id={"t": chip * 2 + self.co},
            device_id_type=MESH,
        )

    def send_core(self, chip):
        self.core_copy(chip).start()

    def send_link(self, chip):
        self.core_copy(chip).wait_recv()
        self.toici[chip] = (self.toici[chip].astype(F32) + self.fromcore[chip].astype(F32)).astype(BF16)
        self.link_copy(chip, self.zc).start()

    def total(self):
        self.core_copy(self.zc).wait_recv()
        value = self.fromcore[self.zc].astype(F32)
        for k in range(1, self.chips):
            chip = lax.rem(self.zc + k, self.chips)
            self.link_copy(chip, chip).wait_recv()
            value = value + self.fromici[chip].astype(F32)
        return value

    def finish(self):
        for chip in range(self.chips):
            self.core_copy(chip).wait_send()
        for k in range(1, self.chips):
            chip = lax.rem(self.zc + k, self.chips)
            self.link_copy(chip, self.zc).wait_send()


def norm_stats(x):
    mean = jnp.mean(x, axis=-1, keepdims=True)
    centred = x - mean
    inverse = lax.rsqrt(jnp.mean(centred * centred, axis=-1, keepdims=True) + EPSILON)
    return centred * inverse, inverse


def widen(tab, width):
    return jnp.concatenate([tab] * (width // tab.shape[1]), axis=1)


def turn(x, cos, sine, sign):
    width = x.shape[1]
    cos, sine = widen(cos, width), widen(sine, width)
    front = lax.rem(lax.broadcasted_iota(jnp.int32, (1, width), 1), HD) < ROT // 2
    partner = jnp.where(front, pltpu.roll(x, width - ROT // 2, 1), pltpu.roll(x, ROT // 2, 1))
    return x * cos + sign * (partner * sine)


def head_masks(width, dtype):
    lane = lax.broadcasted_iota(jnp.int32, (1, width), 1) // HD
    return [(lane == h).astype(F32).astype(dtype) for h in range(width // HD)]


def pair_bias(qb, kb, size, segcol, segrow):
    qpos = lax.broadcasted_iota(jnp.int32, (size, size), 0) + qb * size
    kpos = lax.broadcasted_iota(jnp.int32, (size, size), 1) + kb * size
    same = segcol[rows_of(qb, size), :] == segrow[:, rows_of(kb, size)]
    return jnp.where(same & (kpos <= qpos), 0.0, NEG_LARGE)


TILE = 256
SKEW = 1


class Forward:
    def __init__(self, tn, size, x, w, vecs, segs, tables, kept, keep):
        self.tn, self.size, self.chips = tn, size, tn // 2
        self.x, self.keep = x, keep
        self.wt, self.wi, self.wo, self.wp = w
        self.vec, self.bt, self.bi = vecs
        self.segcol, self.segrow = segs
        self.tables = tables
        self.n, self.q, self.k, self.v, self.o, self.lse, self.g, self.gp = kept
        self.width, self.units = self.q.shape[1], self.g.shape[1]
        self.heads = self.width // HD

    def norm(self, t):
        own, _ = norm_stats(self.x[...])
        self.n[rows_of(t, self.size), :] = own.astype(BF16)

    def heads_in(self, b):
        width, vec, bt = self.width, self.vec, self.bt
        rows = rows_of(b, self.size)
        h1 = (self.n[rows, :].astype(F32) * vec[0:1, :] + vec[1:2, :]).astype(BF16)
        cos, sine = (tab[rows, :] for tab in self.tables)
        q = dot(h1, self.wt[:, 0:width], NN) + bt[:, 0:width]
        low = turn(q, cos, sine, 1.0).astype(BF16).astype(F32)
        self.q[rows, :] = (low * (1.0 / math.sqrt(HD))).astype(BF16)
        k = dot(h1, self.wt[:, width : 2 * width], NN) + bt[:, width : 2 * width]
        self.k[rows, :] = turn(k, cos, sine, 1.0).astype(BF16)
        v = dot(h1, self.wt[:, 2 * width : 3 * width], NN) + bt[:, 2 * width : 3 * width]
        self.v[rows, :] = v.astype(BF16)

    def mixer_in(self, b):
        rows = rows_of(b, self.size)
        h2 = (self.n[rows, :].astype(F32) * self.vec[2:3, :] + self.vec[3:4, :]).astype(BF16)

        def mix(j, carry):
            cols = rows_of(j, TILE)
            u = dot(h2, self.wi[:, cols], NN) + self.bi[:, cols]
            half = 0.5 + 0.5 * lax.erf(u * (1.0 / math.sqrt(2.0)))
            self.g[rows, cols] = (u * half).astype(BF16)
            bell = jnp.exp(-0.5 * u * u) * (1.0 / math.sqrt(2.0 * math.pi))
            self.gp[rows, cols] = (half + u * bell).astype(BF16)
            return carry

        lax.fori_loop(0, self.units // TILE, mix, 0)

    def attend(self, b):
        size, width, heads = self.size, self.width, self.heads
        masks = head_masks(width, F32)
        lane = lax.broadcasted_iota(jnp.int32, (1, 128), 1)
        rows = rows_of(b, size)
        qb = self.q[rows, :]
        qs = [qb * masks[h].astype(BF16) for h in range(heads)]

        def step(i, carry):
            peaks, sums, acc = carry
            kb = b - i
            keys = self.k[rows_of(kb, size), :]
            vals = self.v[rows_of(kb, size), :]
            bias = pair_bias(b, kb, size, self.segcol, self.segrow)
            new_peaks, new_sums = [], []
            scale = jnp.zeros((size, width), F32)
            add = jnp.zeros((size, width), F32)
            for h in range(heads):
                s = dot(qs[h], keys, NT) + bias
                peak = jnp.maximum(peaks[h], jnp.max(s, axis=1, keepdims=True))
                p = jnp.exp(s - peak)
                fade = jnp.exp(peaks[h] - peak)
                new_peaks.append(peak)
                new_sums.append(sums[h] * fade + jnp.sum(p, axis=1, keepdims=True))
                scale = scale + fade * masks[h]
                add = add + dot(p.astype(BF16), vals * masks[h].astype(BF16), NN)
            return tuple(new_peaks), tuple(new_sums), acc * scale + add

        start = (
            tuple(jnp.full((size, 1), NEG_LARGE, F32) for _ in range(heads)),
            tuple(jnp.zeros((size, 1), F32) for _ in range(heads)),
            jnp.zeros((size, width), F32),
        )
        peaks, sums, acc = lax.fori_loop(0, b + 1, step, start)
        scale = jnp.zeros((size, width), F32)
        lse = jnp.zeros((size, 128), F32)
        for h in range(heads):
            scale = scale + (1.0 / sums[h]) * masks[h]
            lse = jnp.where(lane == h, peaks[h] + jnp.log(sums[h]), lse)
        self.lse[rows, :] = lse
        self.o[rows, :] = acc * scale

    def branches(self, b, store):
        rows = rows_of(b, self.size)

        def part(j, carry):
            cols = rows_of(j, TILE)
            value = dot(self.g[rows, :], self.wo[:, cols], NN)
            store(cols, value + dot(self.o[rows, :].astype(BF16), self.wp[:, cols], NN))
            return carry

        lax.fori_loop(0, self.x.shape[1] // TILE, part, 0)

    def into(self, ref, chip):
        def store(cols, value):
            ref[chip, :, cols] = value.astype(BF16)

        return store

    def into_keep(self, cols, value):
        self.keep[:, cols] = value


def arrivals(spread):
    yield spread.t
    yield spread.peer_core()
    for i in range(1, spread.chips):
        yield spread.same_core(i)
        yield spread.other_core(i)


def far_first(spread):
    out = []
    for i in range(1, spread.chips):
        chip = lax.rem(spread.zc + i, spread.chips)
        out += [chip * 2 + 1 - spread.co, chip * 2 + spread.co]
    return out + [spread.zc * 2 + 1 - spread.co, spread.t]


def branch_sums(layer, spread, gather, tick=lambda: None):
    for i in range(1, spread.chips):
        chip = lax.rem(spread.zc + i, spread.chips)
        layer.branches(chip * 2 + 1 - spread.co, layer.into(gather.tocore, chip))
        gather.send_core(chip)
        layer.branches(chip * 2 + spread.co, layer.into(gather.toici, chip))
        gather.send_link(chip)
        tick()
    layer.branches(spread.zc * 2 + 1 - spread.co, layer.into(gather.tocore, spread.zc))
    gather.send_core(spread.zc)
    layer.branches(spread.t, layer.into_keep)
    tick()


def forward_kernel(
    tn, size,
    x_ref, wt, wi, wo, wp, vec, bt, bi, segcol, segrow, ctab, stab,
    xo_ref, n_ref, q_ref, k_ref, v_ref, o_ref, lse_ref, g_ref, gp_ref,
    keep, tocore, fromcore, toici, fromici, ssem, fsem, rsem, cs, cr, ls, lr,
):
    group_barrier(tn)
    spread = Spread(tn, n_ref, size, ssem, fsem, rsem)
    gather = Gather(tn, tocore, fromcore, toici, fromici, (cs, cr, ls, lr))
    layer = Forward(
        tn, size, x_ref, (wt, wi, wo, wp), (vec, bt, bi), (segcol, segrow), (ctab, stab),
        (n_ref, q_ref, k_ref, v_ref, o_ref, lse_ref, g_ref, gp_ref), keep,
    )
    layer.norm(spread.t)
    spread.start()
    for b in arrivals(spread):
        layer.heads_in(b)
        layer.mixer_in(b)
    for b in far_first(spread):
        layer.attend(b)
    branch_sums(layer, spread, gather)
    xo_ref[...] = x_ref[...] + vec[4:5, :] + keep[...] + gather.total()
    spread.finish()
    gather.finish()


def backward_kernel(
    tn, size,
    dy_ref, x_ref, wt, wi, wo, wp, vec, segcol, segrow, ctab, stab,
    n_ref, q_ref, k_ref, v_ref, o_ref, lse_ref, g_ref, gp_ref,
    dx_ref, dwt, dwi, dwo, dwp, dvec, dbt, dbi,
    gb, do, du, dt, dq, dk, dv, dh2, keep,
    tocore, fromcore, toici, fromici, ssem, fsem, rsem, cs, cr, ls, lr,
):
    chips = tn // 2
    width = q_ref.shape[1]
    heads = width // HD
    units = g_ref.shape[1]
    model = x_ref.shape[1]
    group_barrier(tn)
    spread = Spread(tn, gb, size, ssem, fsem, rsem)
    gather = Gather(tn, tocore, fromcore, toici, fromici, (cs, cr, ls, lr))
    t, zc, co = spread.t, spread.zc, spread.co
    own = dy_ref[...].astype(F32).astype(BF16)
    gb[rows_of(t, size), :] = own
    spread.start()
    dvec[...] = jnp.zeros_like(dvec)
    dbt[...] = jnp.zeros_like(dbt)
    dbi[...] = jnp.zeros_like(dbi)
    dvec[4:5, :] = jnp.sum(own.astype(F32), axis=0, keepdims=True)
    dq[...] = jnp.zeros_like(dq)
    dk[...] = jnp.zeros_like(dk)
    dv[...] = jnp.zeros_like(dv)

    def mixer(b):
        rows = rows_of(b, size)
        grad = gb[rows, :]
        do[rows, :] = dot(grad, wp[...], NT).astype(BF16)

        def unit(j, carry):
            cols = rows_of(j, TILE)
            d = (dot(grad, wo[cols, :], NT) * gp_ref[rows, cols].astype(F32)).astype(BF16)
            du[rows, cols] = d
            dbi[0:1, cols] += jnp.sum(d.astype(F32), axis=0, keepdims=True)
            return carry

        lax.fori_loop(0, units // TILE, unit, 0)

        def back(j, carry):
            cols = rows_of(j, TILE)
            d = dot(du[rows, :], wi[cols, :], NT)
            dvec[2:3, cols] += jnp.sum(d * n_ref[rows, cols].astype(F32), axis=0, keepdims=True)
            dvec[3:4, cols] += jnp.sum(d, axis=0, keepdims=True)
            dh2[rows, cols] = d * vec[2:3, cols]
            return carry

        lax.fori_loop(0, model // TILE, back, 0)

    mixer(t)
    mixer(spread.peer_core())
    for i in range(1, chips):
        mixer(spread.same_core(i))
        mixer(spread.other_core(i))

    masks = head_masks(width, BF16)
    lane = lax.broadcasted_iota(jnp.int32, (1, 128), 1)
    up = zc >= (chips + 1) // 2
    tsize = tn

    def pair(qb, kb):
        qrows, krows = rows_of(qb, size), rows_of(kb, size)
        q, keys, vals = q_ref[qrows, :], k_ref[krows, :], v_ref[krows, :]
        grad = do[qrows, :]
        prod = grad.astype(F32) * o_ref[qrows, :]
        lse = lse_ref[qrows, :]
        bias = pair_bias(qb, kb, size, segcol, segrow)
        dq_new = jnp.zeros((size, width), F32)
        dk_new = jnp.zeros((size, width), F32)
        dv_new = jnp.zeros((size, width), F32)
        for h in range(heads):
            qh, gh = q * masks[h], grad * masks[h]
            total = jnp.sum(jnp.where(lane == h, lse, 0.0), axis=1, keepdims=True)
            delta = jnp.sum(prod * masks[h].astype(F32), axis=1, keepdims=True)
            p = jnp.exp(dot(qh, keys, NT) + bias - total)
            ds = (p * (dot(gh, vals, NT) - delta)).astype(BF16)
            dv_new = dv_new + dot(p.astype(BF16), gh, TN)
            dk_new = dk_new + dot(ds, qh, TN)
            dq_new = dq_new + dot(ds, keys * masks[h], NN)
        dq[qrows, :] += dq_new
        dk[krows, :] += dk_new
        dv[krows, :] += dv_new

    def attend_back(stage):
        pivot = jnp.where(up, stage, tsize - 1 - stage)

        def step(j, carry):
            pair(jnp.where(up, pivot + j, pivot), jnp.where(up, pivot, pivot - j))
            return carry

        lax.fori_loop(0, tsize - stage, step, 0)
        rows = rows_of(pivot, size)
        cos, sine = ctab[rows, :], stab[rows, :]
        dt[rows, 0:width] = turn(dq[rows, :] * (1.0 / math.sqrt(HD)), cos, sine, -1.0).astype(BF16)
        dt[rows, width : 2 * width] = turn(dk[rows, :], cos, sine, -1.0).astype(BF16)
        dt[rows, 2 * width : 3 * width] = dv[rows, :].astype(BF16)
        block = dt[rows, :]
        dbt[...] += jnp.sum(block.astype(F32), axis=0, keepdims=True)

        def back(j, carry):
            cols = rows_of(j, TILE)
            d = dot(block, wt[cols, :], NT)
            dvec[0:1, cols] += jnp.sum(d * n_ref[rows, cols].astype(F32), axis=0, keepdims=True)
            dvec[1:2, cols] += jnp.sum(d, axis=0, keepdims=True)
            dh2[rows, cols] = dh2[rows, cols] + d * vec[0:1, cols]
            return carry

        lax.fori_loop(0, model // TILE, back, 0)
        value = dh2[rows, :]
        chip, core = pivot // 2, lax.rem(pivot, 2)

        @pl.when(core != co)
        def _():
            tocore[chip] = value.astype(BF16)
            gather.send_core(chip)

        @pl.when((core == co) & (chip != zc))
        def _():
            toici[chip] = value.astype(BF16)

        @pl.when(pivot == t)
        def _():
            keep[...] = value

        if stage % 2 == 1:

            @pl.when(chip != zc)
            def _():
                gather.send_link(chip)

    for stage in range(tn):
        attend_back(stage)

    def grad_one(j, carry):
        cols = rows_of(j, TILE)
        h1 = (n_ref[:, cols].astype(F32) * vec[0:1, cols] + vec[1:2, cols]).astype(BF16)
        dwt[cols, :] = dot(h1, dt[...], TN).astype(dwt.dtype)
        return carry

    lax.fori_loop(0, model // TILE, grad_one, 0)

    def grad_two(j, carry):
        cols = rows_of(j, TILE)
        h2 = (n_ref[:, cols].astype(F32) * vec[2:3, cols] + vec[3:4, cols]).astype(BF16)
        dwi[cols, :] = dot(h2, du[...], TN).astype(dwi.dtype)
        return carry

    lax.fori_loop(0, model // TILE, grad_two, 0)

    def grad_three(j, carry):
        cols = rows_of(j, TILE)
        dwo[cols, :] = dot(g_ref[:, cols], gb[...], TN).astype(dwo.dtype)
        return carry

    lax.fori_loop(0, units // TILE, grad_three, 0)
    small = min(TILE, width)

    def grad_four(j, carry):
        cols = rows_of(j, small)
        dwp[cols, :] = dot(o_ref[:, cols].astype(BF16), gb[...], TN).astype(dwp.dtype)
        return carry

    lax.fori_loop(0, width // small, grad_four, 0)

    own_n, inverse = norm_stats(x_ref[...])
    e = keep[...] + gather.total()
    inner = e - jnp.mean(e, axis=-1, keepdims=True) - own_n * jnp.mean(e * own_n, axis=-1, keepdims=True)
    dx_ref[...] = dy_ref[...].astype(F32) + inner * inverse
    spread.finish()
    gather.finish()


VM = pl.BlockSpec(memory_space=pltpu.VMEM)


def shape(dims, dtype):
    return jax.ShapeDtypeStruct(tuple(dims), dtype)


def group_sems(chips, tn):
    dma = pltpu.SemaphoreType.DMA
    return [dma((chips,)), dma((chips,)), dma((tn,)), dma((chips,)), dma((chips,)), dma((chips,)), dma((chips,))]


def group_buffers(chips, size, model):
    return [pltpu.VMEM((chips, size, model), BF16) for _ in range(4)]


def params_of(cid):
    return pltpu.CompilerParams(collective_id=cid, has_side_effects=True, vmem_limit_bytes=VMEM_LIMIT)


def forward_layer(tn, x, weights, vec, bt, bi, tables):
    wt, wi, wo, wp = weights
    size, model = x.shape
    length = size * tn
    width, units, chips = wp.shape[0], wo.shape[0], tn // 2
    outs = (
        shape((size, model), F32),
        shape((length, model), BF16),
        shape((length, width), BF16),
        shape((length, width), BF16),
        shape((length, width), BF16),
        shape((length, width), F32),
        shape((length, 128), F32),
        shape((length, units), BF16),
        shape((length, units), BF16),
    )
    return pl.pallas_call(
        functools.partial(forward_kernel, tn, size),
        out_shape=outs,
        in_specs=[VM] * 12,
        out_specs=[VM] * len(outs),
        scratch_shapes=[pltpu.VMEM((size, model), F32)] + group_buffers(chips, size, model) + group_sems(chips, tn),
        compiler_params=params_of(0),
        name="forward",
    )(x, wt, wi, wo, wp, vec, bt, bi, *tables)


def backward_layer(tn, dy, x, weights, vec, tables, kept):
    wt, wi, wo, wp = weights
    size, model = x.shape
    length = size * tn
    width, units, chips = wp.shape[0], wo.shape[0], tn // 2
    outs = (
        shape((size, model), F32),
        shape(wt.shape, BF16),
        shape(wi.shape, BF16),
        shape(wo.shape, BF16),
        shape(wp.shape, BF16),
        shape((8, model), F32),
        shape((1, 3 * width), F32),
        shape((1, units), F32),
    )
    return pl.pallas_call(
        functools.partial(backward_kernel, tn, size),
        out_shape=outs,
        in_specs=[VM] * 19,
        out_specs=[VM] * len(outs),
        scratch_shapes=[
            pltpu.VMEM((length, model), BF16),
            pltpu.VMEM((length, width), BF16),
            pltpu.VMEM((length, units), BF16),
            pltpu.VMEM((length, 3 * width), BF16),
            pltpu.VMEM((length, width), F32),
            pltpu.VMEM((length, width), F32),
            pltpu.VMEM((length, width), F32),
            pltpu.VMEM((length, model), F32),
            pltpu.VMEM((size, model), F32),
        ]
        + group_buffers(chips, size, model)
        + group_sems(chips, tn),
        compiler_params=params_of(1),
        name="backward",
    )(dy, x, wt, wi, wo, wp, vec, *tables, *kept)


class Place:
    def __init__(self, gn, tn):
        self.gn, self.tn = gn, tn
        self.h, self.t = lax.axis_index("h"), lax.axis_index("t")
        self.g = lax.axis_index("dp") * 2 + self.h
        self.c = self.h * tn + self.t
        self.bits = [1 << i for i in range(gn.bit_length() - 1)]

    def group(self, g):
        return {"dp": g // 2, "h": lax.rem(g, 2)}

    def line(self, c):
        return {"h": c // self.tn, "t": lax.rem(c, self.tn)}

    def other(self, k):
        return lax.rem(self.t + k, self.tn)


def flip(value, bit):
    return value + bit * (1 - 2 * lax.rem(value // bit, 2))


def remote(src, dst, send, recv, device):
    return pltpu.make_async_remote_copy(src, dst, send, recv, device_id=device, device_id_type=MESH)


def runs_by_step(place, bits):
    runs, steps = [(place.g, 1)], []
    for bit in bits:
        steps.append((bit, runs))
        if len(runs) == 1 and runs[0][1] == bit:
            runs = [(runs[0][0] // (2 * bit) * (2 * bit), 2 * bit)]
        else:
            runs = runs + [(flip(start, bit), count) for start, count in runs]
    return steps


def bit_orders(place):
    bits = place.bits
    return [bits, bits[:1] + bits[:0:-1]]


class Doubling:
    def __init__(self, place, ref, block, cols, order, sems, slot):
        self.place, self.ref, self.block, self.cols, self.order = place, ref, block, cols, order
        self.send, self.recv, self.slot = sems[0], sems[1], slot
        self.levels = [[] for _ in order]
        for i, bit in enumerate(order):
            for bits in range(1 << i):
                held = [order[j] for j in range(i) if bits >> j & 1]
                self.levels[len(held)].append((bit, held))

    def at(self, held):
        g = self.place.g
        for bit in held:
            g = flip(g, bit)
        return g

    def copy(self, bit, held):
        start = self.at(held)
        rows = pl.ds(pl.multiple_of(start * self.block, self.block), self.block)
        ref = self.ref.at[rows, self.cols]
        index = sum(held) + bit
        return remote(
            ref,
            ref,
            self.send.at[self.slot, index],
            self.recv.at[self.slot, index],
            self.place.group(flip(self.place.g, bit)),
        )

    def arrive(self, held):
        start = self.at(held)
        rows = pl.ds(pl.multiple_of(start * self.block, self.block), self.block)
        ref = self.ref.at[rows, self.cols]
        index = sum(held)
        peer = self.place.group(flip(self.place.g, held[-1]))
        remote(ref, ref, self.send.at[self.slot, index], self.recv.at[self.slot, index], peer).wait_recv()

    def advance(self, level):
        seen = set()
        for bit, held in self.levels[level]:
            if held and tuple(held) not in seen:
                seen.add(tuple(held))
                self.arrive(held)
            self.copy(bit, held).start()

    def whole(self):
        last = self.order[-1]
        for level in self.levels:
            for bit, held in level:
                if bit == last:
                    self.arrive(held + [bit])

    def finish(self):
        for level in self.levels:
            for item in level:
                self.copy(*item).wait_send()


def halves(cols):
    return [pl.ds(0, cols // 2), pl.ds(cols // 2, cols // 2)]


def line_barrier(place, extra):
    sem = pltpu.get_barrier_semaphore()
    span = 2 * place.tn
    for k in range(1, span):
        pl.semaphore_signal(sem, inc=1, device_id=place.line(lax.rem(place.c + k, span)), device_id_type=MESH)
    for bit in place.bits[1:]:
        pl.semaphore_signal(sem, inc=1, device_id=place.group(flip(place.g, bit)), device_id_type=MESH)
    peers = span - 1 + len(place.bits) - 1
    source, moved = extra

    @pl.when(moved)
    def _():
        pl.semaphore_signal(sem, inc=1, device_id=source, device_id_type=MESH)
        pl.semaphore_wait(sem, peers + 1)

    @pl.when(jnp.logical_not(moved))
    def _():
        pl.semaphore_wait(sem, peers)


def proj_places(place):
    gn, tn = place.gn, place.tn
    r = place.g * tn + place.t
    target = place.group(lax.rem(r, gn)) | {"t": r // gn}
    q = place.t * gn + place.g
    source = place.group(q // tn) | {"t": lax.rem(q, tn)}
    return target, source, r, q


def slot_rows(index, size):
    return pl.ds(pl.multiple_of(index * size, size), size)


class Opening:
    def __init__(self, place, layers, tok, cot, seg, vec, tri, inn, outer, proj, tok_o, cot_o, seg_o, vec_o, w, sems):
        self.place, self.layers = place, layers
        self.tok, self.cot, self.seg, self.vec = tok, cot, seg, vec
        self.tri, self.inn, self.outer, self.proj = tri, inn, outer, proj
        self.tok_o, self.cot_o, self.seg_o, self.vec_o = tok_o, cot_o, seg_o, vec_o
        self.wts, self.wis, self.wos, self.wps = w
        (
            self.ssem, self.rsem, self.lsem, self.asend, self.arecv, self.psend, self.precv,
            self.msend, self.mrecv, self.gsend, self.grecv,
        ) = sems
        self.half = tok.shape[1]
        self.target, self.source, self.r, self.q = proj_places(place)
        self.moved = self.q != self.r
        self.local, self.sends, self.shared_with = [], [], {}
        self.locals_of = {}

    def barrier(self):
        line_barrier(self.place, (self.source, self.moved))

    def near(self, src, dst, key):
        cp = pltpu.make_async_copy(src, dst, self.lsem.at[len(self.local)])
        cp.start()
        self.local.append(cp)
        self.locals_of[key] = cp

    def hop(self, src, dst, slot, i):
        c, tn = self.place.c, self.place.tn
        to = i * tn + c // 2
        rows = slot_rows(lax.rem(c, 2), self.half)
        near = pltpu.make_async_copy(src.at[i], dst.at[rows], self.msend.at[slot, i])
        far = remote(
            src.at[i], dst.at[rows], self.msend.at[slot, i], self.mrecv.at[slot, lax.rem(c, 2)],
            self.place.line(to),
        )
        return to == c, near, far

    def move(self, src, dst, slot):
        for i in range(2):
            stays, near, far = self.hop(src, dst, slot, i)
            pl.when(stays)(near.start)
            pl.when(jnp.logical_not(stays))(far.start)

    def moved_in(self, src, dst, slot):
        for i in range(2):
            stays, near, far = self.hop(src, dst, slot, i)
            pl.when(stays)(near.wait)
            pl.when(jnp.logical_not(stays))(far.wait_send)
        for s in range(2):
            cp = remote(
                src.at[0], dst.at[pl.ds(s * self.half, self.half)], self.msend.at[slot, 0],
                self.mrecv.at[slot, s], self.place.line(self.place.c),
            )
            pl.when(2 * self.place.t + s != self.place.c)(cp.wait_recv)

    def share(self, key, src_of, dst, size, slot):
        g, t, tn = self.place.g, self.place.t, self.place.tn
        rows = slot_rows(g * tn + t, size)
        self.near(src_of(t), dst.at[rows], key)
        for k in range(1, tn):
            to = self.place.other(k)
            cp = remote(src_of(to), dst.at[rows], self.asend.at[slot, k], self.arecv.at[slot, t], {"t": to})
            cp.start()
            self.sends.append(cp)
        self.shared_with[key] = (dst, size, slot)

    def shared(self, key):
        dst, size, slot = self.shared_with[key]
        self.locals_of[key].wait()
        for k in range(1, self.place.tn):
            frm = self.place.other(k)
            ref = dst.at[slot_rows(self.place.g * self.place.tn + frm, size)]
            remote(ref, ref, self.asend.at[slot, k], self.arecv.at[slot, frm], {"t": frm}).wait_recv()

    def share_layer(self, layer):
        depth = self.tri.shape[2]
        base = 1 + 2 * layer
        self.share(("t", layer), lambda to: self.tri.at[layer, to], self.wts[layer], depth, base)
        self.share(("i", layer), lambda to: self.inn.at[layer, to], self.wis[layer], depth, base + 1)
        g = self.place.g
        self.near(self.outer.at[layer], self.wos[layer].at[slot_rows(g, self.outer.shape[1])], ("o", layer))
        here, far = self.proj_copies(layer)
        pl.when(self.moved)(far.start)
        pl.when(jnp.logical_not(self.moved))(here.start)

    def proj_copies(self, layer):
        prows = self.proj.shape[1]
        src = self.proj.at[layer]
        here = pltpu.make_async_copy(src, self.wps[layer].at[slot_rows(self.place.g, prows)], self.psend.at[layer])
        dst = self.wps[layer].at[slot_rows(lax.rem(self.r, self.place.gn), prows)]
        return here, remote(src, dst, self.psend.at[layer], self.precv.at[layer], self.target)

    def proj_ready(self, layer):
        here, far = self.proj_copies(layer)

        @pl.when(self.moved)
        def _():
            far.wait_recv()
            far.wait_send()

        pl.when(jnp.logical_not(self.moved))(here.wait)

    def start(self):
        place, span = self.place, 2 * self.place.tn
        self.move(self.tok, self.tok_o, 0)
        vec_rows = self.vec.shape[0]
        self.share("v", lambda to: self.vec, self.vec_o, vec_rows, 0)
        self.near(self.seg, self.seg_o.at[slot_rows(place.c, 8)], "s")
        for k in range(1, span):
            to = lax.rem(place.c + k, span)
            dst = self.seg_o.at[slot_rows(place.c, 8)]
            cp = remote(self.seg, dst, self.gsend.at[k], self.grecv.at[place.c], place.line(to))
            cp.start()
            self.sends.append(cp)
        self.share_layer(0)
        orders = bit_orders(place)
        self.chunks, slot = [], 0
        tn, depth = place.tn, self.tri.shape[2]
        todo = []
        for layer in range(self.layers):
            todo += [
                [(("t", layer), self.wts[layer], tn * depth)],
                [(("i", layer), self.wis[layer], tn * depth)],
                [
                    (("o", layer), self.wos[layer], self.outer.shape[1]),
                    (("p", layer), self.wps[layer], self.proj.shape[1]),
                ],
            ]
        todo[0].insert(0, ("v", self.vec_o, tn * vec_rows))
        self.keys = [[key for key, _, _ in chunk] for chunk in todo]
        for chunk in todo:
            parts = []
            for _, ref, block in chunk:
                pieces = halves(ref.shape[1]) if ref.shape[1] >= 256 else [pl.ds(0, ref.shape[1])]
                for i, piece in enumerate(pieces):
                    parts.append(Doubling(place, ref, block, piece, orders[i], (self.ssem, self.rsem), slot))
                    slot += 1
            self.chunks.append(parts)
        self.steps = len(place.bits)
        self.turn, self.turns = 0, len(self.chunks) + SKEW * (self.steps - 1)
        self.complete = set()

    def ready(self, i):
        for key in self.keys[i]:
            if key == "v" or key[0] in ("t", "i"):
                self.shared(key)
            elif key[0] == "o":
                self.locals_of[key].wait()
            else:
                self.proj_ready(key[1])

    def tick(self, until=None):
        while self.turn < self.turns and (until is None or self.turn <= until):
            for step in reversed(range(self.steps)):
                i = self.turn - SKEW * step
                if 0 <= i < len(self.chunks):
                    if step == 0:
                        self.ready(i)
                    for part in self.chunks[i]:
                        part.advance(step)
            self.turn += 1
            if until is None:
                break

    def have(self, key):
        i = [key in keys for keys in self.keys].index(True)
        if i not in self.complete:
            self.complete.add(i)
            self.tick(i + SKEW * (self.steps - 1))
            for part in self.chunks[i]:
                part.whole()

    def segments_in(self):
        place, span = self.place, 2 * self.place.tn
        self.locals_of["s"].wait()
        for k in range(1, span):
            frm = lax.rem(place.c + k, span)
            ref = self.seg_o.at[slot_rows(frm, 8)]
            remote(ref, ref, self.gsend.at[k], self.grecv.at[frm], place.line(frm)).wait_recv()

    def finish(self):
        self.tick(self.turns)
        for parts in self.chunks:
            for part in parts:
                part.finish()
        for cp in self.sends:
            cp.wait_send()


def ascend_kernel(
    gn, tn, layers, size,
    tok, cot, seg, vec, tri, inn, outer, proj, ctab, stab, e32, m32, e96, m96,
    gb_o, segcol, segrow, vecs_o, bts_o, bis_o, xs_o, w_o, kept_o,
    w, kept, xs, x_low, cot_low, gb, keep, seg_in, vec_in, vec_wide, bt_wide,
    bufs, group, opening_sems, save_sem, tok_sem,
):
    place = Place(gn, tn)
    opening = Opening(
        place, layers, tok, cot, seg, vec, tri, inn, outer, proj, x_low, cot_low, seg_in, vec_in, w, opening_sems
    )
    opening.barrier()
    opening.start()
    saves = []

    def save(src, dst):
        cp = pltpu.make_async_copy(src, dst, save_sem.at[len(saves)])
        cp.start()
        saves.append(cp)

    opening.tick(0)
    opening.moved_in(tok, x_low, 0)
    xs[0][...] = x_low[...].astype(F32)
    spreads, gathers, stages = [], [], []
    for layer in range(layers):
        ssem, fsem, rsem, cs, cr, ls, lr = group[layer]
        spreads.append(Spread(tn, kept[layer][0], size, ssem, fsem, rsem))
        gathers.append(Gather(tn, *bufs, (cs, cr, ls, lr)))
        stages.append(
            Forward(
                tn, size, xs[layer], tuple(w[k][layer] for k in range(4)),
                (vecs_o.at[layer], bts_o.at[layer], bis_o.at[layer]), (segcol, segrow), (ctab, stab),
                kept[layer], keep,
            )
        )
    stages[0].norm(place.t)
    spreads[0].start()
    opening.tick(1)
    for layer in range(1, layers):
        opening.share_layer(layer)
    opening.segments_in()
    block = segcol.shape[0] // (2 * tn)
    eye = lax.broadcasted_iota(jnp.int32, (block, block), 0) == lax.broadcasted_iota(jnp.int32, (block, block), 1)
    for i in range(2 * tn):
        row = jnp.where(place.h == 0, seg_in[8 * i : 8 * i + 1, :], seg_in[8 * i + 1 : 8 * i + 2, :])
        spot = lax.broadcasted_iota(jnp.int32, (1, block), 1) + i * block
        row = jnp.where(row == 0, -1 - spot, row).astype(F32)
        segrow[:, i * block : (i + 1) * block] = row
        segcol[i * block : (i + 1) * block, :] = jnp.sum(jnp.where(eye, row, 0.0), axis=1, keepdims=True)
    opening.have("v")
    shards = gn * tn
    vec_rows = vec.shape[0]
    vec_wide[...] = vec_in[...].astype(F32)
    lane = lax.broadcasted_iota(jnp.int32, (1, 128), 1)
    for layer in range(layers):

        def line(k):
            return vec_wide[pl.ds(4 * layer + k, shards, stride=vec_rows), :]

        def spread_out(value, place_of, mask):
            return jnp.sum(dot(value.astype(BF16), place_of, NN) * mask, axis=0, keepdims=True)

        thick = line(2)
        parts = [jnp.where(lane // 32 == i, thick, 0.0) for i in range(4)]
        thin = line(3)
        gains = [jnp.where(lane // 32 == i, thin, 0.0) for i in range(2)]
        rows = [spread_out(p, e32[...], m32[...]) for p in parts + gains]
        vecs_o[layer] = jnp.concatenate(
            [rows[2], rows[3], rows[4], rows[5], rows[0] + rows[1]] + [jnp.zeros_like(rows[0])] * 3, axis=0
        )
        bt_wide[...] = spread_out(line(1), e96[...], m96[...])
        wide = bts_o.shape[2] // 3
        for i in range(3):
            start = pl.multiple_of(i * wide * tn + place.t * wide, 128)
            bts_o[layer, :, i * wide : (i + 1) * wide] = bt_wide[:, pl.ds(start, wide)]
        for i in range(gn):
            bis_o[layer, :, i * 128 : (i + 1) * 128] = vec_wide[
                pl.ds((i * tn + place.t) * vec_rows + 4 * layer, 1), :
            ]

    for layer in range(layers):
        stage, spread, gather = stages[layer], spreads[layer], gathers[layer]
        if layer > 0:
            stage.norm(place.t)
            spread.start()
        opening.have(("t", layer))
        for i, b in enumerate(arrivals(spread)):
            stage.heads_in(b)
            if i == 1:
                opening.tick()
        if layer + 1 == layers:
            opening.moved_in(cot, cot_low, 1)
            gb[rows_of(place.t, size), :] = cot_low[...]
            ahead = Spread(tn, gb, size, *group[layers][:3])
            ahead.start()
        for i, b in enumerate(far_first(spread)):
            stage.attend(b)
            if i == 1:
                opening.tick()
        if layer == 0:
            opening.move(cot, cot_low, 1)
        opening.have(("i", layer))
        save(kept[layer][0], kept_o[layer][0])
        for i in range(1, 6):
            save(kept[layer][i], kept_o[layer][i])
        for i, b in enumerate(far_first(spread)):
            stage.mixer_in(b)
            if i == 1:
                opening.tick()
        save(kept[layer][6], kept_o[layer][6])
        save(kept[layer][7], kept_o[layer][7])
        save(xs[layer], xs_o[layer])
        if layer + 1 == layers:
            for _ in arrivals(ahead):
                pass
            save(gb, gb_o)
        opening.have(("o", layer))
        for k in range(4):
            save(w[k][layer], w_o[k][layer])
        if layer + 1 < layers:
            branch_sums(stage, spread, gather, opening.tick)
            xs[layer + 1][...] = xs[layer][...] + vecs_o[layer, 4:5, :] + keep[...] + gather.total()
            gather.finish()
        spread.finish()
    ahead.finish()
    opening.finish()
    for cp in saves:
        cp.wait()


ANY = pl.BlockSpec(memory_space=pl.ANY)


def constant_tables(span, shards, model):
    angle = np.arange(span, dtype=np.float32)[:, None] * (
        np.float32(10000.0) ** (-(2.0 * np.arange(ROT // 2, dtype=np.float32)) / np.float32(ROT))
    )
    cosine, sine = np.cos(angle).astype(np.float32), np.sin(angle).astype(np.float32)
    none = np.zeros((span, HD - ROT), np.float32)
    reps = 128 // HD
    ctab = np.concatenate([cosine, cosine, none + 1.0] * reps, axis=1)
    stab = np.concatenate([-sine, sine, none] * reps, axis=1)
    return tuple(jnp.asarray(tab, F32) for tab in (ctab, stab))


def placement(piece, shards):
    j, col = np.arange(128)[:, None], np.arange(piece * shards)[None, :]
    put = (j % piece == col % piece) if 128 % piece == 0 else (j == col % piece)
    mask = np.arange(shards)[:, None] == col // piece
    return jnp.asarray(put, BF16), jnp.asarray(mask, F32)


def kept_shapes(length, model, width, units):
    return [
        ((length, model), BF16),
        ((length, width), BF16),
        ((length, width), BF16),
        ((length, width), BF16),
        ((length, width), F32),
        ((length, 128), F32),
        ((length, units), BF16),
        ((length, units), BF16),
    ]


def ascend_call(gn, tn, tokens, cotangent, segments, vec, tri, inn, outer, proj, tables, placing):
    layers = outer.shape[0]
    _, half, model = tokens.shape
    size = 2 * half
    length = size * tn
    depth = tri.shape[2]
    wshapes = [
        (gn * tn * depth, tri.shape[3]), (gn * tn * depth, inn.shape[3]),
        (gn * outer.shape[1], model), (gn * proj.shape[1], model),
    ]
    width, units, chips = wshapes[3][0], wshapes[2][0], tn // 2
    kept = kept_shapes(length, model, width, units)
    dma = pltpu.SemaphoreType.DMA
    outs = [
        (shape((length, model), BF16), ANY),
        (shape((length, 1), F32), VM),
        (shape((1, length), F32), VM),
        (shape((layers, 8, model), F32), VM),
        (shape((layers, 1, 3 * width), F32), VM),
        (shape((layers, 1, units), F32), VM),
    ]
    outs += [(shape((size, model), F32), ANY)] * layers
    for dims in wshapes:
        outs += [(shape(dims, BF16), ANY)] * layers
    for _ in range(layers):
        outs += [(shape(*item), ANY) for item in kept]
    scratch = []
    for dims in wshapes:
        scratch += [pltpu.VMEM(dims, BF16)] * layers
    for _ in range(layers):
        scratch += [pltpu.VMEM(*item) for item in kept]
    scratch += [pltpu.VMEM((size, model), F32)] * layers
    scratch += [
        pltpu.VMEM((size, model), BF16),
        pltpu.VMEM((size, model), BF16),
        pltpu.VMEM((length, model), BF16),
        pltpu.VMEM((size, model), F32),
        pltpu.VMEM((2 * tn * 8, 128), jnp.int32),
        pltpu.VMEM((gn * tn * vec.shape[0], 128), BF16),
        pltpu.VMEM((gn * tn * vec.shape[0], 128), F32),
        pltpu.VMEM((1, 3 * model), F32),
    ]
    scratch += group_buffers(chips, size, model)
    for _ in range(layers + 1):
        scratch += group_sems(chips, tn)
    slots = 1 + 8 * layers
    scratch += [
        dma((slots, gn)), dma((slots, gn)), dma((2 + 3 * layers,)),
        dma((1 + 2 * layers, tn)), dma((1 + 2 * layers, tn)),
        dma((layers,)), dma((layers,)), dma((2, 2)), dma((2, 2)),
        dma((2 * tn,)), dma((2 * tn,)),
    ]
    scratch += [dma((14 * layers,)), dma((1,))]

    def body(*refs):
        refs = list(refs)

        def take(count):
            out, refs[:] = refs[:count], refs[count:]
            return out

        ins = take(14)
        gb_o, segcol, segrow, vecs_o, bts_o, bis_o = take(6)
        xs_o = take(layers)
        w_o = [take(layers) for _ in range(4)]
        kept_o = [take(8) for _ in range(layers)]
        w = [take(layers) for _ in range(4)]
        kept_s = [take(8) for _ in range(layers)]
        xs = take(layers)
        x_low, cot_low, gb, keep, seg_in, vec_in, vec_wide, bt_wide = take(8)
        bufs = take(4)
        group = [take(7) for _ in range(layers + 1)]
        sems = take(11)
        save_sem, tok_sem = take(2)
        ascend_kernel(
            gn, tn, layers, size, *ins, gb_o, segcol, segrow, vecs_o, bts_o, bis_o, xs_o, w_o, kept_o,
            w, kept_s, xs, x_low, cot_low, gb, keep, seg_in, vec_in, vec_wide, bt_wide, bufs, group, sems,
            save_sem, tok_sem,
        )

    return pl.pallas_call(
        body,
        out_shape=tuple(o for o, _ in outs),
        in_specs=[ANY] * 8 + [VM] * 6,
        out_specs=tuple(spec for _, spec in outs),
        scratch_shapes=scratch,
        compiler_params=params_of(2),
        name="ascend",
    )(tokens, cotangent, segments, vec, tri, inn, outer, proj, *tables, *placing)


class Halving:
    def __init__(self, place, acc, inbox, block, cols, order, sems, slot):
        self.place, self.acc, self.inbox, self.block, self.cols = place, acc, inbox, block, cols
        self.send, self.recv, self.slot = sems[0], sems[1], slot
        self.plan, index, base = [], 0, 0
        for bit, runs in reversed(runs_by_step(place, order)):
            entry = []
            for start, count in runs:
                entry.append((bit, start, count, index, base))
                index += 1
                base += count
            self.plan.append(entry)

    def copy(self, bit, start, count, index, base):
        rows = pl.ds(pl.multiple_of(flip(start, bit) * self.block, self.block), count * self.block)
        return remote(
            self.acc.at[rows, self.cols],
            self.inbox.at[pl.ds(base * self.block, count * self.block), self.cols],
            self.send.at[self.slot, index],
            self.recv.at[self.slot, index],
            self.place.group(flip(self.place.g, bit)),
        )

    def advance(self, step):
        if step > 0:
            for item in self.plan[step - 1]:
                self.copy(*item).wait_recv()
                _, start, count, _, base = item

                def add(i, carry):
                    rows = pl.ds(pl.multiple_of((start + i) * self.block, self.block), self.block)
                    came = pl.ds(pl.multiple_of((base + i) * self.block, self.block), self.block)
                    value = self.acc[rows, self.cols].astype(F32) + self.inbox[came, self.cols].astype(F32)
                    self.acc[rows, self.cols] = value.astype(BF16)
                    return carry

                lax.fori_loop(0, count, add, 0)
        if step < len(self.plan):
            for item in self.plan[step]:
                self.copy(*item).start()

    def finish(self):
        for entry in self.plan:
            for item in entry:
                self.copy(*item).wait_send()

class Slots:
    def __init__(self, ref, first, size):
        self.ref, self.first, self.size = ref, first, size

    def rows(self, slot):
        return slot_rows(self.first + slot, self.size)

    @property
    def at(self):
        return _SlotRefs(self)

    def __getitem__(self, slot):
        return self.ref[self.rows(slot), :]


class _SlotRefs:
    def __init__(self, slots):
        self.slots = slots

    def __getitem__(self, slot):
        return self.slots.ref.at[self.slots.rows(slot)]


class Reducing:
    def __init__(self, place, layers, accs, boxes, outs, sems):
        self.place, self.layers = place, layers
        self.accs, self.boxes = accs, boxes
        self.cross, self.proj_o, self.outer_o = outs[:2], outs[2], outs[3]
        self.hs, self.hr, self.cs, self.cr, self.ps, self.pr, self.os = sems
        self.target, self.source, self.r, self.q = proj_places(place)
        self.moved = self.q != self.r
        orders = bit_orders(place)
        self.parts, slot = {}, 0
        for layer in range(layers):
            for kind in range(4):
                acc = accs[kind][layer]
                parts = []
                for k, cols in enumerate(halves(acc.shape[1])):
                    box = boxes[kind].at[layer]
                    block = acc.shape[0] // place.gn
                    parts.append(Halving(place, acc, box, block, cols, orders[k], (self.hs, self.hr), slot))
                    slot += 1
                self.parts[kind, layer] = parts
        self.steps = len(place.bits) + 1
        self.taken = {key: 0 for key in self.parts}

    def advance(self, kind, layer):
        step = self.taken[kind, layer]
        self.taken[kind, layer] = step + 1
        for part in self.parts[kind, layer]:
            part.advance(step)
        if step == self.steps - 1:
            self.owned(kind, layer)

    def own_rows(self, kind, layer, index, pieces):
        acc = self.accs[kind][layer]
        rows = acc.shape[0] // pieces
        return acc.at[slot_rows(index, rows)]

    def cross_copy(self, kind, layer, k):
        place = self.place
        to = place.other(k)
        src = self.own_rows(kind, layer, place.g * place.tn + to, place.gn * place.tn)
        dst = self.cross[kind].at[layer, place.t]
        return remote(src, dst, self.cs.at[kind, layer, k], self.cr.at[kind, layer, place.t], {"t": to})

    def proj_copies(self, layer):
        src = self.own_rows(3, layer, self.place.g, self.place.gn)
        here = pltpu.make_async_copy(src, self.proj_o.at[layer], self.ps.at[layer])
        return here, remote(src, self.proj_o.at[layer], self.ps.at[layer], self.pr.at[layer], self.source)

    def own_copy(self, kind, layer):
        place = self.place
        if kind == 2:
            src, dst = self.own_rows(2, layer, place.g, place.gn), self.outer_o.at[layer]
        else:
            src = self.own_rows(kind, layer, place.g * place.tn + place.t, place.gn * place.tn)
            dst = self.cross[kind].at[layer, place.t]
        return pltpu.make_async_copy(src, dst, self.os.at[kind, layer])

    def owned(self, kind, layer):
        if kind < 3:
            self.own_copy(kind, layer).start()
        if kind < 2:
            for k in range(1, self.place.tn):
                self.cross_copy(kind, layer, k).start()
        if kind == 3:
            here, far = self.proj_copies(layer)
            pl.when(self.moved)(far.start)
            pl.when(jnp.logical_not(self.moved))(here.start)

    def finish(self):
        for (kind, layer), parts in self.parts.items():
            for part in parts:
                part.finish()
            if kind < 3:
                self.own_copy(kind, layer).wait()
            if kind < 2:
                for k in range(1, self.place.tn):
                    frm = self.place.other(k)
                    ref = self.cross[kind].at[layer, frm]
                    remote(
                        ref, ref, self.cs.at[kind, layer, k], self.cr.at[kind, layer, frm], {"t": frm}
                    ).wait_recv()
                    self.cross_copy(kind, layer, k).wait_send()
            if kind == 3:
                here, far = self.proj_copies(layer)
                pl.when(self.moved)(far.wait)
                pl.when(jnp.logical_not(self.moved))(here.wait)


FIRST = {
    "outer": ((2, 0), (3, 0)),
    "inner": ((1, 0),),
    "s1": ((2, 0), (3, 0)),
    "triple": ((0, 0), (1, 0)),
    "sum": ((2, 0), (3, 0)),
}
LATER = {
    "spread": ((0, 1),),
    "near": ((1, 1),),
    "arrived": ((2, 1), (3, 1), (0, 1)),
    "outer": ((2, 0), (3, 0), (1, 1)),
    "inner": ((1, 0), (0, 1)),
    "s1": ((2, 0), (3, 0)),
    "triple": ((0, 0), (1, 0), (2, 0), (3, 0)),
}


def descend_kernel(
    gn, tn, layers, size,
    grads, segcol, segrow, vecs, ctab, stab, xs, ws, kepts,
    out_o, grad_o, flat_o, triple_o, inner_o, proj_o, outer_o,
    w, kept, dy, x, gb, do, dt, dk, dv, keep, dbt, dbi, bufs, accs, boxes, flatbox,
    group, reduce_sems, load_sem, ms, mr, fs, fr,
):
    place = Place(gn, tn)
    g, t, c = place.g, place.t, place.c
    wt, wi, wo, wp = w
    n, q, k, v, o, lse, gact, gp = kept
    chips = tn // 2
    width, units, model = q.shape[1], gact.shape[1], dy.shape[1]
    heads = width // HD
    dq, dh, du = o, gact, gp
    loads = {}

    def load(layer, names):
        for name in names:
            if name == "x":
                src, dst = xs[layer], x
            elif name == "cot":
                src, dst = grads, gb
            elif name[0] == "w":
                i = int(name[1])
                src, dst = ws[i][layer], w[i]
            else:
                i = int(name[1])
                src, dst = kepts[layer][i], kept[i]
            cp = pltpu.make_async_copy(src, dst, load_sem.at[len(loads)])
            cp.start()
            loads[layer, name] = cp

    waited = set()

    def need(layer, names):
        for name in names:
            if (layer, name) not in waited:
                waited.add((layer, name))
                loads[layer, name].wait()

    last = layers - 1
    load(last, ["w2", "w3", "k6", "k4", "cot", "k7", "k5", "w1", "k0", "k1", "k2", "k3", "w0", "x"])
    reducing = Reducing(place, layers, accs, boxes, (triple_o, inner_o, proj_o, outer_o), reduce_sems)
    line_barrier(place, (reducing.target, reducing.moved))
    half = out_o.shape[1]

    def hop(src, dst, slot, s):
        to = 2 * t + s
        part = src.at[pl.ds(s * half, half)]
        near = pltpu.make_async_copy(part, dst.at[place.h], ms.at[slot, s])
        far = remote(part, dst.at[place.h], ms.at[slot, s], mr.at[slot, place.h], place.line(to))
        return to == c, near, far

    def move(src, dst, slot):
        for s in range(2):
            stays, near, far = hop(src, dst, slot, s)
            pl.when(stays)(near.start)
            pl.when(jnp.logical_not(stays))(far.start)

    def moved_in(src, dst, slot):
        for s in range(2):
            stays, near, far = hop(src, dst, slot, s)
            pl.when(stays)(near.wait)
            pl.when(jnp.logical_not(stays))(far.wait_send)
        for i in range(2):
            cp = remote(
                src.at[pl.ds(0, half)], dst.at[i], ms.at[slot, 0], mr.at[slot, i], place.line(c)
            )
            pl.when(i * tn + c // 2 != c)(cp.wait_recv)

    exchanges = [("g", bit) for bit in place.bits] + [("t", 1 << i) for i in range(tn.bit_length() - 1)]

    def exchange(layer, i):
        kind, bit = exchanges[i]
        to = place.group(flip(g, bit)) if kind == "g" else {"t": flip(t, bit)}
        return remote(flat_o.at[layer], flatbox.at[layer, i], fs.at[layer, i], fr.at[layer, i], to)

    def flat_turn(layer, i):
        if i > 0:
            exchange(layer, i - 1).wait()
            flat_o[layer] += flatbox[layer, i - 1]
        if i < len(exchanges):
            exchange(layer, i).start()

    masks = head_masks(width, BF16)
    lane = lax.broadcasted_iota(jnp.int32, (1, 128), 1)
    up = place.t // 2 >= (chips + 1) // 2

    def pair(qb, kb):
        qrows, krows = rows_of(qb, size), rows_of(kb, size)
        queries, keys, vals = q[qrows, :], k[krows, :], v[krows, :]
        grad = do[qrows, :]
        side = lse[qrows, :]
        bias = pair_bias(qb, kb, size, segcol, segrow)
        dq_new = jnp.zeros((size, width), F32)
        dk_new = jnp.zeros((size, width), F32)
        dv_new = jnp.zeros((size, width), F32)
        for h in range(heads):
            qh, gh = queries * masks[h], grad * masks[h]
            total = jnp.sum(jnp.where(lane == h, side, 0.0), axis=1, keepdims=True)
            delta = jnp.sum(jnp.where(lane == 64 + h, side, 0.0), axis=1, keepdims=True)
            p = jnp.exp(dot(qh, keys, NT) + bias - total)
            ds = (p * (dot(gh, vals, NT) - delta)).astype(BF16)
            dv_new = dv_new + dot(p.astype(BF16), gh, TN)
            dk_new = dk_new + dot(ds, qh, TN)
            dq_new = dq_new + dot(ds, keys * masks[h], NN)
        dq[qrows, :] += dq_new
        dk[krows, :] += dk_new
        dv[krows, :] += dv_new

    def columns(count, tile, body):
        def step(j, carry):
            body(rows_of(j, tile))
            return carry

        lax.fori_loop(0, count // tile, step, 0)

    need(last, ["w2", "w3", "k6", "k4"])
    top = Spread(tn, gb, size, *group[layers][:3])
    room, spare = accs[2][0], accs[1][0]
    top_gather = Gather(
        tn, bufs[0], Slots(room, 0, size), bufs[2], Slots(room, chips, size), tuple(group[layers][3:])
    )
    stage_top = Forward(
        tn, size, x, (wt, wi, wo, wp), (vecs.at[last], None, None), (segcol, segrow), (ctab, stab), kept, keep
    )
    branch_sums(stage_top, top, top_gather)
    need(last, ["cot"])
    dy[...] = gb[rows_of(t, size), :].astype(F32)
    flat_o[...] = jnp.zeros_like(flat_o)
    out_in = spare.at[pl.ds(0, size)]

    def give_output():
        need(last, ["x"])
        out_in[...] = (x[...] + vecs[last, 4:5, :] + keep[...] + top_gather.total()).astype(BF16)
        top_gather.finish()
        move(out_in, out_o, 0)

    for layer in reversed(range(layers)):
        flat = flat_o.at[layer]
        vec = vecs.at[layer]
        dwt, dwi, dwo, dwp = (accs[i][layer] for i in range(4))
        ssem, fsem, rsem, cs, cr, ls, lr = group[layer]
        spread = Spread(tn, gb, size, ssem, fsem, rsem)
        gather = Gather(tn, *bufs, (cs, cr, ls, lr))
        zc, co = spread.zc, spread.co

        def ticks(where, layer=layer):
            for kind, late in (FIRST if layer == last else LATER).get(where, ()):
                if layer + late < layers and reducing.taken[kind, layer + late] < reducing.steps:
                    reducing.advance(kind, layer + late)

        own = dy[...].astype(BF16)
        if layer < last:
            gb[rows_of(t, size), :] = own
            spread.start()
        flat[4:5, :] = jnp.sum(own.astype(F32), axis=0, keepdims=True)
        dbt[...] = jnp.zeros_like(dbt)
        dbi[...] = jnp.zeros_like(dbi)
        dk[...] = jnp.zeros_like(dk)
        dv[...] = jnp.zeros_like(dv)
        ticks("spread")
        if layer < last:
            flat_turn(layer + 1, 0)
        for count, b in enumerate(arrivals(spread) if layer < last else range(tn)):
            need(layer, ["w3", "k4", "w2", "k7", "k5"])
            rows = rows_of(b, size)
            grad = gb[rows, :]
            heads_grad = dot(grad, wp[...], NT).astype(BF16)
            do[rows, :] = heads_grad
            prod = heads_grad.astype(F32) * o[rows, :]
            side = lse[rows, :]
            for h in range(heads):
                delta = jnp.sum(prod * masks[h].astype(F32), axis=1, keepdims=True)
                side = jnp.where(lane == 64 + h, delta, side)
            lse[rows, :] = side

            def unit(cols):
                d = (dot(grad, wo[cols, :], NT) * gp[rows, cols].astype(F32)).astype(BF16)
                du[rows, cols] = d
                dbi[0:1, cols] += jnp.sum(d.astype(F32), axis=0, keepdims=True)

            columns(units, TILE, unit)
            if layer < last:
                flat_turn(layer + 1, count + 1)
            if count == 1:
                ticks("near")
        ticks("arrived")
        need(layer, ["k6"])
        if layer < last:
            spread.finish()
            if layer == last - 1:
                moved_in(out_in, out_o, 0)

        def grad_outer(cols):
            dwo[cols, :] = dot(gact[:, cols], gb[...], TN).astype(BF16)

        columns(units, TILE, grad_outer)

        def grad_proj(cols):
            dwp[cols, :] = dot(o[:, cols].astype(BF16), gb[...], TN).astype(BF16)

        columns(width, TILE, grad_proj)
        if layer == last:
            give_output()
        ticks("outer")
        if layer < last:
            flat_turn(layer + 1, len(exchanges))
        need(layer, ["w1", "k0"])
        if layer > 0:
            load(layer - 1, ["w2", "w3"])
        dq[...] = jnp.zeros_like(dq)
        for b in range(tn):
            rows = pl.ds(b * size, size)

            def back(cols):
                d = dot(du[rows, :], wi[cols, :], NT)
                flat[2:3, cols] += jnp.sum(d * n[rows, cols].astype(F32), axis=0, keepdims=True)
                flat[3:4, cols] += jnp.sum(d, axis=0, keepdims=True)
                dh[rows, cols] = (d * vec[2:3, cols]).astype(BF16)

            columns(model, TILE, back)

        def grad_inner(cols):
            h2 = (n[:, cols].astype(F32) * vec[2:3, cols] + vec[3:4, cols]).astype(BF16)
            dwi[cols, :] = dot(h2, du[...], TN).astype(BF16)

        columns(model, TILE, grad_inner)
        ticks("inner")
        if layer > 0:
            load(layer - 1, ["w1", "k7"])
        need(layer, ["k1", "k2", "k3", "w0"])

        for stage in range(tn):
            pivot = jnp.where(up, stage, tn - 1 - stage)

            def step(j, carry):
                pair(jnp.where(up, pivot + j, pivot), jnp.where(up, pivot, pivot - j))
                return carry

            lax.fori_loop(0, tn - stage, step, 0)
            rows = rows_of(pivot, size)
            cos, sine = ctab[rows, :], stab[rows, :]
            dt[rows, 0:width] = turn(dq[rows, :] * (1.0 / math.sqrt(HD)), cos, sine, -1.0).astype(BF16)
            dt[rows, width : 2 * width] = turn(dk[rows, :], cos, sine, -1.0).astype(BF16)
            dt[rows, 2 * width : 3 * width] = dv[rows, :].astype(BF16)
            block = dt[rows, :]
            dbt[...] += jnp.sum(block.astype(F32), axis=0, keepdims=True)
            chip, core = pivot // 2, lax.rem(pivot, 2)

            def back(cols):
                d = dot(block, wt[cols, :], NT)
                flat[0:1, cols] += jnp.sum(d * n[rows, cols].astype(F32), axis=0, keepdims=True)
                flat[1:2, cols] += jnp.sum(d, axis=0, keepdims=True)
                value = dh[rows, cols].astype(F32) + d * vec[0:1, cols]

                @pl.when(core != co)
                def _():
                    gather.tocore[chip, :, cols] = value.astype(BF16)

                @pl.when((core == co) & (chip != zc))
                def _():
                    gather.toici[chip, :, cols] = value.astype(BF16)

                @pl.when(pivot == t)
                def _():
                    keep[:, cols] = value

            columns(model, TILE, back)

            @pl.when(core != co)
            def _():
                gather.send_core(chip)

            if stage % 2 == 1:

                @pl.when(chip != zc)
                def _():
                    gather.send_link(chip)

            ticks(f"s{stage}")

        wide = width
        for i in range(3):
            start = pl.multiple_of(t * wide, 128)
            flat[5 + i : 6 + i, pl.ds(start, wide)] = dbt[:, i * wide : (i + 1) * wide]
        for i in range(gn):
            row, start = divmod(i * tn * 128, model)
            flat[8 + row : 9 + row, pl.ds(pl.multiple_of(start + t * 128, 128), 128)] = dbi[:, i * 128 : (i + 1) * 128]
        if layer > 0:
            load(layer - 1, ["w0", "k1", "k2", "k3", "k4", "k5", "k6"])

        def grad_triple(cols):
            h1 = (n[:, cols].astype(F32) * vec[0:1, cols] + vec[1:2, cols]).astype(BF16)
            dwt[cols, :] = dot(h1, dt[...], TN).astype(BF16)

        columns(model, TILE, grad_triple)
        if layer > 0:
            load(layer - 1, ["k0"])
        ticks("triple")
        if layer == 0:
            flat_turn(0, 0)
        need(layer, ["x"])
        own_n, inverse = norm_stats(x[...])
        e = keep[...] + gather.total()
        inner = e - jnp.mean(e, axis=-1, keepdims=True) - own_n * jnp.mean(e * own_n, axis=-1, keepdims=True)
        dy[...] = dy[...] + inner * inverse
        if layer > 0:
            load(layer - 1, ["x"])
        gather.finish()
        ticks("sum")

    low = gb.at[pl.ds(0, size)]
    low[...] = dy[...].astype(BF16)
    move(low, grad_o, 1)
    rest = [(0, 0), (1, 0), (2, 0), (3, 0), (0, 0), (1, 0), (0, 0)]
    for i, (kind, layer) in enumerate(rest):
        if i + 1 <= len(exchanges):
            flat_turn(0, i + 1)
        reducing.advance(kind, layer)
    for layer in reversed(range(layers)):
        for kind in range(4):
            while reducing.taken[kind, layer] < reducing.steps:
                reducing.advance(kind, layer)
    reducing.finish()
    moved_in(low, grad_o, 1)


def descend_call(gn, tn, grads, segcol, segrow, vecs, tables, xs, ws, kepts):
    layers = len(xs)
    size, model = xs[0].shape
    length = size * tn
    shapes = [ws[i][0].shape for i in range(4)]
    width, units, chips = shapes[3][0], shapes[2][0], tn // 2
    kept = kept_shapes(length, model, width, units)
    dma = pltpu.SemaphoreType.DMA
    shard = shapes[0][0] // (gn * tn)
    prows, orows = shapes[3][0] // gn, shapes[2][0] // gn
    exchanges = (gn * tn).bit_length() - 1
    outs = (
        shape((2, size // 2, model), BF16),
        shape((2, size // 2, model), BF16),
        shape((layers, 16, model), F32),
        shape((layers, tn, shard, 3 * width), BF16),
        shape((layers, tn, shard, units), BF16),
        shape((layers, prows, model), BF16),
        shape((layers, orows, model), BF16),
    )
    scratch = [pltpu.VMEM(dims, BF16) for dims in shapes]
    scratch += [pltpu.VMEM(*item) for item in kept]
    scratch += [
        pltpu.VMEM((size, model), F32),
        pltpu.VMEM((size, model), F32),
        pltpu.VMEM((length, model), BF16),
        pltpu.VMEM((length, width), BF16),
        pltpu.VMEM((length, 3 * width), BF16),
        pltpu.VMEM((length, width), F32),
        pltpu.VMEM((length, width), F32),
        pltpu.VMEM((size, model), F32),
        pltpu.VMEM((1, 3 * width), F32),
        pltpu.VMEM((1, units), F32),
    ]
    scratch += group_buffers(chips, size, model)
    for dims in shapes:
        scratch += [pltpu.VMEM(dims, BF16)] * layers
    scratch += [pltpu.VMEM((layers, (gn - 1) * dims[0] // gn, dims[1]), BF16) for dims in shapes]
    scratch += [pltpu.VMEM((layers, exchanges, 16, model), F32)]
    for _ in range(layers + 1):
        scratch += group_sems(chips, tn)
    slots = 8 * layers
    scratch += [
        dma((slots, gn)), dma((slots, gn)), dma((2, layers, tn)), dma((2, layers, tn)), dma((layers,)), dma((layers,)),
        dma((3, layers)),
        dma((14 * layers,)), dma((2, 2)), dma((2, 2)), dma((layers, exchanges)), dma((layers, exchanges)),
    ]

    def body(*refs):
        refs = list(refs)

        def take(count):
            out, refs[:] = refs[:count], refs[count:]
            return out

        ins = take(6)
        x_in = take(layers)
        w_in = [take(layers) for _ in range(4)]
        kept_in = [take(8) for _ in range(layers)]
        results = take(7)
        w, kept_s = take(4), take(8)
        work = take(10)
        bufs = take(4)
        accs = [take(layers) for _ in range(4)]
        boxes = take(4)
        flatbox = take(1)[0]
        group = [take(7) for _ in range(layers + 1)]
        reduce_sems = take(7)
        descend_kernel(
            gn, tn, layers, size, *ins, x_in, w_in, kept_in, *results, w, kept_s, *work, bufs, accs, boxes,
            flatbox, group, reduce_sems, *take(5),
        )

    flat_ws = [ws[i][layer] for i in range(4) for layer in range(layers)]
    flat_kept = [ref for layer in range(layers) for ref in kepts[layer]]
    return pl.pallas_call(
        body,
        out_shape=outs,
        in_specs=[ANY] + [VM] * 5 + [ANY] * (layers + len(flat_ws) + len(flat_kept)),
        out_specs=(ANY, ANY, VM, ANY, ANY, ANY, ANY),
        scratch_shapes=scratch,
        compiler_params=params_of(3),
        name="descend",
    )(grads, segcol, segrow, vecs, *tables, *xs, *flat_ws, *flat_kept)


GROUPS = ("dp", "h")
EVERY = ("dp", "h", "t")


def to_group(tn, blocks):
    h, t = lax.axis_index("h"), lax.axis_index("t")
    count = 2 * tn
    parity = lax.rem(t, 2)
    got = []
    for j in range(2):
        moves = [(c, ((c + j) % 2) * tn + c // 2) for c in range(count)]
        piece = jnp.where(lax.rem(parity + j, 2) == 0, blocks[0], blocks[1])
        got.append(lax.ppermute(piece, ("h", "t"), moves))
    low = jnp.where(h == 0, got[0], got[1])
    high = jnp.where(h == 0, got[1], got[0])
    return jnp.concatenate([low, high], axis=0)


def from_group(tn, rows):
    h, t = lax.axis_index("h"), lax.axis_index("t")
    count = 2 * tn
    parity = lax.rem(t, 2)
    size = rows.shape[0] // 2
    got = []
    for j in range(2):
        moves = [(((c + j) % 2) * tn + c // 2, c) for c in range(count)]
        piece = jnp.where(lax.rem(h + j, 2) == 0, rows[:size], rows[size:])
        got.append(lax.ppermute(piece, ("h", "t"), moves))
    first = jnp.where(parity == 0, got[0], got[1])
    second = jnp.where(parity == 0, got[1], got[0])
    return jnp.stack([first, second], axis=0)


def proj_moves(gn, tn):
    return [(r, (r % gn) * tn + r // gn) for r in range(gn * tn)]


def slice_columns(weight, gn, tn):
    rows, cols = weight.shape
    return weight.reshape(rows, gn, tn, cols // (gn * tn)).transpose(2, 0, 1, 3).reshape(tn, rows, cols // tn)


def slice_triple(weight, tn):
    rows, cols = weight.shape
    return weight.reshape(rows, 3, tn, cols // (3 * tn)).transpose(2, 0, 1, 3).reshape(tn, rows, cols // tn)


def gather_weights(gn, tn, triple, proj, inner, outer):
    def spread(parts):
        moved = lax.all_to_all(parts, "t", 0, 0, tiled=True)
        whole = lax.all_gather(moved.reshape(-1, moved.shape[-1]), GROUPS, axis=0, tiled=True)
        return whole

    wt = spread(slice_triple(triple, tn))
    wi = spread(slice_columns(inner, gn, tn))
    wo = lax.all_gather(outer, GROUPS, axis=0, tiled=True)
    wp = lax.all_gather(lax.ppermute(proj, EVERY, proj_moves(gn, tn)), GROUPS, axis=0, tiled=True)
    return wt, wi, wo, wp


def reduce_weights(gn, tn, dwt, dwi, dwo, dwp):
    def back(parts):
        mine = lax.psum_scatter(parts, GROUPS, scatter_dimension=0, tiled=True)
        rows = mine.shape[0] // tn
        return lax.all_to_all(mine.reshape(tn, rows, -1), "t", 0, 0, tiled=True).astype(F32)

    triple = back(dwt)
    rows = triple.shape[1]
    triple = triple.reshape(tn, rows, 3, -1).transpose(1, 2, 0, 3).reshape(rows, -1)
    inner = back(dwi)
    inner = inner.reshape(tn, rows, gn, -1).transpose(1, 2, 0, 3).reshape(rows, -1)
    outer = lax.psum_scatter(dwo, GROUPS, scatter_dimension=0, tiled=True).astype(F32)
    proj = lax.psum_scatter(dwp, GROUPS, scatter_dimension=0, tiled=True)
    proj = lax.ppermute(proj, EVERY, [(b, a) for a, b in proj_moves(gn, tn)]).astype(F32)
    return triple, proj, inner, outer


def per_device(
    gn, tn,
    tokens, segments, cotangent, triple_weight, triple_bias, proj_weight, proj_bias, inner_weight, inner_bias,
    outer_weight, outer_bias, first_gain, first_shift, second_gain, second_shift,
):
    layers = triple_weight.shape[0]
    model = tokens.shape[2]
    span = tokens.shape[1] * 2 * tn
    h, t = lax.axis_index("h"), lax.axis_index("t")
    device = (lax.axis_index("dp") * 2 + h) * tn + t
    shards = gn * tn
    heads_wide = model // tn
    units = outer_weight.shape[1] * gn

    rows = triple_weight.shape[1]
    block = tokens.shape[1]
    tables = constant_tables(span, shards, model)
    direct = rows % 16 == 0 and block == 128 and layers * 4 <= 16 and units == model
    if direct:
        head = jnp.stack(
            [
                inner_bias,
                jnp.pad(triple_bias, ((0, 0), (0, 128 - triple_bias.shape[1]))),
                jnp.concatenate([proj_bias, outer_bias, first_gain, first_shift], axis=1),
                jnp.pad(jnp.concatenate([second_gain, second_shift], axis=1), ((0, 0), (0, 64))),
            ],
            axis=1,
        ).reshape(4 * layers, 128)
        opened = ascend_call(
            gn, tn, tokens, cotangent, jnp.pad(segments, ((0, 6), (0, 0))),
            jnp.pad(head, ((0, 16 - 4 * layers), (0, 0))),
            triple_weight.reshape(layers, rows, 3, tn, -1).transpose(0, 3, 1, 2, 4).reshape(layers, tn, rows, -1),
            inner_weight.reshape(layers, rows, gn, tn, -1).transpose(0, 3, 1, 2, 4).reshape(layers, tn, rows, -1),
            outer_weight, proj_weight, tables,
            placement(model // shards, shards) + placement(3 * model // shards, shards),
        )
        opened = list(opened)
        grad_all, segcol, segrow, vecs, _, _ = opened[:6]
        opened = opened[6:]
        inputs = opened[:layers]
        weights = [tuple(opened[layers + k * layers + layer] for k in range(4)) for layer in range(layers)]
        kept = [opened[5 * layers + 8 * i : 5 * layers + 8 * (i + 1)] for i in range(layers)]
        output, tokens_grad, summed, triple, inner, proj, outer = descend_call(
            gn, tn, grad_all, segcol, segrow, vecs, tables, inputs,
            [[weights[layer][k] for layer in range(layers)] for k in range(4)], kept,
        )
        summed = summed.reshape(layers, -1)
        triple = triple.reshape(layers, tn, rows, 3, -1).transpose(0, 2, 3, 1, 4).reshape(layers, rows, -1).astype(F32)
        inner = inner.reshape(layers, tn, rows, gn, -1).transpose(0, 2, 3, 1, 4).reshape(layers, rows, -1).astype(F32)
        proj, outer = proj.astype(F32), outer.astype(F32)
    else:
        small = (triple_bias, inner_bias, proj_bias, outer_bias, first_gain, first_shift, second_gain, second_shift)
        starts = [0]
        for item in small:
            starts.append(starts[-1] + item.shape[1])
        packed = jnp.concatenate(small, axis=1)
        x = to_group(tn, tokens).astype(F32)
        cot = to_group(tn, cotangent).astype(F32)
        segs_all = lax.all_gather(segments, ("h", "t"), axis=1, tiled=True)
        everything = lax.all_gather(packed[None], EVERY, axis=0, tiled=True).astype(F32)
        weights = [
            gather_weights(
                gn, tn, triple_weight[layer], proj_weight[layer], inner_weight[layer], outer_weight[layer]
            )
            for layer in range(layers)
        ]
        segs = jnp.where(h == 0, segs_all[0], segs_all[1])
        segs = jnp.where(segs == 0, -1 - jnp.arange(span, dtype=jnp.int32), segs).astype(F32)
        tables = (segs[:, None], segs[None, :]) + tables

        def vector(layer, i):
            return everything[:, layer, starts[i] : starts[i + 1]].reshape(-1)

        vecs, inputs, kept = [], [], []
        for layer in range(layers):
            bt = lax.dynamic_index_in_dim(vector(layer, 0).reshape(3, tn, heads_wide), t, 1, keepdims=False)
            bi = lax.dynamic_index_in_dim(vector(layer, 1).reshape(gn, tn, -1), t, 1, keepdims=False)
            zero = jnp.zeros((model,), F32)
            vecs.append(
                jnp.stack(
                    [vector(layer, 4), vector(layer, 5), vector(layer, 6), vector(layer, 7)]
                    + [vector(layer, 2) + vector(layer, 3), zero, zero, zero]
                )
            )
            inputs.append(x)
            x, *saved = forward_layer(
                tn, x, weights[layer], vecs[layer], bt.reshape(1, -1), bi.reshape(1, -1), tables
            )
            kept.append(saved)
        output = x.astype(BF16)
        grad = cot
        mats, flats = [None] * layers, [None] * layers
        for layer in reversed(range(layers)):
            grad, dwt, dwi, dwo, dwp, dvec, dbt, dbi = backward_layer(
                tn, grad, inputs[layer], weights[layer], vecs[layer], tables, kept[layer]
            )
            mats[layer] = reduce_weights(gn, tn, dwt, dwi, dwo, dwp)
            part = lax.dynamic_update_slice(
                jnp.zeros((3, tn, heads_wide), F32), dbt.reshape(3, 1, heads_wide), (0, t, 0)
            )
            side = lax.dynamic_update_slice(
                jnp.zeros((gn, tn, units // gn), F32), dbi.reshape(gn, 1, units // gn), (0, t, 0)
            )
            flats[layer] = jnp.concatenate([dvec[:5].reshape(-1), part.reshape(-1), side.reshape(-1)])
        output, tokens_grad = from_group(tn, output), from_group(tn, grad.astype(BF16))
        triple, proj, inner, outer = (jnp.stack([m[k] for m in mats]) for k in range(4))
        summed = lax.psum(jnp.stack(flats), EVERY)

    def own(start, length):
        piece = length // shards
        return lax.dynamic_slice_in_dim(summed, start + device * piece, piece, 1)

    base = 5 * model
    bias_sum = own(4 * model, model)
    return (
        output,
        tokens_grad,
        triple,
        own(base, 2 * model),
        own(base + 2 * model, model),
        proj,
        bias_sum,
        inner,
        own(base + 3 * model, units * tn),
        outer,
        bias_sum,
        own(0, model),
        own(model, model),
        own(2 * model, model),
        own(3 * model, model),
    )


def solution(mesh):
    dp, ctx = mesh.shape["dp"], mesh.shape["ctx"]
    tn = ctx // 2
    gn = 2 * dp
    fine = Mesh(mesh.devices.reshape(dp, 2, tn), EVERY)
    seq = P("dp", ("h", "t"), None)
    mat = P(None, EVERY, None)
    row = P(None, EVERY)
    in_specs = (seq, P("dp", ("h", "t")), seq, mat, row, mat, row, mat, row, mat, row, row, row, row, row)
    out_specs = (seq, seq, mat, row, row, mat, row, mat, row, mat, row, row, row, row, row)
    return jax.shard_map(
        functools.partial(per_device, gn, tn), mesh=fine, in_specs=in_specs, out_specs=out_specs, check_vma=False
    )
```

```python
import functools
import math

import jax
import jax.numpy as jnp
import numpy as np
from jax import lax
from jax.experimental import pallas as pl
from jax.experimental.pallas import tpu as pltpu
from jax.sharding import Mesh
from jax.sharding import PartitionSpec as P

HD = 64
ROT = 16
EPSILON = 1e-05
NEG_LARGE = -1e30
MESH = pl.DeviceIdType.MESH
BF16 = jnp.bfloat16
F32 = jnp.float32
VMEM_LIMIT = 60 * 1024 * 1024


def dot(a, b, dims):
    return lax.dot_general(a, b, (dims, ((), ())), preferred_element_type=F32)


NN = ((1,), (0,))
NT = ((1,), (1,))
TN = ((0,), (0,))


def rows_of(b, size):
    return pl.ds(pl.multiple_of(b * size, size), size)


def group_barrier(tn):
    t = lax.axis_index("t")
    zc, co = t // 2, lax.rem(t, 2)
    chips = tn // 2
    sem = pltpu.get_barrier_semaphore()
    peers = [zc * 2 + 1 - co] + [lax.rem(zc + k, chips) * 2 + co for k in range(1, chips)]
    for p in peers:
        pl.semaphore_signal(sem, inc=1, device_id={"t": p}, device_id_type=MESH)
    pl.semaphore_wait(sem, len(peers))


class Spread:
    def __init__(self, tn, buf, size, ssem, fsem, rsem):
        self.tn, self.buf, self.size = tn, buf, size
        self.ssem, self.fsem, self.rsem = ssem, fsem, rsem
        self.t = lax.axis_index("t")
        self.zc, self.co = self.t // 2, lax.rem(self.t, 2)
        self.chips = tn // 2

    def copy(self, block, send, to):
        ref = self.buf.at[rows_of(block, self.size)]
        return pltpu.make_async_remote_copy(
            ref, ref, send, self.rsem.at[block], device_id={"t": to}, device_id_type=MESH
        )

    def start(self):
        for k in range(1, self.chips):
            chip = lax.rem(self.zc + k, self.chips)
            self.copy(self.t, self.ssem.at[k], chip * 2 + self.co).start()
        self.copy(self.t, self.ssem.at[0], self.zc * 2 + 1 - self.co).start()

    def peer_core(self):
        b = self.zc * 2 + 1 - self.co
        self.copy(b, self.ssem.at[0], b).wait_recv()
        return b

    def same_core(self, k):
        b = lax.rem(self.zc + self.chips - k, self.chips) * 2 + self.co
        self.copy(b, self.fsem.at[k], b).wait_recv()
        self.copy(b, self.fsem.at[k], self.zc * 2 + 1 - self.co).start()
        return b

    def other_core(self, k):
        b = lax.rem(self.zc + self.chips - k, self.chips) * 2 + 1 - self.co
        self.copy(b, self.fsem.at[k], b).wait_recv()
        return b

    def finish(self):
        for k in range(self.chips):
            self.copy(self.t, self.ssem.at[k], self.t).wait_send()
        for k in range(1, self.chips):
            self.copy(self.t, self.fsem.at[k], self.t).wait_send()


class Gather:
    def __init__(self, tn, tocore, fromcore, toici, fromici, sems):
        self.tn = tn
        self.tocore, self.fromcore, self.toici, self.fromici = tocore, fromcore, toici, fromici
        self.cs, self.cr, self.ls, self.lr = sems
        self.t = lax.axis_index("t")
        self.zc, self.co = self.t // 2, lax.rem(self.t, 2)
        self.chips = tn // 2

    def core_copy(self, chip):
        return pltpu.make_async_remote_copy(
            self.tocore.at[chip],
            self.fromcore.at[chip],
            self.cs.at[chip],
            self.cr.at[chip],
            device_id={"t": self.zc * 2 + 1 - self.co},
            device_id_type=MESH,
        )

    def link_copy(self, chip, slot):
        return pltpu.make_async_remote_copy(
            self.toici.at[chip],
            self.fromici.at[slot],
            self.ls.at[chip],
            self.lr.at[slot],
            device_id={"t": chip * 2 + self.co},
            device_id_type=MESH,
        )

    def send_core(self, chip):
        self.core_copy(chip).start()

    def send_link(self, chip):
        self.core_copy(chip).wait_recv()
        self.toici[chip] = (self.toici[chip].astype(F32) + self.fromcore[chip].astype(F32)).astype(BF16)
        self.link_copy(chip, self.zc).start()

    def total(self):
        self.core_copy(self.zc).wait_recv()
        value = self.fromcore[self.zc].astype(F32)
        for k in range(1, self.chips):
            chip = lax.rem(self.zc + k, self.chips)
            self.link_copy(chip, chip).wait_recv()
            value = value + self.fromici[chip].astype(F32)
        return value

    def finish(self):
        for chip in range(self.chips):
            self.core_copy(chip).wait_send()
        for k in range(1, self.chips):
            chip = lax.rem(self.zc + k, self.chips)
            self.link_copy(chip, self.zc).wait_send()


def norm_stats(x):
    mean = jnp.mean(x, axis=-1, keepdims=True)
    centred = x - mean
    inverse = lax.rsqrt(jnp.mean(centred * centred, axis=-1, keepdims=True) + EPSILON)
    return centred * inverse, inverse


def widen(tab, width):
    return jnp.concatenate([tab] * (width // tab.shape[1]), axis=1)


def turn(x, cos, sine, sign):
    width = x.shape[1]
    cos, sine = widen(cos, width), widen(sine, width)
    front = lax.rem(lax.broadcasted_iota(jnp.int32, (1, width), 1), HD) < ROT // 2
    partner = jnp.where(front, pltpu.roll(x, width - ROT // 2, 1), pltpu.roll(x, ROT // 2, 1))
    return x * cos + sign * (partner * sine)


def head_masks(width, dtype):
    lane = lax.broadcasted_iota(jnp.int32, (1, width), 1) // HD
    return [(lane == h).astype(F32).astype(dtype) for h in range(width // HD)]


def pair_bias(qb, kb, size, segcol, segrow):
    qpos = lax.broadcasted_iota(jnp.int32, (size, size), 0) + qb * size
    kpos = lax.broadcasted_iota(jnp.int32, (size, size), 1) + kb * size
    same = segcol[rows_of(qb, size), :] == segrow[:, rows_of(kb, size)]
    return jnp.where(same & (kpos <= qpos), 0.0, NEG_LARGE)


TILE = 256
SKEW = 1


class Forward:
    def __init__(self, tn, size, x, w, vecs, segs, tables, kept, keep):
        self.tn, self.size, self.chips = tn, size, tn // 2
        self.x, self.keep = x, keep
        self.wt, self.wi, self.wo, self.wp = w
        self.vec, self.bt, self.bi = vecs
        self.segcol, self.segrow = segs
        self.tables = tables
        self.n, self.q, self.k, self.v, self.o, self.lse, self.g, self.gp = kept
        self.width, self.units = self.q.shape[1], self.g.shape[1]
        self.heads = self.width // HD

    def norm(self, t):
        own, _ = norm_stats(self.x[...])
        self.n[rows_of(t, self.size), :] = own.astype(BF16)

    def heads_in(self, b):
        width, vec, bt = self.width, self.vec, self.bt
        rows = rows_of(b, self.size)
        h1 = (self.n[rows, :].astype(F32) * vec[0:1, :] + vec[1:2, :]).astype(BF16)
        cos, sine = (tab[rows, :] for tab in self.tables)
        q = dot(h1, self.wt[:, 0:width], NN) + bt[:, 0:width]
        low = turn(q, cos, sine, 1.0).astype(BF16).astype(F32)
        self.q[rows, :] = (low * (1.0 / math.sqrt(HD))).astype(BF16)
        k = dot(h1, self.wt[:, width : 2 * width], NN) + bt[:, width : 2 * width]
        self.k[rows, :] = turn(k, cos, sine, 1.0).astype(BF16)
        v = dot(h1, self.wt[:, 2 * width : 3 * width], NN) + bt[:, 2 * width : 3 * width]
        self.v[rows, :] = v.astype(BF16)

    def mixer_in(self, b, blocks=1):
        rows = rows_of(b, self.size * blocks)
        h2 = (self.n[rows, :].astype(F32) * self.vec[2:3, :] + self.vec[3:4, :]).astype(BF16)

        def mix(j, carry):
            cols = rows_of(j, TILE)
            u = dot(h2, self.wi[:, cols], NN) + self.bi[:, cols]
            half = 0.5 + 0.5 * lax.erf(u * (1.0 / math.sqrt(2.0)))
            self.g[rows, cols] = (u * half).astype(BF16)
            bell = jnp.exp(-0.5 * u * u) * (1.0 / math.sqrt(2.0 * math.pi))
            self.gp[rows, cols] = (half + u * bell).astype(BF16)
            return carry

        lax.fori_loop(0, self.units // TILE, mix, 0)

    def attend(self, b):
        size, width, heads = self.size, self.width, self.heads
        masks = head_masks(width, F32)
        lane = lax.broadcasted_iota(jnp.int32, (1, 128), 1)
        rows = rows_of(b, size)
        qb = self.q[rows, :]
        qs = [qb * masks[h].astype(BF16) for h in range(heads)]

        def step(i, carry):
            peaks, sums, acc = carry
            kb = b - i
            keys = self.k[rows_of(kb, size), :]
            vals = self.v[rows_of(kb, size), :]
            bias = pair_bias(b, kb, size, self.segcol, self.segrow)
            new_peaks, new_sums = [], []
            scale = jnp.zeros((size, width), F32)
            add = jnp.zeros((size, width), F32)
            for h in range(heads):
                s = dot(qs[h], keys, NT) + bias
                peak = jnp.maximum(peaks[h], jnp.max(s, axis=1, keepdims=True))
                p = jnp.exp(s - peak)
                fade = jnp.exp(peaks[h] - peak)
                new_peaks.append(peak)
                new_sums.append(sums[h] * fade + jnp.sum(p, axis=1, keepdims=True))
                scale = scale + fade * masks[h]
                add = add + dot(p.astype(BF16), vals * masks[h].astype(BF16), NN)
            return tuple(new_peaks), tuple(new_sums), acc * scale + add

        start = (
            tuple(jnp.full((size, 1), NEG_LARGE, F32) for _ in range(heads)),
            tuple(jnp.zeros((size, 1), F32) for _ in range(heads)),
            jnp.zeros((size, width), F32),
        )
        peaks, sums, acc = lax.fori_loop(0, b + 1, step, start)
        scale = jnp.zeros((size, width), F32)
        lse = jnp.zeros((size, 128), F32)
        for h in range(heads):
            scale = scale + (1.0 / sums[h]) * masks[h]
            lse = jnp.where(lane == h, peaks[h] + jnp.log(sums[h]), lse)
        self.lse[rows, :] = lse
        self.o[rows, :] = acc * scale

    def branches(self, b, store):
        rows = rows_of(b, self.size)

        def part(j, carry):
            cols = rows_of(j, TILE)
            value = dot(self.g[rows, :], self.wo[:, cols], NN)
            store(cols, value + dot(self.o[rows, :].astype(BF16), self.wp[:, cols], NN))
            return carry

        lax.fori_loop(0, self.x.shape[1] // TILE, part, 0)

    def into(self, ref, chip):
        def store(cols, value):
            ref[chip, :, cols] = value.astype(BF16)

        return store

    def into_keep(self, cols, value):
        self.keep[:, cols] = value


def arrivals(spread):
    yield spread.t
    yield spread.peer_core()
    for i in range(1, spread.chips):
        yield spread.same_core(i)
        yield spread.other_core(i)


def far_first(spread):
    out = []
    for i in range(1, spread.chips):
        chip = lax.rem(spread.zc + i, spread.chips)
        out += [chip * 2 + 1 - spread.co, chip * 2 + spread.co]
    return out + [spread.zc * 2 + 1 - spread.co, spread.t]


def branch_sums(layer, spread, gather, tick=lambda: None):
    for i in range(1, spread.chips):
        chip = lax.rem(spread.zc + i, spread.chips)
        layer.branches(chip * 2 + 1 - spread.co, layer.into(gather.tocore, chip))
        gather.send_core(chip)
        layer.branches(chip * 2 + spread.co, layer.into(gather.toici, chip))
        gather.send_link(chip)
        tick()
    layer.branches(spread.zc * 2 + 1 - spread.co, layer.into(gather.tocore, spread.zc))
    gather.send_core(spread.zc)
    layer.branches(spread.t, layer.into_keep)
    tick()


def forward_kernel(
    tn, size,
    x_ref, wt, wi, wo, wp, vec, bt, bi, segcol, segrow, ctab, stab,
    xo_ref, n_ref, q_ref, k_ref, v_ref, o_ref, lse_ref, g_ref, gp_ref,
    keep, tocore, fromcore, toici, fromici, ssem, fsem, rsem, cs, cr, ls, lr,
):
    group_barrier(tn)
    spread = Spread(tn, n_ref, size, ssem, fsem, rsem)
    gather = Gather(tn, tocore, fromcore, toici, fromici, (cs, cr, ls, lr))
    layer = Forward(
        tn, size, x_ref, (wt, wi, wo, wp), (vec, bt, bi), (segcol, segrow), (ctab, stab),
        (n_ref, q_ref, k_ref, v_ref, o_ref, lse_ref, g_ref, gp_ref), keep,
    )
    layer.norm(spread.t)
    spread.start()
    for b in arrivals(spread):
        layer.heads_in(b)
        layer.mixer_in(b)
    for b in far_first(spread):
        layer.attend(b)
    branch_sums(layer, spread, gather)
    xo_ref[...] = x_ref[...] + vec[4:5, :] + keep[...] + gather.total()
    spread.finish()
    gather.finish()


def backward_kernel(
    tn, size,
    dy_ref, x_ref, wt, wi, wo, wp, vec, segcol, segrow, ctab, stab,
    n_ref, q_ref, k_ref, v_ref, o_ref, lse_ref, g_ref, gp_ref,
    dx_ref, dwt, dwi, dwo, dwp, dvec, dbt, dbi,
    gb, do, du, dt, dq, dk, dv, dh2, keep,
    tocore, fromcore, toici, fromici, ssem, fsem, rsem, cs, cr, ls, lr,
):
    chips = tn // 2
    width = q_ref.shape[1]
    heads = width // HD
    units = g_ref.shape[1]
    model = x_ref.shape[1]
    group_barrier(tn)
    spread = Spread(tn, gb, size, ssem, fsem, rsem)
    gather = Gather(tn, tocore, fromcore, toici, fromici, (cs, cr, ls, lr))
    t, zc, co = spread.t, spread.zc, spread.co
    own = dy_ref[...].astype(F32).astype(BF16)
    gb[rows_of(t, size), :] = own
    spread.start()
    dvec[...] = jnp.zeros_like(dvec)
    dbt[...] = jnp.zeros_like(dbt)
    dbi[...] = jnp.zeros_like(dbi)
    dvec[4:5, :] = jnp.sum(own.astype(F32), axis=0, keepdims=True)
    dq[...] = jnp.zeros_like(dq)
    dk[...] = jnp.zeros_like(dk)
    dv[...] = jnp.zeros_like(dv)

    def mixer(b):
        rows = rows_of(b, size)
        grad = gb[rows, :]
        do[rows, :] = dot(grad, wp[...], NT).astype(BF16)

        def unit(j, carry):
            cols = rows_of(j, TILE)
            d = (dot(grad, wo[cols, :], NT) * gp_ref[rows, cols].astype(F32)).astype(BF16)
            du[rows, cols] = d
            dbi[0:1, cols] += jnp.sum(d.astype(F32), axis=0, keepdims=True)
            return carry

        lax.fori_loop(0, units // TILE, unit, 0)

        def back(j, carry):
            cols = rows_of(j, TILE)
            d = dot(du[rows, :], wi[cols, :], NT)
            dvec[2:3, cols] += jnp.sum(d * n_ref[rows, cols].astype(F32), axis=0, keepdims=True)
            dvec[3:4, cols] += jnp.sum(d, axis=0, keepdims=True)
            dh2[rows, cols] = d * vec[2:3, cols]
            return carry

        lax.fori_loop(0, model // TILE, back, 0)

    mixer(t)
    mixer(spread.peer_core())
    for i in range(1, chips):
        mixer(spread.same_core(i))
        mixer(spread.other_core(i))

    masks = head_masks(width, BF16)
    lane = lax.broadcasted_iota(jnp.int32, (1, 128), 1)
    up = zc >= (chips + 1) // 2
    tsize = tn

    def pair(qb, kb):
        qrows, krows = rows_of(qb, size), rows_of(kb, size)
        q, keys, vals = q_ref[qrows, :], k_ref[krows, :], v_ref[krows, :]
        grad = do[qrows, :]
        prod = grad.astype(F32) * o_ref[qrows, :]
        lse = lse_ref[qrows, :]
        bias = pair_bias(qb, kb, size, segcol, segrow)
        dq_new = jnp.zeros((size, width), F32)
        dk_new = jnp.zeros((size, width), F32)
        dv_new = jnp.zeros((size, width), F32)
        for h in range(heads):
            qh, gh = q * masks[h], grad * masks[h]
            total = jnp.sum(jnp.where(lane == h, lse, 0.0), axis=1, keepdims=True)
            delta = jnp.sum(prod * masks[h].astype(F32), axis=1, keepdims=True)
            p = jnp.exp(dot(qh, keys, NT) + bias - total)
            ds = (p * (dot(gh, vals, NT) - delta)).astype(BF16)
            dv_new = dv_new + dot(p.astype(BF16), gh, TN)
            dk_new = dk_new + dot(ds, qh, TN)
            dq_new = dq_new + dot(ds, keys * masks[h], NN)
        dq[qrows, :] += dq_new
        dk[krows, :] += dk_new
        dv[krows, :] += dv_new

    def attend_back(stage):
        pivot = jnp.where(up, stage, tsize - 1 - stage)

        def step(j, carry):
            pair(jnp.where(up, pivot + j, pivot), jnp.where(up, pivot, pivot - j))
            return carry

        lax.fori_loop(0, tsize - stage, step, 0)
        rows = rows_of(pivot, size)
        cos, sine = ctab[rows, :], stab[rows, :]
        dt[rows, 0:width] = turn(dq[rows, :] * (1.0 / math.sqrt(HD)), cos, sine, -1.0).astype(BF16)
        dt[rows, width : 2 * width] = turn(dk[rows, :], cos, sine, -1.0).astype(BF16)
        dt[rows, 2 * width : 3 * width] = dv[rows, :].astype(BF16)
        block = dt[rows, :]
        dbt[...] += jnp.sum(block.astype(F32), axis=0, keepdims=True)

        def back(j, carry):
            cols = rows_of(j, TILE)
            d = dot(block, wt[cols, :], NT)
            dvec[0:1, cols] += jnp.sum(d * n_ref[rows, cols].astype(F32), axis=0, keepdims=True)
            dvec[1:2, cols] += jnp.sum(d, axis=0, keepdims=True)
            dh2[rows, cols] = dh2[rows, cols] + d * vec[0:1, cols]
            return carry

        lax.fori_loop(0, model // TILE, back, 0)
        value = dh2[rows, :]
        chip, core = pivot // 2, lax.rem(pivot, 2)

        @pl.when(core != co)
        def _():
            tocore[chip] = value.astype(BF16)
            gather.send_core(chip)

        @pl.when((core == co) & (chip != zc))
        def _():
            toici[chip] = value.astype(BF16)

        @pl.when(pivot == t)
        def _():
            keep[...] = value

        if stage % 2 == 1:

            @pl.when(chip != zc)
            def _():
                gather.send_link(chip)

    for stage in range(tn):
        attend_back(stage)

    def grad_one(j, carry):
        cols = rows_of(j, TILE)
        h1 = (n_ref[:, cols].astype(F32) * vec[0:1, cols] + vec[1:2, cols]).astype(BF16)
        dwt[cols, :] = dot(h1, dt[...], TN).astype(dwt.dtype)
        return carry

    lax.fori_loop(0, model // TILE, grad_one, 0)

    def grad_two(j, carry):
        cols = rows_of(j, TILE)
        h2 = (n_ref[:, cols].astype(F32) * vec[2:3, cols] + vec[3:4, cols]).astype(BF16)
        dwi[cols, :] = dot(h2, du[...], TN).astype(dwi.dtype)
        return carry

    lax.fori_loop(0, model // TILE, grad_two, 0)

    def grad_three(j, carry):
        cols = rows_of(j, TILE)
        dwo[cols, :] = dot(g_ref[:, cols], gb[...], TN).astype(dwo.dtype)
        return carry

    lax.fori_loop(0, units // TILE, grad_three, 0)
    small = min(TILE, width)

    def grad_four(j, carry):
        cols = rows_of(j, small)
        dwp[cols, :] = dot(o_ref[:, cols].astype(BF16), gb[...], TN).astype(dwp.dtype)
        return carry

    lax.fori_loop(0, width // small, grad_four, 0)

    own_n, inverse = norm_stats(x_ref[...])
    e = keep[...] + gather.total()
    inner = e - jnp.mean(e, axis=-1, keepdims=True) - own_n * jnp.mean(e * own_n, axis=-1, keepdims=True)
    dx_ref[...] = dy_ref[...].astype(F32) + inner * inverse
    spread.finish()
    gather.finish()


VM = pl.BlockSpec(memory_space=pltpu.VMEM)


def shape(dims, dtype):
    return jax.ShapeDtypeStruct(tuple(dims), dtype)


def group_sems(chips, tn):
    dma = pltpu.SemaphoreType.DMA
    return [dma((chips,)), dma((chips,)), dma((tn,)), dma((chips,)), dma((chips,)), dma((chips,)), dma((chips,))]


def group_buffers(chips, size, model):
    return [pltpu.VMEM((chips, size, model), BF16) for _ in range(4)]


def params_of(cid):
    return pltpu.CompilerParams(collective_id=cid, has_side_effects=True, vmem_limit_bytes=VMEM_LIMIT)


def forward_layer(tn, x, weights, vec, bt, bi, tables):
    wt, wi, wo, wp = weights
    size, model = x.shape
    length = size * tn
    width, units, chips = wp.shape[0], wo.shape[0], tn // 2
    outs = (
        shape((size, model), F32),
        shape((length, model), BF16),
        shape((length, width), BF16),
        shape((length, width), BF16),
        shape((length, width), BF16),
        shape((length, width), F32),
        shape((length, 128), F32),
        shape((length, units), BF16),
        shape((length, units), BF16),
    )
    return pl.pallas_call(
        functools.partial(forward_kernel, tn, size),
        out_shape=outs,
        in_specs=[VM] * 12,
        out_specs=[VM] * len(outs),
        scratch_shapes=[pltpu.VMEM((size, model), F32)] + group_buffers(chips, size, model) + group_sems(chips, tn),
        compiler_params=params_of(0),
        name="forward",
    )(x, wt, wi, wo, wp, vec, bt, bi, *tables)


def backward_layer(tn, dy, x, weights, vec, tables, kept):
    wt, wi, wo, wp = weights
    size, model = x.shape
    length = size * tn
    width, units, chips = wp.shape[0], wo.shape[0], tn // 2
    outs = (
        shape((size, model), F32),
        shape(wt.shape, BF16),
        shape(wi.shape, BF16),
        shape(wo.shape, BF16),
        shape(wp.shape, BF16),
        shape((8, model), F32),
        shape((1, 3 * width), F32),
        shape((1, units), F32),
    )
    return pl.pallas_call(
        functools.partial(backward_kernel, tn, size),
        out_shape=outs,
        in_specs=[VM] * 19,
        out_specs=[VM] * len(outs),
        scratch_shapes=[
            pltpu.VMEM((length, model), BF16),
            pltpu.VMEM((length, width), BF16),
            pltpu.VMEM((length, units), BF16),
            pltpu.VMEM((length, 3 * width), BF16),
            pltpu.VMEM((length, width), F32),
            pltpu.VMEM((length, width), F32),
            pltpu.VMEM((length, width), F32),
            pltpu.VMEM((length, model), F32),
            pltpu.VMEM((size, model), F32),
        ]
        + group_buffers(chips, size, model)
        + group_sems(chips, tn),
        compiler_params=params_of(1),
        name="backward",
    )(dy, x, wt, wi, wo, wp, vec, *tables, *kept)


class Place:
    def __init__(self, gn, tn):
        self.gn, self.tn = gn, tn
        self.h, self.t = lax.axis_index("h"), lax.axis_index("t")
        self.g = lax.axis_index("dp") * 2 + self.h
        self.c = self.h * tn + self.t
        self.bits = [1 << i for i in range(gn.bit_length() - 1)]

    def group(self, g):
        return {"dp": g // 2, "h": lax.rem(g, 2)}

    def line(self, c):
        return {"h": c // self.tn, "t": lax.rem(c, self.tn)}

    def other(self, k):
        return lax.rem(self.t + k, self.tn)


def flip(value, bit):
    return value + bit * (1 - 2 * lax.rem(value // bit, 2))


def remote(src, dst, send, recv, device):
    return pltpu.make_async_remote_copy(src, dst, send, recv, device_id=device, device_id_type=MESH)


def runs_by_step(place, bits):
    runs, steps = [(place.g, 1)], []
    for bit in bits:
        steps.append((bit, runs))
        if len(runs) == 1 and runs[0][1] == bit:
            runs = [(runs[0][0] // (2 * bit) * (2 * bit), 2 * bit)]
        else:
            runs = runs + [(flip(start, bit), count) for start, count in runs]
    return steps


def bit_orders(place):
    bits = place.bits
    return [bits, bits[:1] + bits[:0:-1]]


class Doubling:
    def __init__(self, place, ref, block, cols, order, sems, slot):
        self.place, self.ref, self.block, self.cols, self.order = place, ref, block, cols, order
        self.send, self.recv, self.slot = sems[0], sems[1], slot
        self.levels = [[] for _ in order]
        for i, bit in enumerate(order):
            for bits in range(1 << i):
                held = [order[j] for j in range(i) if bits >> j & 1]
                self.levels[len(held)].append((bit, held))

    def at(self, held):
        g = self.place.g
        for bit in held:
            g = flip(g, bit)
        return g

    def copy(self, bit, held):
        start = self.at(held)
        rows = pl.ds(pl.multiple_of(start * self.block, self.block), self.block)
        ref = self.ref.at[rows, self.cols]
        index = sum(held) + bit
        return remote(
            ref,
            ref,
            self.send.at[self.slot, index],
            self.recv.at[self.slot, index],
            self.place.group(flip(self.place.g, bit)),
        )

    def arrive(self, held):
        start = self.at(held)
        rows = pl.ds(pl.multiple_of(start * self.block, self.block), self.block)
        ref = self.ref.at[rows, self.cols]
        index = sum(held)
        peer = self.place.group(flip(self.place.g, held[-1]))
        remote(ref, ref, self.send.at[self.slot, index], self.recv.at[self.slot, index], peer).wait_recv()

    def advance(self, level):
        seen = set()
        for bit, held in self.levels[level]:
            if held and tuple(held) not in seen:
                seen.add(tuple(held))
                self.arrive(held)
            self.copy(bit, held).start()

    def whole(self):
        last = self.order[-1]
        for level in self.levels:
            for bit, held in level:
                if bit == last:
                    self.arrive(held + [bit])

    def finish(self):
        for level in self.levels:
            for item in level:
                self.copy(*item).wait_send()


def halves(cols):
    return [pl.ds(0, cols // 2), pl.ds(cols // 2, cols // 2)]


def line_barrier(place, extra):
    sem = pltpu.get_barrier_semaphore()
    span = 2 * place.tn
    for k in range(1, span):
        pl.semaphore_signal(sem, inc=1, device_id=place.line(lax.rem(place.c + k, span)), device_id_type=MESH)
    for bit in place.bits[1:]:
        pl.semaphore_signal(sem, inc=1, device_id=place.group(flip(place.g, bit)), device_id_type=MESH)
    peers = span - 1 + len(place.bits) - 1
    source, moved = extra

    @pl.when(moved)
    def _():
        pl.semaphore_signal(sem, inc=1, device_id=source, device_id_type=MESH)
        pl.semaphore_wait(sem, peers + 1)

    @pl.when(jnp.logical_not(moved))
    def _():
        pl.semaphore_wait(sem, peers)


def proj_places(place):
    gn, tn = place.gn, place.tn
    r = place.g * tn + place.t
    target = place.group(lax.rem(r, gn)) | {"t": r // gn}
    q = place.t * gn + place.g
    source = place.group(q // tn) | {"t": lax.rem(q, tn)}
    return target, source, r, q


def slot_rows(index, size):
    return pl.ds(pl.multiple_of(index * size, size), size)


class Opening:
    def __init__(self, place, layers, tok, cot, seg, vec, tri, inn, outer, proj, tok_o, cot_o, seg_o, vec_o, w, sems):
        self.place, self.layers = place, layers
        self.tok, self.cot, self.seg, self.vec = tok, cot, seg, vec
        self.tri, self.inn, self.outer, self.proj = tri, inn, outer, proj
        self.tok_o, self.cot_o, self.seg_o, self.vec_o = tok_o, cot_o, seg_o, vec_o
        self.wts, self.wis, self.wos, self.wps = w
        (
            self.ssem, self.rsem, self.lsem, self.asend, self.arecv, self.psend, self.precv,
            self.msend, self.mrecv, self.gsend, self.grecv,
        ) = sems
        self.half = tok.shape[1]
        self.target, self.source, self.r, self.q = proj_places(place)
        self.moved = self.q != self.r
        self.local, self.sends, self.shared_with = [], [], {}
        self.locals_of = {}

    def barrier(self):
        line_barrier(self.place, (self.source, self.moved))

    def near(self, src, dst, key):
        cp = pltpu.make_async_copy(src, dst, self.lsem.at[len(self.local)])
        cp.start()
        self.local.append(cp)
        self.locals_of[key] = cp

    def hop(self, src, dst, slot, i):
        c, tn = self.place.c, self.place.tn
        to = i * tn + c // 2
        rows = slot_rows(lax.rem(c, 2), self.half)
        near = pltpu.make_async_copy(src.at[i], dst.at[rows], self.msend.at[slot, i])
        far = remote(
            src.at[i], dst.at[rows], self.msend.at[slot, i], self.mrecv.at[slot, lax.rem(c, 2)],
            self.place.line(to),
        )
        return to == c, near, far

    def move(self, src, dst, slot):
        for i in range(2):
            stays, near, far = self.hop(src, dst, slot, i)
            pl.when(stays)(near.start)
            pl.when(jnp.logical_not(stays))(far.start)

    def moved_in(self, src, dst, slot):
        for i in range(2):
            stays, near, far = self.hop(src, dst, slot, i)
            pl.when(stays)(near.wait)
            pl.when(jnp.logical_not(stays))(far.wait_send)
        for s in range(2):
            cp = remote(
                src.at[0], dst.at[pl.ds(s * self.half, self.half)], self.msend.at[slot, 0],
                self.mrecv.at[slot, s], self.place.line(self.place.c),
            )
            pl.when(2 * self.place.t + s != self.place.c)(cp.wait_recv)

    def share(self, key, src_of, dst, size, slot):
        g, t, tn = self.place.g, self.place.t, self.place.tn
        rows = slot_rows(g * tn + t, size)
        self.near(src_of(t), dst.at[rows], key)
        for k in range(1, tn):
            to = self.place.other(k)
            cp = remote(src_of(to), dst.at[rows], self.asend.at[slot, k], self.arecv.at[slot, t], {"t": to})
            cp.start()
            self.sends.append(cp)
        self.shared_with[key] = (dst, size, slot)

    def shared(self, key):
        dst, size, slot = self.shared_with[key]
        self.locals_of[key].wait()
        for k in range(1, self.place.tn):
            frm = self.place.other(k)
            ref = dst.at[slot_rows(self.place.g * self.place.tn + frm, size)]
            remote(ref, ref, self.asend.at[slot, k], self.arecv.at[slot, frm], {"t": frm}).wait_recv()

    def share_layer(self, layer):
        depth = self.tri.shape[2]
        base = 1 + 2 * layer
        self.share(("t", layer), lambda to: self.tri.at[layer, to], self.wts[layer], depth, base)
        self.share(("i", layer), lambda to: self.inn.at[layer, to], self.wis[layer], depth, base + 1)
        g = self.place.g
        self.near(self.outer.at[layer], self.wos[layer].at[slot_rows(g, self.outer.shape[1])], ("o", layer))
        here, far = self.proj_copies(layer)
        pl.when(self.moved)(far.start)
        pl.when(jnp.logical_not(self.moved))(here.start)

    def proj_copies(self, layer):
        prows = self.proj.shape[1]
        src = self.proj.at[layer]
        here = pltpu.make_async_copy(src, self.wps[layer].at[slot_rows(self.place.g, prows)], self.psend.at[layer])
        dst = self.wps[layer].at[slot_rows(lax.rem(self.r, self.place.gn), prows)]
        return here, remote(src, dst, self.psend.at[layer], self.precv.at[layer], self.target)

    def proj_ready(self, layer):
        here, far = self.proj_copies(layer)

        @pl.when(self.moved)
        def _():
            far.wait_recv()
            far.wait_send()

        pl.when(jnp.logical_not(self.moved))(here.wait)

    def start(self):
        place, span = self.place, 2 * self.place.tn
        self.move(self.tok, self.tok_o, 0)
        vec_rows = self.vec.shape[0]
        self.share("v", lambda to: self.vec, self.vec_o, vec_rows, 0)
        self.near(self.seg, self.seg_o.at[slot_rows(place.c, 8)], "s")
        for k in range(1, span):
            to = lax.rem(place.c + k, span)
            dst = self.seg_o.at[slot_rows(place.c, 8)]
            cp = remote(self.seg, dst, self.gsend.at[k], self.grecv.at[place.c], place.line(to))
            cp.start()
            self.sends.append(cp)
        self.share_layer(0)
        orders = bit_orders(place)
        self.chunks, slot = [], 0
        tn, depth = place.tn, self.tri.shape[2]
        todo = []
        for layer in range(self.layers):
            todo += [
                [(("t", layer), self.wts[layer], tn * depth)],
                [(("i", layer), self.wis[layer], tn * depth)],
                [
                    (("o", layer), self.wos[layer], self.outer.shape[1]),
                    (("p", layer), self.wps[layer], self.proj.shape[1]),
                ],
            ]
        todo[0].insert(0, ("v", self.vec_o, tn * vec_rows))
        self.keys = [[key for key, _, _ in chunk] for chunk in todo]
        for chunk in todo:
            parts = []
            for _, ref, block in chunk:
                pieces = halves(ref.shape[1]) if ref.shape[1] >= 256 else [pl.ds(0, ref.shape[1])]
                for i, piece in enumerate(pieces):
                    parts.append(Doubling(place, ref, block, piece, orders[i], (self.ssem, self.rsem), slot))
                    slot += 1
            self.chunks.append(parts)
        self.steps = len(place.bits)
        self.turn, self.turns = 0, len(self.chunks) + SKEW * (self.steps - 1)
        self.complete = set()

    def ready(self, i):
        for key in self.keys[i]:
            if key == "v" or key[0] in ("t", "i"):
                self.shared(key)
            elif key[0] == "o":
                self.locals_of[key].wait()
            else:
                self.proj_ready(key[1])

    def tick(self, until=None):
        while self.turn < self.turns and (until is None or self.turn <= until):
            for step in reversed(range(self.steps)):
                i = self.turn - SKEW * step
                if 0 <= i < len(self.chunks):
                    if step == 0:
                        self.ready(i)
                    for part in self.chunks[i]:
                        part.advance(step)
            self.turn += 1
            if until is None:
                break

    def have(self, key):
        i = [key in keys for keys in self.keys].index(True)
        if i not in self.complete:
            self.complete.add(i)
            self.tick(i + SKEW * (self.steps - 1))
            for part in self.chunks[i]:
                part.whole()

    def segments_in(self):
        place, span = self.place, 2 * self.place.tn
        self.locals_of["s"].wait()
        for k in range(1, span):
            frm = lax.rem(place.c + k, span)
            ref = self.seg_o.at[slot_rows(frm, 8)]
            remote(ref, ref, self.gsend.at[k], self.grecv.at[frm], place.line(frm)).wait_recv()

    def finish(self):
        self.tick(self.turns)
        for parts in self.chunks:
            for part in parts:
                part.finish()
        for cp in self.sends:
            cp.wait_send()


def ascend_kernel(
    gn, tn, layers, size,
    tok, cot, seg, vec, tri, inn, outer, proj, ctab, stab, e32, m32, e96, m96,
    gb_o, segcol, segrow, vecs_o, bts_o, bis_o, xs_o, w_o, kept_o,
    w, kept, xs, x_low, cot_low, gb, keep, seg_in, vec_in, vec_wide, bt_wide,
    bufs, group, opening_sems, save_sem, tok_sem,
):
    place = Place(gn, tn)
    opening = Opening(
        place, layers, tok, cot, seg, vec, tri, inn, outer, proj, x_low, cot_low, seg_in, vec_in, w, opening_sems
    )
    opening.barrier()
    opening.start()
    saves = []

    def save(src, dst):
        cp = pltpu.make_async_copy(src, dst, save_sem.at[len(saves)])
        cp.start()
        saves.append(cp)

    opening.tick(0)
    opening.moved_in(tok, x_low, 0)
    xs[0][...] = x_low[...].astype(F32)
    spreads, gathers, stages = [], [], []
    for layer in range(layers):
        ssem, fsem, rsem, cs, cr, ls, lr = group[layer]
        spreads.append(Spread(tn, kept[layer][0], size, ssem, fsem, rsem))
        gathers.append(Gather(tn, *bufs, (cs, cr, ls, lr)))
        stages.append(
            Forward(
                tn, size, xs[layer], tuple(w[k][layer] for k in range(4)),
                (vecs_o.at[layer], bts_o.at[layer], bis_o.at[layer]), (segcol, segrow), (ctab, stab),
                kept[layer], keep,
            )
        )
    stages[0].norm(place.t)
    spreads[0].start()
    opening.tick(1)
    for layer in range(1, layers):
        opening.share_layer(layer)
    opening.segments_in()
    block = segcol.shape[0] // (2 * tn)
    eye = lax.broadcasted_iota(jnp.int32, (block, block), 0) == lax.broadcasted_iota(jnp.int32, (block, block), 1)
    for i in range(2 * tn):
        row = jnp.where(place.h == 0, seg_in[8 * i : 8 * i + 1, :], seg_in[8 * i + 1 : 8 * i + 2, :])
        spot = lax.broadcasted_iota(jnp.int32, (1, block), 1) + i * block
        row = jnp.where(row == 0, -1 - spot, row).astype(F32)
        segrow[:, i * block : (i + 1) * block] = row
        segcol[i * block : (i + 1) * block, :] = jnp.sum(jnp.where(eye, row, 0.0), axis=1, keepdims=True)
    opening.have("v")
    shards = gn * tn
    vec_rows = vec.shape[0]
    vec_wide[...] = vec_in[...].astype(F32)
    lane = lax.broadcasted_iota(jnp.int32, (1, 128), 1)
    for layer in range(layers):

        def line(k):
            return vec_wide[pl.ds(4 * layer + k, shards, stride=vec_rows), :]

        def spread_out(value, place_of, mask):
            return jnp.sum(dot(value.astype(BF16), place_of, NN) * mask, axis=0, keepdims=True)

        thick = line(2)
        parts = [jnp.where(lane // 32 == i, thick, 0.0) for i in range(4)]
        thin = line(3)
        gains = [jnp.where(lane // 32 == i, thin, 0.0) for i in range(2)]
        rows = [spread_out(p, e32[...], m32[...]) for p in parts + gains]
        vecs_o[layer] = jnp.concatenate(
            [rows[2], rows[3], rows[4], rows[5], rows[0] + rows[1]] + [jnp.zeros_like(rows[0])] * 3, axis=0
        )
        bt_wide[...] = spread_out(line(1), e96[...], m96[...])
        wide = bts_o.shape[2] // 3
        for i in range(3):
            start = pl.multiple_of(i * wide * tn + place.t * wide, 128)
            bts_o[layer, :, i * wide : (i + 1) * wide] = bt_wide[:, pl.ds(start, wide)]
        for i in range(gn):
            bis_o[layer, :, i * 128 : (i + 1) * 128] = vec_wide[
                pl.ds((i * tn + place.t) * vec_rows + 4 * layer, 1), :
            ]

    for layer in range(layers):
        stage, spread, gather = stages[layer], spreads[layer], gathers[layer]
        if layer > 0:
            stage.norm(place.t)
            spread.start()
        opening.have(("t", layer))
        for i, b in enumerate(arrivals(spread)):
            stage.heads_in(b)
            if i == 1:
                opening.tick()
        if layer + 1 == layers:
            opening.moved_in(cot, cot_low, 1)
            gb[rows_of(place.t, size), :] = cot_low[...]
            ahead = Spread(tn, gb, size, *group[layers][:3])
            ahead.start()
        for i, b in enumerate(far_first(spread)):
            stage.attend(b)
            if i == 1:
                opening.tick()
        if layer == 0:
            opening.move(cot, cot_low, 1)
        opening.have(("i", layer))
        save(kept[layer][0], kept_o[layer][0])
        for i in range(1, 6):
            save(kept[layer][i], kept_o[layer][i])
        for i in range(spread.chips):
            stage.mixer_in(i, 2)
            if i == 0:
                opening.tick()
        save(kept[layer][6], kept_o[layer][6])
        save(kept[layer][7], kept_o[layer][7])
        save(xs[layer], xs_o[layer])
        if layer + 1 == layers:
            for _ in arrivals(ahead):
                pass
            save(gb, gb_o)
        opening.have(("o", layer))
        for k in range(4):
            save(w[k][layer], w_o[k][layer])
        if layer + 1 < layers:
            branch_sums(stage, spread, gather, opening.tick)
            xs[layer + 1][...] = xs[layer][...] + vecs_o[layer, 4:5, :] + keep[...] + gather.total()
            gather.finish()
        spread.finish()
    ahead.finish()
    opening.finish()
    for cp in saves:
        cp.wait()


ANY = pl.BlockSpec(memory_space=pl.ANY)


def constant_tables(span, shards, model):
    angle = np.arange(span, dtype=np.float32)[:, None] * (
        np.float32(10000.0) ** (-(2.0 * np.arange(ROT // 2, dtype=np.float32)) / np.float32(ROT))
    )
    cosine, sine = np.cos(angle).astype(np.float32), np.sin(angle).astype(np.float32)
    none = np.zeros((span, HD - ROT), np.float32)
    reps = 128 // HD
    ctab = np.concatenate([cosine, cosine, none + 1.0] * reps, axis=1)
    stab = np.concatenate([-sine, sine, none] * reps, axis=1)
    return tuple(jnp.asarray(tab, F32) for tab in (ctab, stab))


def placement(piece, shards):
    j, col = np.arange(128)[:, None], np.arange(piece * shards)[None, :]
    put = (j % piece == col % piece) if 128 % piece == 0 else (j == col % piece)
    mask = np.arange(shards)[:, None] == col // piece
    return jnp.asarray(put, BF16), jnp.asarray(mask, F32)


def kept_shapes(length, model, width, units):
    return [
        ((length, model), BF16),
        ((length, width), BF16),
        ((length, width), BF16),
        ((length, width), BF16),
        ((length, width), F32),
        ((length, 128), F32),
        ((length, units), BF16),
        ((length, units), BF16),
    ]


def ascend_call(gn, tn, tokens, cotangent, segments, vec, tri, inn, outer, proj, tables, placing):
    layers = outer.shape[0]
    _, half, model = tokens.shape
    size = 2 * half
    length = size * tn
    depth = tri.shape[2]
    wshapes = [
        (gn * tn * depth, tri.shape[3]), (gn * tn * depth, inn.shape[3]),
        (gn * outer.shape[1], model), (gn * proj.shape[1], model),
    ]
    width, units, chips = wshapes[3][0], wshapes[2][0], tn // 2
    kept = kept_shapes(length, model, width, units)
    dma = pltpu.SemaphoreType.DMA
    outs = [
        (shape((length, model), BF16), ANY),
        (shape((length, 1), F32), VM),
        (shape((1, length), F32), VM),
        (shape((layers, 8, model), F32), VM),
        (shape((layers, 1, 3 * width), F32), VM),
        (shape((layers, 1, units), F32), VM),
    ]
    outs += [(shape((size, model), F32), ANY)] * layers
    for dims in wshapes:
        outs += [(shape(dims, BF16), ANY)] * layers
    for _ in range(layers):
        outs += [(shape(*item), ANY) for item in kept]
    scratch = []
    for dims in wshapes:
        scratch += [pltpu.VMEM(dims, BF16)] * layers
    for _ in range(layers):
        scratch += [pltpu.VMEM(*item) for item in kept]
    scratch += [pltpu.VMEM((size, model), F32)] * layers
    scratch += [
        pltpu.VMEM((size, model), BF16),
        pltpu.VMEM((size, model), BF16),
        pltpu.VMEM((length, model), BF16),
        pltpu.VMEM((size, model), F32),
        pltpu.VMEM((2 * tn * 8, 128), jnp.int32),
        pltpu.VMEM((gn * tn * vec.shape[0], 128), BF16),
        pltpu.VMEM((gn * tn * vec.shape[0], 128), F32),
        pltpu.VMEM((1, 3 * model), F32),
    ]
    scratch += group_buffers(chips, size, model)
    for _ in range(layers + 1):
        scratch += group_sems(chips, tn)
    slots = 1 + 8 * layers
    scratch += [
        dma((slots, gn)), dma((slots, gn)), dma((2 + 3 * layers,)),
        dma((1 + 2 * layers, tn)), dma((1 + 2 * layers, tn)),
        dma((layers,)), dma((layers,)), dma((2, 2)), dma((2, 2)),
        dma((2 * tn,)), dma((2 * tn,)),
    ]
    scratch += [dma((14 * layers,)), dma((1,))]

    def body(*refs):
        refs = list(refs)

        def take(count):
            out, refs[:] = refs[:count], refs[count:]
            return out

        ins = take(14)
        gb_o, segcol, segrow, vecs_o, bts_o, bis_o = take(6)
        xs_o = take(layers)
        w_o = [take(layers) for _ in range(4)]
        kept_o = [take(8) for _ in range(layers)]
        w = [take(layers) for _ in range(4)]
        kept_s = [take(8) for _ in range(layers)]
        xs = take(layers)
        x_low, cot_low, gb, keep, seg_in, vec_in, vec_wide, bt_wide = take(8)
        bufs = take(4)
        group = [take(7) for _ in range(layers + 1)]
        sems = take(11)
        save_sem, tok_sem = take(2)
        ascend_kernel(
            gn, tn, layers, size, *ins, gb_o, segcol, segrow, vecs_o, bts_o, bis_o, xs_o, w_o, kept_o,
            w, kept_s, xs, x_low, cot_low, gb, keep, seg_in, vec_in, vec_wide, bt_wide, bufs, group, sems,
            save_sem, tok_sem,
        )

    return pl.pallas_call(
        body,
        out_shape=tuple(o for o, _ in outs),
        in_specs=[ANY] * 8 + [VM] * 6,
        out_specs=tuple(spec for _, spec in outs),
        scratch_shapes=scratch,
        compiler_params=params_of(2),
        name="ascend",
    )(tokens, cotangent, segments, vec, tri, inn, outer, proj, *tables, *placing)


class Halving:
    def __init__(self, place, acc, inbox, block, cols, order, sems, slot):
        self.place, self.acc, self.inbox, self.block, self.cols = place, acc, inbox, block, cols
        self.send, self.recv, self.slot = sems[0], sems[1], slot
        self.plan, index, base = [], 0, 0
        for bit, runs in reversed(runs_by_step(place, order)):
            entry = []
            for start, count in runs:
                entry.append((bit, start, count, index, base))
                index += 1
                base += count
            self.plan.append(entry)

    def copy(self, bit, start, count, index, base):
        rows = pl.ds(pl.multiple_of(flip(start, bit) * self.block, self.block), count * self.block)
        return remote(
            self.acc.at[rows, self.cols],
            self.inbox.at[pl.ds(base * self.block, count * self.block), self.cols],
            self.send.at[self.slot, index],
            self.recv.at[self.slot, index],
            self.place.group(flip(self.place.g, bit)),
        )

    def advance(self, step):
        if step > 0:
            for item in self.plan[step - 1]:
                self.copy(*item).wait_recv()
                _, start, count, _, base = item

                def add(i, carry):
                    rows = pl.ds(pl.multiple_of((start + i) * self.block, self.block), self.block)
                    came = pl.ds(pl.multiple_of((base + i) * self.block, self.block), self.block)
                    value = self.acc[rows, self.cols].astype(F32) + self.inbox[came, self.cols].astype(F32)
                    self.acc[rows, self.cols] = value.astype(BF16)
                    return carry

                lax.fori_loop(0, count, add, 0)
        if step < len(self.plan):
            for item in self.plan[step]:
                self.copy(*item).start()

    def finish(self):
        for entry in self.plan:
            for item in entry:
                self.copy(*item).wait_send()

class Slots:
    def __init__(self, ref, first, size):
        self.ref, self.first, self.size = ref, first, size

    def rows(self, slot):
        return slot_rows(self.first + slot, self.size)

    @property
    def at(self):
        return _SlotRefs(self)

    def __getitem__(self, slot):
        return self.ref[self.rows(slot), :]


class _SlotRefs:
    def __init__(self, slots):
        self.slots = slots

    def __getitem__(self, slot):
        return self.slots.ref.at[self.slots.rows(slot)]


class Reducing:
    def __init__(self, place, layers, accs, boxes, outs, sems):
        self.place, self.layers = place, layers
        self.accs, self.boxes = accs, boxes
        self.cross, self.proj_o, self.outer_o = outs[:2], outs[2], outs[3]
        self.hs, self.hr, self.cs, self.cr, self.ps, self.pr, self.os = sems
        self.target, self.source, self.r, self.q = proj_places(place)
        self.moved = self.q != self.r
        orders = bit_orders(place)
        self.parts, slot = {}, 0
        for layer in range(layers):
            for kind in range(4):
                acc = accs[kind][layer]
                parts = []
                for k, cols in enumerate(halves(acc.shape[1])):
                    box = boxes[kind].at[layer]
                    block = acc.shape[0] // place.gn
                    parts.append(Halving(place, acc, box, block, cols, orders[k], (self.hs, self.hr), slot))
                    slot += 1
                self.parts[kind, layer] = parts
        self.steps = len(place.bits) + 1
        self.taken = {key: 0 for key in self.parts}

    def advance(self, kind, layer):
        step = self.taken[kind, layer]
        self.taken[kind, layer] = step + 1
        for part in self.parts[kind, layer]:
            part.advance(step)
        if step == self.steps - 1:
            self.owned(kind, layer)

    def own_rows(self, kind, layer, index, pieces):
        acc = self.accs[kind][layer]
        rows = acc.shape[0] // pieces
        return acc.at[slot_rows(index, rows)]

    def cross_copy(self, kind, layer, k):
        place = self.place
        to = place.other(k)
        src = self.own_rows(kind, layer, place.g * place.tn + to, place.gn * place.tn)
        dst = self.cross[kind].at[layer, place.t]
        return remote(src, dst, self.cs.at[kind, layer, k], self.cr.at[kind, layer, place.t], {"t": to})

    def proj_copies(self, layer):
        src = self.own_rows(3, layer, self.place.g, self.place.gn)
        here = pltpu.make_async_copy(src, self.proj_o.at[layer], self.ps.at[layer])
        return here, remote(src, self.proj_o.at[layer], self.ps.at[layer], self.pr.at[layer], self.source)

    def own_copy(self, kind, layer):
        place = self.place
        if kind == 2:
            src, dst = self.own_rows(2, layer, place.g, place.gn), self.outer_o.at[layer]
        else:
            src = self.own_rows(kind, layer, place.g * place.tn + place.t, place.gn * place.tn)
            dst = self.cross[kind].at[layer, place.t]
        return pltpu.make_async_copy(src, dst, self.os.at[kind, layer])

    def owned(self, kind, layer):
        if kind < 3:
            self.own_copy(kind, layer).start()
        if kind < 2:
            for k in range(1, self.place.tn):
                self.cross_copy(kind, layer, k).start()
        if kind == 3:
            here, far = self.proj_copies(layer)
            pl.when(self.moved)(far.start)
            pl.when(jnp.logical_not(self.moved))(here.start)

    def finish(self):
        for (kind, layer), parts in self.parts.items():
            for part in parts:
                part.finish()
            if kind < 3:
                self.own_copy(kind, layer).wait()
            if kind < 2:
                for k in range(1, self.place.tn):
                    frm = self.place.other(k)
                    ref = self.cross[kind].at[layer, frm]
                    remote(
                        ref, ref, self.cs.at[kind, layer, k], self.cr.at[kind, layer, frm], {"t": frm}
                    ).wait_recv()
                    self.cross_copy(kind, layer, k).wait_send()
            if kind == 3:
                here, far = self.proj_copies(layer)
                pl.when(self.moved)(far.wait)
                pl.when(jnp.logical_not(self.moved))(here.wait)


FIRST = {
    "outer": ((2, 0), (3, 0)),
    "inner": ((1, 0),),
    "s1": ((2, 0), (3, 0)),
    "triple": ((0, 0), (1, 0)),
    "sum": ((2, 0), (3, 0)),
}
LATER = {
    "spread": ((0, 1),),
    "near": ((1, 1),),
    "arrived": ((2, 1), (3, 1), (0, 1)),
    "outer": ((2, 0), (3, 0), (1, 1)),
    "inner": ((1, 0), (0, 1)),
    "s1": ((2, 0), (3, 0)),
    "s3": ((2, 0), (3, 0), (1, 0)),
    "triple": ((0, 0), (1, 0)),
}


def descend_kernel(
    gn, tn, layers, size,
    grads, segcol, segrow, vecs, ctab, stab, xs, ws, kepts,
    out_o, grad_o, flat_o, triple_o, inner_o, proj_o, outer_o,
    w, kept, dy, x, gb, do, dt, dk, dv, keep, dbt, dbi, bufs, accs, boxes, flatbox,
    group, reduce_sems, load_sem, ms, mr, fs, fr,
):
    place = Place(gn, tn)
    g, t, c = place.g, place.t, place.c
    wt, wi, wo, wp = w
    n, q, k, v, o, lse, gact, gp = kept
    chips = tn // 2
    width, units, model = q.shape[1], gact.shape[1], dy.shape[1]
    heads = width // HD
    dq, dh, du = o, gact, gp
    loads = {}

    def load(layer, names):
        for name in names:
            if name == "x":
                src, dst = xs[layer], x
            elif name == "cot":
                src, dst = grads, gb
            elif name[0] == "w":
                i = int(name[1])
                src, dst = ws[i][layer], w[i]
            else:
                i = int(name[1])
                src, dst = kepts[layer][i], kept[i]
            cp = pltpu.make_async_copy(src, dst, load_sem.at[len(loads)])
            cp.start()
            loads[layer, name] = cp

    waited = set()

    def need(layer, names):
        for name in names:
            if (layer, name) not in waited:
                waited.add((layer, name))
                loads[layer, name].wait()

    last = layers - 1
    load(last, ["w2", "w3", "k6", "k4", "cot", "k7", "k5", "w1", "k0", "k1", "k2", "k3", "w0", "x"])
    reducing = Reducing(place, layers, accs, boxes, (triple_o, inner_o, proj_o, outer_o), reduce_sems)
    line_barrier(place, (reducing.target, reducing.moved))
    half = out_o.shape[1]

    def hop(src, dst, slot, s):
        to = 2 * t + s
        part = src.at[pl.ds(s * half, half)]
        near = pltpu.make_async_copy(part, dst.at[place.h], ms.at[slot, s])
        far = remote(part, dst.at[place.h], ms.at[slot, s], mr.at[slot, place.h], place.line(to))
        return to == c, near, far

    def move(src, dst, slot):
        for s in range(2):
            stays, near, far = hop(src, dst, slot, s)
            pl.when(stays)(near.start)
            pl.when(jnp.logical_not(stays))(far.start)

    def moved_in(src, dst, slot):
        for s in range(2):
            stays, near, far = hop(src, dst, slot, s)
            pl.when(stays)(near.wait)
            pl.when(jnp.logical_not(stays))(far.wait_send)
        for i in range(2):
            cp = remote(
                src.at[pl.ds(0, half)], dst.at[i], ms.at[slot, 0], mr.at[slot, i], place.line(c)
            )
            pl.when(i * tn + c // 2 != c)(cp.wait_recv)

    exchanges = [("g", bit) for bit in place.bits] + [("t", 1 << i) for i in range(tn.bit_length() - 1)]

    def exchange(layer, i):
        kind, bit = exchanges[i]
        to = place.group(flip(g, bit)) if kind == "g" else {"t": flip(t, bit)}
        return remote(flat_o.at[layer], flatbox.at[layer, i], fs.at[layer, i], fr.at[layer, i], to)

    def flat_turn(layer, i):
        if i > 0:
            exchange(layer, i - 1).wait()
            flat_o[layer] += flatbox[layer, i - 1]
        if i < len(exchanges):
            exchange(layer, i).start()

    masks = head_masks(width, BF16)
    lane = lax.broadcasted_iota(jnp.int32, (1, 128), 1)
    up = place.t // 2 >= (chips + 1) // 2

    def pair(qb, kb):
        qrows, krows = rows_of(qb, size), rows_of(kb, size)
        queries, keys, vals = q[qrows, :], k[krows, :], v[krows, :]
        grad = do[qrows, :]
        side = lse[qrows, :]
        bias = pair_bias(qb, kb, size, segcol, segrow)
        dq_new = jnp.zeros((size, width), F32)
        dk_new = jnp.zeros((size, width), F32)
        dv_new = jnp.zeros((size, width), F32)
        for h in range(heads):
            qh, gh = queries * masks[h], grad * masks[h]
            total = jnp.sum(jnp.where(lane == h, side, 0.0), axis=1, keepdims=True)
            delta = jnp.sum(jnp.where(lane == 64 + h, side, 0.0), axis=1, keepdims=True)
            p = jnp.exp(dot(qh, keys, NT) + bias - total)
            ds = (p * (dot(gh, vals, NT) - delta)).astype(BF16)
            dv_new = dv_new + dot(p.astype(BF16), gh, TN)
            dk_new = dk_new + dot(ds, qh, TN)
            dq_new = dq_new + dot(ds, keys * masks[h], NN)
        dq[qrows, :] += dq_new
        dk[krows, :] += dk_new
        dv[krows, :] += dv_new

    def columns(count, tile, body):
        def step(j, carry):
            body(rows_of(j, tile))
            return carry

        lax.fori_loop(0, count // tile, step, 0)

    need(last, ["w2", "w3", "k6", "k4"])
    top = Spread(tn, gb, size, *group[layers][:3])
    room, spare = accs[2][0], accs[1][0]
    top_gather = Gather(
        tn, bufs[0], Slots(room, 0, size), bufs[2], Slots(room, chips, size), tuple(group[layers][3:])
    )
    stage_top = Forward(
        tn, size, x, (wt, wi, wo, wp), (vecs.at[last], None, None), (segcol, segrow), (ctab, stab), kept, keep
    )
    branch_sums(stage_top, top, top_gather)
    need(last, ["cot"])
    dy[...] = gb[rows_of(t, size), :].astype(F32)
    flat_o[...] = jnp.zeros_like(flat_o)
    out_in = spare.at[pl.ds(0, size)]

    def give_output():
        need(last, ["x"])
        out_in[...] = (x[...] + vecs[last, 4:5, :] + keep[...] + top_gather.total()).astype(BF16)
        top_gather.finish()
        move(out_in, out_o, 0)

    for layer in reversed(range(layers)):
        flat = flat_o.at[layer]
        vec = vecs.at[layer]
        dwt, dwi, dwo, dwp = (accs[i][layer] for i in range(4))
        ssem, fsem, rsem, cs, cr, ls, lr = group[layer]
        spread = Spread(tn, gb, size, ssem, fsem, rsem)
        gather = Gather(tn, *bufs, (cs, cr, ls, lr))
        zc, co = spread.zc, spread.co

        def ticks(where, layer=layer):
            for kind, late in (FIRST if layer == last else LATER).get(where, ()):
                if layer + late < layers and reducing.taken[kind, layer + late] < reducing.steps:
                    reducing.advance(kind, layer + late)

        own = dy[...].astype(BF16)
        if layer < last:
            gb[rows_of(t, size), :] = own
            spread.start()
        flat[4:5, :] = jnp.sum(own.astype(F32), axis=0, keepdims=True)
        dbt[...] = jnp.zeros_like(dbt)
        dbi[...] = jnp.zeros_like(dbi)
        dk[...] = jnp.zeros_like(dk)
        dv[...] = jnp.zeros_like(dv)
        ticks("spread")
        if layer < last:
            flat_turn(layer + 1, 0)
        for count, b in enumerate(arrivals(spread) if layer < last else range(chips)):
            need(layer, ["w3", "k4", "w2", "k7", "k5"])
            rows = rows_of(b, size) if layer < last else rows_of(b, 2 * size)
            grad = gb[rows, :]
            heads_grad = dot(grad, wp[...], NT).astype(BF16)
            do[rows, :] = heads_grad
            prod = heads_grad.astype(F32) * o[rows, :]
            side = lse[rows, :]
            for h in range(heads):
                delta = jnp.sum(prod * masks[h].astype(F32), axis=1, keepdims=True)
                side = jnp.where(lane == 64 + h, delta, side)
            lse[rows, :] = side

            def unit(cols):
                d = (dot(grad, wo[cols, :], NT) * gp[rows, cols].astype(F32)).astype(BF16)
                du[rows, cols] = d
                dbi[0:1, cols] += jnp.sum(d.astype(F32), axis=0, keepdims=True)

            columns(units, TILE, unit)
            if layer < last:
                flat_turn(layer + 1, count + 1)
            if count == 1:
                ticks("near")
        ticks("arrived")
        need(layer, ["k6"])
        if layer < last:
            spread.finish()
            if layer == last - 1:
                moved_in(out_in, out_o, 0)

        def grad_outer(cols):
            dwo[cols, :] = dot(gact[:, cols], gb[...], TN).astype(BF16)

        columns(units, TILE, grad_outer)

        def grad_proj(cols):
            dwp[cols, :] = dot(o[:, cols].astype(BF16), gb[...], TN).astype(BF16)

        columns(width, TILE, grad_proj)
        if layer == last:
            give_output()
        ticks("outer")
        if layer < last:
            flat_turn(layer + 1, len(exchanges))
        need(layer, ["w1", "k0"])
        if layer > 0:
            load(layer - 1, ["w2", "w3"])
        dq[...] = jnp.zeros_like(dq)

        def back_mixer(cols):
            d = dot(du[...], wi[cols, :], NT)
            flat[2:3, cols] = jnp.sum(d * n[:, cols].astype(F32), axis=0, keepdims=True)
            flat[3:4, cols] = jnp.sum(d, axis=0, keepdims=True)
            dh[:, cols] = (d * vec[2:3, cols]).astype(BF16)

        columns(model, TILE, back_mixer)

        def grad_inner(cols):
            h2 = (n[:, cols].astype(F32) * vec[2:3, cols] + vec[3:4, cols]).astype(BF16)
            dwi[cols, :] = dot(h2, du[...], TN).astype(BF16)

        columns(model, TILE, grad_inner)
        ticks("inner")
        if layer > 0:
            load(layer - 1, ["w1", "k7"])
        need(layer, ["k1", "k2", "k3", "w0"])

        for stage in range(tn):
            pivot = jnp.where(up, stage, tn - 1 - stage)

            def step(j, carry):
                pair(jnp.where(up, pivot + j, pivot), jnp.where(up, pivot, pivot - j))
                return carry

            lax.fori_loop(0, tn - stage, step, 0)
            rows = rows_of(pivot, size)
            cos, sine = ctab[rows, :], stab[rows, :]
            dt[rows, 0:width] = turn(dq[rows, :] * (1.0 / math.sqrt(HD)), cos, sine, -1.0).astype(BF16)
            dt[rows, width : 2 * width] = turn(dk[rows, :], cos, sine, -1.0).astype(BF16)
            dt[rows, 2 * width : 3 * width] = dv[rows, :].astype(BF16)
            block = dt[rows, :]
            dbt[...] += jnp.sum(block.astype(F32), axis=0, keepdims=True)
            chip, core = pivot // 2, lax.rem(pivot, 2)

            def back(cols):
                d = dot(block, wt[cols, :], NT)
                flat[0:1, cols] += jnp.sum(d * n[rows, cols].astype(F32), axis=0, keepdims=True)
                flat[1:2, cols] += jnp.sum(d, axis=0, keepdims=True)
                value = dh[rows, cols].astype(F32) + d * vec[0:1, cols]

                @pl.when(core != co)
                def _():
                    gather.tocore[chip, :, cols] = value.astype(BF16)

                @pl.when((core == co) & (chip != zc))
                def _():
                    gather.toici[chip, :, cols] = value.astype(BF16)

                @pl.when(pivot == t)
                def _():
                    keep[:, cols] = value

            columns(model, TILE, back)

            @pl.when(core != co)
            def _():
                gather.send_core(chip)

            if stage % 2 == 1:

                @pl.when(chip != zc)
                def _():
                    gather.send_link(chip)

            ticks(f"s{stage}")

        wide = width
        for i in range(3):
            start = pl.multiple_of(t * wide, 128)
            flat[5 + i : 6 + i, pl.ds(start, wide)] = dbt[:, i * wide : (i + 1) * wide]
        for i in range(gn):
            row, start = divmod(i * tn * 128, model)
            flat[8 + row : 9 + row, pl.ds(pl.multiple_of(start + t * 128, 128), 128)] = dbi[:, i * 128 : (i + 1) * 128]
        if layer > 0:
            load(layer - 1, ["w0", "k1", "k2", "k3", "k4", "k5", "k6"])

        def grad_triple(cols):
            h1 = (n[:, cols].astype(F32) * vec[0:1, cols] + vec[1:2, cols]).astype(BF16)
            dwt[cols, :] = dot(h1, dt[...], TN).astype(BF16)

        columns(model, TILE, grad_triple)
        if layer > 0:
            load(layer - 1, ["k0"])
        ticks("triple")
        if layer == 0:
            flat_turn(0, 0)
        need(layer, ["x"])
        own_n, inverse = norm_stats(x[...])
        e = keep[...] + gather.total()
        inner = e - jnp.mean(e, axis=-1, keepdims=True) - own_n * jnp.mean(e * own_n, axis=-1, keepdims=True)
        dy[...] = dy[...] + inner * inverse
        if layer > 0:
            load(layer - 1, ["x"])
        gather.finish()
        ticks("sum")

    low = gb.at[pl.ds(0, size)]
    low[...] = dy[...].astype(BF16)
    move(low, grad_o, 1)
    rest = [(0, 0), (2, 0), (3, 0), (0, 0), (1, 0), (0, 0)]
    for i, (kind, layer) in enumerate(rest):
        if i + 1 <= len(exchanges):
            flat_turn(0, i + 1)
        reducing.advance(kind, layer)
    for layer in reversed(range(layers)):
        for kind in range(4):
            while reducing.taken[kind, layer] < reducing.steps:
                reducing.advance(kind, layer)
    reducing.finish()
    moved_in(low, grad_o, 1)


def descend_call(gn, tn, grads, segcol, segrow, vecs, tables, xs, ws, kepts):
    layers = len(xs)
    size, model = xs[0].shape
    length = size * tn
    shapes = [ws[i][0].shape for i in range(4)]
    width, units, chips = shapes[3][0], shapes[2][0], tn // 2
    kept = kept_shapes(length, model, width, units)
    dma = pltpu.SemaphoreType.DMA
    shard = shapes[0][0] // (gn * tn)
    prows, orows = shapes[3][0] // gn, shapes[2][0] // gn
    exchanges = (gn * tn).bit_length() - 1
    outs = (
        shape((2, size // 2, model), BF16),
        shape((2, size // 2, model), BF16),
        shape((layers, 16, model), F32),
        shape((layers, tn, shard, 3 * width), BF16),
        shape((layers, tn, shard, units), BF16),
        shape((layers, prows, model), BF16),
        shape((layers, orows, model), BF16),
    )
    scratch = [pltpu.VMEM(dims, BF16) for dims in shapes]
    scratch += [pltpu.VMEM(*item) for item in kept]
    scratch += [
        pltpu.VMEM((size, model), F32),
        pltpu.VMEM((size, model), F32),
        pltpu.VMEM((length, model), BF16),
        pltpu.VMEM((length, width), BF16),
        pltpu.VMEM((length, 3 * width), BF16),
        pltpu.VMEM((length, width), F32),
        pltpu.VMEM((length, width), F32),
        pltpu.VMEM((size, model), F32),
        pltpu.VMEM((1, 3 * width), F32),
        pltpu.VMEM((1, units), F32),
    ]
    scratch += group_buffers(chips, size, model)
    for dims in shapes:
        scratch += [pltpu.VMEM(dims, BF16)] * layers
    scratch += [pltpu.VMEM((layers, (gn - 1) * dims[0] // gn, dims[1]), BF16) for dims in shapes]
    scratch += [pltpu.VMEM((layers, exchanges, 16, model), F32)]
    for _ in range(layers + 1):
        scratch += group_sems(chips, tn)
    slots = 8 * layers
    scratch += [
        dma((slots, gn)), dma((slots, gn)), dma((2, layers, tn)), dma((2, layers, tn)), dma((layers,)), dma((layers,)),
        dma((3, layers)),
        dma((14 * layers,)), dma((2, 2)), dma((2, 2)), dma((layers, exchanges)), dma((layers, exchanges)),
    ]

    def body(*refs):
        refs = list(refs)

        def take(count):
            out, refs[:] = refs[:count], refs[count:]
            return out

        ins = take(6)
        x_in = take(layers)
        w_in = [take(layers) for _ in range(4)]
        kept_in = [take(8) for _ in range(layers)]
        results = take(7)
        w, kept_s = take(4), take(8)
        work = take(10)
        bufs = take(4)
        accs = [take(layers) for _ in range(4)]
        boxes = take(4)
        flatbox = take(1)[0]
        group = [take(7) for _ in range(layers + 1)]
        reduce_sems = take(7)
        descend_kernel(
            gn, tn, layers, size, *ins, x_in, w_in, kept_in, *results, w, kept_s, *work, bufs, accs, boxes,
            flatbox, group, reduce_sems, *take(5),
        )

    flat_ws = [ws[i][layer] for i in range(4) for layer in range(layers)]
    flat_kept = [ref for layer in range(layers) for ref in kepts[layer]]
    return pl.pallas_call(
        body,
        out_shape=outs,
        in_specs=[ANY] + [VM] * 5 + [ANY] * (layers + len(flat_ws) + len(flat_kept)),
        out_specs=(ANY, ANY, VM, ANY, ANY, ANY, ANY),
        scratch_shapes=scratch,
        compiler_params=params_of(3),
        name="descend",
    )(grads, segcol, segrow, vecs, *tables, *xs, *flat_ws, *flat_kept)


GROUPS = ("dp", "h")
EVERY = ("dp", "h", "t")


def to_group(tn, blocks):
    h, t = lax.axis_index("h"), lax.axis_index("t")
    count = 2 * tn
    parity = lax.rem(t, 2)
    got = []
    for j in range(2):
        moves = [(c, ((c + j) % 2) * tn + c // 2) for c in range(count)]
        piece = jnp.where(lax.rem(parity + j, 2) == 0, blocks[0], blocks[1])
        got.append(lax.ppermute(piece, ("h", "t"), moves))
    low = jnp.where(h == 0, got[0], got[1])
    high = jnp.where(h == 0, got[1], got[0])
    return jnp.concatenate([low, high], axis=0)


def from_group(tn, rows):
    h, t = lax.axis_index("h"), lax.axis_index("t")
    count = 2 * tn
    parity = lax.rem(t, 2)
    size = rows.shape[0] // 2
    got = []
    for j in range(2):
        moves = [(((c + j) % 2) * tn + c // 2, c) for c in range(count)]
        piece = jnp.where(lax.rem(h + j, 2) == 0, rows[:size], rows[size:])
        got.append(lax.ppermute(piece, ("h", "t"), moves))
    first = jnp.where(parity == 0, got[0], got[1])
    second = jnp.where(parity == 0, got[1], got[0])
    return jnp.stack([first, second], axis=0)


def proj_moves(gn, tn):
    return [(r, (r % gn) * tn + r // gn) for r in range(gn * tn)]


def slice_columns(weight, gn, tn):
    rows, cols = weight.shape
    return weight.reshape(rows, gn, tn, cols // (gn * tn)).transpose(2, 0, 1, 3).reshape(tn, rows, cols // tn)


def slice_triple(weight, tn):
    rows, cols = weight.shape
    return weight.reshape(rows, 3, tn, cols // (3 * tn)).transpose(2, 0, 1, 3).reshape(tn, rows, cols // tn)


def gather_weights(gn, tn, triple, proj, inner, outer):
    def spread(parts):
        moved = lax.all_to_all(parts, "t", 0, 0, tiled=True)
        whole = lax.all_gather(moved.reshape(-1, moved.shape[-1]), GROUPS, axis=0, tiled=True)
        return whole

    wt = spread(slice_triple(triple, tn))
    wi = spread(slice_columns(inner, gn, tn))
    wo = lax.all_gather(outer, GROUPS, axis=0, tiled=True)
    wp = lax.all_gather(lax.ppermute(proj, EVERY, proj_moves(gn, tn)), GROUPS, axis=0, tiled=True)
    return wt, wi, wo, wp


def reduce_weights(gn, tn, dwt, dwi, dwo, dwp):
    def back(parts):
        mine = lax.psum_scatter(parts, GROUPS, scatter_dimension=0, tiled=True)
        rows = mine.shape[0] // tn
        return lax.all_to_all(mine.reshape(tn, rows, -1), "t", 0, 0, tiled=True).astype(F32)

    triple = back(dwt)
    rows = triple.shape[1]
    triple = triple.reshape(tn, rows, 3, -1).transpose(1, 2, 0, 3).reshape(rows, -1)
    inner = back(dwi)
    inner = inner.reshape(tn, rows, gn, -1).transpose(1, 2, 0, 3).reshape(rows, -1)
    outer = lax.psum_scatter(dwo, GROUPS, scatter_dimension=0, tiled=True).astype(F32)
    proj = lax.psum_scatter(dwp, GROUPS, scatter_dimension=0, tiled=True)
    proj = lax.ppermute(proj, EVERY, [(b, a) for a, b in proj_moves(gn, tn)]).astype(F32)
    return triple, proj, inner, outer


def per_device(
    gn, tn,
    tokens, segments, cotangent, triple_weight, triple_bias, proj_weight, proj_bias, inner_weight, inner_bias,
    outer_weight, outer_bias, first_gain, first_shift, second_gain, second_shift,
):
    layers = triple_weight.shape[0]
    model = tokens.shape[2]
    span = tokens.shape[1] * 2 * tn
    h, t = lax.axis_index("h"), lax.axis_index("t")
    device = (lax.axis_index("dp") * 2 + h) * tn + t
    shards = gn * tn
    heads_wide = model // tn
    units = outer_weight.shape[1] * gn

    rows = triple_weight.shape[1]
    block = tokens.shape[1]
    tables = constant_tables(span, shards, model)
    direct = rows % 16 == 0 and block == 128 and layers * 4 <= 16 and units == model
    if direct:
        head = jnp.stack(
            [
                inner_bias,
                jnp.pad(triple_bias, ((0, 0), (0, 128 - triple_bias.shape[1]))),
                jnp.concatenate([proj_bias, outer_bias, first_gain, first_shift], axis=1),
                jnp.pad(jnp.concatenate([second_gain, second_shift], axis=1), ((0, 0), (0, 64))),
            ],
            axis=1,
        ).reshape(4 * layers, 128)
        opened = ascend_call(
            gn, tn, tokens, cotangent, jnp.pad(segments, ((0, 6), (0, 0))),
            jnp.pad(head, ((0, 16 - 4 * layers), (0, 0))),
            triple_weight.reshape(layers, rows, 3, tn, -1).transpose(0, 3, 1, 2, 4).reshape(layers, tn, rows, -1),
            inner_weight.reshape(layers, rows, gn, tn, -1).transpose(0, 3, 1, 2, 4).reshape(layers, tn, rows, -1),
            outer_weight, proj_weight, tables,
            placement(model // shards, shards) + placement(3 * model // shards, shards),
        )
        opened = list(opened)
        grad_all, segcol, segrow, vecs, _, _ = opened[:6]
        opened = opened[6:]
        inputs = opened[:layers]
        weights = [tuple(opened[layers + k * layers + layer] for k in range(4)) for layer in range(layers)]
        kept = [opened[5 * layers + 8 * i : 5 * layers + 8 * (i + 1)] for i in range(layers)]
        output, tokens_grad, summed, triple, inner, proj, outer = descend_call(
            gn, tn, grad_all, segcol, segrow, vecs, tables, inputs,
            [[weights[layer][k] for layer in range(layers)] for k in range(4)], kept,
        )
        summed = summed.reshape(layers, -1)
        triple = triple.reshape(layers, tn, rows, 3, -1).transpose(0, 2, 3, 1, 4).reshape(layers, rows, -1).astype(F32)
        inner = inner.reshape(layers, tn, rows, gn, -1).transpose(0, 2, 3, 1, 4).reshape(layers, rows, -1).astype(F32)
        proj, outer = proj.astype(F32), outer.astype(F32)
    else:
        small = (triple_bias, inner_bias, proj_bias, outer_bias, first_gain, first_shift, second_gain, second_shift)
        starts = [0]
        for item in small:
            starts.append(starts[-1] + item.shape[1])
        packed = jnp.concatenate(small, axis=1)
        x = to_group(tn, tokens).astype(F32)
        cot = to_group(tn, cotangent).astype(F32)
        segs_all = lax.all_gather(segments, ("h", "t"), axis=1, tiled=True)
        everything = lax.all_gather(packed[None], EVERY, axis=0, tiled=True).astype(F32)
        weights = [
            gather_weights(
                gn, tn, triple_weight[layer], proj_weight[layer], inner_weight[layer], outer_weight[layer]
            )
            for layer in range(layers)
        ]
        segs = jnp.where(h == 0, segs_all[0], segs_all[1])
        segs = jnp.where(segs == 0, -1 - jnp.arange(span, dtype=jnp.int32), segs).astype(F32)
        tables = (segs[:, None], segs[None, :]) + tables

        def vector(layer, i):
            return everything[:, layer, starts[i] : starts[i + 1]].reshape(-1)

        vecs, inputs, kept = [], [], []
        for layer in range(layers):
            bt = lax.dynamic_index_in_dim(vector(layer, 0).reshape(3, tn, heads_wide), t, 1, keepdims=False)
            bi = lax.dynamic_index_in_dim(vector(layer, 1).reshape(gn, tn, -1), t, 1, keepdims=False)
            zero = jnp.zeros((model,), F32)
            vecs.append(
                jnp.stack(
                    [vector(layer, 4), vector(layer, 5), vector(layer, 6), vector(layer, 7)]
                    + [vector(layer, 2) + vector(layer, 3), zero, zero, zero]
                )
            )
            inputs.append(x)
            x, *saved = forward_layer(
                tn, x, weights[layer], vecs[layer], bt.reshape(1, -1), bi.reshape(1, -1), tables
            )
            kept.append(saved)
        output = x.astype(BF16)
        grad = cot
        mats, flats = [None] * layers, [None] * layers
        for layer in reversed(range(layers)):
            grad, dwt, dwi, dwo, dwp, dvec, dbt, dbi = backward_layer(
                tn, grad, inputs[layer], weights[layer], vecs[layer], tables, kept[layer]
            )
            mats[layer] = reduce_weights(gn, tn, dwt, dwi, dwo, dwp)
            part = lax.dynamic_update_slice(
                jnp.zeros((3, tn, heads_wide), F32), dbt.reshape(3, 1, heads_wide), (0, t, 0)
            )
            side = lax.dynamic_update_slice(
                jnp.zeros((gn, tn, units // gn), F32), dbi.reshape(gn, 1, units // gn), (0, t, 0)
            )
            flats[layer] = jnp.concatenate([dvec[:5].reshape(-1), part.reshape(-1), side.reshape(-1)])
        output, tokens_grad = from_group(tn, output), from_group(tn, grad.astype(BF16))
        triple, proj, inner, outer = (jnp.stack([m[k] for m in mats]) for k in range(4))
        summed = lax.psum(jnp.stack(flats), EVERY)

    def own(start, length):
        piece = length // shards
        return lax.dynamic_slice_in_dim(summed, start + device * piece, piece, 1)

    base = 5 * model
    bias_sum = own(4 * model, model)
    return (
        output,
        tokens_grad,
        triple,
        own(base, 2 * model),
        own(base + 2 * model, model),
        proj,
        bias_sum,
        inner,
        own(base + 3 * model, units * tn),
        outer,
        bias_sum,
        own(0, model),
        own(model, model),
        own(2 * model, model),
        own(3 * model, model),
    )


def solution(mesh):
    dp, ctx = mesh.shape["dp"], mesh.shape["ctx"]
    tn = ctx // 2
    gn = 2 * dp
    fine = Mesh(mesh.devices.reshape(dp, 2, tn), EVERY)
    seq = P("dp", ("h", "t"), None)
    mat = P(None, EVERY, None)
    row = P(None, EVERY)
    in_specs = (seq, P("dp", ("h", "t")), seq, mat, row, mat, row, mat, row, mat, row, row, row, row, row)
    out_specs = (seq, seq, mat, row, row, mat, row, mat, row, mat, row, row, row, row, row)
    return jax.shard_map(
        functools.partial(per_device, gn, tn), mesh=fine, in_specs=in_specs, out_specs=out_specs, check_vma=False
    )
```

```python
import functools
import math

import jax
import jax.numpy as jnp
import numpy as np
from jax import lax
from jax.experimental import pallas as pl
from jax.experimental.pallas import tpu as pltpu
from jax.sharding import Mesh
from jax.sharding import PartitionSpec as P

HD = 64
ROT = 16
EPSILON = 1e-05
NEG_LARGE = -1e30
MESH = pl.DeviceIdType.MESH
BF16 = jnp.bfloat16
F32 = jnp.float32
VMEM_LIMIT = 60 * 1024 * 1024


def dot(a, b, dims):
    return lax.dot_general(a, b, (dims, ((), ())), preferred_element_type=F32)


NN = ((1,), (0,))
NT = ((1,), (1,))
TN = ((0,), (0,))


def rows_of(b, size):
    return pl.ds(pl.multiple_of(b * size, size), size)


def group_barrier(tn):
    t = lax.axis_index("t")
    zc, co = t // 2, lax.rem(t, 2)
    chips = tn // 2
    sem = pltpu.get_barrier_semaphore()
    peers = [zc * 2 + 1 - co] + [lax.rem(zc + k, chips) * 2 + co for k in range(1, chips)]
    for p in peers:
        pl.semaphore_signal(sem, inc=1, device_id={"t": p}, device_id_type=MESH)
    pl.semaphore_wait(sem, len(peers))


class Spread:
    def __init__(self, tn, buf, size, ssem, fsem, rsem):
        self.tn, self.buf, self.size = tn, buf, size
        self.ssem, self.fsem, self.rsem = ssem, fsem, rsem
        self.t = lax.axis_index("t")
        self.zc, self.co = self.t // 2, lax.rem(self.t, 2)
        self.chips = tn // 2

    def copy(self, block, send, to):
        ref = self.buf.at[rows_of(block, self.size)]
        return pltpu.make_async_remote_copy(
            ref, ref, send, self.rsem.at[block], device_id={"t": to}, device_id_type=MESH
        )

    def start(self):
        for k in range(1, self.chips):
            chip = lax.rem(self.zc + k, self.chips)
            self.copy(self.t, self.ssem.at[k], chip * 2 + self.co).start()
        self.copy(self.t, self.ssem.at[0], self.zc * 2 + 1 - self.co).start()

    def peer_core(self):
        b = self.zc * 2 + 1 - self.co
        self.copy(b, self.ssem.at[0], b).wait_recv()
        return b

    def same_core(self, k):
        b = lax.rem(self.zc + self.chips - k, self.chips) * 2 + self.co
        self.copy(b, self.fsem.at[k], b).wait_recv()
        self.copy(b, self.fsem.at[k], self.zc * 2 + 1 - self.co).start()
        return b

    def other_core(self, k):
        b = lax.rem(self.zc + self.chips - k, self.chips) * 2 + 1 - self.co
        self.copy(b, self.fsem.at[k], b).wait_recv()
        return b

    def finish(self):
        for k in range(self.chips):
            self.copy(self.t, self.ssem.at[k], self.t).wait_send()
        for k in range(1, self.chips):
            self.copy(self.t, self.fsem.at[k], self.t).wait_send()


class Gather:
    def __init__(self, tn, tocore, fromcore, toici, fromici, sems):
        self.tn = tn
        self.tocore, self.fromcore, self.toici, self.fromici = tocore, fromcore, toici, fromici
        self.cs, self.cr, self.ls, self.lr = sems
        self.t = lax.axis_index("t")
        self.zc, self.co = self.t // 2, lax.rem(self.t, 2)
        self.chips = tn // 2

    def core_copy(self, chip):
        return pltpu.make_async_remote_copy(
            self.tocore.at[chip],
            self.fromcore.at[chip],
            self.cs.at[chip],
            self.cr.at[chip],
            device_id={"t": self.zc * 2 + 1 - self.co},
            device_id_type=MESH,
        )

    def link_copy(self, chip, slot):
        return pltpu.make_async_remote_copy(
            self.toici.at[chip],
            self.fromici.at[slot],
            self.ls.at[chip],
            self.lr.at[slot],
            device_id={"t": chip * 2 + self.co},
            device_id_type=MESH,
        )

    def send_core(self, chip):
        self.core_copy(chip).start()

    def send_link(self, chip):
        self.core_copy(chip).wait_recv()
        self.toici[chip] = (self.toici[chip].astype(F32) + self.fromcore[chip].astype(F32)).astype(BF16)
        self.link_copy(chip, self.zc).start()

    def total(self):
        self.core_copy(self.zc).wait_recv()
        value = self.fromcore[self.zc].astype(F32)
        for k in range(1, self.chips):
            chip = lax.rem(self.zc + k, self.chips)
            self.link_copy(chip, chip).wait_recv()
            value = value + self.fromici[chip].astype(F32)
        return value

    def finish(self):
        for chip in range(self.chips):
            self.core_copy(chip).wait_send()
        for k in range(1, self.chips):
            chip = lax.rem(self.zc + k, self.chips)
            self.link_copy(chip, self.zc).wait_send()


def norm_stats(x):
    mean = jnp.mean(x, axis=-1, keepdims=True)
    centred = x - mean
    inverse = lax.rsqrt(jnp.mean(centred * centred, axis=-1, keepdims=True) + EPSILON)
    return centred * inverse, inverse


def widen(tab, width):
    return jnp.concatenate([tab] * (width // tab.shape[1]), axis=1)


def turn(x, cos, sine, sign):
    width = x.shape[1]
    cos, sine = widen(cos, width), widen(sine, width)
    front = lax.rem(lax.broadcasted_iota(jnp.int32, (1, width), 1), HD) < ROT // 2
    partner = jnp.where(front, pltpu.roll(x, width - ROT // 2, 1), pltpu.roll(x, ROT // 2, 1))
    return x * cos + sign * (partner * sine)


def head_masks(width, dtype):
    lane = lax.broadcasted_iota(jnp.int32, (1, width), 1) // HD
    return [(lane == h).astype(F32).astype(dtype) for h in range(width // HD)]


def pair_bias(qb, kb, size, segcol, segrow):
    qpos = lax.broadcasted_iota(jnp.int32, (size, size), 0) + qb * size
    kpos = lax.broadcasted_iota(jnp.int32, (size, size), 1) + kb * size
    same = segcol[rows_of(qb, size), :] == segrow[:, rows_of(kb, size)]
    return jnp.where(same & (kpos <= qpos), 0.0, NEG_LARGE)


TILE = 256
SKEW = 1


class Forward:
    def __init__(self, tn, size, x, w, vecs, segs, tables, kept, keep):
        self.tn, self.size, self.chips = tn, size, tn // 2
        self.x, self.keep = x, keep
        self.wt, self.wi, self.wo, self.wp = w
        self.vec, self.bt, self.bi = vecs
        self.segcol, self.segrow = segs
        self.tables = tables
        self.n, self.q, self.k, self.v, self.o, self.lse, self.g, self.gp = kept
        self.width, self.units = self.q.shape[1], self.g.shape[1]
        self.heads = self.width // HD

    def norm(self, t):
        own, _ = norm_stats(self.x[...])
        self.n[rows_of(t, self.size), :] = own.astype(BF16)

    def heads_in(self, b):
        width, vec, bt = self.width, self.vec, self.bt
        rows = rows_of(b, self.size)
        h1 = (self.n[rows, :].astype(F32) * vec[0:1, :] + vec[1:2, :]).astype(BF16)
        cos, sine = (tab[rows, :] for tab in self.tables)
        q = dot(h1, self.wt[:, 0:width], NN) + bt[:, 0:width]
        low = turn(q, cos, sine, 1.0).astype(BF16).astype(F32)
        self.q[rows, :] = (low * (1.0 / math.sqrt(HD))).astype(BF16)
        k = dot(h1, self.wt[:, width : 2 * width], NN) + bt[:, width : 2 * width]
        self.k[rows, :] = turn(k, cos, sine, 1.0).astype(BF16)
        v = dot(h1, self.wt[:, 2 * width : 3 * width], NN) + bt[:, 2 * width : 3 * width]
        self.v[rows, :] = v.astype(BF16)

    def mixer_in(self, b, blocks=1):
        rows = rows_of(b, self.size * blocks)
        h2 = (self.n[rows, :].astype(F32) * self.vec[2:3, :] + self.vec[3:4, :]).astype(BF16)

        def mix(j, carry):
            cols = rows_of(j, TILE)
            u = dot(h2, self.wi[:, cols], NN) + self.bi[:, cols]
            half = 0.5 + 0.5 * lax.erf(u * (1.0 / math.sqrt(2.0)))
            self.g[rows, cols] = (u * half).astype(BF16)
            bell = jnp.exp(-0.5 * u * u) * (1.0 / math.sqrt(2.0 * math.pi))
            self.gp[rows, cols] = (half + u * bell).astype(BF16)
            return carry

        lax.fori_loop(0, self.units // TILE, mix, 0)

    def attend(self, b):
        size, width, heads = self.size, self.width, self.heads
        masks = head_masks(width, F32)
        lane = lax.broadcasted_iota(jnp.int32, (1, 128), 1)
        rows = rows_of(b, size)
        qb = self.q[rows, :]
        qs = [qb * masks[h].astype(BF16) for h in range(heads)]

        def step(i, carry):
            peaks, sums, acc = carry
            kb = b - i
            keys = self.k[rows_of(kb, size), :]
            vals = self.v[rows_of(kb, size), :]
            bias = pair_bias(b, kb, size, self.segcol, self.segrow)
            new_peaks, new_sums = [], []
            scale = jnp.zeros((size, width), F32)
            add = jnp.zeros((size, width), F32)
            for h in range(heads):
                s = dot(qs[h], keys, NT) + bias
                peak = jnp.maximum(peaks[h], jnp.max(s, axis=1, keepdims=True))
                p = jnp.exp(s - peak)
                fade = jnp.exp(peaks[h] - peak)
                new_peaks.append(peak)
                new_sums.append(sums[h] * fade + jnp.sum(p, axis=1, keepdims=True))
                scale = scale + fade * masks[h]
                add = add + dot(p.astype(BF16), vals * masks[h].astype(BF16), NN)
            return tuple(new_peaks), tuple(new_sums), acc * scale + add

        start = (
            tuple(jnp.full((size, 1), NEG_LARGE, F32) for _ in range(heads)),
            tuple(jnp.zeros((size, 1), F32) for _ in range(heads)),
            jnp.zeros((size, width), F32),
        )
        peaks, sums, acc = lax.fori_loop(0, b + 1, step, start)
        scale = jnp.zeros((size, width), F32)
        lse = jnp.zeros((size, 128), F32)
        for h in range(heads):
            scale = scale + (1.0 / sums[h]) * masks[h]
            lse = jnp.where(lane == h, peaks[h] + jnp.log(sums[h]), lse)
        self.lse[rows, :] = lse
        self.o[rows, :] = acc * scale

    def branches(self, b, store):
        rows = rows_of(b, self.size)

        def part(j, carry):
            cols = rows_of(j, TILE)
            value = dot(self.g[rows, :], self.wo[:, cols], NN)
            store(cols, value + dot(self.o[rows, :].astype(BF16), self.wp[:, cols], NN))
            return carry

        lax.fori_loop(0, self.x.shape[1] // TILE, part, 0)

    def into(self, ref, chip):
        def store(cols, value):
            ref[chip, :, cols] = value.astype(BF16)

        return store

    def into_keep(self, cols, value):
        self.keep[:, cols] = value


def arrivals(spread):
    yield spread.t
    yield spread.peer_core()
    for i in range(1, spread.chips):
        yield spread.same_core(i)
        yield spread.other_core(i)


def far_first(spread):
    out = []
    for i in range(1, spread.chips):
        chip = lax.rem(spread.zc + i, spread.chips)
        out += [chip * 2 + 1 - spread.co, chip * 2 + spread.co]
    return out + [spread.zc * 2 + 1 - spread.co, spread.t]


def branch_sums(layer, spread, gather, tick=lambda: None):
    for i in range(1, spread.chips):
        chip = lax.rem(spread.zc + i, spread.chips)
        layer.branches(chip * 2 + 1 - spread.co, layer.into(gather.tocore, chip))
        gather.send_core(chip)
        layer.branches(chip * 2 + spread.co, layer.into(gather.toici, chip))
        gather.send_link(chip)
        tick()
    layer.branches(spread.zc * 2 + 1 - spread.co, layer.into(gather.tocore, spread.zc))
    gather.send_core(spread.zc)
    layer.branches(spread.t, layer.into_keep)
    tick()


def forward_kernel(
    tn, size,
    x_ref, wt, wi, wo, wp, vec, bt, bi, segcol, segrow, ctab, stab,
    xo_ref, n_ref, q_ref, k_ref, v_ref, o_ref, lse_ref, g_ref, gp_ref,
    keep, tocore, fromcore, toici, fromici, ssem, fsem, rsem, cs, cr, ls, lr,
):
    group_barrier(tn)
    spread = Spread(tn, n_ref, size, ssem, fsem, rsem)
    gather = Gather(tn, tocore, fromcore, toici, fromici, (cs, cr, ls, lr))
    layer = Forward(
        tn, size, x_ref, (wt, wi, wo, wp), (vec, bt, bi), (segcol, segrow), (ctab, stab),
        (n_ref, q_ref, k_ref, v_ref, o_ref, lse_ref, g_ref, gp_ref), keep,
    )
    layer.norm(spread.t)
    spread.start()
    for b in arrivals(spread):
        layer.heads_in(b)
        layer.mixer_in(b)
    for b in far_first(spread):
        layer.attend(b)
    branch_sums(layer, spread, gather)
    xo_ref[...] = x_ref[...] + vec[4:5, :] + keep[...] + gather.total()
    spread.finish()
    gather.finish()


def backward_kernel(
    tn, size,
    dy_ref, x_ref, wt, wi, wo, wp, vec, segcol, segrow, ctab, stab,
    n_ref, q_ref, k_ref, v_ref, o_ref, lse_ref, g_ref, gp_ref,
    dx_ref, dwt, dwi, dwo, dwp, dvec, dbt, dbi,
    gb, do, du, dt, dq, dk, dv, dh2, keep,
    tocore, fromcore, toici, fromici, ssem, fsem, rsem, cs, cr, ls, lr,
):
    chips = tn // 2
    width = q_ref.shape[1]
    heads = width // HD
    units = g_ref.shape[1]
    model = x_ref.shape[1]
    group_barrier(tn)
    spread = Spread(tn, gb, size, ssem, fsem, rsem)
    gather = Gather(tn, tocore, fromcore, toici, fromici, (cs, cr, ls, lr))
    t, zc, co = spread.t, spread.zc, spread.co
    own = dy_ref[...].astype(F32).astype(BF16)
    gb[rows_of(t, size), :] = own
    spread.start()
    dvec[...] = jnp.zeros_like(dvec)
    dbt[...] = jnp.zeros_like(dbt)
    dbi[...] = jnp.zeros_like(dbi)
    dvec[4:5, :] = jnp.sum(own.astype(F32), axis=0, keepdims=True)
    dq[...] = jnp.zeros_like(dq)
    dk[...] = jnp.zeros_like(dk)
    dv[...] = jnp.zeros_like(dv)

    def mixer(b):
        rows = rows_of(b, size)
        grad = gb[rows, :]
        do[rows, :] = dot(grad, wp[...], NT).astype(BF16)

        def unit(j, carry):
            cols = rows_of(j, TILE)
            d = (dot(grad, wo[cols, :], NT) * gp_ref[rows, cols].astype(F32)).astype(BF16)
            du[rows, cols] = d
            dbi[0:1, cols] += jnp.sum(d.astype(F32), axis=0, keepdims=True)
            return carry

        lax.fori_loop(0, units // TILE, unit, 0)

        def back(j, carry):
            cols = rows_of(j, TILE)
            d = dot(du[rows, :], wi[cols, :], NT)
            dvec[2:3, cols] += jnp.sum(d * n_ref[rows, cols].astype(F32), axis=0, keepdims=True)
            dvec[3:4, cols] += jnp.sum(d, axis=0, keepdims=True)
            dh2[rows, cols] = d * vec[2:3, cols]
            return carry

        lax.fori_loop(0, model // TILE, back, 0)

    mixer(t)
    mixer(spread.peer_core())
    for i in range(1, chips):
        mixer(spread.same_core(i))
        mixer(spread.other_core(i))

    masks = head_masks(width, BF16)
    lane = lax.broadcasted_iota(jnp.int32, (1, 128), 1)
    up = zc >= (chips + 1) // 2
    tsize = tn

    def pair(qb, kb):
        qrows, krows = rows_of(qb, size), rows_of(kb, size)
        q, keys, vals = q_ref[qrows, :], k_ref[krows, :], v_ref[krows, :]
        grad = do[qrows, :]
        prod = grad.astype(F32) * o_ref[qrows, :]
        lse = lse_ref[qrows, :]
        bias = pair_bias(qb, kb, size, segcol, segrow)
        dq_new = jnp.zeros((size, width), F32)
        dk_new = jnp.zeros((size, width), F32)
        dv_new = jnp.zeros((size, width), F32)
        for h in range(heads):
            qh, gh = q * masks[h], grad * masks[h]
            total = jnp.sum(jnp.where(lane == h, lse, 0.0), axis=1, keepdims=True)
            delta = jnp.sum(prod * masks[h].astype(F32), axis=1, keepdims=True)
            p = jnp.exp(dot(qh, keys, NT) + bias - total)
            ds = (p * (dot(gh, vals, NT) - delta)).astype(BF16)
            dv_new = dv_new + dot(p.astype(BF16), gh, TN)
            dk_new = dk_new + dot(ds, qh, TN)
            dq_new = dq_new + dot(ds, keys * masks[h], NN)
        dq[qrows, :] += dq_new
        dk[krows, :] += dk_new
        dv[krows, :] += dv_new

    def attend_back(stage):
        pivot = jnp.where(up, stage, tsize - 1 - stage)

        def step(j, carry):
            pair(jnp.where(up, pivot + j, pivot), jnp.where(up, pivot, pivot - j))
            return carry

        lax.fori_loop(0, tsize - stage, step, 0)
        rows = rows_of(pivot, size)
        cos, sine = ctab[rows, :], stab[rows, :]
        dt[rows, 0:width] = turn(dq[rows, :] * (1.0 / math.sqrt(HD)), cos, sine, -1.0).astype(BF16)
        dt[rows, width : 2 * width] = turn(dk[rows, :], cos, sine, -1.0).astype(BF16)
        dt[rows, 2 * width : 3 * width] = dv[rows, :].astype(BF16)
        block = dt[rows, :]
        dbt[...] += jnp.sum(block.astype(F32), axis=0, keepdims=True)

        def back(j, carry):
            cols = rows_of(j, TILE)
            d = dot(block, wt[cols, :], NT)
            dvec[0:1, cols] += jnp.sum(d * n_ref[rows, cols].astype(F32), axis=0, keepdims=True)
            dvec[1:2, cols] += jnp.sum(d, axis=0, keepdims=True)
            dh2[rows, cols] = dh2[rows, cols] + d * vec[0:1, cols]
            return carry

        lax.fori_loop(0, model // TILE, back, 0)
        value = dh2[rows, :]
        chip, core = pivot // 2, lax.rem(pivot, 2)

        @pl.when(core != co)
        def _():
            tocore[chip] = value.astype(BF16)
            gather.send_core(chip)

        @pl.when((core == co) & (chip != zc))
        def _():
            toici[chip] = value.astype(BF16)

        @pl.when(pivot == t)
        def _():
            keep[...] = value

        if stage % 2 == 1:

            @pl.when(chip != zc)
            def _():
                gather.send_link(chip)

    for stage in range(tn):
        attend_back(stage)

    def grad_one(j, carry):
        cols = rows_of(j, TILE)
        h1 = (n_ref[:, cols].astype(F32) * vec[0:1, cols] + vec[1:2, cols]).astype(BF16)
        dwt[cols, :] = dot(h1, dt[...], TN).astype(dwt.dtype)
        return carry

    lax.fori_loop(0, model // TILE, grad_one, 0)

    def grad_two(j, carry):
        cols = rows_of(j, TILE)
        h2 = (n_ref[:, cols].astype(F32) * vec[2:3, cols] + vec[3:4, cols]).astype(BF16)
        dwi[cols, :] = dot(h2, du[...], TN).astype(dwi.dtype)
        return carry

    lax.fori_loop(0, model // TILE, grad_two, 0)

    def grad_three(j, carry):
        cols = rows_of(j, TILE)
        dwo[cols, :] = dot(g_ref[:, cols], gb[...], TN).astype(dwo.dtype)
        return carry

    lax.fori_loop(0, units // TILE, grad_three, 0)
    small = min(TILE, width)

    def grad_four(j, carry):
        cols = rows_of(j, small)
        dwp[cols, :] = dot(o_ref[:, cols].astype(BF16), gb[...], TN).astype(dwp.dtype)
        return carry

    lax.fori_loop(0, width // small, grad_four, 0)

    own_n, inverse = norm_stats(x_ref[...])
    e = keep[...] + gather.total()
    inner = e - jnp.mean(e, axis=-1, keepdims=True) - own_n * jnp.mean(e * own_n, axis=-1, keepdims=True)
    dx_ref[...] = dy_ref[...].astype(F32) + inner * inverse
    spread.finish()
    gather.finish()


VM = pl.BlockSpec(memory_space=pltpu.VMEM)


def shape(dims, dtype):
    return jax.ShapeDtypeStruct(tuple(dims), dtype)


def group_sems(chips, tn):
    dma = pltpu.SemaphoreType.DMA
    return [dma((chips,)), dma((chips,)), dma((tn,)), dma((chips,)), dma((chips,)), dma((chips,)), dma((chips,))]


def group_buffers(chips, size, model):
    return [pltpu.VMEM((chips, size, model), BF16) for _ in range(4)]


def params_of(cid):
    return pltpu.CompilerParams(collective_id=cid, has_side_effects=True, vmem_limit_bytes=VMEM_LIMIT)


def forward_layer(tn, x, weights, vec, bt, bi, tables):
    wt, wi, wo, wp = weights
    size, model = x.shape
    length = size * tn
    width, units, chips = wp.shape[0], wo.shape[0], tn // 2
    outs = (
        shape((size, model), F32),
        shape((length, model), BF16),
        shape((length, width), BF16),
        shape((length, width), BF16),
        shape((length, width), BF16),
        shape((length, width), F32),
        shape((length, 128), F32),
        shape((length, units), BF16),
        shape((length, units), BF16),
    )
    return pl.pallas_call(
        functools.partial(forward_kernel, tn, size),
        out_shape=outs,
        in_specs=[VM] * 12,
        out_specs=[VM] * len(outs),
        scratch_shapes=[pltpu.VMEM((size, model), F32)] + group_buffers(chips, size, model) + group_sems(chips, tn),
        compiler_params=params_of(0),
        name="forward",
    )(x, wt, wi, wo, wp, vec, bt, bi, *tables)


def backward_layer(tn, dy, x, weights, vec, tables, kept):
    wt, wi, wo, wp = weights
    size, model = x.shape
    length = size * tn
    width, units, chips = wp.shape[0], wo.shape[0], tn // 2
    outs = (
        shape((size, model), F32),
        shape(wt.shape, BF16),
        shape(wi.shape, BF16),
        shape(wo.shape, BF16),
        shape(wp.shape, BF16),
        shape((8, model), F32),
        shape((1, 3 * width), F32),
        shape((1, units), F32),
    )
    return pl.pallas_call(
        functools.partial(backward_kernel, tn, size),
        out_shape=outs,
        in_specs=[VM] * 19,
        out_specs=[VM] * len(outs),
        scratch_shapes=[
            pltpu.VMEM((length, model), BF16),
            pltpu.VMEM((length, width), BF16),
            pltpu.VMEM((length, units), BF16),
            pltpu.VMEM((length, 3 * width), BF16),
            pltpu.VMEM((length, width), F32),
            pltpu.VMEM((length, width), F32),
            pltpu.VMEM((length, width), F32),
            pltpu.VMEM((length, model), F32),
            pltpu.VMEM((size, model), F32),
        ]
        + group_buffers(chips, size, model)
        + group_sems(chips, tn),
        compiler_params=params_of(1),
        name="backward",
    )(dy, x, wt, wi, wo, wp, vec, *tables, *kept)


class Place:
    def __init__(self, gn, tn):
        self.gn, self.tn = gn, tn
        self.h, self.t = lax.axis_index("h"), lax.axis_index("t")
        self.g = lax.axis_index("dp") * 2 + self.h
        self.c = self.h * tn + self.t
        self.bits = [1 << i for i in range(gn.bit_length() - 1)]

    def group(self, g):
        return {"dp": g // 2, "h": lax.rem(g, 2)}

    def line(self, c):
        return {"h": c // self.tn, "t": lax.rem(c, self.tn)}

    def other(self, k):
        return lax.rem(self.t + k, self.tn)


def flip(value, bit):
    return value + bit * (1 - 2 * lax.rem(value // bit, 2))


def remote(src, dst, send, recv, device):
    return pltpu.make_async_remote_copy(src, dst, send, recv, device_id=device, device_id_type=MESH)


def runs_by_step(place, bits):
    runs, steps = [(place.g, 1)], []
    for bit in bits:
        steps.append((bit, runs))
        if len(runs) == 1 and runs[0][1] == bit:
            runs = [(runs[0][0] // (2 * bit) * (2 * bit), 2 * bit)]
        else:
            runs = runs + [(flip(start, bit), count) for start, count in runs]
    return steps


def bit_orders(place):
    bits = place.bits
    return [bits, bits[:1] + bits[:0:-1]]


class Doubling:
    def __init__(self, place, ref, block, cols, order, sems, slot):
        self.place, self.ref, self.block, self.cols, self.order = place, ref, block, cols, order
        self.send, self.recv, self.slot = sems[0], sems[1], slot
        self.levels = [[] for _ in order]
        for i, bit in enumerate(order):
            for bits in range(1 << i):
                held = [order[j] for j in range(i) if bits >> j & 1]
                self.levels[len(held)].append((bit, held))

    def at(self, held):
        g = self.place.g
        for bit in held:
            g = flip(g, bit)
        return g

    def copy(self, bit, held):
        start = self.at(held)
        rows = pl.ds(pl.multiple_of(start * self.block, self.block), self.block)
        ref = self.ref.at[rows, self.cols]
        index = sum(held) + bit
        return remote(
            ref,
            ref,
            self.send.at[self.slot, index],
            self.recv.at[self.slot, index],
            self.place.group(flip(self.place.g, bit)),
        )

    def arrive(self, held):
        start = self.at(held)
        rows = pl.ds(pl.multiple_of(start * self.block, self.block), self.block)
        ref = self.ref.at[rows, self.cols]
        index = sum(held)
        peer = self.place.group(flip(self.place.g, held[-1]))
        remote(ref, ref, self.send.at[self.slot, index], self.recv.at[self.slot, index], peer).wait_recv()

    def advance(self, level):
        seen = set()
        for bit, held in self.levels[level]:
            if held and tuple(held) not in seen:
                seen.add(tuple(held))
                self.arrive(held)
            self.copy(bit, held).start()

    def whole(self):
        last = self.order[-1]
        for level in self.levels:
            for bit, held in level:
                if bit == last:
                    self.arrive(held + [bit])

    def finish(self):
        for level in self.levels:
            for item in level:
                self.copy(*item).wait_send()


def halves(cols):
    return [pl.ds(0, cols // 2), pl.ds(cols // 2, cols // 2)]


def line_barrier(place, extra):
    sem = pltpu.get_barrier_semaphore()
    span = 2 * place.tn
    for k in range(1, span):
        pl.semaphore_signal(sem, inc=1, device_id=place.line(lax.rem(place.c + k, span)), device_id_type=MESH)
    for bit in place.bits[1:]:
        pl.semaphore_signal(sem, inc=1, device_id=place.group(flip(place.g, bit)), device_id_type=MESH)
    peers = span - 1 + len(place.bits) - 1
    source, moved = extra

    @pl.when(moved)
    def _():
        pl.semaphore_signal(sem, inc=1, device_id=source, device_id_type=MESH)
        pl.semaphore_wait(sem, peers + 1)

    @pl.when(jnp.logical_not(moved))
    def _():
        pl.semaphore_wait(sem, peers)


def proj_places(place):
    gn, tn = place.gn, place.tn
    r = place.g * tn + place.t
    target = place.group(lax.rem(r, gn)) | {"t": r // gn}
    q = place.t * gn + place.g
    source = place.group(q // tn) | {"t": lax.rem(q, tn)}
    return target, source, r, q


def slot_rows(index, size):
    return pl.ds(pl.multiple_of(index * size, size), size)


class Opening:
    def __init__(self, place, layers, tok, cot, seg, vec, tri, inn, outer, proj, tok_o, cot_o, seg_o, vec_o, w, sems):
        self.place, self.layers = place, layers
        self.tok, self.cot, self.seg, self.vec = tok, cot, seg, vec
        self.tri, self.inn, self.outer, self.proj = tri, inn, outer, proj
        self.tok_o, self.cot_o, self.seg_o, self.vec_o = tok_o, cot_o, seg_o, vec_o
        self.wts, self.wis, self.wos, self.wps = w
        (
            self.ssem, self.rsem, self.lsem, self.asend, self.arecv, self.psend, self.precv,
            self.msend, self.mrecv, self.gsend, self.grecv,
        ) = sems
        self.half = tok.shape[1]
        self.target, self.source, self.r, self.q = proj_places(place)
        self.moved = self.q != self.r
        self.local, self.sends, self.shared_with = [], [], {}
        self.locals_of = {}

    def barrier(self):
        line_barrier(self.place, (self.source, self.moved))

    def near(self, src, dst, key):
        cp = pltpu.make_async_copy(src, dst, self.lsem.at[len(self.local)])
        cp.start()
        self.local.append(cp)
        self.locals_of[key] = cp

    def hop(self, src, dst, slot, i):
        c, tn = self.place.c, self.place.tn
        to = i * tn + c // 2
        rows = slot_rows(lax.rem(c, 2), self.half)
        near = pltpu.make_async_copy(src.at[i], dst.at[rows], self.msend.at[slot, i])
        far = remote(
            src.at[i], dst.at[rows], self.msend.at[slot, i], self.mrecv.at[slot, lax.rem(c, 2)],
            self.place.line(to),
        )
        return to == c, near, far

    def move(self, src, dst, slot):
        for i in range(2):
            stays, near, far = self.hop(src, dst, slot, i)
            pl.when(stays)(near.start)
            pl.when(jnp.logical_not(stays))(far.start)

    def moved_in(self, src, dst, slot):
        for i in range(2):
            stays, near, far = self.hop(src, dst, slot, i)
            pl.when(stays)(near.wait)
            pl.when(jnp.logical_not(stays))(far.wait_send)
        for s in range(2):
            cp = remote(
                src.at[0], dst.at[pl.ds(s * self.half, self.half)], self.msend.at[slot, 0],
                self.mrecv.at[slot, s], self.place.line(self.place.c),
            )
            pl.when(2 * self.place.t + s != self.place.c)(cp.wait_recv)

    def share(self, key, src_of, dst, size, slot):
        g, t, tn = self.place.g, self.place.t, self.place.tn
        rows = slot_rows(g * tn + t, size)
        self.near(src_of(t), dst.at[rows], key)
        for k in range(1, tn):
            to = self.place.other(k)
            cp = remote(src_of(to), dst.at[rows], self.asend.at[slot, k], self.arecv.at[slot, t], {"t": to})
            cp.start()
            self.sends.append(cp)
        self.shared_with[key] = (dst, size, slot)

    def shared(self, key):
        dst, size, slot = self.shared_with[key]
        self.locals_of[key].wait()
        for k in range(1, self.place.tn):
            frm = self.place.other(k)
            ref = dst.at[slot_rows(self.place.g * self.place.tn + frm, size)]
            remote(ref, ref, self.asend.at[slot, k], self.arecv.at[slot, frm], {"t": frm}).wait_recv()

    def share_layer(self, layer):
        depth = self.tri.shape[2]
        base = 1 + 2 * layer
        self.share(("t", layer), lambda to: self.tri.at[layer, to], self.wts[layer], depth, base)
        self.share(("i", layer), lambda to: self.inn.at[layer, to], self.wis[layer], depth, base + 1)
        g = self.place.g
        self.near(self.outer.at[layer], self.wos[layer].at[slot_rows(g, self.outer.shape[1])], ("o", layer))
        here, far = self.proj_copies(layer)
        pl.when(self.moved)(far.start)
        pl.when(jnp.logical_not(self.moved))(here.start)

    def proj_copies(self, layer):
        prows = self.proj.shape[1]
        src = self.proj.at[layer]
        here = pltpu.make_async_copy(src, self.wps[layer].at[slot_rows(self.place.g, prows)], self.psend.at[layer])
        dst = self.wps[layer].at[slot_rows(lax.rem(self.r, self.place.gn), prows)]
        return here, remote(src, dst, self.psend.at[layer], self.precv.at[layer], self.target)

    def proj_ready(self, layer):
        here, far = self.proj_copies(layer)

        @pl.when(self.moved)
        def _():
            far.wait_recv()
            far.wait_send()

        pl.when(jnp.logical_not(self.moved))(here.wait)

    def start(self):
        place, span = self.place, 2 * self.place.tn
        self.move(self.tok, self.tok_o, 0)
        vec_rows = self.vec.shape[0]
        self.share("v", lambda to: self.vec, self.vec_o, vec_rows, 0)
        self.near(self.seg, self.seg_o.at[slot_rows(place.c, 8)], "s")
        for k in range(1, span):
            to = lax.rem(place.c + k, span)
            dst = self.seg_o.at[slot_rows(place.c, 8)]
            cp = remote(self.seg, dst, self.gsend.at[k], self.grecv.at[place.c], place.line(to))
            cp.start()
            self.sends.append(cp)
        self.share_layer(0)
        orders = bit_orders(place)
        self.chunks, slot = [], 0
        tn, depth = place.tn, self.tri.shape[2]
        todo = []
        for layer in range(self.layers):
            todo += [
                [(("t", layer), self.wts[layer], tn * depth)],
                [(("i", layer), self.wis[layer], tn * depth)],
                [
                    (("o", layer), self.wos[layer], self.outer.shape[1]),
                    (("p", layer), self.wps[layer], self.proj.shape[1]),
                ],
            ]
        todo[0].insert(0, ("v", self.vec_o, tn * vec_rows))
        self.keys = [[key for key, _, _ in chunk] for chunk in todo]
        for chunk in todo:
            parts = []
            for _, ref, block in chunk:
                pieces = halves(ref.shape[1]) if ref.shape[1] >= 256 else [pl.ds(0, ref.shape[1])]
                for i, piece in enumerate(pieces):
                    parts.append(Doubling(place, ref, block, piece, orders[i], (self.ssem, self.rsem), slot))
                    slot += 1
            self.chunks.append(parts)
        self.steps = len(place.bits)
        self.turn, self.turns = 0, len(self.chunks) + SKEW * (self.steps - 1)
        self.complete = set()

    def ready(self, i):
        for key in self.keys[i]:
            if key == "v" or key[0] in ("t", "i"):
                self.shared(key)
            elif key[0] == "o":
                self.locals_of[key].wait()
            else:
                self.proj_ready(key[1])

    def tick(self, until=None):
        while self.turn < self.turns and (until is None or self.turn <= until):
            for step in reversed(range(self.steps)):
                i = self.turn - SKEW * step
                if 0 <= i < len(self.chunks):
                    if step == 0:
                        self.ready(i)
                    for part in self.chunks[i]:
                        part.advance(step)
            self.turn += 1
            if until is None:
                break

    def have(self, key):
        i = [key in keys for keys in self.keys].index(True)
        if i not in self.complete:
            self.complete.add(i)
            self.tick(i + SKEW * (self.steps - 1))
            for part in self.chunks[i]:
                part.whole()

    def segments_in(self):
        place, span = self.place, 2 * self.place.tn
        self.locals_of["s"].wait()
        for k in range(1, span):
            frm = lax.rem(place.c + k, span)
            ref = self.seg_o.at[slot_rows(frm, 8)]
            remote(ref, ref, self.gsend.at[k], self.grecv.at[frm], place.line(frm)).wait_recv()

    def finish(self):
        self.tick(self.turns)
        for parts in self.chunks:
            for part in parts:
                part.finish()
        for cp in self.sends:
            cp.wait_send()


def ascend_kernel(
    gn, tn, layers, size,
    tok, cot, seg, vec, tri, inn, outer, proj, ctab, stab, e32, m32, e96, m96,
    gb_o, segcol, segrow, vecs_o, bts_o, bis_o, xs_o, w_o, kept_o,
    w, kept, xs, x_low, cot_low, gb, keep, seg_in, vec_in, vec_wide, bt_wide,
    bufs, group, opening_sems, save_sem, tok_sem,
):
    place = Place(gn, tn)
    opening = Opening(
        place, layers, tok, cot, seg, vec, tri, inn, outer, proj, x_low, cot_low, seg_in, vec_in, w, opening_sems
    )
    opening.barrier()
    opening.start()
    saves = []

    def save(src, dst):
        cp = pltpu.make_async_copy(src, dst, save_sem.at[len(saves)])
        cp.start()
        saves.append(cp)

    opening.tick(0)
    opening.moved_in(tok, x_low, 0)
    xs[0][...] = x_low[...].astype(F32)
    spreads, gathers, stages = [], [], []
    for layer in range(layers):
        ssem, fsem, rsem, cs, cr, ls, lr = group[layer]
        spreads.append(Spread(tn, kept[layer][0], size, ssem, fsem, rsem))
        gathers.append(Gather(tn, *bufs, (cs, cr, ls, lr)))
        stages.append(
            Forward(
                tn, size, xs[layer], tuple(w[k][layer] for k in range(4)),
                (vecs_o.at[layer], bts_o.at[layer], bis_o.at[layer]), (segcol, segrow), (ctab, stab),
                kept[layer], keep,
            )
        )
    stages[0].norm(place.t)
    spreads[0].start()
    opening.tick(1)
    for layer in range(1, layers):
        opening.share_layer(layer)
    opening.segments_in()
    block = segcol.shape[0] // (2 * tn)
    eye = lax.broadcasted_iota(jnp.int32, (block, block), 0) == lax.broadcasted_iota(jnp.int32, (block, block), 1)
    for i in range(2 * tn):
        row = jnp.where(place.h == 0, seg_in[8 * i : 8 * i + 1, :], seg_in[8 * i + 1 : 8 * i + 2, :])
        spot = lax.broadcasted_iota(jnp.int32, (1, block), 1) + i * block
        row = jnp.where(row == 0, -1 - spot, row).astype(F32)
        segrow[:, i * block : (i + 1) * block] = row
        segcol[i * block : (i + 1) * block, :] = jnp.sum(jnp.where(eye, row, 0.0), axis=1, keepdims=True)
    opening.have("v")
    shards = gn * tn
    vec_rows = vec.shape[0]
    vec_wide[...] = vec_in[...].astype(F32)
    lane = lax.broadcasted_iota(jnp.int32, (1, 128), 1)
    for layer in range(layers):

        def line(k):
            return vec_wide[pl.ds(4 * layer + k, shards, stride=vec_rows), :]

        def spread_out(value, place_of, mask):
            return jnp.sum(dot(value.astype(BF16), place_of, NN) * mask, axis=0, keepdims=True)

        thick = line(2)
        parts = [jnp.where(lane // 32 == i, thick, 0.0) for i in range(4)]
        thin = line(3)
        gains = [jnp.where(lane // 32 == i, thin, 0.0) for i in range(2)]
        rows = [spread_out(p, e32[...], m32[...]) for p in parts + gains]
        vecs_o[layer] = jnp.concatenate(
            [rows[2], rows[3], rows[4], rows[5], rows[0] + rows[1]] + [jnp.zeros_like(rows[0])] * 3, axis=0
        )
        bt_wide[...] = spread_out(line(1), e96[...], m96[...])
        wide = bts_o.shape[2] // 3
        for i in range(3):
            start = pl.multiple_of(i * wide * tn + place.t * wide, 128)
            bts_o[layer, :, i * wide : (i + 1) * wide] = bt_wide[:, pl.ds(start, wide)]
        for i in range(gn):
            bis_o[layer, :, i * 128 : (i + 1) * 128] = vec_wide[
                pl.ds((i * tn + place.t) * vec_rows + 4 * layer, 1), :
            ]

    for layer in range(layers):
        stage, spread, gather = stages[layer], spreads[layer], gathers[layer]
        if layer > 0:
            stage.norm(place.t)
            spread.start()
        opening.have(("t", layer))
        save(w[0][layer], w_o[0][layer])
        for i, b in enumerate(arrivals(spread)):
            stage.heads_in(b)
            if i == 1:
                opening.tick()
        if layer + 1 == layers:
            opening.moved_in(cot, cot_low, 1)
            gb[rows_of(place.t, size), :] = cot_low[...]
            ahead = Spread(tn, gb, size, *group[layers][:3])
            ahead.start()
        for i, b in enumerate(far_first(spread)):
            stage.attend(b)
            if i == 1 and layer > 0:
                opening.tick()
        if layer == 0:
            opening.move(cot, cot_low, 1)
        opening.have(("i", layer))
        save(w[1][layer], w_o[1][layer])
        save(kept[layer][0], kept_o[layer][0])
        for i in range(1, 6):
            save(kept[layer][i], kept_o[layer][i])
        for i in range(spread.chips):
            stage.mixer_in(i, 2)
            if i == 0:
                opening.tick()
        save(kept[layer][6], kept_o[layer][6])
        save(kept[layer][7], kept_o[layer][7])
        save(xs[layer], xs_o[layer])
        if layer + 1 == layers:
            for _ in arrivals(ahead):
                pass
            save(gb, gb_o)
        opening.have(("o", layer))
        for k in range(2, 4):
            save(w[k][layer], w_o[k][layer])
        if layer + 1 < layers:
            branch_sums(stage, spread, gather, opening.tick)
            xs[layer + 1][...] = xs[layer][...] + vecs_o[layer, 4:5, :] + keep[...] + gather.total()
            gather.finish()
        spread.finish()
    ahead.finish()
    opening.finish()
    for cp in saves:
        cp.wait()


ANY = pl.BlockSpec(memory_space=pl.ANY)


def constant_tables(span, shards, model):
    angle = np.arange(span, dtype=np.float32)[:, None] * (
        np.float32(10000.0) ** (-(2.0 * np.arange(ROT // 2, dtype=np.float32)) / np.float32(ROT))
    )
    cosine, sine = np.cos(angle).astype(np.float32), np.sin(angle).astype(np.float32)
    none = np.zeros((span, HD - ROT), np.float32)
    reps = 128 // HD
    ctab = np.concatenate([cosine, cosine, none + 1.0] * reps, axis=1)
    stab = np.concatenate([-sine, sine, none] * reps, axis=1)
    return tuple(jnp.asarray(tab, F32) for tab in (ctab, stab))


def placement(piece, shards):
    j, col = np.arange(128)[:, None], np.arange(piece * shards)[None, :]
    put = (j % piece == col % piece) if 128 % piece == 0 else (j == col % piece)
    mask = np.arange(shards)[:, None] == col // piece
    return jnp.asarray(put, BF16), jnp.asarray(mask, F32)


def kept_shapes(length, model, width, units):
    return [
        ((length, model), BF16),
        ((length, width), BF16),
        ((length, width), BF16),
        ((length, width), BF16),
        ((length, width), F32),
        ((length, 128), F32),
        ((length, units), BF16),
        ((length, units), BF16),
    ]


def ascend_call(gn, tn, tokens, cotangent, segments, vec, tri, inn, outer, proj, tables, placing):
    layers = outer.shape[0]
    _, half, model = tokens.shape
    size = 2 * half
    length = size * tn
    depth = tri.shape[2]
    wshapes = [
        (gn * tn * depth, tri.shape[3]), (gn * tn * depth, inn.shape[3]),
        (gn * outer.shape[1], model), (gn * proj.shape[1], model),
    ]
    width, units, chips = wshapes[3][0], wshapes[2][0], tn // 2
    kept = kept_shapes(length, model, width, units)
    dma = pltpu.SemaphoreType.DMA
    outs = [
        (shape((length, model), BF16), ANY),
        (shape((length, 1), F32), VM),
        (shape((1, length), F32), VM),
        (shape((layers, 8, model), F32), VM),
        (shape((layers, 1, 3 * width), F32), VM),
        (shape((layers, 1, units), F32), VM),
    ]
    outs += [(shape((size, model), F32), ANY)] * layers
    for dims in wshapes:
        outs += [(shape(dims, BF16), ANY)] * layers
    for _ in range(layers):
        outs += [(shape(*item), ANY) for item in kept]
    scratch = []
    for dims in wshapes:
        scratch += [pltpu.VMEM(dims, BF16)] * layers
    for _ in range(layers):
        scratch += [pltpu.VMEM(*item) for item in kept]
    scratch += [pltpu.VMEM((size, model), F32)] * layers
    scratch += [
        pltpu.VMEM((size, model), BF16),
        pltpu.VMEM((size, model), BF16),
        pltpu.VMEM((length, model), BF16),
        pltpu.VMEM((size, model), F32),
        pltpu.VMEM((2 * tn * 8, 128), jnp.int32),
        pltpu.VMEM((gn * tn * vec.shape[0], 128), BF16),
        pltpu.VMEM((gn * tn * vec.shape[0], 128), F32),
        pltpu.VMEM((1, 3 * model), F32),
    ]
    scratch += group_buffers(chips, size, model)
    for _ in range(layers + 1):
        scratch += group_sems(chips, tn)
    slots = 1 + 8 * layers
    scratch += [
        dma((slots, gn)), dma((slots, gn)), dma((2 + 3 * layers,)),
        dma((1 + 2 * layers, tn)), dma((1 + 2 * layers, tn)),
        dma((layers,)), dma((layers,)), dma((2, 2)), dma((2, 2)),
        dma((2 * tn,)), dma((2 * tn,)),
    ]
    scratch += [dma((14 * layers,)), dma((1,))]

    def body(*refs):
        refs = list(refs)

        def take(count):
            out, refs[:] = refs[:count], refs[count:]
            return out

        ins = take(14)
        gb_o, segcol, segrow, vecs_o, bts_o, bis_o = take(6)
        xs_o = take(layers)
        w_o = [take(layers) for _ in range(4)]
        kept_o = [take(8) for _ in range(layers)]
        w = [take(layers) for _ in range(4)]
        kept_s = [take(8) for _ in range(layers)]
        xs = take(layers)
        x_low, cot_low, gb, keep, seg_in, vec_in, vec_wide, bt_wide = take(8)
        bufs = take(4)
        group = [take(7) for _ in range(layers + 1)]
        sems = take(11)
        save_sem, tok_sem = take(2)
        ascend_kernel(
            gn, tn, layers, size, *ins, gb_o, segcol, segrow, vecs_o, bts_o, bis_o, xs_o, w_o, kept_o,
            w, kept_s, xs, x_low, cot_low, gb, keep, seg_in, vec_in, vec_wide, bt_wide, bufs, group, sems,
            save_sem, tok_sem,
        )

    return pl.pallas_call(
        body,
        out_shape=tuple(o for o, _ in outs),
        in_specs=[ANY] * 8 + [VM] * 6,
        out_specs=tuple(spec for _, spec in outs),
        scratch_shapes=scratch,
        compiler_params=params_of(2),
        name="ascend",
    )(tokens, cotangent, segments, vec, tri, inn, outer, proj, *tables, *placing)


class Halving:
    def __init__(self, place, acc, inbox, block, cols, order, sems, slot):
        self.place, self.acc, self.inbox, self.block, self.cols = place, acc, inbox, block, cols
        self.send, self.recv, self.slot = sems[0], sems[1], slot
        self.plan, index, base = [], 0, 0
        for bit, runs in reversed(runs_by_step(place, order)):
            entry = []
            for start, count in runs:
                entry.append((bit, start, count, index, base))
                index += 1
                base += count
            self.plan.append(entry)

    def copy(self, bit, start, count, index, base):
        rows = pl.ds(pl.multiple_of(flip(start, bit) * self.block, self.block), count * self.block)
        return remote(
            self.acc.at[rows, self.cols],
            self.inbox.at[pl.ds(base * self.block, count * self.block), self.cols],
            self.send.at[self.slot, index],
            self.recv.at[self.slot, index],
            self.place.group(flip(self.place.g, bit)),
        )

    def advance(self, step):
        if step > 0:
            for item in self.plan[step - 1]:
                self.copy(*item).wait_recv()
                _, start, count, _, base = item

                def add(i, carry):
                    rows = pl.ds(pl.multiple_of((start + i) * self.block, self.block), self.block)
                    came = pl.ds(pl.multiple_of((base + i) * self.block, self.block), self.block)
                    value = self.acc[rows, self.cols].astype(F32) + self.inbox[came, self.cols].astype(F32)
                    self.acc[rows, self.cols] = value.astype(BF16)
                    return carry

                lax.fori_loop(0, count, add, 0)
        if step < len(self.plan):
            for item in self.plan[step]:
                self.copy(*item).start()

    def finish(self):
        for entry in self.plan:
            for item in entry:
                self.copy(*item).wait_send()

class Slots:
    def __init__(self, ref, first, size):
        self.ref, self.first, self.size = ref, first, size

    def rows(self, slot):
        return slot_rows(self.first + slot, self.size)

    @property
    def at(self):
        return _SlotRefs(self)

    def __getitem__(self, slot):
        return self.ref[self.rows(slot), :]


class _SlotRefs:
    def __init__(self, slots):
        self.slots = slots

    def __getitem__(self, slot):
        return self.slots.ref.at[self.slots.rows(slot)]


class Reducing:
    def __init__(self, place, layers, accs, boxes, outs, sems):
        self.place, self.layers = place, layers
        self.accs, self.boxes = accs, boxes
        self.cross, self.proj_o, self.outer_o = outs[:2], outs[2], outs[3]
        self.hs, self.hr, self.cs, self.cr, self.ps, self.pr, self.os = sems
        self.target, self.source, self.r, self.q = proj_places(place)
        self.moved = self.q != self.r
        orders = bit_orders(place)
        self.parts, slot = {}, 0
        for layer in range(layers):
            for kind in range(4):
                acc = accs[kind][layer]
                parts = []
                for k, cols in enumerate(halves(acc.shape[1])):
                    box = boxes[kind].at[layer]
                    block = acc.shape[0] // place.gn
                    parts.append(Halving(place, acc, box, block, cols, orders[k], (self.hs, self.hr), slot))
                    slot += 1
                self.parts[kind, layer] = parts
        self.steps = len(place.bits) + 1
        self.taken = {key: 0 for key in self.parts}

    def advance(self, kind, layer):
        step = self.taken[kind, layer]
        self.taken[kind, layer] = step + 1
        for part in self.parts[kind, layer]:
            part.advance(step)
        if step == self.steps - 1:
            self.owned(kind, layer)

    def own_rows(self, kind, layer, index, pieces):
        acc = self.accs[kind][layer]
        rows = acc.shape[0] // pieces
        return acc.at[slot_rows(index, rows)]

    def cross_copy(self, kind, layer, k):
        place = self.place
        to = place.other(k)
        src = self.own_rows(kind, layer, place.g * place.tn + to, place.gn * place.tn)
        dst = self.cross[kind].at[layer, place.t]
        return remote(src, dst, self.cs.at[kind, layer, k], self.cr.at[kind, layer, place.t], {"t": to})

    def proj_copies(self, layer):
        src = self.own_rows(3, layer, self.place.g, self.place.gn)
        here = pltpu.make_async_copy(src, self.proj_o.at[layer], self.ps.at[layer])
        return here, remote(src, self.proj_o.at[layer], self.ps.at[layer], self.pr.at[layer], self.source)

    def own_copy(self, kind, layer):
        place = self.place
        if kind == 2:
            src, dst = self.own_rows(2, layer, place.g, place.gn), self.outer_o.at[layer]
        else:
            src = self.own_rows(kind, layer, place.g * place.tn + place.t, place.gn * place.tn)
            dst = self.cross[kind].at[layer, place.t]
        return pltpu.make_async_copy(src, dst, self.os.at[kind, layer])

    def owned(self, kind, layer):
        if kind < 3:
            self.own_copy(kind, layer).start()
        if kind < 2:
            for k in range(1, self.place.tn):
                self.cross_copy(kind, layer, k).start()
        if kind == 3:
            here, far = self.proj_copies(layer)
            pl.when(self.moved)(far.start)
            pl.when(jnp.logical_not(self.moved))(here.start)

    def finish(self):
        for (kind, layer), parts in self.parts.items():
            for part in parts:
                part.finish()
            if kind < 3:
                self.own_copy(kind, layer).wait()
            if kind < 2:
                for k in range(1, self.place.tn):
                    frm = self.place.other(k)
                    ref = self.cross[kind].at[layer, frm]
                    remote(
                        ref, ref, self.cs.at[kind, layer, k], self.cr.at[kind, layer, frm], {"t": frm}
                    ).wait_recv()
                    self.cross_copy(kind, layer, k).wait_send()
            if kind == 3:
                here, far = self.proj_copies(layer)
                pl.when(self.moved)(far.wait)
                pl.when(jnp.logical_not(self.moved))(here.wait)


FIRST = {
    "outer": ((2, 0), (3, 0)),
    "inner": ((1, 0),),
    "s1": ((2, 0), (3, 0)),
    "triple": ((0, 0), (1, 0)),
    "sum": ((2, 0), (3, 0)),
}
LATER = {
    "spread": ((0, 1),),
    "near": ((1, 1),),
    "arrived": ((2, 1), (3, 1), (0, 1)),
    "outer": ((2, 0), (3, 0), (1, 1)),
    "inner": ((1, 0), (0, 1)),
    "s1": ((2, 0), (3, 0)),
    "s3": ((2, 0), (3, 0), (1, 0)),
    "triple": ((0, 0), (1, 0)),
}


def descend_kernel(
    gn, tn, layers, size,
    grads, segcol, segrow, vecs, ctab, stab, xs, ws, kepts,
    out_o, grad_o, flat_o, triple_o, inner_o, proj_o, outer_o,
    w, kept, dy, x, gb, do, dt, dk, dv, keep, dbt, dbi, bufs, accs, boxes, flatbox,
    group, reduce_sems, load_sem, ms, mr, fs, fr,
):
    place = Place(gn, tn)
    g, t, c = place.g, place.t, place.c
    wt, wi, wo, wp = w
    n, q, k, v, o, lse, gact, gp = kept
    chips = tn // 2
    width, units, model = q.shape[1], gact.shape[1], dy.shape[1]
    heads = width // HD
    dq, dh, du = o, gact, gp
    loads = {}

    def load(layer, names):
        for name in names:
            if name == "x":
                src, dst = xs[layer], x
            elif name == "cot":
                src, dst = grads, gb
            elif name[0] == "w":
                i = int(name[1])
                src, dst = ws[i][layer], w[i]
            else:
                i = int(name[1])
                src, dst = kepts[layer][i], kept[i]
            cp = pltpu.make_async_copy(src, dst, load_sem.at[len(loads)])
            cp.start()
            loads[layer, name] = cp

    waited = set()

    def need(layer, names):
        for name in names:
            if (layer, name) not in waited:
                waited.add((layer, name))
                loads[layer, name].wait()

    last = layers - 1
    load(last, ["w2", "w3", "k6", "k4", "cot", "k7", "k5", "w1", "k0", "k1", "k2", "k3", "w0", "x"])
    reducing = Reducing(place, layers, accs, boxes, (triple_o, inner_o, proj_o, outer_o), reduce_sems)
    line_barrier(place, (reducing.target, reducing.moved))
    half = out_o.shape[1]

    def hop(src, dst, slot, s):
        to = 2 * t + s
        part = src.at[pl.ds(s * half, half)]
        near = pltpu.make_async_copy(part, dst.at[place.h], ms.at[slot, s])
        far = remote(part, dst.at[place.h], ms.at[slot, s], mr.at[slot, place.h], place.line(to))
        return to == c, near, far

    def move(src, dst, slot):
        for s in range(2):
            stays, near, far = hop(src, dst, slot, s)
            pl.when(stays)(near.start)
            pl.when(jnp.logical_not(stays))(far.start)

    def moved_in(src, dst, slot):
        for s in range(2):
            stays, near, far = hop(src, dst, slot, s)
            pl.when(stays)(near.wait)
            pl.when(jnp.logical_not(stays))(far.wait_send)
        for i in range(2):
            cp = remote(
                src.at[pl.ds(0, half)], dst.at[i], ms.at[slot, 0], mr.at[slot, i], place.line(c)
            )
            pl.when(i * tn + c // 2 != c)(cp.wait_recv)

    exchanges = [("g", bit) for bit in place.bits] + [("t", 1 << i) for i in range(tn.bit_length() - 1)]

    def exchange(layer, i):
        kind, bit = exchanges[i]
        to = place.group(flip(g, bit)) if kind == "g" else {"t": flip(t, bit)}
        return remote(flat_o.at[layer], flatbox.at[layer, i], fs.at[layer, i], fr.at[layer, i], to)

    def flat_turn(layer, i):
        if i > 0:
            exchange(layer, i - 1).wait()
            flat_o[layer] += flatbox[layer, i - 1]
        if i < len(exchanges):
            exchange(layer, i).start()

    masks = head_masks(width, BF16)
    lane = lax.broadcasted_iota(jnp.int32, (1, 128), 1)
    up = place.t // 2 >= (chips + 1) // 2

    def pair(qb, kb):
        qrows, krows = rows_of(qb, size), rows_of(kb, size)
        queries, keys, vals = q[qrows, :], k[krows, :], v[krows, :]
        grad = do[qrows, :]
        side = lse[qrows, :]
        bias = pair_bias(qb, kb, size, segcol, segrow)
        dq_new = jnp.zeros((size, width), F32)
        dk_new = jnp.zeros((size, width), F32)
        dv_new = jnp.zeros((size, width), F32)
        for h in range(heads):
            qh, gh = queries * masks[h], grad * masks[h]
            total = jnp.sum(jnp.where(lane == h, side, 0.0), axis=1, keepdims=True)
            delta = jnp.sum(jnp.where(lane == 64 + h, side, 0.0), axis=1, keepdims=True)
            p = jnp.exp(dot(qh, keys, NT) + bias - total)
            ds = (p * (dot(gh, vals, NT) - delta)).astype(BF16)
            dv_new = dv_new + dot(p.astype(BF16), gh, TN)
            dk_new = dk_new + dot(ds, qh, TN)
            dq_new = dq_new + dot(ds, keys * masks[h], NN)
        dq[qrows, :] += dq_new
        dk[krows, :] += dk_new
        dv[krows, :] += dv_new

    def columns(count, tile, body):
        def step(j, carry):
            body(rows_of(j, tile))
            return carry

        lax.fori_loop(0, count // tile, step, 0)

    need(last, ["w2", "w3", "k6", "k4"])
    top = Spread(tn, gb, size, *group[layers][:3])
    room, spare = accs[2][0], accs[1][0]
    top_gather = Gather(
        tn, bufs[0], Slots(room, 0, size), bufs[2], Slots(room, chips, size), tuple(group[layers][3:])
    )
    stage_top = Forward(
        tn, size, x, (wt, wi, wo, wp), (vecs.at[last], None, None), (segcol, segrow), (ctab, stab), kept, keep
    )
    branch_sums(stage_top, top, top_gather)
    need(last, ["cot"])
    dy[...] = gb[rows_of(t, size), :].astype(F32)
    flat_o[...] = jnp.zeros_like(flat_o)
    out_in = spare.at[pl.ds(0, size)]

    def give_output():
        need(last, ["x"])
        out_in[...] = (x[...] + vecs[last, 4:5, :] + keep[...] + top_gather.total()).astype(BF16)
        top_gather.finish()
        move(out_in, out_o, 0)

    for layer in reversed(range(layers)):
        flat = flat_o.at[layer]
        vec = vecs.at[layer]
        dwt, dwi, dwo, dwp = (accs[i][layer] for i in range(4))
        ssem, fsem, rsem, cs, cr, ls, lr = group[layer]
        spread = Spread(tn, gb, size, ssem, fsem, rsem)
        gather = Gather(tn, *bufs, (cs, cr, ls, lr))
        zc, co = spread.zc, spread.co

        def ticks(where, layer=layer):
            for kind, late in (FIRST if layer == last else LATER).get(where, ()):
                if layer + late < layers and reducing.taken[kind, layer + late] < reducing.steps:
                    reducing.advance(kind, layer + late)

        own = dy[...].astype(BF16)
        if layer < last:
            gb[rows_of(t, size), :] = own
            spread.start()
        flat[4:5, :] = jnp.sum(own.astype(F32), axis=0, keepdims=True)
        dbt[...] = jnp.zeros_like(dbt)
        dbi[...] = jnp.zeros_like(dbi)
        dk[...] = jnp.zeros_like(dk)
        dv[...] = jnp.zeros_like(dv)
        ticks("spread")
        if layer < last:
            flat_turn(layer + 1, 0)
        for count, b in enumerate(arrivals(spread) if layer < last else range(chips)):
            need(layer, ["w3", "k4", "w2", "k7", "k5"])
            rows = rows_of(b, size) if layer < last else rows_of(b, 2 * size)
            grad = gb[rows, :]
            heads_grad = dot(grad, wp[...], NT).astype(BF16)
            do[rows, :] = heads_grad
            prod = heads_grad.astype(F32) * o[rows, :]
            side = lse[rows, :]
            for h in range(heads):
                delta = jnp.sum(prod * masks[h].astype(F32), axis=1, keepdims=True)
                side = jnp.where(lane == 64 + h, delta, side)
            lse[rows, :] = side

            def unit(cols):
                d = (dot(grad, wo[cols, :], NT) * gp[rows, cols].astype(F32)).astype(BF16)
                du[rows, cols] = d
                dbi[0:1, cols] += jnp.sum(d.astype(F32), axis=0, keepdims=True)

            columns(units, TILE, unit)
            if layer < last:
                flat_turn(layer + 1, count + 1)
            if count == 1:
                ticks("near")
        ticks("arrived")
        need(layer, ["k6"])
        if layer < last:
            spread.finish()
            if layer == last - 1:
                moved_in(out_in, out_o, 0)

        def grad_outer(cols):
            dwo[cols, :] = dot(gact[:, cols], gb[...], TN).astype(BF16)

        columns(units, TILE, grad_outer)

        def grad_proj(cols):
            dwp[cols, :] = dot(o[:, cols].astype(BF16), gb[...], TN).astype(BF16)

        columns(width, TILE, grad_proj)
        if layer == last:
            give_output()
        ticks("outer")
        if layer < last:
            flat_turn(layer + 1, len(exchanges))
        need(layer, ["w1", "k0"])
        if layer > 0:
            load(layer - 1, ["w2", "w3"])
        dq[...] = jnp.zeros_like(dq)

        def back_mixer(cols):
            d = dot(du[...], wi[cols, :], NT)
            flat[2:3, cols] = jnp.sum(d * n[:, cols].astype(F32), axis=0, keepdims=True)
            flat[3:4, cols] = jnp.sum(d, axis=0, keepdims=True)
            dh[:, cols] = (d * vec[2:3, cols]).astype(BF16)

        columns(model, TILE, back_mixer)

        def grad_inner(cols):
            h2 = (n[:, cols].astype(F32) * vec[2:3, cols] + vec[3:4, cols]).astype(BF16)
            dwi[cols, :] = dot(h2, du[...], TN).astype(BF16)

        columns(model, TILE, grad_inner)
        ticks("inner")
        if layer > 0:
            load(layer - 1, ["w1", "k7"])
        need(layer, ["k1", "k2", "k3", "w0"])

        for stage in range(tn):
            pivot = jnp.where(up, stage, tn - 1 - stage)

            def step(j, carry):
                pair(jnp.where(up, pivot + j, pivot), jnp.where(up, pivot, pivot - j))
                return carry

            lax.fori_loop(0, tn - stage, step, 0)
            rows = rows_of(pivot, size)
            cos, sine = ctab[rows, :], stab[rows, :]
            dt[rows, 0:width] = turn(dq[rows, :] * (1.0 / math.sqrt(HD)), cos, sine, -1.0).astype(BF16)
            dt[rows, width : 2 * width] = turn(dk[rows, :], cos, sine, -1.0).astype(BF16)
            dt[rows, 2 * width : 3 * width] = dv[rows, :].astype(BF16)
            block = dt[rows, :]
            dbt[...] += jnp.sum(block.astype(F32), axis=0, keepdims=True)
            chip, core = pivot // 2, lax.rem(pivot, 2)

            def back(cols):
                d = dot(block, wt[cols, :], NT)
                flat[0:1, cols] += jnp.sum(d * n[rows, cols].astype(F32), axis=0, keepdims=True)
                flat[1:2, cols] += jnp.sum(d, axis=0, keepdims=True)
                value = dh[rows, cols].astype(F32) + d * vec[0:1, cols]

                @pl.when(core != co)
                def _():
                    gather.tocore[chip, :, cols] = value.astype(BF16)

                @pl.when((core == co) & (chip != zc))
                def _():
                    gather.toici[chip, :, cols] = value.astype(BF16)

                @pl.when(pivot == t)
                def _():
                    keep[:, cols] = value

            columns(model, TILE, back)

            @pl.when(core != co)
            def _():
                gather.send_core(chip)

            if stage % 2 == 1:

                @pl.when(chip != zc)
                def _():
                    gather.send_link(chip)

            ticks(f"s{stage}")

        wide = width
        for i in range(3):
            start = pl.multiple_of(t * wide, 128)
            flat[5 + i : 6 + i, pl.ds(start, wide)] = dbt[:, i * wide : (i + 1) * wide]
        for i in range(gn):
            row, start = divmod(i * tn * 128, model)
            flat[8 + row : 9 + row, pl.ds(pl.multiple_of(start + t * 128, 128), 128)] = dbi[:, i * 128 : (i + 1) * 128]
        if layer > 0:
            load(layer - 1, ["w0", "k1", "k2", "k3", "k4", "k5", "k6"])

        def grad_triple(cols):
            h1 = (n[:, cols].astype(F32) * vec[0:1, cols] + vec[1:2, cols]).astype(BF16)
            dwt[cols, :] = dot(h1, dt[...], TN).astype(BF16)

        columns(model, TILE, grad_triple)
        if layer > 0:
            load(layer - 1, ["k0"])
        ticks("triple")
        if layer == 0:
            flat_turn(0, 0)
        need(layer, ["x"])
        own_n, inverse = norm_stats(x[...])
        e = keep[...] + gather.total()
        inner = e - jnp.mean(e, axis=-1, keepdims=True) - own_n * jnp.mean(e * own_n, axis=-1, keepdims=True)
        dy[...] = dy[...] + inner * inverse
        if layer > 0:
            load(layer - 1, ["x"])
        gather.finish()
        ticks("sum")

    low = gb.at[pl.ds(0, size)]
    low[...] = dy[...].astype(BF16)
    move(low, grad_o, 1)
    rest = [(0, 0), (2, 0), (3, 0), (0, 0), (1, 0), (0, 0)]
    for i, (kind, layer) in enumerate(rest):
        if i + 1 <= len(exchanges):
            flat_turn(0, i + 1)
        reducing.advance(kind, layer)
    for layer in reversed(range(layers)):
        for kind in range(4):
            while reducing.taken[kind, layer] < reducing.steps:
                reducing.advance(kind, layer)
    reducing.finish()
    moved_in(low, grad_o, 1)


def descend_call(gn, tn, grads, segcol, segrow, vecs, tables, xs, ws, kepts):
    layers = len(xs)
    size, model = xs[0].shape
    length = size * tn
    shapes = [ws[i][0].shape for i in range(4)]
    width, units, chips = shapes[3][0], shapes[2][0], tn // 2
    kept = kept_shapes(length, model, width, units)
    dma = pltpu.SemaphoreType.DMA
    shard = shapes[0][0] // (gn * tn)
    prows, orows = shapes[3][0] // gn, shapes[2][0] // gn
    exchanges = (gn * tn).bit_length() - 1
    outs = (
        shape((2, size // 2, model), BF16),
        shape((2, size // 2, model), BF16),
        shape((layers, 16, model), F32),
        shape((layers, tn, shard, 3 * width), BF16),
        shape((layers, tn, shard, units), BF16),
        shape((layers, prows, model), BF16),
        shape((layers, orows, model), BF16),
    )
    scratch = [pltpu.VMEM(dims, BF16) for dims in shapes]
    scratch += [pltpu.VMEM(*item) for item in kept]
    scratch += [
        pltpu.VMEM((size, model), F32),
        pltpu.VMEM((size, model), F32),
        pltpu.VMEM((length, model), BF16),
        pltpu.VMEM((length, width), BF16),
        pltpu.VMEM((length, 3 * width), BF16),
        pltpu.VMEM((length, width), F32),
        pltpu.VMEM((length, width), F32),
        pltpu.VMEM((size, model), F32),
        pltpu.VMEM((1, 3 * width), F32),
        pltpu.VMEM((1, units), F32),
    ]
    scratch += group_buffers(chips, size, model)
    for dims in shapes:
        scratch += [pltpu.VMEM(dims, BF16)] * layers
    scratch += [pltpu.VMEM((layers, (gn - 1) * dims[0] // gn, dims[1]), BF16) for dims in shapes]
    scratch += [pltpu.VMEM((layers, exchanges, 16, model), F32)]
    for _ in range(layers + 1):
        scratch += group_sems(chips, tn)
    slots = 8 * layers
    scratch += [
        dma((slots, gn)), dma((slots, gn)), dma((2, layers, tn)), dma((2, layers, tn)), dma((layers,)), dma((layers,)),
        dma((3, layers)),
        dma((14 * layers,)), dma((2, 2)), dma((2, 2)), dma((layers, exchanges)), dma((layers, exchanges)),
    ]

    def body(*refs):
        refs = list(refs)

        def take(count):
            out, refs[:] = refs[:count], refs[count:]
            return out

        ins = take(6)
        x_in = take(layers)
        w_in = [take(layers) for _ in range(4)]
        kept_in = [take(8) for _ in range(layers)]
        results = take(7)
        w, kept_s = take(4), take(8)
        work = take(10)
        bufs = take(4)
        accs = [take(layers) for _ in range(4)]
        boxes = take(4)
        flatbox = take(1)[0]
        group = [take(7) for _ in range(layers + 1)]
        reduce_sems = take(7)
        descend_kernel(
            gn, tn, layers, size, *ins, x_in, w_in, kept_in, *results, w, kept_s, *work, bufs, accs, boxes,
            flatbox, group, reduce_sems, *take(5),
        )

    flat_ws = [ws[i][layer] for i in range(4) for layer in range(layers)]
    flat_kept = [ref for layer in range(layers) for ref in kepts[layer]]
    return pl.pallas_call(
        body,
        out_shape=outs,
        in_specs=[ANY] + [VM] * 5 + [ANY] * (layers + len(flat_ws) + len(flat_kept)),
        out_specs=(ANY, ANY, VM, ANY, ANY, ANY, ANY),
        scratch_shapes=scratch,
        compiler_params=params_of(3),
        name="descend",
    )(grads, segcol, segrow, vecs, *tables, *xs, *flat_ws, *flat_kept)


GROUPS = ("dp", "h")
EVERY = ("dp", "h", "t")


def to_group(tn, blocks):
    h, t = lax.axis_index("h"), lax.axis_index("t")
    count = 2 * tn
    parity = lax.rem(t, 2)
    got = []
    for j in range(2):
        moves = [(c, ((c + j) % 2) * tn + c // 2) for c in range(count)]
        piece = jnp.where(lax.rem(parity + j, 2) == 0, blocks[0], blocks[1])
        got.append(lax.ppermute(piece, ("h", "t"), moves))
    low = jnp.where(h == 0, got[0], got[1])
    high = jnp.where(h == 0, got[1], got[0])
    return jnp.concatenate([low, high], axis=0)


def from_group(tn, rows):
    h, t = lax.axis_index("h"), lax.axis_index("t")
    count = 2 * tn
    parity = lax.rem(t, 2)
    size = rows.shape[0] // 2
    got = []
    for j in range(2):
        moves = [(((c + j) % 2) * tn + c // 2, c) for c in range(count)]
        piece = jnp.where(lax.rem(h + j, 2) == 0, rows[:size], rows[size:])
        got.append(lax.ppermute(piece, ("h", "t"), moves))
    first = jnp.where(parity == 0, got[0], got[1])
    second = jnp.where(parity == 0, got[1], got[0])
    return jnp.stack([first, second], axis=0)


def proj_moves(gn, tn):
    return [(r, (r % gn) * tn + r // gn) for r in range(gn * tn)]


def slice_columns(weight, gn, tn):
    rows, cols = weight.shape
    return weight.reshape(rows, gn, tn, cols // (gn * tn)).transpose(2, 0, 1, 3).reshape(tn, rows, cols // tn)


def slice_triple(weight, tn):
    rows, cols = weight.shape
    return weight.reshape(rows, 3, tn, cols // (3 * tn)).transpose(2, 0, 1, 3).reshape(tn, rows, cols // tn)


def gather_weights(gn, tn, triple, proj, inner, outer):
    def spread(parts):
        moved = lax.all_to_all(parts, "t", 0, 0, tiled=True)
        whole = lax.all_gather(moved.reshape(-1, moved.shape[-1]), GROUPS, axis=0, tiled=True)
        return whole

    wt = spread(slice_triple(triple, tn))
    wi = spread(slice_columns(inner, gn, tn))
    wo = lax.all_gather(outer, GROUPS, axis=0, tiled=True)
    wp = lax.all_gather(lax.ppermute(proj, EVERY, proj_moves(gn, tn)), GROUPS, axis=0, tiled=True)
    return wt, wi, wo, wp


def reduce_weights(gn, tn, dwt, dwi, dwo, dwp):
    def back(parts):
        mine = lax.psum_scatter(parts, GROUPS, scatter_dimension=0, tiled=True)
        rows = mine.shape[0] // tn
        return lax.all_to_all(mine.reshape(tn, rows, -1), "t", 0, 0, tiled=True).astype(F32)

    triple = back(dwt)
    rows = triple.shape[1]
    triple = triple.reshape(tn, rows, 3, -1).transpose(1, 2, 0, 3).reshape(rows, -1)
    inner = back(dwi)
    inner = inner.reshape(tn, rows, gn, -1).transpose(1, 2, 0, 3).reshape(rows, -1)
    outer = lax.psum_scatter(dwo, GROUPS, scatter_dimension=0, tiled=True).astype(F32)
    proj = lax.psum_scatter(dwp, GROUPS, scatter_dimension=0, tiled=True)
    proj = lax.ppermute(proj, EVERY, [(b, a) for a, b in proj_moves(gn, tn)]).astype(F32)
    return triple, proj, inner, outer


def per_device(
    gn, tn,
    tokens, segments, cotangent, triple_weight, triple_bias, proj_weight, proj_bias, inner_weight, inner_bias,
    outer_weight, outer_bias, first_gain, first_shift, second_gain, second_shift,
):
    layers = triple_weight.shape[0]
    model = tokens.shape[2]
    span = tokens.shape[1] * 2 * tn
    h, t = lax.axis_index("h"), lax.axis_index("t")
    device = (lax.axis_index("dp") * 2 + h) * tn + t
    shards = gn * tn
    heads_wide = model // tn
    units = outer_weight.shape[1] * gn

    rows = triple_weight.shape[1]
    block = tokens.shape[1]
    tables = constant_tables(span, shards, model)
    direct = rows % 16 == 0 and block == 128 and layers * 4 <= 16 and units == model
    if direct:
        head = jnp.stack(
            [
                inner_bias,
                jnp.pad(triple_bias, ((0, 0), (0, 128 - triple_bias.shape[1]))),
                jnp.concatenate([proj_bias, outer_bias, first_gain, first_shift], axis=1),
                jnp.pad(jnp.concatenate([second_gain, second_shift], axis=1), ((0, 0), (0, 64))),
            ],
            axis=1,
        ).reshape(4 * layers, 128)
        opened = ascend_call(
            gn, tn, tokens, cotangent, jnp.pad(segments, ((0, 6), (0, 0))),
            jnp.pad(head, ((0, 16 - 4 * layers), (0, 0))),
            triple_weight.reshape(layers, rows, 3, tn, -1).transpose(0, 3, 1, 2, 4).reshape(layers, tn, rows, -1),
            inner_weight.reshape(layers, rows, gn, tn, -1).transpose(0, 3, 1, 2, 4).reshape(layers, tn, rows, -1),
            outer_weight, proj_weight, tables,
            placement(model // shards, shards) + placement(3 * model // shards, shards),
        )
        opened = list(opened)
        grad_all, segcol, segrow, vecs, _, _ = opened[:6]
        opened = opened[6:]
        inputs = opened[:layers]
        weights = [tuple(opened[layers + k * layers + layer] for k in range(4)) for layer in range(layers)]
        kept = [opened[5 * layers + 8 * i : 5 * layers + 8 * (i + 1)] for i in range(layers)]
        output, tokens_grad, summed, triple, inner, proj, outer = descend_call(
            gn, tn, grad_all, segcol, segrow, vecs, tables, inputs,
            [[weights[layer][k] for layer in range(layers)] for k in range(4)], kept,
        )
        summed = summed.reshape(layers, -1)
        triple = triple.reshape(layers, tn, rows, 3, -1).transpose(0, 2, 3, 1, 4).reshape(layers, rows, -1).astype(F32)
        inner = inner.reshape(layers, tn, rows, gn, -1).transpose(0, 2, 3, 1, 4).reshape(layers, rows, -1).astype(F32)
        proj, outer = proj.astype(F32), outer.astype(F32)
    else:
        small = (triple_bias, inner_bias, proj_bias, outer_bias, first_gain, first_shift, second_gain, second_shift)
        starts = [0]
        for item in small:
            starts.append(starts[-1] + item.shape[1])
        packed = jnp.concatenate(small, axis=1)
        x = to_group(tn, tokens).astype(F32)
        cot = to_group(tn, cotangent).astype(F32)
        segs_all = lax.all_gather(segments, ("h", "t"), axis=1, tiled=True)
        everything = lax.all_gather(packed[None], EVERY, axis=0, tiled=True).astype(F32)
        weights = [
            gather_weights(
                gn, tn, triple_weight[layer], proj_weight[layer], inner_weight[layer], outer_weight[layer]
            )
            for layer in range(layers)
        ]
        segs = jnp.where(h == 0, segs_all[0], segs_all[1])
        segs = jnp.where(segs == 0, -1 - jnp.arange(span, dtype=jnp.int32), segs).astype(F32)
        tables = (segs[:, None], segs[None, :]) + tables

        def vector(layer, i):
            return everything[:, layer, starts[i] : starts[i + 1]].reshape(-1)

        vecs, inputs, kept = [], [], []
        for layer in range(layers):
            bt = lax.dynamic_index_in_dim(vector(layer, 0).reshape(3, tn, heads_wide), t, 1, keepdims=False)
            bi = lax.dynamic_index_in_dim(vector(layer, 1).reshape(gn, tn, -1), t, 1, keepdims=False)
            zero = jnp.zeros((model,), F32)
            vecs.append(
                jnp.stack(
                    [vector(layer, 4), vector(layer, 5), vector(layer, 6), vector(layer, 7)]
                    + [vector(layer, 2) + vector(layer, 3), zero, zero, zero]
                )
            )
            inputs.append(x)
            x, *saved = forward_layer(
                tn, x, weights[layer], vecs[layer], bt.reshape(1, -1), bi.reshape(1, -1), tables
            )
            kept.append(saved)
        output = x.astype(BF16)
        grad = cot
        mats, flats = [None] * layers, [None] * layers
        for layer in reversed(range(layers)):
            grad, dwt, dwi, dwo, dwp, dvec, dbt, dbi = backward_layer(
                tn, grad, inputs[layer], weights[layer], vecs[layer], tables, kept[layer]
            )
            mats[layer] = reduce_weights(gn, tn, dwt, dwi, dwo, dwp)
            part = lax.dynamic_update_slice(
                jnp.zeros((3, tn, heads_wide), F32), dbt.reshape(3, 1, heads_wide), (0, t, 0)
            )
            side = lax.dynamic_update_slice(
                jnp.zeros((gn, tn, units // gn), F32), dbi.reshape(gn, 1, units // gn), (0, t, 0)
            )
            flats[layer] = jnp.concatenate([dvec[:5].reshape(-1), part.reshape(-1), side.reshape(-1)])
        output, tokens_grad = from_group(tn, output), from_group(tn, grad.astype(BF16))
        triple, proj, inner, outer = (jnp.stack([m[k] for m in mats]) for k in range(4))
        summed = lax.psum(jnp.stack(flats), EVERY)

    def own(start, length):
        piece = length // shards
        return lax.dynamic_slice_in_dim(summed, start + device * piece, piece, 1)

    base = 5 * model
    bias_sum = own(4 * model, model)
    return (
        output,
        tokens_grad,
        triple,
        own(base, 2 * model),
        own(base + 2 * model, model),
        proj,
        bias_sum,
        inner,
        own(base + 3 * model, units * tn),
        outer,
        bias_sum,
        own(0, model),
        own(model, model),
        own(2 * model, model),
        own(3 * model, model),
    )


def solution(mesh):
    dp, ctx = mesh.shape["dp"], mesh.shape["ctx"]
    tn = ctx // 2
    gn = 2 * dp
    fine = Mesh(mesh.devices.reshape(dp, 2, tn), EVERY)
    seq = P("dp", ("h", "t"), None)
    mat = P(None, EVERY, None)
    row = P(None, EVERY)
    in_specs = (seq, P("dp", ("h", "t")), seq, mat, row, mat, row, mat, row, mat, row, row, row, row, row)
    out_specs = (seq, seq, mat, row, row, mat, row, mat, row, mat, row, row, row, row, row)
    return jax.shard_map(
        functools.partial(per_device, gn, tn), mesh=fine, in_specs=in_specs, out_specs=out_specs, check_vma=False
    )
```

```python
import functools
import math

import jax
import jax.numpy as jnp
import numpy as np
from jax import lax
from jax.experimental import pallas as pl
from jax.experimental.pallas import tpu as pltpu
from jax.sharding import Mesh
from jax.sharding import PartitionSpec as P

HD = 64
ROT = 16
EPSILON = 1e-05
NEG_LARGE = -1e30
MESH = pl.DeviceIdType.MESH
BF16 = jnp.bfloat16
F32 = jnp.float32
VMEM_LIMIT = 60 * 1024 * 1024


def dot(a, b, dims):
    return lax.dot_general(a, b, (dims, ((), ())), preferred_element_type=F32)


NN = ((1,), (0,))
NT = ((1,), (1,))
TN = ((0,), (0,))


def rows_of(b, size):
    return pl.ds(pl.multiple_of(b * size, size), size)


def group_barrier(tn):
    t = lax.axis_index("t")
    zc, co = t // 2, lax.rem(t, 2)
    chips = tn // 2
    sem = pltpu.get_barrier_semaphore()
    peers = [zc * 2 + 1 - co] + [lax.rem(zc + k, chips) * 2 + co for k in range(1, chips)]
    for p in peers:
        pl.semaphore_signal(sem, inc=1, device_id={"t": p}, device_id_type=MESH)
    pl.semaphore_wait(sem, len(peers))


class Spread:
    def __init__(self, tn, buf, size, ssem, fsem, rsem):
        self.tn, self.buf, self.size = tn, buf, size
        self.ssem, self.fsem, self.rsem = ssem, fsem, rsem
        self.t = lax.axis_index("t")
        self.zc, self.co = self.t // 2, lax.rem(self.t, 2)
        self.chips = tn // 2

    def copy(self, block, send, to):
        ref = self.buf.at[rows_of(block, self.size)]
        return pltpu.make_async_remote_copy(
            ref, ref, send, self.rsem.at[block], device_id={"t": to}, device_id_type=MESH
        )

    def start(self):
        for k in range(1, self.chips):
            chip = lax.rem(self.zc + k, self.chips)
            self.copy(self.t, self.ssem.at[k], chip * 2 + self.co).start()
        self.copy(self.t, self.ssem.at[0], self.zc * 2 + 1 - self.co).start()

    def peer_core(self):
        b = self.zc * 2 + 1 - self.co
        self.copy(b, self.ssem.at[0], b).wait_recv()
        return b

    def same_core(self, k):
        b = lax.rem(self.zc + self.chips - k, self.chips) * 2 + self.co
        self.copy(b, self.fsem.at[k], b).wait_recv()
        self.copy(b, self.fsem.at[k], self.zc * 2 + 1 - self.co).start()
        return b

    def other_core(self, k):
        b = lax.rem(self.zc + self.chips - k, self.chips) * 2 + 1 - self.co
        self.copy(b, self.fsem.at[k], b).wait_recv()
        return b

    def finish(self):
        for k in range(self.chips):
            self.copy(self.t, self.ssem.at[k], self.t).wait_send()
        for k in range(1, self.chips):
            self.copy(self.t, self.fsem.at[k], self.t).wait_send()


class Gather:
    def __init__(self, tn, tocore, fromcore, toici, fromici, sems):
        self.tn = tn
        self.tocore, self.fromcore, self.toici, self.fromici = tocore, fromcore, toici, fromici
        self.cs, self.cr, self.ls, self.lr = sems
        self.t = lax.axis_index("t")
        self.zc, self.co = self.t // 2, lax.rem(self.t, 2)
        self.chips = tn // 2

    def core_copy(self, chip):
        return pltpu.make_async_remote_copy(
            self.tocore.at[chip],
            self.fromcore.at[chip],
            self.cs.at[chip],
            self.cr.at[chip],
            device_id={"t": self.zc * 2 + 1 - self.co},
            device_id_type=MESH,
        )

    def link_copy(self, chip, slot):
        return pltpu.make_async_remote_copy(
            self.toici.at[chip],
            self.fromici.at[slot],
            self.ls.at[chip],
            self.lr.at[slot],
            device_id={"t": chip * 2 + self.co},
            device_id_type=MESH,
        )

    def send_core(self, chip):
        self.core_copy(chip).start()

    def send_link(self, chip):
        self.core_copy(chip).wait_recv()
        self.toici[chip] = (self.toici[chip].astype(F32) + self.fromcore[chip].astype(F32)).astype(BF16)
        self.link_copy(chip, self.zc).start()

    def total(self):
        self.core_copy(self.zc).wait_recv()
        value = self.fromcore[self.zc].astype(F32)
        for k in range(1, self.chips):
            chip = lax.rem(self.zc + k, self.chips)
            self.link_copy(chip, chip).wait_recv()
            value = value + self.fromici[chip].astype(F32)
        return value

    def finish(self):
        for chip in range(self.chips):
            self.core_copy(chip).wait_send()
        for k in range(1, self.chips):
            chip = lax.rem(self.zc + k, self.chips)
            self.link_copy(chip, self.zc).wait_send()


def norm_stats(x):
    mean = jnp.mean(x, axis=-1, keepdims=True)
    centred = x - mean
    inverse = lax.rsqrt(jnp.mean(centred * centred, axis=-1, keepdims=True) + EPSILON)
    return centred * inverse, inverse


def widen(tab, width):
    return jnp.concatenate([tab] * (width // tab.shape[1]), axis=1)


def turn(x, cos, sine, sign):
    width = x.shape[1]
    cos, sine = widen(cos, width), widen(sine, width)
    front = lax.rem(lax.broadcasted_iota(jnp.int32, (1, width), 1), HD) < ROT // 2
    partner = jnp.where(front, pltpu.roll(x, width - ROT // 2, 1), pltpu.roll(x, ROT // 2, 1))
    return x * cos + sign * (partner * sine)


def head_masks(width, dtype):
    lane = lax.broadcasted_iota(jnp.int32, (1, width), 1) // HD
    return [(lane == h).astype(F32).astype(dtype) for h in range(width // HD)]


def pair_bias(qb, kb, size, segcol, segrow):
    qpos = lax.broadcasted_iota(jnp.int32, (size, size), 0) + qb * size
    kpos = lax.broadcasted_iota(jnp.int32, (size, size), 1) + kb * size
    same = segcol[rows_of(qb, size), :] == segrow[:, rows_of(kb, size)]
    return jnp.where(same & (kpos <= qpos), 0.0, NEG_LARGE)


TILE = 256
SKEW = 1


class Forward:
    def __init__(self, tn, size, x, w, vecs, segs, tables, kept, keep):
        self.tn, self.size, self.chips = tn, size, tn // 2
        self.x, self.keep = x, keep
        self.wt, self.wi, self.wo, self.wp = w
        self.vec, self.bt, self.bi = vecs
        self.segcol, self.segrow = segs
        self.tables = tables
        self.n, self.q, self.k, self.v, self.o, self.lse, self.g, self.gp = kept
        self.width, self.units = self.q.shape[1], self.g.shape[1]
        self.heads = self.width // HD

    def norm(self, t):
        own, _ = norm_stats(self.x[...])
        self.n[rows_of(t, self.size), :] = own.astype(BF16)

    def heads_in(self, b):
        width, vec, bt = self.width, self.vec, self.bt
        rows = rows_of(b, self.size)
        h1 = (self.n[rows, :].astype(F32) * vec[0:1, :] + vec[1:2, :]).astype(BF16)
        cos, sine = (tab[rows, :] for tab in self.tables)
        q = dot(h1, self.wt[:, 0:width], NN) + bt[:, 0:width]
        low = turn(q, cos, sine, 1.0).astype(BF16).astype(F32)
        self.q[rows, :] = (low * (1.0 / math.sqrt(HD))).astype(BF16)
        k = dot(h1, self.wt[:, width : 2 * width], NN) + bt[:, width : 2 * width]
        self.k[rows, :] = turn(k, cos, sine, 1.0).astype(BF16)
        v = dot(h1, self.wt[:, 2 * width : 3 * width], NN) + bt[:, 2 * width : 3 * width]
        self.v[rows, :] = v.astype(BF16)

    def mixer_in(self, b, blocks=1):
        rows = rows_of(b, self.size * blocks)
        h2 = (self.n[rows, :].astype(F32) * self.vec[2:3, :] + self.vec[3:4, :]).astype(BF16)

        def mix(j, carry):
            cols = rows_of(j, TILE)
            u = dot(h2, self.wi[:, cols], NN) + self.bi[:, cols]
            half = 0.5 + 0.5 * lax.erf(u * (1.0 / math.sqrt(2.0)))
            self.g[rows, cols] = (u * half).astype(BF16)
            bell = jnp.exp(-0.5 * u * u) * (1.0 / math.sqrt(2.0 * math.pi))
            self.gp[rows, cols] = (half + u * bell).astype(BF16)
            return carry

        lax.fori_loop(0, self.units // TILE, mix, 0)

    def attend(self, b):
        size, width, heads = self.size, self.width, self.heads
        masks = head_masks(width, F32)
        lane = lax.broadcasted_iota(jnp.int32, (1, 128), 1)
        rows = rows_of(b, size)
        qb = self.q[rows, :]
        qs = [qb * masks[h].astype(BF16) for h in range(heads)]

        def step(i, carry):
            peaks, sums, acc = carry
            kb = b - i
            keys = self.k[rows_of(kb, size), :]
            vals = self.v[rows_of(kb, size), :]
            bias = pair_bias(b, kb, size, self.segcol, self.segrow)
            new_peaks, new_sums = [], []
            scale = jnp.zeros((size, width), F32)
            add = jnp.zeros((size, width), F32)
            for h in range(heads):
                s = dot(qs[h], keys, NT) + bias
                peak = jnp.maximum(peaks[h], jnp.max(s, axis=1, keepdims=True))
                p = jnp.exp(s - peak)
                fade = jnp.exp(peaks[h] - peak)
                new_peaks.append(peak)
                new_sums.append(sums[h] * fade + jnp.sum(p, axis=1, keepdims=True))
                scale = scale + fade * masks[h]
                add = add + dot(p.astype(BF16), vals * masks[h].astype(BF16), NN)
            return tuple(new_peaks), tuple(new_sums), acc * scale + add

        start = (
            tuple(jnp.full((size, 1), NEG_LARGE, F32) for _ in range(heads)),
            tuple(jnp.zeros((size, 1), F32) for _ in range(heads)),
            jnp.zeros((size, width), F32),
        )
        peaks, sums, acc = lax.fori_loop(0, b + 1, step, start)
        scale = jnp.zeros((size, width), F32)
        lse = jnp.zeros((size, 128), F32)
        for h in range(heads):
            scale = scale + (1.0 / sums[h]) * masks[h]
            lse = jnp.where(lane == h, peaks[h] + jnp.log(sums[h]), lse)
        self.lse[rows, :] = lse
        self.o[rows, :] = acc * scale

    def branches(self, b, store):
        rows = rows_of(b, self.size)

        def part(j, carry):
            cols = rows_of(j, TILE)
            value = dot(self.g[rows, :], self.wo[:, cols], NN)
            store(cols, value + dot(self.o[rows, :].astype(BF16), self.wp[:, cols], NN))
            return carry

        lax.fori_loop(0, self.x.shape[1] // TILE, part, 0)

    def into(self, ref, chip):
        def store(cols, value):
            ref[chip, :, cols] = value.astype(BF16)

        return store

    def into_keep(self, cols, value):
        self.keep[:, cols] = value


def arrivals(spread):
    yield spread.t
    yield spread.peer_core()
    for i in range(1, spread.chips):
        yield spread.same_core(i)
        yield spread.other_core(i)


def far_first(spread):
    out = []
    for i in range(1, spread.chips):
        chip = lax.rem(spread.zc + i, spread.chips)
        out += [chip * 2 + 1 - spread.co, chip * 2 + spread.co]
    return out + [spread.zc * 2 + 1 - spread.co, spread.t]


def branch_sums(layer, spread, gather, tick=lambda: None):
    for i in range(1, spread.chips):
        chip = lax.rem(spread.zc + i, spread.chips)
        layer.branches(chip * 2 + 1 - spread.co, layer.into(gather.tocore, chip))
        gather.send_core(chip)
        layer.branches(chip * 2 + spread.co, layer.into(gather.toici, chip))
        gather.send_link(chip)
        tick()
    layer.branches(spread.zc * 2 + 1 - spread.co, layer.into(gather.tocore, spread.zc))
    gather.send_core(spread.zc)
    layer.branches(spread.t, layer.into_keep)
    tick()


def forward_kernel(
    tn, size,
    x_ref, wt, wi, wo, wp, vec, bt, bi, segcol, segrow, ctab, stab,
    xo_ref, n_ref, q_ref, k_ref, v_ref, o_ref, lse_ref, g_ref, gp_ref,
    keep, tocore, fromcore, toici, fromici, ssem, fsem, rsem, cs, cr, ls, lr,
):
    group_barrier(tn)
    spread = Spread(tn, n_ref, size, ssem, fsem, rsem)
    gather = Gather(tn, tocore, fromcore, toici, fromici, (cs, cr, ls, lr))
    layer = Forward(
        tn, size, x_ref, (wt, wi, wo, wp), (vec, bt, bi), (segcol, segrow), (ctab, stab),
        (n_ref, q_ref, k_ref, v_ref, o_ref, lse_ref, g_ref, gp_ref), keep,
    )
    layer.norm(spread.t)
    spread.start()
    for b in arrivals(spread):
        layer.heads_in(b)
        layer.mixer_in(b)
    for b in far_first(spread):
        layer.attend(b)
    branch_sums(layer, spread, gather)
    xo_ref[...] = x_ref[...] + vec[4:5, :] + keep[...] + gather.total()
    spread.finish()
    gather.finish()


def backward_kernel(
    tn, size,
    dy_ref, x_ref, wt, wi, wo, wp, vec, segcol, segrow, ctab, stab,
    n_ref, q_ref, k_ref, v_ref, o_ref, lse_ref, g_ref, gp_ref,
    dx_ref, dwt, dwi, dwo, dwp, dvec, dbt, dbi,
    gb, do, du, dt, dq, dk, dv, dh2, keep,
    tocore, fromcore, toici, fromici, ssem, fsem, rsem, cs, cr, ls, lr,
):
    chips = tn // 2
    width = q_ref.shape[1]
    heads = width // HD
    units = g_ref.shape[1]
    model = x_ref.shape[1]
    group_barrier(tn)
    spread = Spread(tn, gb, size, ssem, fsem, rsem)
    gather = Gather(tn, tocore, fromcore, toici, fromici, (cs, cr, ls, lr))
    t, zc, co = spread.t, spread.zc, spread.co
    own = dy_ref[...].astype(F32).astype(BF16)
    gb[rows_of(t, size), :] = own
    spread.start()
    dvec[...] = jnp.zeros_like(dvec)
    dbt[...] = jnp.zeros_like(dbt)
    dbi[...] = jnp.zeros_like(dbi)
    dvec[4:5, :] = jnp.sum(own.astype(F32), axis=0, keepdims=True)
    dq[...] = jnp.zeros_like(dq)
    dk[...] = jnp.zeros_like(dk)
    dv[...] = jnp.zeros_like(dv)

    def mixer(b):
        rows = rows_of(b, size)
        grad = gb[rows, :]
        do[rows, :] = dot(grad, wp[...], NT).astype(BF16)

        def unit(j, carry):
            cols = rows_of(j, TILE)
            d = (dot(grad, wo[cols, :], NT) * gp_ref[rows, cols].astype(F32)).astype(BF16)
            du[rows, cols] = d
            dbi[0:1, cols] += jnp.sum(d.astype(F32), axis=0, keepdims=True)
            return carry

        lax.fori_loop(0, units // TILE, unit, 0)

        def back(j, carry):
            cols = rows_of(j, TILE)
            d = dot(du[rows, :], wi[cols, :], NT)
            dvec[2:3, cols] += jnp.sum(d * n_ref[rows, cols].astype(F32), axis=0, keepdims=True)
            dvec[3:4, cols] += jnp.sum(d, axis=0, keepdims=True)
            dh2[rows, cols] = d * vec[2:3, cols]
            return carry

        lax.fori_loop(0, model // TILE, back, 0)

    mixer(t)
    mixer(spread.peer_core())
    for i in range(1, chips):
        mixer(spread.same_core(i))
        mixer(spread.other_core(i))

    masks = head_masks(width, BF16)
    lane = lax.broadcasted_iota(jnp.int32, (1, 128), 1)
    up = zc >= (chips + 1) // 2
    tsize = tn

    def pair(qb, kb):
        qrows, krows = rows_of(qb, size), rows_of(kb, size)
        q, keys, vals = q_ref[qrows, :], k_ref[krows, :], v_ref[krows, :]
        grad = do[qrows, :]
        prod = grad.astype(F32) * o_ref[qrows, :]
        lse = lse_ref[qrows, :]
        bias = pair_bias(qb, kb, size, segcol, segrow)
        dq_new = jnp.zeros((size, width), F32)
        dk_new = jnp.zeros((size, width), F32)
        dv_new = jnp.zeros((size, width), F32)
        for h in range(heads):
            qh, gh = q * masks[h], grad * masks[h]
            total = jnp.sum(jnp.where(lane == h, lse, 0.0), axis=1, keepdims=True)
            delta = jnp.sum(prod * masks[h].astype(F32), axis=1, keepdims=True)
            p = jnp.exp(dot(qh, keys, NT) + bias - total)
            ds = (p * (dot(gh, vals, NT) - delta)).astype(BF16)
            dv_new = dv_new + dot(p.astype(BF16), gh, TN)
            dk_new = dk_new + dot(ds, qh, TN)
            dq_new = dq_new + dot(ds, keys * masks[h], NN)
        dq[qrows, :] += dq_new
        dk[krows, :] += dk_new
        dv[krows, :] += dv_new

    def attend_back(stage):
        pivot = jnp.where(up, stage, tsize - 1 - stage)

        def step(j, carry):
            pair(jnp.where(up, pivot + j, pivot), jnp.where(up, pivot, pivot - j))
            return carry

        lax.fori_loop(0, tsize - stage, step, 0)
        rows = rows_of(pivot, size)
        cos, sine = ctab[rows, :], stab[rows, :]
        dt[rows, 0:width] = turn(dq[rows, :] * (1.0 / math.sqrt(HD)), cos, sine, -1.0).astype(BF16)
        dt[rows, width : 2 * width] = turn(dk[rows, :], cos, sine, -1.0).astype(BF16)
        dt[rows, 2 * width : 3 * width] = dv[rows, :].astype(BF16)
        block = dt[rows, :]
        dbt[...] += jnp.sum(block.astype(F32), axis=0, keepdims=True)

        def back(j, carry):
            cols = rows_of(j, TILE)
            d = dot(block, wt[cols, :], NT)
            dvec[0:1, cols] += jnp.sum(d * n_ref[rows, cols].astype(F32), axis=0, keepdims=True)
            dvec[1:2, cols] += jnp.sum(d, axis=0, keepdims=True)
            dh2[rows, cols] = dh2[rows, cols] + d * vec[0:1, cols]
            return carry

        lax.fori_loop(0, model // TILE, back, 0)
        value = dh2[rows, :]
        chip, core = pivot // 2, lax.rem(pivot, 2)

        @pl.when(core != co)
        def _():
            tocore[chip] = value.astype(BF16)
            gather.send_core(chip)

        @pl.when((core == co) & (chip != zc))
        def _():
            toici[chip] = value.astype(BF16)

        @pl.when(pivot == t)
        def _():
            keep[...] = value

        if stage % 2 == 1:

            @pl.when(chip != zc)
            def _():
                gather.send_link(chip)

    for stage in range(tn):
        attend_back(stage)

    def grad_one(j, carry):
        cols = rows_of(j, TILE)
        h1 = (n_ref[:, cols].astype(F32) * vec[0:1, cols] + vec[1:2, cols]).astype(BF16)
        dwt[cols, :] = dot(h1, dt[...], TN).astype(dwt.dtype)
        return carry

    lax.fori_loop(0, model // TILE, grad_one, 0)

    def grad_two(j, carry):
        cols = rows_of(j, TILE)
        h2 = (n_ref[:, cols].astype(F32) * vec[2:3, cols] + vec[3:4, cols]).astype(BF16)
        dwi[cols, :] = dot(h2, du[...], TN).astype(dwi.dtype)
        return carry

    lax.fori_loop(0, model // TILE, grad_two, 0)

    def grad_three(j, carry):
        cols = rows_of(j, TILE)
        dwo[cols, :] = dot(g_ref[:, cols], gb[...], TN).astype(dwo.dtype)
        return carry

    lax.fori_loop(0, units // TILE, grad_three, 0)
    small = min(TILE, width)

    def grad_four(j, carry):
        cols = rows_of(j, small)
        dwp[cols, :] = dot(o_ref[:, cols].astype(BF16), gb[...], TN).astype(dwp.dtype)
        return carry

    lax.fori_loop(0, width // small, grad_four, 0)

    own_n, inverse = norm_stats(x_ref[...])
    e = keep[...] + gather.total()
    inner = e - jnp.mean(e, axis=-1, keepdims=True) - own_n * jnp.mean(e * own_n, axis=-1, keepdims=True)
    dx_ref[...] = dy_ref[...].astype(F32) + inner * inverse
    spread.finish()
    gather.finish()


VM = pl.BlockSpec(memory_space=pltpu.VMEM)


def shape(dims, dtype):
    return jax.ShapeDtypeStruct(tuple(dims), dtype)


def group_sems(chips, tn):
    dma = pltpu.SemaphoreType.DMA
    return [dma((chips,)), dma((chips,)), dma((tn,)), dma((chips,)), dma((chips,)), dma((chips,)), dma((chips,))]


def group_buffers(chips, size, model):
    return [pltpu.VMEM((chips, size, model), BF16) for _ in range(4)]


def params_of(cid):
    return pltpu.CompilerParams(collective_id=cid, has_side_effects=True, vmem_limit_bytes=VMEM_LIMIT)


def forward_layer(tn, x, weights, vec, bt, bi, tables):
    wt, wi, wo, wp = weights
    size, model = x.shape
    length = size * tn
    width, units, chips = wp.shape[0], wo.shape[0], tn // 2
    outs = (
        shape((size, model), F32),
        shape((length, model), BF16),
        shape((length, width), BF16),
        shape((length, width), BF16),
        shape((length, width), BF16),
        shape((length, width), F32),
        shape((length, 128), F32),
        shape((length, units), BF16),
        shape((length, units), BF16),
    )
    return pl.pallas_call(
        functools.partial(forward_kernel, tn, size),
        out_shape=outs,
        in_specs=[VM] * 12,
        out_specs=[VM] * len(outs),
        scratch_shapes=[pltpu.VMEM((size, model), F32)] + group_buffers(chips, size, model) + group_sems(chips, tn),
        compiler_params=params_of(0),
        name="forward",
    )(x, wt, wi, wo, wp, vec, bt, bi, *tables)


def backward_layer(tn, dy, x, weights, vec, tables, kept):
    wt, wi, wo, wp = weights
    size, model = x.shape
    length = size * tn
    width, units, chips = wp.shape[0], wo.shape[0], tn // 2
    outs = (
        shape((size, model), F32),
        shape(wt.shape, BF16),
        shape(wi.shape, BF16),
        shape(wo.shape, BF16),
        shape(wp.shape, BF16),
        shape((8, model), F32),
        shape((1, 3 * width), F32),
        shape((1, units), F32),
    )
    return pl.pallas_call(
        functools.partial(backward_kernel, tn, size),
        out_shape=outs,
        in_specs=[VM] * 19,
        out_specs=[VM] * len(outs),
        scratch_shapes=[
            pltpu.VMEM((length, model), BF16),
            pltpu.VMEM((length, width), BF16),
            pltpu.VMEM((length, units), BF16),
            pltpu.VMEM((length, 3 * width), BF16),
            pltpu.VMEM((length, width), F32),
            pltpu.VMEM((length, width), F32),
            pltpu.VMEM((length, width), F32),
            pltpu.VMEM((length, model), F32),
            pltpu.VMEM((size, model), F32),
        ]
        + group_buffers(chips, size, model)
        + group_sems(chips, tn),
        compiler_params=params_of(1),
        name="backward",
    )(dy, x, wt, wi, wo, wp, vec, *tables, *kept)


class Place:
    def __init__(self, gn, tn):
        self.gn, self.tn = gn, tn
        self.h, self.t = lax.axis_index("h"), lax.axis_index("t")
        self.g = lax.axis_index("dp") * 2 + self.h
        self.c = self.h * tn + self.t
        self.bits = [1 << i for i in range(gn.bit_length() - 1)]

    def group(self, g):
        return {"dp": g // 2, "h": lax.rem(g, 2)}

    def line(self, c):
        return {"h": c // self.tn, "t": lax.rem(c, self.tn)}

    def other(self, k):
        return lax.rem(self.t + k, self.tn)


def flip(value, bit):
    return value + bit * (1 - 2 * lax.rem(value // bit, 2))


def remote(src, dst, send, recv, device):
    return pltpu.make_async_remote_copy(src, dst, send, recv, device_id=device, device_id_type=MESH)


def runs_by_step(place, bits):
    runs, steps = [(place.g, 1)], []
    for bit in bits:
        steps.append((bit, runs))
        if len(runs) == 1 and runs[0][1] == bit:
            runs = [(runs[0][0] // (2 * bit) * (2 * bit), 2 * bit)]
        else:
            runs = runs + [(flip(start, bit), count) for start, count in runs]
    return steps


def bit_orders(place):
    bits = place.bits
    return [bits, bits[:1] + bits[:0:-1]]


class Doubling:
    def __init__(self, place, ref, block, cols, order, sems, slot):
        self.place, self.ref, self.block, self.cols, self.order = place, ref, block, cols, order
        self.send, self.recv, self.slot = sems[0], sems[1], slot
        self.levels = [[] for _ in order]
        for i, bit in enumerate(order):
            for bits in range(1 << i):
                held = [order[j] for j in range(i) if bits >> j & 1]
                self.levels[len(held)].append((bit, held))

    def at(self, held):
        g = self.place.g
        for bit in held:
            g = flip(g, bit)
        return g

    def copy(self, bit, held):
        start = self.at(held)
        rows = pl.ds(pl.multiple_of(start * self.block, self.block), self.block)
        ref = self.ref.at[rows, self.cols]
        index = sum(held) + bit
        return remote(
            ref,
            ref,
            self.send.at[self.slot, index],
            self.recv.at[self.slot, index],
            self.place.group(flip(self.place.g, bit)),
        )

    def arrive(self, held):
        start = self.at(held)
        rows = pl.ds(pl.multiple_of(start * self.block, self.block), self.block)
        ref = self.ref.at[rows, self.cols]
        index = sum(held)
        peer = self.place.group(flip(self.place.g, held[-1]))
        remote(ref, ref, self.send.at[self.slot, index], self.recv.at[self.slot, index], peer).wait_recv()

    def advance(self, level):
        seen = set()
        for bit, held in self.levels[level]:
            if held and tuple(held) not in seen:
                seen.add(tuple(held))
                self.arrive(held)
            self.copy(bit, held).start()

    def whole(self):
        last = self.order[-1]
        for level in self.levels:
            for bit, held in level:
                if bit == last:
                    self.arrive(held + [bit])

    def finish(self):
        for level in self.levels:
            for item in level:
                self.copy(*item).wait_send()


def halves(cols):
    return [pl.ds(0, cols // 2), pl.ds(cols // 2, cols // 2)]


def line_barrier(place, extra):
    sem = pltpu.get_barrier_semaphore()
    span = 2 * place.tn
    for k in range(1, span):
        pl.semaphore_signal(sem, inc=1, device_id=place.line(lax.rem(place.c + k, span)), device_id_type=MESH)
    for bit in place.bits[1:]:
        pl.semaphore_signal(sem, inc=1, device_id=place.group(flip(place.g, bit)), device_id_type=MESH)
    peers = span - 1 + len(place.bits) - 1
    source, moved = extra

    @pl.when(moved)
    def _():
        pl.semaphore_signal(sem, inc=1, device_id=source, device_id_type=MESH)
        pl.semaphore_wait(sem, peers + 1)

    @pl.when(jnp.logical_not(moved))
    def _():
        pl.semaphore_wait(sem, peers)


def proj_places(place):
    gn, tn = place.gn, place.tn
    r = place.g * tn + place.t
    target = place.group(lax.rem(r, gn)) | {"t": r // gn}
    q = place.t * gn + place.g
    source = place.group(q // tn) | {"t": lax.rem(q, tn)}
    return target, source, r, q


def slot_rows(index, size):
    return pl.ds(pl.multiple_of(index * size, size), size)


class Opening:
    def __init__(self, place, layers, tok, cot, seg, vec, tri, inn, outer, proj, tok_o, cot_o, seg_o, vec_o, w, sems):
        self.place, self.layers = place, layers
        self.tok, self.cot, self.seg, self.vec = tok, cot, seg, vec
        self.tri, self.inn, self.outer, self.proj = tri, inn, outer, proj
        self.tok_o, self.cot_o, self.seg_o, self.vec_o = tok_o, cot_o, seg_o, vec_o
        self.wts, self.wis, self.wos, self.wps = w
        (
            self.ssem, self.rsem, self.lsem, self.asend, self.arecv, self.psend, self.precv,
            self.msend, self.mrecv, self.gsend, self.grecv,
        ) = sems
        self.half = tok.shape[1]
        self.target, self.source, self.r, self.q = proj_places(place)
        self.moved = self.q != self.r
        self.local, self.sends, self.shared_with = [], [], {}
        self.locals_of = {}

    def barrier(self):
        line_barrier(self.place, (self.source, self.moved))

    def near(self, src, dst, key):
        cp = pltpu.make_async_copy(src, dst, self.lsem.at[len(self.local)])
        cp.start()
        self.local.append(cp)
        self.locals_of[key] = cp

    def hop(self, src, dst, slot, i):
        c, tn = self.place.c, self.place.tn
        to = i * tn + c // 2
        rows = slot_rows(lax.rem(c, 2), self.half)
        near = pltpu.make_async_copy(src.at[i], dst.at[rows], self.msend.at[slot, i])
        far = remote(
            src.at[i], dst.at[rows], self.msend.at[slot, i], self.mrecv.at[slot, lax.rem(c, 2)],
            self.place.line(to),
        )
        return to == c, near, far

    def move(self, src, dst, slot):
        for i in range(2):
            stays, near, far = self.hop(src, dst, slot, i)
            pl.when(stays)(near.start)
            pl.when(jnp.logical_not(stays))(far.start)

    def moved_in(self, src, dst, slot):
        for i in range(2):
            stays, near, far = self.hop(src, dst, slot, i)
            pl.when(stays)(near.wait)
            pl.when(jnp.logical_not(stays))(far.wait_send)
        for s in range(2):
            cp = remote(
                src.at[0], dst.at[pl.ds(s * self.half, self.half)], self.msend.at[slot, 0],
                self.mrecv.at[slot, s], self.place.line(self.place.c),
            )
            pl.when(2 * self.place.t + s != self.place.c)(cp.wait_recv)

    def share(self, key, src_of, dst, size, slot):
        g, t, tn = self.place.g, self.place.t, self.place.tn
        rows = slot_rows(g * tn + t, size)
        self.near(src_of(t), dst.at[rows], key)
        for k in range(1, tn):
            to = self.place.other(k)
            cp = remote(src_of(to), dst.at[rows], self.asend.at[slot, k], self.arecv.at[slot, t], {"t": to})
            cp.start()
            self.sends.append(cp)
        self.shared_with[key] = (dst, size, slot)

    def shared(self, key):
        dst, size, slot = self.shared_with[key]
        self.locals_of[key].wait()
        for k in range(1, self.place.tn):
            frm = self.place.other(k)
            ref = dst.at[slot_rows(self.place.g * self.place.tn + frm, size)]
            remote(ref, ref, self.asend.at[slot, k], self.arecv.at[slot, frm], {"t": frm}).wait_recv()

    def share_layer(self, layer):
        depth = self.tri.shape[2]
        base = 1 + 2 * layer
        self.share(("t", layer), lambda to: self.tri.at[layer, to], self.wts[layer], depth, base)
        self.share(("i", layer), lambda to: self.inn.at[layer, to], self.wis[layer], depth, base + 1)
        g = self.place.g
        self.near(self.outer.at[layer], self.wos[layer].at[slot_rows(g, self.outer.shape[1])], ("o", layer))
        here, far = self.proj_copies(layer)
        pl.when(self.moved)(far.start)
        pl.when(jnp.logical_not(self.moved))(here.start)

    def proj_copies(self, layer):
        prows = self.proj.shape[1]
        src = self.proj.at[layer]
        here = pltpu.make_async_copy(src, self.wps[layer].at[slot_rows(self.place.g, prows)], self.psend.at[layer])
        dst = self.wps[layer].at[slot_rows(lax.rem(self.r, self.place.gn), prows)]
        return here, remote(src, dst, self.psend.at[layer], self.precv.at[layer], self.target)

    def proj_ready(self, layer):
        here, far = self.proj_copies(layer)

        @pl.when(self.moved)
        def _():
            far.wait_recv()
            far.wait_send()

        pl.when(jnp.logical_not(self.moved))(here.wait)

    def start(self):
        place, span = self.place, 2 * self.place.tn
        self.move(self.tok, self.tok_o, 0)
        vec_rows = self.vec.shape[0]
        self.share("v", lambda to: self.vec, self.vec_o, vec_rows, 0)
        self.near(self.seg, self.seg_o.at[slot_rows(place.c, 8)], "s")
        for k in range(1, span):
            to = lax.rem(place.c + k, span)
            dst = self.seg_o.at[slot_rows(place.c, 8)]
            cp = remote(self.seg, dst, self.gsend.at[k], self.grecv.at[place.c], place.line(to))
            cp.start()
            self.sends.append(cp)
        self.share_layer(0)
        orders = bit_orders(place)
        self.chunks, slot = [], 0
        tn, depth = place.tn, self.tri.shape[2]
        todo = []
        for layer in range(self.layers):
            todo += [
                [(("t", layer), self.wts[layer], tn * depth)],
                [(("i", layer), self.wis[layer], tn * depth)],
                [
                    (("o", layer), self.wos[layer], self.outer.shape[1]),
                    (("p", layer), self.wps[layer], self.proj.shape[1]),
                ],
            ]
        todo[0].insert(0, ("v", self.vec_o, tn * vec_rows))
        self.keys = [[key for key, _, _ in chunk] for chunk in todo]
        for chunk in todo:
            parts = []
            for _, ref, block in chunk:
                pieces = halves(ref.shape[1]) if ref.shape[1] >= 256 else [pl.ds(0, ref.shape[1])]
                for i, piece in enumerate(pieces):
                    parts.append(Doubling(place, ref, block, piece, orders[i], (self.ssem, self.rsem), slot))
                    slot += 1
            self.chunks.append(parts)
        self.steps = len(place.bits)
        self.turn, self.turns = 0, len(self.chunks) + SKEW * (self.steps - 1)
        self.complete = set()

    def ready(self, i):
        for key in self.keys[i]:
            if key == "v" or key[0] in ("t", "i"):
                self.shared(key)
            elif key[0] == "o":
                self.locals_of[key].wait()
            else:
                self.proj_ready(key[1])

    def tick(self, until=None):
        while self.turn < self.turns and (until is None or self.turn <= until):
            for step in reversed(range(self.steps)):
                i = self.turn - SKEW * step
                if 0 <= i < len(self.chunks):
                    if step == 0:
                        self.ready(i)
                    for part in self.chunks[i]:
                        part.advance(step)
            self.turn += 1
            if until is None:
                break

    def have(self, key):
        i = [key in keys for keys in self.keys].index(True)
        if i not in self.complete:
            self.complete.add(i)
            self.tick(i + SKEW * (self.steps - 1))
            for part in self.chunks[i]:
                part.whole()

    def segments_in(self):
        place, span = self.place, 2 * self.place.tn
        self.locals_of["s"].wait()
        for k in range(1, span):
            frm = lax.rem(place.c + k, span)
            ref = self.seg_o.at[slot_rows(frm, 8)]
            remote(ref, ref, self.gsend.at[k], self.grecv.at[frm], place.line(frm)).wait_recv()

    def finish(self):
        self.tick(self.turns)
        for parts in self.chunks:
            for part in parts:
                part.finish()
        for cp in self.sends:
            cp.wait_send()


def ascend_kernel(
    gn, tn, layers, size,
    tok, cot, seg, vec, tri, inn, outer, proj, ctab, stab, e32, m32, e96, m96,
    gb_o, segcol, segrow, vecs_o, bts_o, bis_o, xs_o, w_o, kept_o,
    w, kept, xs, x_low, cot_low, gb, keep, seg_in, vec_in, vec_wide, bt_wide,
    bufs, group, opening_sems, save_sem, tok_sem,
):
    place = Place(gn, tn)
    opening = Opening(
        place, layers, tok, cot, seg, vec, tri, inn, outer, proj, x_low, cot_low, seg_in, vec_in, w, opening_sems
    )
    opening.barrier()
    opening.start()
    saves = []

    def save(src, dst):
        cp = pltpu.make_async_copy(src, dst, save_sem.at[len(saves)])
        cp.start()
        saves.append(cp)

    opening.tick(0)
    opening.moved_in(tok, x_low, 0)
    xs[0][...] = x_low[...].astype(F32)
    spreads, gathers, stages = [], [], []
    for layer in range(layers):
        ssem, fsem, rsem, cs, cr, ls, lr = group[layer]
        spreads.append(Spread(tn, kept[layer][0], size, ssem, fsem, rsem))
        gathers.append(Gather(tn, *bufs, (cs, cr, ls, lr)))
        stages.append(
            Forward(
                tn, size, xs[layer], tuple(w[k][layer] for k in range(4)),
                (vecs_o.at[layer], bts_o.at[layer], bis_o.at[layer]), (segcol, segrow), (ctab, stab),
                kept[layer], keep,
            )
        )
    stages[0].norm(place.t)
    spreads[0].start()
    opening.tick(1)
    for layer in range(1, layers):
        opening.share_layer(layer)
    opening.segments_in()
    block = segcol.shape[0] // (2 * tn)
    eye = lax.broadcasted_iota(jnp.int32, (block, block), 0) == lax.broadcasted_iota(jnp.int32, (block, block), 1)
    for i in range(2 * tn):
        row = jnp.where(place.h == 0, seg_in[8 * i : 8 * i + 1, :], seg_in[8 * i + 1 : 8 * i + 2, :])
        spot = lax.broadcasted_iota(jnp.int32, (1, block), 1) + i * block
        row = jnp.where(row == 0, -1 - spot, row).astype(F32)
        segrow[:, i * block : (i + 1) * block] = row
        segcol[i * block : (i + 1) * block, :] = jnp.sum(jnp.where(eye, row, 0.0), axis=1, keepdims=True)
    opening.have("v")
    shards = gn * tn
    vec_rows = vec.shape[0]
    vec_wide[...] = vec_in[...].astype(F32)
    lane = lax.broadcasted_iota(jnp.int32, (1, 128), 1)
    for layer in range(layers):

        def line(k):
            return vec_wide[pl.ds(4 * layer + k, shards, stride=vec_rows), :]

        def spread_out(value, place_of, mask):
            return jnp.sum(dot(value.astype(BF16), place_of, NN) * mask, axis=0, keepdims=True)

        thick = line(2)
        parts = [jnp.where(lane // 32 == i, thick, 0.0) for i in range(4)]
        thin = line(3)
        gains = [jnp.where(lane // 32 == i, thin, 0.0) for i in range(2)]
        rows = [spread_out(p, e32[...], m32[...]) for p in parts + gains]
        vecs_o[layer] = jnp.concatenate(
            [rows[2], rows[3], rows[4], rows[5], rows[0] + rows[1]] + [jnp.zeros_like(rows[0])] * 3, axis=0
        )
        bt_wide[...] = spread_out(line(1), e96[...], m96[...])
        wide = bts_o.shape[2] // 3
        for i in range(3):
            start = pl.multiple_of(i * wide * tn + place.t * wide, 128)
            bts_o[layer, :, i * wide : (i + 1) * wide] = bt_wide[:, pl.ds(start, wide)]
        for i in range(gn):
            bis_o[layer, :, i * 128 : (i + 1) * 128] = vec_wide[
                pl.ds((i * tn + place.t) * vec_rows + 4 * layer, 1), :
            ]

    for layer in range(layers):
        stage, spread, gather = stages[layer], spreads[layer], gathers[layer]
        if layer > 0:
            stage.norm(place.t)
            spread.start()
        opening.have(("t", layer))
        save(w[0][layer], w_o[0][layer])
        for i, b in enumerate(arrivals(spread)):
            stage.heads_in(b)
            if i == 1:
                opening.tick()
        if layer + 1 == layers:
            opening.moved_in(cot, cot_low, 1)
            gb[rows_of(place.t, size), :] = cot_low[...]
            ahead = Spread(tn, gb, size, *group[layers][:3])
            ahead.start()
        for i, b in enumerate(far_first(spread)):
            stage.attend(b)
            if i == 1 and layer > 0:
                opening.tick()
        if layer == 0:
            opening.move(cot, cot_low, 1)
        opening.have(("i", layer))
        save(w[1][layer], w_o[1][layer])
        save(kept[layer][0], kept_o[layer][0])
        for i in range(1, 6):
            save(kept[layer][i], kept_o[layer][i])
        for i in range(spread.chips):
            stage.mixer_in(i, 2)
            if i == 0:
                opening.tick()
        save(kept[layer][6], kept_o[layer][6])
        save(kept[layer][7], kept_o[layer][7])
        save(xs[layer], xs_o[layer])
        if layer + 1 == layers:
            for _ in arrivals(ahead):
                pass
            save(gb, gb_o)
        opening.have(("o", layer))
        for k in range(2, 4):
            save(w[k][layer], w_o[k][layer])
        if layer + 1 < layers:
            branch_sums(stage, spread, gather, opening.tick)
            xs[layer + 1][...] = xs[layer][...] + vecs_o[layer, 4:5, :] + keep[...] + gather.total()
            gather.finish()
        spread.finish()
    ahead.finish()
    opening.finish()
    for cp in saves:
        cp.wait()


ANY = pl.BlockSpec(memory_space=pl.ANY)


def constant_tables(span, shards, model):
    angle = np.arange(span, dtype=np.float32)[:, None] * (
        np.float32(10000.0) ** (-(2.0 * np.arange(ROT // 2, dtype=np.float32)) / np.float32(ROT))
    )
    cosine, sine = np.cos(angle).astype(np.float32), np.sin(angle).astype(np.float32)
    none = np.zeros((span, HD - ROT), np.float32)
    reps = 128 // HD
    ctab = np.concatenate([cosine, cosine, none + 1.0] * reps, axis=1)
    stab = np.concatenate([-sine, sine, none] * reps, axis=1)
    return tuple(jnp.asarray(tab, F32) for tab in (ctab, stab))


def placement(piece, shards):
    j, col = np.arange(128)[:, None], np.arange(piece * shards)[None, :]
    put = (j % piece == col % piece) if 128 % piece == 0 else (j == col % piece)
    mask = np.arange(shards)[:, None] == col // piece
    return jnp.asarray(put, BF16), jnp.asarray(mask, F32)


def kept_shapes(length, model, width, units):
    return [
        ((length, model), BF16),
        ((length, width), BF16),
        ((length, width), BF16),
        ((length, width), BF16),
        ((length, width), F32),
        ((length, 128), F32),
        ((length, units), BF16),
        ((length, units), BF16),
    ]


def ascend_call(gn, tn, tokens, cotangent, segments, vec, tri, inn, outer, proj, tables, placing):
    layers = outer.shape[0]
    _, half, model = tokens.shape
    size = 2 * half
    length = size * tn
    depth = tri.shape[2]
    wshapes = [
        (gn * tn * depth, tri.shape[3]), (gn * tn * depth, inn.shape[3]),
        (gn * outer.shape[1], model), (gn * proj.shape[1], model),
    ]
    width, units, chips = wshapes[3][0], wshapes[2][0], tn // 2
    kept = kept_shapes(length, model, width, units)
    dma = pltpu.SemaphoreType.DMA
    outs = [
        (shape((length, model), BF16), ANY),
        (shape((length, 1), F32), VM),
        (shape((1, length), F32), VM),
        (shape((layers, 8, model), F32), VM),
        (shape((layers, 1, 3 * width), F32), VM),
        (shape((layers, 1, units), F32), VM),
    ]
    outs += [(shape((size, model), F32), ANY)] * layers
    for dims in wshapes:
        outs += [(shape(dims, BF16), ANY)] * layers
    for _ in range(layers):
        outs += [(shape(*item), ANY) for item in kept]
    scratch = []
    for dims in wshapes:
        scratch += [pltpu.VMEM(dims, BF16)] * layers
    for _ in range(layers):
        scratch += [pltpu.VMEM(*item) for item in kept]
    scratch += [pltpu.VMEM((size, model), F32)] * layers
    scratch += [
        pltpu.VMEM((size, model), BF16),
        pltpu.VMEM((size, model), BF16),
        pltpu.VMEM((length, model), BF16),
        pltpu.VMEM((size, model), F32),
        pltpu.VMEM((2 * tn * 8, 128), jnp.int32),
        pltpu.VMEM((gn * tn * vec.shape[0], 128), BF16),
        pltpu.VMEM((gn * tn * vec.shape[0], 128), F32),
        pltpu.VMEM((1, 3 * model), F32),
    ]
    scratch += group_buffers(chips, size, model)
    for _ in range(layers + 1):
        scratch += group_sems(chips, tn)
    slots = 1 + 8 * layers
    scratch += [
        dma((slots, gn)), dma((slots, gn)), dma((2 + 3 * layers,)),
        dma((1 + 2 * layers, tn)), dma((1 + 2 * layers, tn)),
        dma((layers,)), dma((layers,)), dma((2, 2)), dma((2, 2)),
        dma((2 * tn,)), dma((2 * tn,)),
    ]
    scratch += [dma((14 * layers,)), dma((1,))]

    def body(*refs):
        refs = list(refs)

        def take(count):
            out, refs[:] = refs[:count], refs[count:]
            return out

        ins = take(14)
        gb_o, segcol, segrow, vecs_o, bts_o, bis_o = take(6)
        xs_o = take(layers)
        w_o = [take(layers) for _ in range(4)]
        kept_o = [take(8) for _ in range(layers)]
        w = [take(layers) for _ in range(4)]
        kept_s = [take(8) for _ in range(layers)]
        xs = take(layers)
        x_low, cot_low, gb, keep, seg_in, vec_in, vec_wide, bt_wide = take(8)
        bufs = take(4)
        group = [take(7) for _ in range(layers + 1)]
        sems = take(11)
        save_sem, tok_sem = take(2)
        ascend_kernel(
            gn, tn, layers, size, *ins, gb_o, segcol, segrow, vecs_o, bts_o, bis_o, xs_o, w_o, kept_o,
            w, kept_s, xs, x_low, cot_low, gb, keep, seg_in, vec_in, vec_wide, bt_wide, bufs, group, sems,
            save_sem, tok_sem,
        )

    return pl.pallas_call(
        body,
        out_shape=tuple(o for o, _ in outs),
        in_specs=[ANY] * 8 + [VM] * 6,
        out_specs=tuple(spec for _, spec in outs),
        scratch_shapes=scratch,
        compiler_params=params_of(2),
        name="ascend",
    )(tokens, cotangent, segments, vec, tri, inn, outer, proj, *tables, *placing)


class Halving:
    def __init__(self, place, acc, inbox, block, cols, order, sems, slot):
        self.place, self.acc, self.inbox, self.block, self.cols = place, acc, inbox, block, cols
        self.send, self.recv, self.slot = sems[0], sems[1], slot
        self.plan, index, base = [], 0, 0
        for bit, runs in reversed(runs_by_step(place, order)):
            entry = []
            for start, count in runs:
                entry.append((bit, start, count, index, base))
                index += 1
                base += count
            self.plan.append(entry)

    def copy(self, bit, start, count, index, base):
        rows = pl.ds(pl.multiple_of(flip(start, bit) * self.block, self.block), count * self.block)
        return remote(
            self.acc.at[rows, self.cols],
            self.inbox.at[pl.ds(base * self.block, count * self.block), self.cols],
            self.send.at[self.slot, index],
            self.recv.at[self.slot, index],
            self.place.group(flip(self.place.g, bit)),
        )

    def advance(self, step):
        if step > 0:
            for item in self.plan[step - 1]:
                self.copy(*item).wait_recv()
                _, start, count, _, base = item

                def add(i, carry):
                    rows = pl.ds(pl.multiple_of((start + i) * self.block, self.block), self.block)
                    came = pl.ds(pl.multiple_of((base + i) * self.block, self.block), self.block)
                    value = self.acc[rows, self.cols].astype(F32) + self.inbox[came, self.cols].astype(F32)
                    self.acc[rows, self.cols] = value.astype(BF16)
                    return carry

                lax.fori_loop(0, count, add, 0)
        if step < len(self.plan):
            for item in self.plan[step]:
                self.copy(*item).start()

    def finish(self):
        for entry in self.plan:
            for item in entry:
                self.copy(*item).wait_send()

class Slots:
    def __init__(self, ref, first, size):
        self.ref, self.first, self.size = ref, first, size

    def rows(self, slot):
        return slot_rows(self.first + slot, self.size)

    @property
    def at(self):
        return _SlotRefs(self)

    def __getitem__(self, slot):
        return self.ref[self.rows(slot), :]


class _SlotRefs:
    def __init__(self, slots):
        self.slots = slots

    def __getitem__(self, slot):
        return self.slots.ref.at[self.slots.rows(slot)]


class Reducing:
    def __init__(self, place, layers, accs, boxes, outs, sems):
        self.place, self.layers = place, layers
        self.accs, self.boxes = accs, boxes
        self.cross, self.proj_o, self.outer_o = outs[:2], outs[2], outs[3]
        self.hs, self.hr, self.cs, self.cr, self.ps, self.pr, self.os = sems
        self.target, self.source, self.r, self.q = proj_places(place)
        self.moved = self.q != self.r
        orders = bit_orders(place)
        self.parts, slot = {}, 0
        for layer in range(layers):
            for kind in range(4):
                acc = accs[kind][layer]
                parts = []
                for k, cols in enumerate(halves(acc.shape[1])):
                    box = boxes[kind].at[layer]
                    block = acc.shape[0] // place.gn
                    parts.append(Halving(place, acc, box, block, cols, orders[k], (self.hs, self.hr), slot))
                    slot += 1
                self.parts[kind, layer] = parts
        self.steps = len(place.bits) + 1
        self.taken = {key: 0 for key in self.parts}

    def advance(self, kind, layer):
        step = self.taken[kind, layer]
        self.taken[kind, layer] = step + 1
        for part in self.parts[kind, layer]:
            part.advance(step)
        if step == self.steps - 1:
            self.owned(kind, layer)

    def own_rows(self, kind, layer, index, pieces):
        acc = self.accs[kind][layer]
        rows = acc.shape[0] // pieces
        return acc.at[slot_rows(index, rows)]

    def cross_copy(self, kind, layer, k):
        place = self.place
        to = place.other(k)
        src = self.own_rows(kind, layer, place.g * place.tn + to, place.gn * place.tn)
        dst = self.cross[kind].at[layer, place.t]
        return remote(src, dst, self.cs.at[kind, layer, k], self.cr.at[kind, layer, place.t], {"t": to})

    def proj_copies(self, layer):
        src = self.own_rows(3, layer, self.place.g, self.place.gn)
        here = pltpu.make_async_copy(src, self.proj_o.at[layer], self.ps.at[layer])
        return here, remote(src, self.proj_o.at[layer], self.ps.at[layer], self.pr.at[layer], self.source)

    def own_copy(self, kind, layer):
        place = self.place
        if kind == 2:
            src, dst = self.own_rows(2, layer, place.g, place.gn), self.outer_o.at[layer]
        else:
            src = self.own_rows(kind, layer, place.g * place.tn + place.t, place.gn * place.tn)
            dst = self.cross[kind].at[layer, place.t]
        return pltpu.make_async_copy(src, dst, self.os.at[kind, layer])

    def owned(self, kind, layer):
        if kind < 3:
            self.own_copy(kind, layer).start()
        if kind < 2:
            for k in range(1, self.place.tn):
                self.cross_copy(kind, layer, k).start()
        if kind == 3:
            here, far = self.proj_copies(layer)
            pl.when(self.moved)(far.start)
            pl.when(jnp.logical_not(self.moved))(here.start)

    def finish(self):
        for (kind, layer), parts in self.parts.items():
            for part in parts:
                part.finish()
            if kind < 3:
                self.own_copy(kind, layer).wait()
            if kind < 2:
                for k in range(1, self.place.tn):
                    frm = self.place.other(k)
                    ref = self.cross[kind].at[layer, frm]
                    remote(
                        ref, ref, self.cs.at[kind, layer, k], self.cr.at[kind, layer, frm], {"t": frm}
                    ).wait_recv()
                    self.cross_copy(kind, layer, k).wait_send()
            if kind == 3:
                here, far = self.proj_copies(layer)
                pl.when(self.moved)(far.wait)
                pl.when(jnp.logical_not(self.moved))(here.wait)


FIRST = {
    "outer": ((2, 0), (3, 0)),
    "inner": ((1, 0),),
    "s1": ((2, 0), (3, 0)),
    "triple": ((0, 0), (1, 0)),
    "sum": ((2, 0), (3, 0)),
}
LATER = {
    "spread": ((0, 1),),
    "arrived": ((2, 1), (3, 1), (0, 1), (1, 1)),
    "outer": ((2, 0), (3, 0)),
    "inner": ((1, 0), (0, 1), (1, 1)),
    "s1": ((2, 0), (3, 0)),
    "s3": ((2, 0), (3, 0), (1, 0)),
    "triple": ((0, 0), (1, 0)),
}


def descend_kernel(
    gn, tn, layers, size,
    grads, segcol, segrow, vecs, ctab, stab, xs, ws, kepts,
    out_o, grad_o, flat_o, triple_o, inner_o, proj_o, outer_o,
    w, kept, dy, x, gb, do, dt, dk, dv, keep, dbt, dbi, bufs, accs, boxes, flatbox,
    group, reduce_sems, load_sem, ms, mr, fs, fr,
):
    place = Place(gn, tn)
    g, t, c = place.g, place.t, place.c
    wt, wi, wo, wp = w
    n, q, k, v, o, lse, gact, gp = kept
    chips = tn // 2
    width, units, model = q.shape[1], gact.shape[1], dy.shape[1]
    heads = width // HD
    dq, dh, du = o, gact, gp
    loads = {}

    def load(layer, names):
        for name in names:
            if name == "x":
                src, dst = xs[layer], x
            elif name == "cot":
                src, dst = grads, gb
            elif name[0] == "w":
                i = int(name[1])
                src, dst = ws[i][layer], w[i]
            else:
                i = int(name[1])
                src, dst = kepts[layer][i], kept[i]
            cp = pltpu.make_async_copy(src, dst, load_sem.at[len(loads)])
            cp.start()
            loads[layer, name] = cp

    waited = set()

    def need(layer, names):
        for name in names:
            if (layer, name) not in waited:
                waited.add((layer, name))
                loads[layer, name].wait()

    last = layers - 1
    load(last, ["w2", "w3", "k6", "k4", "cot", "k7", "k5", "w1", "k0", "k1", "k2", "k3", "w0", "x"])
    reducing = Reducing(place, layers, accs, boxes, (triple_o, inner_o, proj_o, outer_o), reduce_sems)
    line_barrier(place, (reducing.target, reducing.moved))
    half = out_o.shape[1]

    def hop(src, dst, slot, s):
        to = 2 * t + s
        part = src.at[pl.ds(s * half, half)]
        near = pltpu.make_async_copy(part, dst.at[place.h], ms.at[slot, s])
        far = remote(part, dst.at[place.h], ms.at[slot, s], mr.at[slot, place.h], place.line(to))
        return to == c, near, far

    def move(src, dst, slot):
        for s in range(2):
            stays, near, far = hop(src, dst, slot, s)
            pl.when(stays)(near.start)
            pl.when(jnp.logical_not(stays))(far.start)

    def moved_in(src, dst, slot):
        for s in range(2):
            stays, near, far = hop(src, dst, slot, s)
            pl.when(stays)(near.wait)
            pl.when(jnp.logical_not(stays))(far.wait_send)
        for i in range(2):
            cp = remote(
                src.at[pl.ds(0, half)], dst.at[i], ms.at[slot, 0], mr.at[slot, i], place.line(c)
            )
            pl.when(i * tn + c // 2 != c)(cp.wait_recv)

    exchanges = [("g", bit) for bit in place.bits] + [("t", 1 << i) for i in range(tn.bit_length() - 1)]

    def exchange(layer, i):
        kind, bit = exchanges[i]
        to = place.group(flip(g, bit)) if kind == "g" else {"t": flip(t, bit)}
        return remote(flat_o.at[layer], flatbox.at[layer, i], fs.at[layer, i], fr.at[layer, i], to)

    def flat_turn(layer, i):
        if i > 0:
            exchange(layer, i - 1).wait()
            flat_o[layer] += flatbox[layer, i - 1]
        if i < len(exchanges):
            exchange(layer, i).start()

    masks = head_masks(width, BF16)
    lane = lax.broadcasted_iota(jnp.int32, (1, 128), 1)
    up = place.t // 2 >= (chips + 1) // 2

    def pair(qb, kb):
        qrows, krows = rows_of(qb, size), rows_of(kb, size)
        queries, keys, vals = q[qrows, :], k[krows, :], v[krows, :]
        grad = do[qrows, :]
        side = lse[qrows, :]
        bias = pair_bias(qb, kb, size, segcol, segrow)
        dq_new = jnp.zeros((size, width), F32)
        dk_new = jnp.zeros((size, width), F32)
        dv_new = jnp.zeros((size, width), F32)
        for h in range(heads):
            qh, gh = queries * masks[h], grad * masks[h]
            total = jnp.sum(jnp.where(lane == h, side, 0.0), axis=1, keepdims=True)
            delta = jnp.sum(jnp.where(lane == 64 + h, side, 0.0), axis=1, keepdims=True)
            p = jnp.exp(dot(qh, keys, NT) + bias - total)
            ds = (p * (dot(gh, vals, NT) - delta)).astype(BF16)
            dv_new = dv_new + dot(p.astype(BF16), gh, TN)
            dk_new = dk_new + dot(ds, qh, TN)
            dq_new = dq_new + dot(ds, keys * masks[h], NN)
        dq[qrows, :] += dq_new
        dk[krows, :] += dk_new
        dv[krows, :] += dv_new

    def columns(count, tile, body):
        def step(j, carry):
            body(rows_of(j, tile))
            return carry

        lax.fori_loop(0, count // tile, step, 0)

    need(last, ["w2", "w3", "k6", "k4"])
    top = Spread(tn, gb, size, *group[layers][:3])
    room, spare = accs[2][0], accs[1][0]
    top_gather = Gather(
        tn, bufs[0], Slots(room, 0, size), bufs[2], Slots(room, chips, size), tuple(group[layers][3:])
    )
    stage_top = Forward(
        tn, size, x, (wt, wi, wo, wp), (vecs.at[last], None, None), (segcol, segrow), (ctab, stab), kept, keep
    )
    branch_sums(stage_top, top, top_gather)
    need(last, ["cot"])
    dy[...] = gb[rows_of(t, size), :].astype(F32)
    flat_o[...] = jnp.zeros_like(flat_o)
    out_in = spare.at[pl.ds(0, size)]

    def give_output():
        need(last, ["x"])
        out_in[...] = (x[...] + vecs[last, 4:5, :] + keep[...] + top_gather.total()).astype(BF16)
        top_gather.finish()
        move(out_in, out_o, 0)

    for layer in reversed(range(layers)):
        flat = flat_o.at[layer]
        vec = vecs.at[layer]
        dwt, dwi, dwo, dwp = (accs[i][layer] for i in range(4))
        ssem, fsem, rsem, cs, cr, ls, lr = group[layer]
        spread = Spread(tn, gb, size, ssem, fsem, rsem)
        gather = Gather(tn, *bufs, (cs, cr, ls, lr))
        zc, co = spread.zc, spread.co

        def ticks(where, layer=layer):
            for kind, late in (FIRST if layer == last else LATER).get(where, ()):
                if layer + late < layers and reducing.taken[kind, layer + late] < reducing.steps:
                    reducing.advance(kind, layer + late)

        own = dy[...].astype(BF16)
        if layer < last:
            gb[rows_of(t, size), :] = own
            spread.start()
        flat[4:5, :] = jnp.sum(own.astype(F32), axis=0, keepdims=True)
        dbt[...] = jnp.zeros_like(dbt)
        dbi[...] = jnp.zeros_like(dbi)
        dk[...] = jnp.zeros_like(dk)
        dv[...] = jnp.zeros_like(dv)
        ticks("spread")
        if layer < last:
            flat_turn(layer + 1, 0)
        for count, b in enumerate(arrivals(spread) if layer < last else range(chips)):
            need(layer, ["w3", "k4", "w2", "k7", "k5"])
            rows = rows_of(b, size) if layer < last else rows_of(b, 2 * size)
            grad = gb[rows, :]
            heads_grad = dot(grad, wp[...], NT).astype(BF16)
            do[rows, :] = heads_grad
            prod = heads_grad.astype(F32) * o[rows, :]
            side = lse[rows, :]
            for h in range(heads):
                delta = jnp.sum(prod * masks[h].astype(F32), axis=1, keepdims=True)
                side = jnp.where(lane == 64 + h, delta, side)
            lse[rows, :] = side

            def unit(cols):
                d = (dot(grad, wo[cols, :], NT) * gp[rows, cols].astype(F32)).astype(BF16)
                du[rows, cols] = d
                dbi[0:1, cols] += jnp.sum(d.astype(F32), axis=0, keepdims=True)

            columns(units, TILE, unit)
            if layer < last:
                flat_turn(layer + 1, count + 1)
            if count == 1:
                ticks("near")
        ticks("arrived")
        need(layer, ["k6"])
        if layer < last:
            spread.finish()
            if layer == last - 1:
                moved_in(out_in, out_o, 0)

        def grad_outer(cols):
            dwo[cols, :] = dot(gact[:, cols], gb[...], TN).astype(BF16)

        columns(units, TILE, grad_outer)

        def grad_proj(cols):
            dwp[cols, :] = dot(o[:, cols].astype(BF16), gb[...], TN).astype(BF16)

        columns(width, TILE, grad_proj)
        if layer == last:
            give_output()
        ticks("outer")
        if layer < last:
            flat_turn(layer + 1, len(exchanges))
        need(layer, ["w1", "k0"])
        if layer > 0:
            load(layer - 1, ["w2", "w3"])
        dq[...] = jnp.zeros_like(dq)

        def back_mixer(cols):
            d = dot(du[...], wi[cols, :], NT)
            flat[2:3, cols] = jnp.sum(d * n[:, cols].astype(F32), axis=0, keepdims=True)
            flat[3:4, cols] = jnp.sum(d, axis=0, keepdims=True)
            dh[:, cols] = (d * vec[2:3, cols]).astype(BF16)

        columns(model, TILE, back_mixer)

        def grad_inner(cols):
            h2 = (n[:, cols].astype(F32) * vec[2:3, cols] + vec[3:4, cols]).astype(BF16)
            dwi[cols, :] = dot(h2, du[...], TN).astype(BF16)

        columns(model, TILE, grad_inner)
        ticks("inner")
        if layer > 0:
            load(layer - 1, ["w1", "k7"])
        need(layer, ["k1", "k2", "k3", "w0"])

        for stage in range(tn):
            pivot = jnp.where(up, stage, tn - 1 - stage)

            def step(j, carry):
                pair(jnp.where(up, pivot + j, pivot), jnp.where(up, pivot, pivot - j))
                return carry

            lax.fori_loop(0, tn - stage, step, 0)
            rows = rows_of(pivot, size)
            cos, sine = ctab[rows, :], stab[rows, :]
            dt[rows, 0:width] = turn(dq[rows, :] * (1.0 / math.sqrt(HD)), cos, sine, -1.0).astype(BF16)
            dt[rows, width : 2 * width] = turn(dk[rows, :], cos, sine, -1.0).astype(BF16)
            dt[rows, 2 * width : 3 * width] = dv[rows, :].astype(BF16)
            block = dt[rows, :]
            dbt[...] += jnp.sum(block.astype(F32), axis=0, keepdims=True)
            chip, core = pivot // 2, lax.rem(pivot, 2)

            def back(cols):
                d = dot(block, wt[cols, :], NT)
                flat[0:1, cols] += jnp.sum(d * n[rows, cols].astype(F32), axis=0, keepdims=True)
                flat[1:2, cols] += jnp.sum(d, axis=0, keepdims=True)
                value = dh[rows, cols].astype(F32) + d * vec[0:1, cols]

                @pl.when(core != co)
                def _():
                    gather.tocore[chip, :, cols] = value.astype(BF16)

                @pl.when((core == co) & (chip != zc))
                def _():
                    gather.toici[chip, :, cols] = value.astype(BF16)

                @pl.when(pivot == t)
                def _():
                    keep[:, cols] = value

            columns(model, TILE, back)

            @pl.when(core != co)
            def _():
                gather.send_core(chip)

            if stage % 2 == 1:

                @pl.when(chip != zc)
                def _():
                    gather.send_link(chip)

            ticks(f"s{stage}")

        wide = width
        for i in range(3):
            start = pl.multiple_of(t * wide, 128)
            flat[5 + i : 6 + i, pl.ds(start, wide)] = dbt[:, i * wide : (i + 1) * wide]
        for i in range(gn):
            row, start = divmod(i * tn * 128, model)
            flat[8 + row : 9 + row, pl.ds(pl.multiple_of(start + t * 128, 128), 128)] = dbi[:, i * 128 : (i + 1) * 128]
        if layer > 0:
            load(layer - 1, ["w0", "k1", "k2", "k3", "k4", "k5", "k6"])

        def grad_triple(cols):
            h1 = (n[:, cols].astype(F32) * vec[0:1, cols] + vec[1:2, cols]).astype(BF16)
            dwt[cols, :] = dot(h1, dt[...], TN).astype(BF16)

        columns(model, TILE, grad_triple)
        if layer > 0:
            load(layer - 1, ["k0"])
        ticks("triple")
        if layer == 0:
            flat_turn(0, 0)
        need(layer, ["x"])
        own_n, inverse = norm_stats(x[...])
        e = keep[...] + gather.total()
        inner = e - jnp.mean(e, axis=-1, keepdims=True) - own_n * jnp.mean(e * own_n, axis=-1, keepdims=True)
        dy[...] = dy[...] + inner * inverse
        if layer > 0:
            load(layer - 1, ["x"])
        gather.finish()
        ticks("sum")

    low = gb.at[pl.ds(0, size)]
    low[...] = dy[...].astype(BF16)
    move(low, grad_o, 1)
    rest = [(0, 0), (2, 0), (3, 0), (0, 0), (1, 0), (0, 0)]
    for i, (kind, layer) in enumerate(rest):
        if i + 1 <= len(exchanges):
            flat_turn(0, i + 1)
        reducing.advance(kind, layer)
    for layer in reversed(range(layers)):
        for kind in range(4):
            while reducing.taken[kind, layer] < reducing.steps:
                reducing.advance(kind, layer)
    reducing.finish()
    moved_in(low, grad_o, 1)


def descend_call(gn, tn, grads, segcol, segrow, vecs, tables, xs, ws, kepts):
    layers = len(xs)
    size, model = xs[0].shape
    length = size * tn
    shapes = [ws[i][0].shape for i in range(4)]
    width, units, chips = shapes[3][0], shapes[2][0], tn // 2
    kept = kept_shapes(length, model, width, units)
    dma = pltpu.SemaphoreType.DMA
    shard = shapes[0][0] // (gn * tn)
    prows, orows = shapes[3][0] // gn, shapes[2][0] // gn
    exchanges = (gn * tn).bit_length() - 1
    outs = (
        shape((2, size // 2, model), BF16),
        shape((2, size // 2, model), BF16),
        shape((layers, 16, model), F32),
        shape((layers, tn, shard, 3 * width), BF16),
        shape((layers, tn, shard, units), BF16),
        shape((layers, prows, model), BF16),
        shape((layers, orows, model), BF16),
    )
    scratch = [pltpu.VMEM(dims, BF16) for dims in shapes]
    scratch += [pltpu.VMEM(*item) for item in kept]
    scratch += [
        pltpu.VMEM((size, model), F32),
        pltpu.VMEM((size, model), F32),
        pltpu.VMEM((length, model), BF16),
        pltpu.VMEM((length, width), BF16),
        pltpu.VMEM((length, 3 * width), BF16),
        pltpu.VMEM((length, width), F32),
        pltpu.VMEM((length, width), F32),
        pltpu.VMEM((size, model), F32),
        pltpu.VMEM((1, 3 * width), F32),
        pltpu.VMEM((1, units), F32),
    ]
    scratch += group_buffers(chips, size, model)
    for dims in shapes:
        scratch += [pltpu.VMEM(dims, BF16)] * layers
    scratch += [pltpu.VMEM((layers, (gn - 1) * dims[0] // gn, dims[1]), BF16) for dims in shapes]
    scratch += [pltpu.VMEM((layers, exchanges, 16, model), F32)]
    for _ in range(layers + 1):
        scratch += group_sems(chips, tn)
    slots = 8 * layers
    scratch += [
        dma((slots, gn)), dma((slots, gn)), dma((2, layers, tn)), dma((2, layers, tn)), dma((layers,)), dma((layers,)),
        dma((3, layers)),
        dma((14 * layers,)), dma((2, 2)), dma((2, 2)), dma((layers, exchanges)), dma((layers, exchanges)),
    ]

    def body(*refs):
        refs = list(refs)

        def take(count):
            out, refs[:] = refs[:count], refs[count:]
            return out

        ins = take(6)
        x_in = take(layers)
        w_in = [take(layers) for _ in range(4)]
        kept_in = [take(8) for _ in range(layers)]
        results = take(7)
        w, kept_s = take(4), take(8)
        work = take(10)
        bufs = take(4)
        accs = [take(layers) for _ in range(4)]
        boxes = take(4)
        flatbox = take(1)[0]
        group = [take(7) for _ in range(layers + 1)]
        reduce_sems = take(7)
        descend_kernel(
            gn, tn, layers, size, *ins, x_in, w_in, kept_in, *results, w, kept_s, *work, bufs, accs, boxes,
            flatbox, group, reduce_sems, *take(5),
        )

    flat_ws = [ws[i][layer] for i in range(4) for layer in range(layers)]
    flat_kept = [ref for layer in range(layers) for ref in kepts[layer]]
    return pl.pallas_call(
        body,
        out_shape=outs,
        in_specs=[ANY] + [VM] * 5 + [ANY] * (layers + len(flat_ws) + len(flat_kept)),
        out_specs=(ANY, ANY, VM, ANY, ANY, ANY, ANY),
        scratch_shapes=scratch,
        compiler_params=params_of(3),
        name="descend",
    )(grads, segcol, segrow, vecs, *tables, *xs, *flat_ws, *flat_kept)


GROUPS = ("dp", "h")
EVERY = ("dp", "h", "t")


def to_group(tn, blocks):
    h, t = lax.axis_index("h"), lax.axis_index("t")
    count = 2 * tn
    parity = lax.rem(t, 2)
    got = []
    for j in range(2):
        moves = [(c, ((c + j) % 2) * tn + c // 2) for c in range(count)]
        piece = jnp.where(lax.rem(parity + j, 2) == 0, blocks[0], blocks[1])
        got.append(lax.ppermute(piece, ("h", "t"), moves))
    low = jnp.where(h == 0, got[0], got[1])
    high = jnp.where(h == 0, got[1], got[0])
    return jnp.concatenate([low, high], axis=0)


def from_group(tn, rows):
    h, t = lax.axis_index("h"), lax.axis_index("t")
    count = 2 * tn
    parity = lax.rem(t, 2)
    size = rows.shape[0] // 2
    got = []
    for j in range(2):
        moves = [(((c + j) % 2) * tn + c // 2, c) for c in range(count)]
        piece = jnp.where(lax.rem(h + j, 2) == 0, rows[:size], rows[size:])
        got.append(lax.ppermute(piece, ("h", "t"), moves))
    first = jnp.where(parity == 0, got[0], got[1])
    second = jnp.where(parity == 0, got[1], got[0])
    return jnp.stack([first, second], axis=0)


def proj_moves(gn, tn):
    return [(r, (r % gn) * tn + r // gn) for r in range(gn * tn)]


def slice_columns(weight, gn, tn):
    rows, cols = weight.shape
    return weight.reshape(rows, gn, tn, cols // (gn * tn)).transpose(2, 0, 1, 3).reshape(tn, rows, cols // tn)


def slice_triple(weight, tn):
    rows, cols = weight.shape
    return weight.reshape(rows, 3, tn, cols // (3 * tn)).transpose(2, 0, 1, 3).reshape(tn, rows, cols // tn)


def gather_weights(gn, tn, triple, proj, inner, outer):
    def spread(parts):
        moved = lax.all_to_all(parts, "t", 0, 0, tiled=True)
        whole = lax.all_gather(moved.reshape(-1, moved.shape[-1]), GROUPS, axis=0, tiled=True)
        return whole

    wt = spread(slice_triple(triple, tn))
    wi = spread(slice_columns(inner, gn, tn))
    wo = lax.all_gather(outer, GROUPS, axis=0, tiled=True)
    wp = lax.all_gather(lax.ppermute(proj, EVERY, proj_moves(gn, tn)), GROUPS, axis=0, tiled=True)
    return wt, wi, wo, wp


def reduce_weights(gn, tn, dwt, dwi, dwo, dwp):
    def back(parts):
        mine = lax.psum_scatter(parts, GROUPS, scatter_dimension=0, tiled=True)
        rows = mine.shape[0] // tn
        return lax.all_to_all(mine.reshape(tn, rows, -1), "t", 0, 0, tiled=True).astype(F32)

    triple = back(dwt)
    rows = triple.shape[1]
    triple = triple.reshape(tn, rows, 3, -1).transpose(1, 2, 0, 3).reshape(rows, -1)
    inner = back(dwi)
    inner = inner.reshape(tn, rows, gn, -1).transpose(1, 2, 0, 3).reshape(rows, -1)
    outer = lax.psum_scatter(dwo, GROUPS, scatter_dimension=0, tiled=True).astype(F32)
    proj = lax.psum_scatter(dwp, GROUPS, scatter_dimension=0, tiled=True)
    proj = lax.ppermute(proj, EVERY, [(b, a) for a, b in proj_moves(gn, tn)]).astype(F32)
    return triple, proj, inner, outer


def per_device(
    gn, tn,
    tokens, segments, cotangent, triple_weight, triple_bias, proj_weight, proj_bias, inner_weight, inner_bias,
    outer_weight, outer_bias, first_gain, first_shift, second_gain, second_shift,
):
    layers = triple_weight.shape[0]
    model = tokens.shape[2]
    span = tokens.shape[1] * 2 * tn
    h, t = lax.axis_index("h"), lax.axis_index("t")
    device = (lax.axis_index("dp") * 2 + h) * tn + t
    shards = gn * tn
    heads_wide = model // tn
    units = outer_weight.shape[1] * gn

    rows = triple_weight.shape[1]
    block = tokens.shape[1]
    tables = constant_tables(span, shards, model)
    direct = rows % 16 == 0 and block == 128 and layers * 4 <= 16 and units == model
    if direct:
        head = jnp.stack(
            [
                inner_bias,
                jnp.pad(triple_bias, ((0, 0), (0, 128 - triple_bias.shape[1]))),
                jnp.concatenate([proj_bias, outer_bias, first_gain, first_shift], axis=1),
                jnp.pad(jnp.concatenate([second_gain, second_shift], axis=1), ((0, 0), (0, 64))),
            ],
            axis=1,
        ).reshape(4 * layers, 128)
        opened = ascend_call(
            gn, tn, tokens, cotangent, jnp.pad(segments, ((0, 6), (0, 0))),
            jnp.pad(head, ((0, 16 - 4 * layers), (0, 0))),
            triple_weight.reshape(layers, rows, 3, tn, -1).transpose(0, 3, 1, 2, 4).reshape(layers, tn, rows, -1),
            inner_weight.reshape(layers, rows, gn, tn, -1).transpose(0, 3, 1, 2, 4).reshape(layers, tn, rows, -1),
            outer_weight, proj_weight, tables,
            placement(model // shards, shards) + placement(3 * model // shards, shards),
        )
        opened = list(opened)
        grad_all, segcol, segrow, vecs, _, _ = opened[:6]
        opened = opened[6:]
        inputs = opened[:layers]
        weights = [tuple(opened[layers + k * layers + layer] for k in range(4)) for layer in range(layers)]
        kept = [opened[5 * layers + 8 * i : 5 * layers + 8 * (i + 1)] for i in range(layers)]
        output, tokens_grad, summed, triple, inner, proj, outer = descend_call(
            gn, tn, grad_all, segcol, segrow, vecs, tables, inputs,
            [[weights[layer][k] for layer in range(layers)] for k in range(4)], kept,
        )
        summed = summed.reshape(layers, -1)
        triple = triple.reshape(layers, tn, rows, 3, -1).transpose(0, 2, 3, 1, 4).reshape(layers, rows, -1).astype(F32)
        inner = inner.reshape(layers, tn, rows, gn, -1).transpose(0, 2, 3, 1, 4).reshape(layers, rows, -1).astype(F32)
        proj, outer = proj.astype(F32), outer.astype(F32)
    else:
        small = (triple_bias, inner_bias, proj_bias, outer_bias, first_gain, first_shift, second_gain, second_shift)
        starts = [0]
        for item in small:
            starts.append(starts[-1] + item.shape[1])
        packed = jnp.concatenate(small, axis=1)
        x = to_group(tn, tokens).astype(F32)
        cot = to_group(tn, cotangent).astype(F32)
        segs_all = lax.all_gather(segments, ("h", "t"), axis=1, tiled=True)
        everything = lax.all_gather(packed[None], EVERY, axis=0, tiled=True).astype(F32)
        weights = [
            gather_weights(
                gn, tn, triple_weight[layer], proj_weight[layer], inner_weight[layer], outer_weight[layer]
            )
            for layer in range(layers)
        ]
        segs = jnp.where(h == 0, segs_all[0], segs_all[1])
        segs = jnp.where(segs == 0, -1 - jnp.arange(span, dtype=jnp.int32), segs).astype(F32)
        tables = (segs[:, None], segs[None, :]) + tables

        def vector(layer, i):
            return everything[:, layer, starts[i] : starts[i + 1]].reshape(-1)

        vecs, inputs, kept = [], [], []
        for layer in range(layers):
            bt = lax.dynamic_index_in_dim(vector(layer, 0).reshape(3, tn, heads_wide), t, 1, keepdims=False)
            bi = lax.dynamic_index_in_dim(vector(layer, 1).reshape(gn, tn, -1), t, 1, keepdims=False)
            zero = jnp.zeros((model,), F32)
            vecs.append(
                jnp.stack(
                    [vector(layer, 4), vector(layer, 5), vector(layer, 6), vector(layer, 7)]
                    + [vector(layer, 2) + vector(layer, 3), zero, zero, zero]
                )
            )
            inputs.append(x)
            x, *saved = forward_layer(
                tn, x, weights[layer], vecs[layer], bt.reshape(1, -1), bi.reshape(1, -1), tables
            )
            kept.append(saved)
        output = x.astype(BF16)
        grad = cot
        mats, flats = [None] * layers, [None] * layers
        for layer in reversed(range(layers)):
            grad, dwt, dwi, dwo, dwp, dvec, dbt, dbi = backward_layer(
                tn, grad, inputs[layer], weights[layer], vecs[layer], tables, kept[layer]
            )
            mats[layer] = reduce_weights(gn, tn, dwt, dwi, dwo, dwp)
            part = lax.dynamic_update_slice(
                jnp.zeros((3, tn, heads_wide), F32), dbt.reshape(3, 1, heads_wide), (0, t, 0)
            )
            side = lax.dynamic_update_slice(
                jnp.zeros((gn, tn, units // gn), F32), dbi.reshape(gn, 1, units // gn), (0, t, 0)
            )
            flats[layer] = jnp.concatenate([dvec[:5].reshape(-1), part.reshape(-1), side.reshape(-1)])
        output, tokens_grad = from_group(tn, output), from_group(tn, grad.astype(BF16))
        triple, proj, inner, outer = (jnp.stack([m[k] for m in mats]) for k in range(4))
        summed = lax.psum(jnp.stack(flats), EVERY)

    def own(start, length):
        piece = length // shards
        return lax.dynamic_slice_in_dim(summed, start + device * piece, piece, 1)

    base = 5 * model
    bias_sum = own(4 * model, model)
    return (
        output,
        tokens_grad,
        triple,
        own(base, 2 * model),
        own(base + 2 * model, model),
        proj,
        bias_sum,
        inner,
        own(base + 3 * model, units * tn),
        outer,
        bias_sum,
        own(0, model),
        own(model, model),
        own(2 * model, model),
        own(3 * model, model),
    )


def solution(mesh):
    dp, ctx = mesh.shape["dp"], mesh.shape["ctx"]
    tn = ctx // 2
    gn = 2 * dp
    fine = Mesh(mesh.devices.reshape(dp, 2, tn), EVERY)
    seq = P("dp", ("h", "t"), None)
    mat = P(None, EVERY, None)
    row = P(None, EVERY)
    in_specs = (seq, P("dp", ("h", "t")), seq, mat, row, mat, row, mat, row, mat, row, row, row, row, row)
    out_specs = (seq, seq, mat, row, row, mat, row, mat, row, mat, row, row, row, row, row)
    return jax.shard_map(
        functools.partial(per_device, gn, tn), mesh=fine, in_specs=in_specs, out_specs=out_specs, check_vma=False
    )
```
